32 devices in a mesh: tp: 2 (over x), cp: 16 (over z, y, core).
Axes of the slice: x: 2, y: 2, z: 4, core: 2. Of those that a mesh axis runs over, the one named last changes fastest.
Arguments:
- residual: bfloat16 [4096, 1024], P('cp'), may hold values from -6 to 6
- cotangent: bfloat16 [4096, 1024], P('cp'), may hold values from -6 to 6
- span_order: int32 [32], replicated, may hold values from 0 to 31, as said below
- positions: int32 [4096], P('cp'), may hold values from 0 to 4096, as said below
- attn_gain: float32 [1024], replicated, may hold values from 0.5 to 1.5
- query_weight: bfloat16 [1024, 2048], P(None, 'tp'), may hold values from -0.1875 to 0.1875
- key_weight: bfloat16 [1024, 1024], P(None, 'tp'), may hold values from -0.1875 to 0.1875
- value_weight: bfloat16 [1024, 1024], P(None, 'tp'), may hold values from -0.1875 to 0.1875
- query_gain: float32 [128], replicated, may hold values from 0.25 to 1.75
- key_gain: float32 [128], replicated, may hold values from 0.25 to 1.75
- out_weight: bfloat16 [2048, 1024], P('tp'), may hold values from -0.5 to 0.5
- mlp_gain: float32 [1024], replicated, may hold values from 0.5 to 1.5
- gate_weight: bfloat16 [1024, 3072], P(None, 'tp'), may hold values from -0.1875 to 0.1875
- up_weight: bfloat16 [1024, 3072], P(None, 'tp'), may hold values from -0.1875 to 0.1875
- down_weight: bfloat16 [3072, 1024], P('tp'), may hold values from -0.109375 to 0.109375
Outputs:
- layer_out: bfloat16 [4096, 1024], P('cp')
- residual_grad: float32 [4096, 1024], P('cp')
- attn_gain_grad: float32 [1024], replicated
- query_weight_grad: float32 [1024, 2048], P(None, 'tp')
- key_weight_grad: float32 [1024, 1024], P(None, 'tp')
- value_weight_grad: float32 [1024, 1024], P(None, 'tp')
- query_gain_grad: float32 [128], replicated
- key_gain_grad: float32 [128], replicated
- out_weight_grad: float32 [2048, 1024], P('tp')
- mlp_gain_grad: float32 [1024], replicated
- gate_weight_grad: float32 [1024, 3072], P(None, 'tp')
- up_weight_grad: float32 [1024, 3072], P(None, 'tp')
- down_weight_grad: float32 [3072, 1024], P('tp')
The draws below stay inside these ranges and needn't reach their ends.
Inputs may be any that keep to these rules, and one draw needn't show every extreme that they name: `span_order`: each of 0 to 31 stands once; entries 2 i and 2 i + 1 add up to 31. `positions`: the row at sequence place p has position p or p + 1; place 0 has position 0 and place 4096 - 1 has position 4096.
All inputs are finite; a program needn't handle non-finite values.
Results may differ from the reference program's by a relative error of at most 0.03.
Values may be sent and summed in bfloat16 or wider, within the bound.
No kernel may reach another device: no remote copies, remote signals or barrier semaphores. Data moves between devices by JAX's collectives and lax.ppermute only.
A program may use at most 320 MiB of HBM per device.

```python
import math
import jax
import jax.numpy as jnp
from jax import lax

D = 1024
HEADS = 16
KV = 8
HD = 128
FF = 3072
SPAN = 128
SPANS = 32
TOKENS = 4096


def paired_order(key):
    chosen = jax.random.permutation(key, SPANS // 2).astype(jnp.int32)
    return jnp.stack([chosen, SPANS - 1 - chosen], axis=1).reshape(SPANS).astype(jnp.int32)


def draw_span_order(key, part):
    return paired_order(key)


def draw_positions(key, part):
    order = paired_order(key)
    key = jax.random.fold_in(key, 7)
    places = (order[:, None] * SPAN + jnp.arange(SPAN, dtype=jnp.int32)[None, :]).reshape(TOKENS)
    extra = jax.random.randint(key, (TOKENS,), 0, 2, dtype=jnp.int32)
    extra = jnp.where(places == 0, 0, jnp.where(places == TOKENS - 1, 1, extra))
    return (places + extra).astype(jnp.int32)


def shard_levels(own_key, dims, split, least, largest):
    gain = 1.0
    for position, parts in split:
        steps = jax.random.uniform(jax.random.fold_in(jax.random.fold_in(own_key, 6), position), (parts,), jnp.float32, least / len(split), largest / len(split))
        gain = gain * jnp.repeat(jnp.exp(steps), dims[position] // parts).reshape((-1,) + (1,) * (len(dims) - 1 - position))
    return gain


def normal_values(rng, dims, scale, bound, cuts=(), kind=jnp.bfloat16):
    level = shard_levels(rng, dims, cuts, -0.22, 0.18) if cuts else 1.0
    values = jax.random.normal(rng, dims, jnp.float32) * scale * level
    return jnp.minimum(jnp.maximum(values, -bound), bound).astype(kind)


def setup_inputs(seed: int = 0) -> dict:
    key_of = jax.random.split(jax.random.key(seed), 16)
    residual = normal_values(key_of[0], (TOKENS, D), 1.0, 6.0, ((0, 16),))
    cotangent = normal_values(key_of[1], (TOKENS, D), 1.0, 6.0, ((0, 16),))
    span_order = draw_span_order(jax.random.fold_in(key_of[15], 71), 0)
    positions = draw_positions(jax.random.fold_in(key_of[15], 71), 0)
    attn_gain = jnp.clip(1.0 + 0.1 * jax.random.normal(key_of[4], (D,), jnp.float32), 0.5, 1.5)
    query_weight = normal_values(key_of[5], (D, HEADS * HD), D ** -0.5, 0.1875, ((1, 2),))
    key_weight = normal_values(key_of[6], (D, KV * HD), D ** -0.5, 0.1875, ((1, 2),))
    value_weight = normal_values(key_of[7], (D, KV * HD), D ** -0.5, 0.1875, ((1, 2),))
    query_gain = jnp.clip(1.0 + 0.15 * jax.random.normal(key_of[8], (HD,), jnp.float32), 0.25, 1.75)
    key_gain = jnp.clip(1.0 + 0.15 * jax.random.normal(key_of[9], (HD,), jnp.float32), 0.25, 1.75)
    out_weight = normal_values(key_of[10], (HEADS * HD, D), (HEADS * HD // 16) ** -0.5, 0.5, ((0, 2),))
    mlp_gain = jnp.clip(1.0 + 0.1 * jax.random.normal(key_of[11], (D,), jnp.float32), 0.5, 1.5)
    gate_weight = normal_values(key_of[12], (D, FF), D ** -0.5, 0.1875, ((1, 2),))
    up_weight = normal_values(key_of[13], (D, FF), D ** -0.5, 0.1875, ((1, 2),))
    down_weight = normal_values(key_of[14], (FF, D), FF ** -0.5, 0.109375, ((0, 2),))
    return dict(residual=residual, cotangent=cotangent, span_order=span_order, positions=positions, attn_gain=attn_gain, query_weight=query_weight, key_weight=key_weight, value_weight=value_weight, query_gain=query_gain, key_gain=key_gain, out_weight=out_weight, mlp_gain=mlp_gain, gate_weight=gate_weight, up_weight=up_weight, down_weight=down_weight)


EPS = 1e-06
ROPE_BASE = 1000000.0
NEG = -1e+30
HIGH = lax.Precision.HIGHEST

@jax.custom_vjp
def low(v):
    return lax.optimization_barrier(v.astype(jnp.bfloat16)).astype(jnp.float32)

@jax.custom_vjp
def low_back(v):
    return v

def low_keep(v):
    return (low(v), None)

def low_pass(kept, grad):
    return (grad,)

def back_keep(v):
    return (v, None)

def back_low(kept, grad):
    return (low(grad),)
low.defvjp(low_keep, low_pass)
low_back.defvjp(back_keep, back_low)

def norm_rows(values):
    return values * lax.rsqrt(lax.optimization_barrier(jnp.mean(values * values, axis=-1, keepdims=True)) + EPS)

def rope_tables(positions, width):
    half = width // 2
    freq = ROPE_BASE ** (-(jnp.arange(half, dtype=jnp.float32) * 2.0) / width)
    angle = positions.astype(jnp.float32)[:, None] * freq[None, :]
    return (jnp.cos(angle), jnp.sin(angle))

def rotate(values, cosine, sine):
    half = values.shape[-1] // 2
    first = values[..., :half]
    second = values[..., half:]
    return jnp.concatenate([first * cosine - second * sine, second * cosine + first * sine], axis=-1)

def attend(query_pair, key_rows, value_rows, allowed):
    raw = jnp.einsum('eth,sh->ets', query_pair, key_rows, precision=HIGH)
    raw = low_back(raw)
    scores = jnp.where(allowed, raw * (1.0 / math.sqrt(HD)), NEG)
    shifted = scores - lax.optimization_barrier(jnp.max(scores, axis=-1, keepdims=True))
    weights = jnp.exp(shifted)
    probs = weights / lax.optimization_barrier(jnp.sum(weights, axis=-1, keepdims=True))
    return jnp.einsum('ets,sh->eth', low(probs), value_rows, precision=HIGH)

def layer(residual, attn_gain, query_weight, key_weight, value_weight, query_gain, key_gain, out_weight, mlp_gain, gate_weight, up_weight, down_weight, places, cosine, sine):
    count = residual.shape[0]
    normed = low(norm_rows(residual) * attn_gain)
    queries = low_back(jnp.dot(normed, query_weight, precision=HIGH)).reshape(count, HEADS, HD)
    keys = low_back(jnp.dot(normed, key_weight, precision=HIGH)).reshape(count, KV, HD)
    values = low(low_back(jnp.dot(normed, value_weight, precision=HIGH))).reshape(count, KV, HD)
    queries = low(rotate(norm_rows(queries) * query_gain, cosine[:, None, :], sine[:, None, :]))
    keys = low(rotate(norm_rows(keys) * key_gain, cosine[:, None, :], sine[:, None, :]))
    allowed = places[None, :] <= places[:, None]
    query_groups = queries.reshape(count, KV, 2, HD).transpose(1, 2, 0, 3)
    key_groups = keys.transpose(1, 0, 2)
    value_groups = values.transpose(1, 0, 2)
    attended = lax.map(jax.checkpoint(lambda item: attend(item[0], item[1], item[2], allowed)), (query_groups, key_groups, value_groups))
    attended = attended.transpose(2, 0, 1, 3).reshape(count, HEADS * HD)
    attended = low(low_back(attended))
    mixed = residual + low_back(jnp.dot(attended, out_weight, precision=HIGH))
    normed_two = low(norm_rows(mixed) * mlp_gain)
    gate = low_back(jnp.dot(normed_two, gate_weight, precision=HIGH))
    upward = low_back(jnp.dot(normed_two, up_weight, precision=HIGH))
    hidden = low(gate * jax.nn.sigmoid(gate) * upward)
    return mixed + jnp.dot(hidden, down_weight, precision=HIGH)

def reference(residual, cotangent, span_order, positions, attn_gain, query_weight, key_weight, value_weight, query_gain, key_gain, out_weight, mlp_gain, gate_weight, up_weight, down_weight):
    places = (span_order[:, None] * SPAN + jnp.arange(SPAN, dtype=jnp.int32)[None, :]).reshape(-1)
    cosine, sine = rope_tables(positions, HD)
    floats = tuple((item.astype(jnp.float32) for item in (residual, attn_gain, query_weight, key_weight, value_weight, query_gain, key_gain, out_weight, mlp_gain, gate_weight, up_weight, down_weight)))

    def forward(*params):
        return layer(*params, places, cosine, sine)
    layer_out, pullback = jax.vjp(forward, *floats)
    grads = pullback(cotangent.astype(jnp.float32))
    return (layer_out.astype(jnp.bfloat16), grads[0], grads[1], grads[2], grads[3], grads[4], grads[5], grads[6], grads[7], grads[8], grads[9], grads[10], grads[11])
```

```python
import functools
import math

import jax
import jax.numpy as jnp
from jax import lax
from jax.experimental import pallas as pl
from jax.experimental.pallas import tpu as pltpu
from jax.sharding import PartitionSpec as P

EPS = 1e-06
ROPE_BASE = 1000000.0
HEAD = 128
LOG2E = 1.4426950408889634
VMEM_LIMIT = 40 * 1024 * 1024
BF = jnp.bfloat16
F32 = jnp.float32


def nn(a, b):
    return lax.dot_general(a, b, (((1,), (0,)), ((), ())), preferred_element_type=F32)


def nt(a, b):
    return lax.dot_general(a, b, (((1,), (1,)), ((), ())), preferred_element_type=F32)


def tn(a, b):
    return lax.dot_general(a, b, (((0,), (0,)), ((), ())), preferred_element_type=F32)


def norm_rows(values):
    scale_rows = lax.rsqrt(jnp.mean(values * values, axis=-1, keepdims=True) + EPS)
    return (values * scale_rows, scale_rows)


def norm_back(grad_normed, normed, scale_rows):
    return scale_rows * (
        grad_normed - normed * jnp.mean(grad_normed * normed, axis=-1, keepdims=True)
    )


def ring_order(chips):
    if chips % 8:
        return list(range(chips))
    rows, cols = 4, chips // 4
    if cols % 2 or cols < 4:
        path = list(range(cols))
    else:
        path = list(range(cols // 2)) + list(range(cols - 1, cols // 2 - 1, -1))
    walk = []
    for row in range(rows):
        across = range(1, cols) if row % 2 == 0 else range(cols - 1, 0, -1)
        walk += [(row, col) for col in across]
    walk = [(0, 0)] + walk + [(row, 0) for row in range(rows - 1, 0, -1)]
    return [row * cols + path[col] for row, col in walk]


class Ring:
    def __init__(self, devices):
        self.chips = devices // 2
        order = ring_order(self.chips)
        self.order = order
        size = self.chips
        self.up = [
            (2 * order[i] + core, 2 * order[(i + 1) % size] + core)
            for i in range(size)
            for core in range(2)
        ]
        self.down = [(b, a) for a, b in self.up]
        self.swap = [(i, i ^ 1) for i in range(devices)]
        place = [0] * size
        for i, chip in enumerate(order):
            place[chip] = i
        index = lax.axis_index("cp")
        self.core = index % 2
        self.here = jnp.asarray(place, jnp.int32)[index // 2]
        self.half = size // 2

    def send_up(self, x):
        return lax.ppermute(x, "cp", self.up)

    def send_down(self, x):
        return lax.ppermute(x, "cp", self.down)

    def sibling(self, x):
        return lax.ppermute(x, "cp", self.swap)

    def gather_steps(self, own):
        upward = downward = own
        for step in range(1, self.half):
            upward = self.send_up(upward)
            downward = self.send_down(downward)
            yield [(-step, upward), (step, downward)]
        cut = own.shape[0] // 2
        yield [
            (
                self.half,
                jnp.concatenate(
                    [self.send_up(upward[:cut]), self.send_down(downward[cut:])], axis=0
                ),
            )
        ]

    def scatter(self, local):
        far = local(self.half).astype(BF)
        cut = far.shape[0] // 2
        upward = self.send_up(far[:cut])
        downward = self.send_down(far[cut:])
        for step in range(self.half - 1, 0, -1):
            mine_up, mine_down = local(step), local(-step)
            if step == self.half - 1:
                upward = jnp.concatenate(
                    [(mine_up[:cut].astype(F32) + upward.astype(F32)).astype(BF), mine_up[cut:].astype(BF)],
                    axis=0,
                )
                downward = jnp.concatenate(
                    [mine_down[:cut].astype(BF), (mine_down[cut:].astype(F32) + downward.astype(F32)).astype(BF)],
                    axis=0,
                )
            else:
                upward = (mine_up.astype(F32) + upward.astype(F32)).astype(BF)
                downward = (mine_down.astype(F32) + downward.astype(F32)).astype(BF)
            upward = self.send_up(upward)
            downward = self.send_down(downward)
        return local(0).astype(F32) + upward.astype(F32) + downward.astype(F32)


def assemble_kernel(count, table_ref, *refs):
    parts, out = refs[:count], refs[count]
    step = pl.program_id(0)
    for i in range(count):

        @pl.when(step == i)
        def _(i=i):
            out[...] = parts[i][...].astype(F32)


def all_reduce(ring, partial):
    rows, columns = partial.shape
    half = rows // 2
    shard = half // ring.chips
    mine = lax.dynamic_slice_in_dim(partial, ring.core * half, half)
    other = ring.sibling(lax.dynamic_slice_in_dim(partial, (1 - ring.core) * half, half))

    def local(offset):
        start = ((ring.here + offset + ring.chips) % ring.chips) * shard
        return (
            lax.dynamic_slice_in_dim(mine, start, shard).astype(F32)
            + lax.dynamic_slice_in_dim(other, start, shard).astype(F32)
        ).astype(BF)

    total = ring.scatter(local).astype(BF)
    parts, places = [total], [ring.here]
    for step in ring.gather_steps(total):
        for offset, part in step:
            parts.append(part)
            places.append((ring.here + offset + ring.chips) % ring.chips)
    others = [ring.sibling(part) for part in parts]
    table = jnp.stack(
        [ring.core * ring.chips + place for place in places]
        + [(1 - ring.core) * ring.chips + place for place in places]
    ).astype(jnp.int32)
    parts = parts + others
    count = len(parts)
    return pl.pallas_call(
        functools.partial(assemble_kernel, count),
        out_shape=jax.ShapeDtypeStruct((rows, columns), F32),
        grid_spec=pltpu.PrefetchScalarGridSpec(
            num_scalar_prefetch=1,
            grid=(count,),
            in_specs=[pl.BlockSpec((shard, columns), lambda i, t: (0, 0))] * count,
            out_specs=pl.BlockSpec((shard, columns), lambda i, t: (t[i], 0)),
        ),
        compiler_params=pltpu.CompilerParams(vmem_limit_bytes=VMEM_LIMIT),
    )(table, *parts)


def total_small(devices, x):
    x = x + lax.ppermute(x, "tp", [(0, 1), (1, 0)])
    bit = 1
    while bit < devices:
        x = x + lax.ppermute(x, "cp", [(i, i ^ bit) for i in range(devices)])
        bit *= 2
    return x


def pair_sum(x):
    x = x.astype(BF)
    return x.astype(F32) + lax.ppermute(x, "tp", [(0, 1), (1, 0)]).astype(F32)


def turn(values, cosine, sine):
    return values * cosine + pltpu.roll(values, values.shape[-1] // 2, 1) * sine


def turn_back(values, cosine, sine):
    return values * cosine - pltpu.roll(values, values.shape[-1] // 2, 1) * sine


def key_value_kernel(
    residual, gain, key_weight, value_weight, key_gain, cosine, sine, normed_out, raw_out, packed_out
):
    unit, _ = norm_rows(residual[...].astype(F32))
    normed = (unit * gain[...]).astype(BF)
    normed_out[...] = normed
    width = key_gain.shape[1]
    raw = nn(normed, key_weight[...])
    raw_out[...] = raw
    values = nn(normed, value_weight[...]).astype(BF)
    for group in range(raw.shape[1] // width):
        here = slice(group * width, (group + 1) * width)
        key_unit, _ = norm_rows(raw[:, here])
        packed_out[:, 2 * group * width : (2 * group + 1) * width] = turn(
            key_unit * key_gain[...], cosine[...], sine[...]
        ).astype(BF)
        packed_out[:, (2 * group + 1) * width : (2 * group + 2) * width] = values[:, here]


def query_kernel(normed, weight, gain, cosine, sine, raw_out, low_out):
    width = gain.shape[1]
    raw = nn(normed[...], weight[...])
    raw_out[...] = raw
    for head in range(raw.shape[1] // width):
        here = slice(head * width, (head + 1) * width)
        unit, _ = norm_rows(raw[:, here])
        low_out[:, here] = turn(unit * gain[...], cosine[...], sine[...]).astype(BF)


def heads_back_kernel(grad, raw, gain, cosine, sine, low_out, gain_out):
    width = gain.shape[1]
    total = jnp.zeros((8, width), F32)
    for head in range(raw.shape[1] // width):
        here = slice(head * width, (head + 1) * width)
        unit, scale_rows = norm_rows(raw[:, here])
        turned = turn_back(grad[:, here].astype(F32), cosine[...], sine[...])
        term = turned * unit
        total = total + jnp.sum(term.reshape(-1, 8, width), axis=0)
        low_out[:, here] = norm_back(turned * gain[...], unit, scale_rows).astype(BF)
    gain_out[...] = total


def whole_call(kernel, outs, *args):
    return pl.pallas_call(
        kernel,
        out_shape=[jax.ShapeDtypeStruct(shape, dtype) for shape, dtype in outs],
        compiler_params=pltpu.CompilerParams(vmem_limit_bytes=VMEM_LIMIT),
    )(*args)


def stacked(ref, start, span, width):
    rows = pl.ds(start, span)
    return jnp.concatenate([ref[rows, :width], ref[rows, width:]], axis=0)


def causal(span, transposed):
    shape = (span, 2 * span) if transposed else (2 * span, span)
    key = lax.broadcasted_iota(jnp.int32, shape, 0 if transposed else 1)
    row = lax.broadcasted_iota(jnp.int32, shape, 1 if transposed else 0)
    return key <= row % span


def forward_kernel(count, own, last, span, width, pick_ref, query, *refs):
    blocks, refs = refs[:count], refs[count:]
    scale = LOG2E / math.sqrt(width)
    if own:
        accum = refs[0]
    else:
        before, accum = refs[0], refs[1]
    outs = refs[1 if own else 2 :]
    if last:
        accum = outs[-1]
    ones = jnp.ones((span, width), BF)

    def weighted(rows, keys, values, allowed=None):
        scores = nt(rows, keys)
        probs = jnp.exp2(scores * scale)
        if allowed is not None:
            probs = jnp.where(allowed, probs, 0.0)
        return nn(probs.astype(BF), values)

    def extended(block, start):
        return jnp.concatenate([block[pl.ds(start, span), width:], ones], axis=1)

    keys = jnp.concatenate([block[:span, :width] for block in blocks], axis=0)
    values = jnp.concatenate([extended(block, 0) for block in blocks], axis=0)
    high = weighted(stacked(query, span, span, width), keys, values)
    if own:
        allowed = causal(span, False)
        for side in range(2):
            block = blocks[0]
            start = side * span
            part = weighted(
                stacked(query, start, span, width),
                block[start : start + span, :width],
                extended(block, start),
                allowed,
            )
            accum[0, side] = part + high if side else part
    else:
        accum[0, 0] = before[0, 0]
        accum[0, 1] = before[0, 1] + high
    for i in range(1 if own else 0, count):
        side = pick_ref[i]
        start = pl.multiple_of(side * span, span)
        block = blocks[i]
        accum[0, side] += weighted(
            stacked(query, start, span, width),
            block[pl.ds(start, span), :width],
            extended(block, start),
        )
    if last:
        wide, low, logs = outs[0], outs[1], outs[2]
        for side in range(2):
            rows = slice(side * span, (side + 1) * span)
            both = accum[0, side]
            mass = both[:, width:]
            out = both[:, :width] / mass
            for head in range(2):
                part = out[head * span : (head + 1) * span]
                columns = slice(head * width, (head + 1) * width)
                wide[rows, columns] = part
                low[rows, columns] = part.astype(BF)
            logs[0, side] = jnp.log2(mass).T[:8]


def attention_forward(query, blocks, picks, before, own, last):
    rows, columns = query.shape
    span = rows // 2
    width = HEAD
    groups = columns // (2 * width)
    count = len(blocks)
    tile = pl.BlockSpec((rows, 2 * width), lambda g: (0, g))
    accum_spec = pl.BlockSpec((1, 2, 2 * span, 2 * width), lambda g: (g, 0, 0, 0))
    accum_shape = jax.ShapeDtypeStruct((groups, 2, 2 * span, 2 * width), F32)
    args = [picks, query, *blocks]
    specs = [pl.BlockSpec(memory_space=pltpu.SMEM)] + [tile] * (1 + count)
    if not own:
        args.append(before)
        specs.append(accum_spec)
    scratch = []
    if last:
        outs = [
            jax.ShapeDtypeStruct((rows, columns), F32),
            jax.ShapeDtypeStruct((rows, columns), BF),
            jax.ShapeDtypeStruct((groups, 2, 8, 2 * span), F32),
        ]
        out_specs = [tile, tile, pl.BlockSpec((1, 2, 8, 2 * span), lambda g: (g, 0, 0, 0))]
        scratch = [pltpu.VMEM((1, 2, 2 * span, 2 * width), F32)]
    else:
        outs, out_specs = [accum_shape], [accum_spec]

    def kernel(*refs):
        if last and own:
            refs = (*refs[: 2 + count], None, *refs[2 + count :])
        elif last:
            refs = (*refs[: 3 + count], None, *refs[3 + count :])
        forward_kernel(count, own, last, span, width, *refs)

    return pl.pallas_call(
        kernel,
        out_shape=outs,
        grid=(groups,),
        in_specs=specs,
        out_specs=out_specs,
        scratch_shapes=scratch,
        compiler_params=pltpu.CompilerParams(vmem_limit_bytes=VMEM_LIMIT),
        cost_estimate=pl.CostEstimate(
            flops=groups * (2 * count + own) * 2 * span * span * width * 4,
            bytes_accessed=rows * columns * 2 * (count + 1) + 8 * groups * 4 * span * 2 * width * 2,
            transcendentals=groups * (2 * count + own) * 2 * span * span,
        ),
    )(*args)


def delta_kernel(grad, out, delta):
    width = grad.shape[1] // 2
    span = grad.shape[0] // 2
    for side in range(2):
        rows = slice(side * span, (side + 1) * span)
        product = grad[rows, :].astype(F32) * out[rows, :]
        stack = jnp.concatenate([product[:, :width], product[:, width:]], axis=0)
        total = jnp.sum(stack.T, axis=0, keepdims=True)
        delta[0, side] = jnp.broadcast_to(total, (8, 2 * span))


def attention_delta(grad, out):
    rows, columns = grad.shape
    width, span = HEAD, rows // 2
    groups = columns // (2 * width)
    tile = pl.BlockSpec((rows, 2 * width), lambda g: (0, g))
    return pl.pallas_call(
        delta_kernel,
        out_shape=jax.ShapeDtypeStruct((groups, 2, 8, 2 * span), F32),
        grid=(groups,),
        in_specs=[tile, tile],
        out_specs=pl.BlockSpec((1, 2, 8, 2 * span), lambda g: (g, 0, 0, 0)),
        compiler_params=pltpu.CompilerParams(vmem_limit_bytes=VMEM_LIMIT),
    )(grad, out)


def backward_kernel(count, own, first, last, span, width, pick_ref, query, grad, logs, delta, *refs):
    blocks, refs = refs[:count], refs[count:]
    if not first:
        before, refs = refs[0], refs[1:]
    outs, refs = refs[:count], refs[count:]
    if last:
        query_out, accum = refs
    else:
        accum = refs[0]
    scale = LOG2E / math.sqrt(width)
    factor = 1.0 / math.sqrt(width)

    def products(side, start, keys, values, allowed=None):
        rows = stacked(query, start, span, width)
        grads = stacked(grad, start, span, width)
        probs = jnp.exp2(nt(keys, rows) * scale - logs[0, side, :1])
        if allowed is not None:
            probs = jnp.where(allowed, probs, 0.0)
        prob_grad = nt(values, grads)
        score_grad = (probs * (prob_grad - delta[0, side, :1])).astype(BF)
        return (
            nn(score_grad, rows),
            nn(probs.astype(BF), grads),
            tn(keys, score_grad),
        )

    keys = jnp.concatenate([block[:span, :width] for block in blocks], axis=0)
    values = jnp.concatenate([block[:span, width:] for block in blocks], axis=0)
    low_keys, low_values, high_query = products(1, span, keys, values)
    if first:
        accum[0, 0] = jnp.zeros_like(high_query)
        accum[0, 1] = high_query
    else:
        accum[0, 0] = before[0, 0]
        accum[0, 1] = before[0, 1] + high_query
    for i in range(count):
        here = slice(i * span, (i + 1) * span)
        key_low, value_low = low_keys[here], low_values[here]
        block = blocks[i]
        if own and i == 0:
            allowed = causal(span, True)
            key_part, value_part, query_part = products(
                0, 0, block[:span, :width], block[:span, width:], allowed
            )
            accum[0, 0] += query_part
            key_low, value_low = key_low + key_part, value_low + value_part
            key_high, value_high, query_part = products(
                1, span, block[span:, :width], block[span:, width:], allowed
            )
            accum[0, 1] += query_part
        else:
            side = pick_ref[i]
            start = pl.multiple_of(side * span, span)
            key_part, value_part, query_part = products(
                side, start, block[pl.ds(start, span), :width], block[pl.ds(start, span), width:]
            )
            accum[0, side] += query_part
            low = side == 0
            key_low = key_low + jnp.where(low, key_part, 0.0)
            value_low = value_low + jnp.where(low, value_part, 0.0)
            key_high = jnp.where(low, 0.0, key_part)
            value_high = jnp.where(low, 0.0, value_part)
        outs[i][:span, :width] = (key_low * factor).astype(BF)
        outs[i][:span, width:] = value_low.astype(BF)
        outs[i][span:, :width] = (key_high * factor).astype(BF)
        outs[i][span:, width:] = value_high.astype(BF)
    if last:
        for side in range(2):
            part = accum[0, side].T * factor
            rows = slice(side * span, (side + 1) * span)
            query_out[rows, :width] = part[:span]
            query_out[rows, width:] = part[span:]


def attention_backward(query, grad, logs, delta, blocks, picks, before, own, last):
    rows, columns = query.shape
    span, width = rows // 2, HEAD
    groups = columns // (2 * width)
    count = len(blocks)
    first = before is None
    tile = pl.BlockSpec((rows, 2 * width), lambda g: (0, g))
    stat = pl.BlockSpec((1, 2, 8, 2 * span), lambda g: (g, 0, 0, 0))
    accum_block = (1, 2, width, 2 * span)
    accum_spec = pl.BlockSpec(accum_block, lambda g: (g, 0, 0, 0))
    args = [picks, query, grad, logs, delta, *blocks]
    specs = [pl.BlockSpec(memory_space=pltpu.SMEM), tile, tile, stat, stat] + [tile] * count
    if not first:
        args.append(before)
        specs.append(accum_spec)
    outs = [jax.ShapeDtypeStruct((rows, columns), BF)] * count
    out_specs = [tile] * count
    scratch = []
    if last:
        outs.append(jax.ShapeDtypeStruct((rows, columns), F32))
        out_specs.append(tile)
        scratch = [pltpu.VMEM(accum_block, F32)]
    else:
        outs.append(jax.ShapeDtypeStruct((groups, 2, width, 2 * span), F32))
        out_specs.append(accum_spec)
    return pl.pallas_call(
        functools.partial(backward_kernel, count, own, first, last, span, width),
        out_shape=outs,
        grid=(groups,),
        in_specs=specs,
        out_specs=out_specs,
        scratch_shapes=scratch,
        compiler_params=pltpu.CompilerParams(vmem_limit_bytes=VMEM_LIMIT),
        cost_estimate=pl.CostEstimate(
            flops=groups * (2 * count + own) * 2 * span * span * width * 10,
            bytes_accessed=rows * columns * 2 * (2 * count + 4),
            transcendentals=groups * (2 * count + own) * 2 * span * span,
        ),
    )(*args)


def body(
    devices,
    residual,
    cotangent,
    span_order,
    positions,
    attn_gain,
    query_weight,
    key_weight,
    value_weight,
    query_gain,
    key_gain,
    out_weight,
    mlp_gain,
    gate_weight,
    up_weight,
    down_weight,
):
    ring = Ring(devices)
    rows, model = residual.shape
    head_dim = query_gain.shape[0]
    span = rows // 2
    index = lax.axis_index("cp")
    pairs = span_order.reshape(-1, 2)
    ordered = lax.dynamic_slice_in_dim(pairs, index, 1)[0]
    in_order = ordered[0] < ordered[1]

    def canonical(x):
        return jnp.where(in_order, x, jnp.roll(x, span, axis=0))

    residual = canonical(residual)
    cotangent = canonical(cotangent)
    positions = canonical(positions)

    lows = jnp.min(pairs, axis=1).reshape(-1, 2)[jnp.asarray(ring.order)]
    lows = lax.dynamic_slice_in_dim(jnp.concatenate([lows, lows]), ring.here, ring.chips)
    lows = jnp.where(ring.core == 0, lows, lows[:, ::-1])
    picks = jnp.where(lows < jnp.min(ordered), 0, 1).astype(jnp.int32)

    half = head_dim // 2
    freq = ROPE_BASE ** (-(jnp.arange(half, dtype=F32) * 2.0) / head_dim)
    angle = positions.astype(F32)[:, None] * freq[None, :]
    cosine, sine = jnp.cos(angle), jnp.sin(angle)
    cosine = jnp.concatenate([cosine, cosine], axis=1)
    sine = jnp.concatenate([-sine, sine], axis=1)

    attn_gain_row = attn_gain.reshape(1, -1)
    mlp_gain_row = mlp_gain.reshape(1, -1)
    query_gain_row = query_gain.reshape(1, -1)
    key_gain_row = key_gain.reshape(1, -1)
    key_columns = key_weight.shape[1]
    query_columns = query_weight.shape[1]

    normed_low, keys_raw, packed = whole_call(
        key_value_kernel,
        [((rows, model), BF), ((rows, key_columns), F32), ((rows, 2 * key_columns), BF)],
        residual, attn_gain_row, key_weight, value_weight, key_gain_row, cosine, sine,
    )
    queries_raw, query_low = whole_call(
        query_kernel,
        [((rows, query_columns), F32), ((rows, query_columns), BF)],
        normed_low, query_weight, query_gain_row, cosine, sine,
    )

    def picks_of(offsets):
        both = [picks[offset % ring.chips] for offset in offsets]
        return jnp.concatenate([jnp.stack([b[0] for b in both]), jnp.stack([b[1] for b in both])])

    calls = [([0], [packed, ring.sibling(packed)])]
    state = attention_forward(query_low, calls[0][1], picks_of([0]), None, True, False)
    steps = list(ring.gather_steps(packed))
    for i, step in enumerate(steps):
        offsets = [offset for offset, _ in step]
        blocks = [block for _, block in step]
        blocks = blocks + [ring.sibling(block) for block in blocks]
        calls.append((offsets, blocks))
        state = attention_forward(
            query_low, blocks, picks_of(offsets), state[0], False, i == len(steps) - 1
        )
    attended, attended_low, logs = state

    residual_wide = residual.astype(F32)
    mixed = residual_wide + pair_sum(nn(attended_low, out_weight))
    normed_two, scale_two = norm_rows(mixed)
    normed_two_low = (normed_two * mlp_gain).astype(BF)
    gate = nn(normed_two_low, gate_weight)
    upward = nn(normed_two_low, up_weight)
    sigmoid_gate = jax.nn.sigmoid(gate)
    activated = gate * sigmoid_gate
    hidden_low = (activated * upward).astype(BF)
    hidden_grad = nt(cotangent, down_weight)
    gate_grad_low = (
        hidden_grad * upward * sigmoid_gate * (1.0 + gate * (1.0 - sigmoid_gate))
    ).astype(BF)
    up_grad_low = (hidden_grad * activated).astype(BF)
    normed_two_part = (nt(gate_grad_low, gate_weight) + nt(up_grad_low, up_weight)).astype(BF)
    normed_two_grad = pair_sum(normed_two_part)
    layer_out = mixed + pair_sum(nn(hidden_low, down_weight))
    both_grad_low = jnp.concatenate([gate_grad_low, up_grad_low], axis=1)
    both_sum = all_reduce(ring, tn(normed_two_low, both_grad_low).astype(BF))
    down_weight_sum = all_reduce(ring, tn(hidden_low, cotangent).astype(BF))

    mlp_gain_term = jnp.sum(normed_two_part.astype(F32) * normed_two, axis=0)
    mixed_grad = cotangent.astype(F32) + norm_back(
        normed_two_grad * mlp_gain, normed_two, scale_two
    )
    mixed_grad_low = mixed_grad.astype(BF)
    attended_grad = nt(mixed_grad_low, out_weight).astype(BF)
    delta = attention_delta(attended_grad, attended)

    query_state = [None]
    query_grads = []

    def local(offset):
        key = abs(offset)
        if key not in done:
            place = [i for i, call in enumerate(calls) if abs(call[0][0]) == key][0]
            offsets, blocks = calls[place]
            last = place == 0
            results = attention_backward(
                query_low, attended_grad, logs, delta, blocks, picks_of(offsets), query_state[0],
                place == 0, last,
            )
            if last:
                query_grads.append(results[-1])
            else:
                query_state[0] = results[-1]
            count = len(offsets)
            done[key] = {}
            for at, own, other in zip(offsets, results[:count], results[count : 2 * count]):
                done[key][at] = own.astype(F32) + ring.sibling(other).astype(F32)
        return done[key][offset]

    done = {}
    packed_grad = ring.scatter(local)
    (query_grad_rows,) = query_grads

    query_grad_low, query_gain_term = whole_call(
        heads_back_kernel,
        [((rows, query_columns), BF), ((8, head_dim), F32)],
        query_grad_rows, queries_raw, query_gain_row, cosine, sine,
    )
    split = packed_grad.reshape(rows, -1, 2, head_dim)
    key_grad = split[:, :, 0].reshape(rows, key_columns)
    value_grad_low = split[:, :, 1].reshape(rows, key_columns).astype(BF)
    key_grad_low, key_gain_term = whole_call(
        heads_back_kernel,
        [((rows, key_columns), BF), ((8, head_dim), F32)],
        key_grad, keys_raw, key_gain_row, cosine, sine,
    )

    normed_part = (
        nt(query_grad_low, query_weight)
        + nt(key_grad_low, key_weight)
        + nt(value_grad_low, value_weight)
    ).astype(BF)
    normed_grad = pair_sum(normed_part)
    out_weight_sum = all_reduce(ring, tn(attended_low, mixed_grad_low).astype(BF))
    projections = jnp.concatenate([query_grad_low, key_grad_low, value_grad_low], axis=1)
    projection_sum = all_reduce(ring, tn(normed_low, projections).astype(BF))

    normed_one, scale_one = norm_rows(residual_wide)
    attn_gain_term = jnp.sum(normed_part.astype(F32) * normed_one, axis=0)
    residual_grad = mixed_grad + norm_back(normed_grad * attn_gain, normed_one, scale_one)

    small = jnp.concatenate(
        [
            attn_gain_term,
            mlp_gain_term,
            jnp.sum(query_gain_term, axis=0),
            jnp.sum(key_gain_term, axis=0),
        ]
    ).reshape(-1, 128)
    small = total_small(devices, small).reshape(-1)
    attn_gain_grad, mlp_gain_grad = small[:model], small[model : 2 * model]
    query_gain_grad = small[2 * model : 2 * model + head_dim]
    key_gain_grad = small[2 * model + head_dim :]
    units = gate_weight.shape[1]
    return (
        canonical(layer_out).astype(BF),
        canonical(residual_grad),
        attn_gain_grad,
        projection_sum[:, :query_columns],
        projection_sum[:, query_columns : query_columns + key_columns],
        projection_sum[:, query_columns + key_columns :],
        query_gain_grad,
        key_gain_grad,
        out_weight_sum,
        mlp_gain_grad,
        both_sum[:, :units],
        both_sum[:, units:],
        down_weight_sum,
    )


def solution(mesh):
    return jax.shard_map(
        functools.partial(body, mesh.shape["cp"]),
        mesh=mesh,
        in_specs=(
            P("cp", None),
            P("cp", None),
            P(),
            P("cp"),
            P(),
            P(None, "tp"),
            P(None, "tp"),
            P(None, "tp"),
            P(),
            P(),
            P("tp", None),
            P(),
            P(None, "tp"),
            P(None, "tp"),
            P("tp", None),
        ),
        out_specs=(
            P("cp", None),
            P("cp", None),
            P(),
            P(None, "tp"),
            P(None, "tp"),
            P(None, "tp"),
            P(),
            P(),
            P("tp", None),
            P(),
            P(None, "tp"),
            P(None, "tp"),
            P("tp", None),
        ),
        check_vma=False,
    )
```

```python
import functools
import math

import jax
import jax.numpy as jnp
from jax import lax
from jax.experimental import pallas as pl
from jax.experimental.pallas import tpu as pltpu
from jax.sharding import PartitionSpec as P

EPS = 1e-06
ROPE_BASE = 1000000.0
HEAD = 128
LOG2E = 1.4426950408889634
VMEM_LIMIT = 40 * 1024 * 1024
LIGHT = pl.CostEstimate(flops=1024, bytes_accessed=1024, transcendentals=0)
BF = jnp.bfloat16
F32 = jnp.float32


def nn(a, b):
    return lax.dot_general(a, b, (((1,), (0,)), ((), ())), preferred_element_type=F32)


def nt(a, b):
    return lax.dot_general(a, b, (((1,), (1,)), ((), ())), preferred_element_type=F32)


def tn(a, b):
    return lax.dot_general(a, b, (((0,), (0,)), ((), ())), preferred_element_type=F32)


def norm_rows(values):
    scale_rows = lax.rsqrt(jnp.mean(values * values, axis=-1, keepdims=True) + EPS)
    return (values * scale_rows, scale_rows)


def norm_back(grad_normed, normed, scale_rows):
    return scale_rows * (
        grad_normed - normed * jnp.mean(grad_normed * normed, axis=-1, keepdims=True)
    )


def tie(*values):
    return lax.optimization_barrier(values)


def waits(after):
    return list(after), [pl.BlockSpec(memory_space=pl.ANY)] * len(after)


def in_hbm(x):
    return pltpu.with_memory_space_constraint(x, pltpu.HBM)


def ring_order(chips):
    if chips % 8:
        return list(range(chips))
    rows, cols = 4, chips // 4
    if cols % 2 or cols < 4:
        path = list(range(cols))
    else:
        path = list(range(cols // 2)) + list(range(cols - 1, cols // 2 - 1, -1))
    walk = []
    for row in range(rows):
        across = range(1, cols) if row % 2 == 0 else range(cols - 1, 0, -1)
        walk += [(row, col) for col in across]
    walk = [(0, 0)] + walk + [(row, 0) for row in range(rows - 1, 0, -1)]
    return [row * cols + path[col] for row, col in walk]


class Ring:
    def __init__(self, devices):
        self.devices = devices
        self.chips = devices // 2
        order = ring_order(self.chips)
        self.order = order
        size = self.chips
        self.up = [
            (2 * order[i] + core, 2 * order[(i + 1) % size] + core)
            for i in range(size)
            for core in range(2)
        ]
        self.down = [(b, a) for a, b in self.up]
        self.swap = [(i, i ^ 1) for i in range(devices)]
        place = [0] * size
        for i, chip in enumerate(order):
            place[chip] = i
        index = lax.axis_index("cp")
        self.core = index % 2
        self.here = jnp.asarray(place, jnp.int32)[index // 2]
        self.half = size // 2
        table = [
            [order[(place[chip] + i) % size] for i in range(size)] + [core]
            for chip in range(size)
            for core in range(2)
        ]
        self.table = lax.dynamic_index_in_dim(
            jnp.asarray(table, jnp.int32), index, 0, keepdims=False
        )

    def send_up(self, x):
        return lax.ppermute(x, "cp", self.up)

    def send_down(self, x):
        return lax.ppermute(x, "cp", self.down)

    def sibling(self, x):
        return lax.ppermute(x, "cp", self.swap)

    def shard_at(self, table, offset, other=False):
        core = table[self.chips]
        return 2 * table[offset % self.chips] + (1 - core if other else core)


class Gradients:
    def __init__(self, ring, pack_rows, pack_columns, pieces):
        self.ring = ring
        self.shape = (pack_rows, pack_columns)
        self.pieces = pieces
        self.mine = [None] * len(pieces)
        self.other = [None] * len(pieces)

    def put(self, index, array):
        ring = self.ring
        groups, rows, columns = self.pieces[index][0]
        self.mine[index] = array
        halves = array.reshape(groups, ring.chips, 2, rows, columns)
        other = lax.dynamic_index_in_dim(halves, 1 - ring.core, 2, keepdims=False)
        self.other[index] = ring.sibling(other.reshape(groups, ring.chips * rows, columns))

    def shards(self, offsets, received, halves, after=()):
        ring, pieces = self.ring, self.pieces
        rows, columns = self.shape
        cut = columns // 2
        count, sides = len(pieces), len(offsets)
        args, specs = [], []
        for offset in offsets:
            for index, ((groups, part_rows, part_columns), _) in enumerate(pieces):
                block = (groups, part_rows, part_columns)
                args += [in_hbm(self.mine[index]), in_hbm(self.other[index])]
                specs += [
                    pl.BlockSpec(block, lambda i, t, at=offset: (0, ring.shard_at(t, at), 0)),
                    pl.BlockSpec(block, lambda i, t, at=offset: (0, t[at % ring.chips], 0)),
                ]
        args += received
        specs += [pl.BlockSpec(x.shape, lambda i, t: (0, 0)) for x in received]
        more_args, more_specs = waits(after)
        total_args = len(args) + len(more_args)

        def kernel(table_ref, *refs):
            outs = refs[total_args:]
            outs[-1][...] = jnp.zeros_like(outs[-1])
            gained = refs[2 * count * sides : len(args)]
            for side in range(sides):
                for index, (_, places) in enumerate(pieces):
                    mine = refs[2 * (count * side + index)]
                    other = refs[2 * (count * side + index) + 1]
                    for group, (row, column) in enumerate(places):
                        total = mine[group].astype(F32) + other[group].astype(F32)
                        high, wide = total.shape
                        here, end = slice(row, row + high), column + wide
                        if halves == "send":
                            for out, start in zip(outs, (0, cut)):
                                left, right = max(column, start), min(end, start + cut)
                                if left < right:
                                    out[here, left - start : right - start] = total[
                                        :, left - column : right - column
                                    ].astype(BF)
                        elif halves == "sum":
                            for more in gained:
                                total = total + more[here, column:end].astype(F32)
                            outs[0][here, column:end] = total.astype(BF)
                        elif halves == "add":
                            start, stop = side * cut, side * cut + cut
                            for left, right, more in (
                                (column, min(end, start), False),
                                (max(column, start), min(end, stop), True),
                                (max(column, stop), end, False),
                            ):
                                if left < right:
                                    part = total[:, left - column : right - column]
                                    if more:
                                        part = part + gained[side][
                                            here, left - start : right - start
                                        ].astype(F32)
                                    outs[side][here, left:right] = part.astype(BF)
                        else:
                            total = total + gained[side][here, column:end].astype(F32)
                            outs[side][here, column:end] = total.astype(BF)

        outs = {"send": [cut, cut], "sum": [columns]}.get(halves, [columns, columns])
        return pl.pallas_call(
            kernel,
            out_shape=[jax.ShapeDtypeStruct((rows, wide), BF) for wide in outs]
            + [jax.ShapeDtypeStruct((8, 128), F32)],
            grid_spec=pltpu.PrefetchScalarGridSpec(
                num_scalar_prefetch=1,
                grid=(1,),
                in_specs=specs + more_specs,
                out_specs=[pl.BlockSpec((rows, wide), lambda i, t: (0, 0)) for wide in outs]
                + [pl.BlockSpec((8, 128), lambda i, t: (0, 0))],
            ),
            compiler_params=pltpu.CompilerParams(vmem_limit_bytes=VMEM_LIMIT),
        cost_estimate=LIGHT,
        )(ring.table, *args, *more_args)

    def scatter(self, after=()):
        ring = self.ring
        up, down, token = self.shards([ring.half], [], "send", after)
        for step in range(ring.half - 1, -1, -1):
            (up, down), after = yield (ring.send_up(up), ring.send_down(down)), token
            if step:
                kind = "add" if step == ring.half - 1 else ""
                up, down, token = self.shards([step, -step], [up, down], kind, after)
        yield self.shards([0], [up, down], "sum", after)

    def gather(self, own):
        ring = self.ring
        cut = own.shape[1] // 2
        up = down = own
        ready = [(0, own)]
        for step in range(1, ring.half):
            up, down = yield (ring.send_up(up), ring.send_down(down)), ready
            ready = [(-step, up), (step, down)]
        left, right = yield (ring.send_up(up[:, :cut]), ring.send_down(down[:, cut:])), ready
        yield None, [(ring.half, jnp.concatenate([left, right], axis=1))]

    def unpack(self, ready, outs, before, after=()):
        ring, pieces = self.ring, self.pieces
        rows, columns = self.shape
        args = [part for _, part, _ in ready]
        count = len(args)
        places_of = [(offset, other) for offset, _, other in ready]

        def kernel(table_ref, *refs):
            step = pl.program_id(0)
            results = refs[-len(outs) :]
            for i in range(count):

                @pl.when(step == i)
                def _(i=i):
                    for out, (index, first, wide) in zip(results, outs):
                        (_, high, _), places = pieces[index]
                        for group, (row, column) in enumerate(places):
                            start = column + first
                            out[group] = refs[i][row : row + high, start : start + wide].astype(F32)

        def place(i, table):
            where = ring.shard_at(table, *places_of[0])
            for j in range(1, count):
                where = jnp.where(i == j, ring.shard_at(table, *places_of[j]), where)
            return (0, where, 0)

        shapes, out_specs = [], []
        for index, _, wide in outs:
            groups, high, _ = pieces[index][0]
            shapes.append(jax.ShapeDtypeStruct((groups, ring.devices * high, wide), F32))
            out_specs.append(pl.BlockSpec((groups, high, wide), place))
        specs = [pl.BlockSpec((rows, columns), lambda i, t: (0, 0))] * count
        aliases = {}
        if before is not None:
            specs += [pl.BlockSpec(memory_space=pl.ANY)] * len(outs)
            aliases = {1 + count + i: i for i in range(len(outs))}
            args += before
        more_args, more_specs = waits(after)
        args += more_args
        specs += more_specs
        return list(
            pl.pallas_call(
                kernel,
                out_shape=shapes,
                grid_spec=pltpu.PrefetchScalarGridSpec(
                    num_scalar_prefetch=1, grid=(count,), in_specs=specs, out_specs=out_specs
                ),
                input_output_aliases=aliases,
                compiler_params=pltpu.CompilerParams(vmem_limit_bytes=VMEM_LIMIT),
        cost_estimate=LIGHT,
            )(ring.table, *args)
        )


def pair_add(own, received, half, after=()):
    more_args, more_specs = waits(after)

    def kernel(*refs):
        refs, outs = refs[:4], refs[4 + len(more_args) :]
        outs[-1][...] = jnp.zeros_like(outs[-1])
        for side in range(2):
            mine, got, out = refs[side], refs[2 + side], outs[side]
            if half:
                rows = got.shape[0]
                here = slice(side * rows, (side + 1) * rows)
                rest = slice((1 - side) * rows, (2 - side) * rows)
                out[here] = (mine[here].astype(F32) + got[...].astype(F32)).astype(BF)
                out[rest] = mine[rest]
            else:
                out[...] = (mine[...].astype(F32) + got[...].astype(F32)).astype(BF)

    shape = jax.ShapeDtypeStruct(own[0].shape, BF)
    return pl.pallas_call(
        kernel,
        out_shape=[shape, shape, jax.ShapeDtypeStruct((8, 128), F32)],
        in_specs=[pl.BlockSpec(memory_space=pltpu.VMEM)] * 4 + more_specs,
        compiler_params=pltpu.CompilerParams(vmem_limit_bytes=VMEM_LIMIT),
        cost_estimate=LIGHT,
    )(*own, *received, *more_args)


class SmallSum:
    def __init__(self, devices, x):
        self.devices, self.bit, self.total = devices, 1, x
        self.under_way = []
        self.send()

    def send(self):
        pairs = [(i, i ^ self.bit) for i in range(self.devices)]
        self.under_way = [lax.ppermute(self.total, "cp", pairs)] if self.bit < self.devices else []
        self.bit *= 2

    def came(self, arrived):
        if arrived:
            self.total = self.total + arrived[0]
            self.send()


def partner(x):
    return lax.ppermute(x, "tp", [(0, 1), (1, 0)])


def both(mine, other):
    return mine.astype(F32) + other.astype(F32)


def turn(values, cosine, sine):
    return values * cosine + pltpu.roll(values, values.shape[-1] // 2, 1) * sine


def turn_back(values, cosine, sine):
    return values * cosine - pltpu.roll(values, values.shape[-1] // 2, 1) * sine


def lower_first(order, table):
    device = 2 * table[0] + table[table.shape[0] - 1]
    return order[2 * device] < order[2 * device + 1]


def key_value_kernel(
    order, table, residual, gain, key_weight, value_weight, key_gain, cosine, sine,
    residual_out, normed_out, raw_out, cosine_out, sine_out, keep, give,
):
    span = residual.shape[0] // 2
    start = jnp.where(lower_first(order, table), 0, span)

    def canonical(ref):
        return jnp.concatenate(
            [
                ref[pl.ds(pl.multiple_of(start, span), span)],
                ref[pl.ds(pl.multiple_of(span - start, span), span)],
            ],
            axis=0,
        )

    rows = canonical(residual)
    residual_out[...] = rows
    unit, _ = norm_rows(rows.astype(F32))
    normed = (unit * gain[...]).astype(BF)
    normed_out[...] = normed
    cosine, sine = canonical(cosine), canonical(sine)
    cosine_out[...], sine_out[...] = cosine, sine
    width = key_gain.shape[1]
    raw = nn(normed, key_weight[...])
    raw_out[...] = raw
    values = nn(normed, value_weight[...]).astype(BF)
    parts = []
    for group in range(raw.shape[1] // width):
        here = slice(group * width, (group + 1) * width)
        key_unit, _ = norm_rows(raw[:, here])
        parts.append(turn(key_unit * key_gain[...], cosine, sine).astype(BF))
        parts.append(values[:, here])
    each = len(parts) // 2
    first = table[table.shape[0] - 1] == 0
    for i in range(each):
        here = slice(i * width, (i + 1) * width)
        keep[:, here] = jnp.where(first, parts[i], parts[each + i])
        give[:, here] = jnp.where(first, parts[each + i], parts[i])


def query_kernel(table, normed, weight, gain, cosine, sine, raw_out, keep, give):
    width = gain.shape[1]
    raw = nn(normed[...], weight[...])
    raw_out[...] = raw
    parts = []
    for head in range(raw.shape[1] // width):
        here = slice(head * width, (head + 1) * width)
        unit, _ = norm_rows(raw[:, here])
        parts.append(turn(unit * gain[...], cosine[...], sine[...]).astype(BF))
    each = len(parts) // 2
    first = table[table.shape[0] - 1] == 0
    for i in range(each):
        here = slice(i * width, (i + 1) * width)
        keep[:, here] = jnp.where(first, parts[i], parts[each + i])
        give[:, here] = jnp.where(first, parts[each + i], parts[i])


def query_back_kernel(table, kept, given, raw, gain, cosine, sine, low_out, gain_out):
    width = gain.shape[1]
    total = jnp.zeros((8, width), F32)
    first = table[table.shape[0] - 1] == 0
    heads = raw.shape[1] // width
    each = heads // 2
    for head in range(heads):
        here = slice(head * width, (head + 1) * width)
        at = slice(head % each * width, (head % each + 1) * width)
        grad = jnp.where(first == (head < each), kept[:, at], given[:, at])
        unit, scale_rows = norm_rows(raw[:, here])
        turned = turn_back(grad, cosine[...], sine[...])
        total = total + jnp.sum((turned * unit).reshape(-1, 8, width), axis=0)
        low_out[:, here] = norm_back(turned * gain[...], unit, scale_rows).astype(BF)
    gain_out[...] = total


def key_value_back_kernel(table, kept, given, raw, gain, cosine, sine, low_out, gain_out):
    width = gain.shape[1]
    groups = raw.shape[1] // width
    each = groups // 2
    total = jnp.zeros((8, width), F32)
    first = table[table.shape[0] - 1] == 0

    def part(group, which):
        place = 2 * (group % each) + which
        here = slice(place * width, (place + 1) * width)
        return jnp.where(
            first == (group < each), kept[:, here].astype(F32), given[:, here].astype(F32)
        )

    for group in range(groups):
        here = slice(group * width, (group + 1) * width)
        unit, scale_rows = norm_rows(raw[:, here])
        turned = turn_back(part(group, 0), cosine[...], sine[...])
        total = total + jnp.sum((turned * unit).reshape(-1, 8, width), axis=0)
        low_out[:, here] = norm_back(turned * gain[...], unit, scale_rows).astype(BF)
        low_out[:, (groups + group) * width : (groups + group + 1) * width] = part(
            group, 1
        ).astype(BF)
    gain_out[...] = total


def whole_call(kernel, scalars, outs, *args, after=()):
    more_args, more_specs = waits(after)
    taken = len(scalars) + len(args)

    def run(*refs):
        kernel(*refs[:taken], *refs[taken + len(more_args) :])

    return pl.pallas_call(
        run,
        out_shape=[jax.ShapeDtypeStruct(shape, dtype) for shape, dtype in outs],
        in_specs=[pl.BlockSpec(memory_space=pltpu.SMEM)] * len(scalars)
        + [pl.BlockSpec(memory_space=pltpu.VMEM)] * len(args)
        + more_specs,
        compiler_params=pltpu.CompilerParams(vmem_limit_bytes=VMEM_LIMIT),
        cost_estimate=LIGHT,
    )(*scalars, *args, *more_args)


def stacked(ref, start, span, width):
    rows = pl.ds(start, span)
    return jnp.concatenate([ref[rows, :width], ref[rows, width:]], axis=0)


def causal(span, transposed):
    shape = (span, 2 * span) if transposed else (2 * span, span)
    key = lax.broadcasted_iota(jnp.int32, shape, 0 if transposed else 1)
    row = lax.broadcasted_iota(jnp.int32, shape, 1 if transposed else 0)
    return key <= row % span


def side_met(order, table, pair, offset, other):
    last = table.shape[0] - 1
    core = table[last]

    def lower(device):
        return jnp.minimum(order[2 * device], order[2 * device + 1])

    mine = lower(2 * table[0] + (1 - core if pair else core))
    theirs = lower(2 * table[offset % last] + (1 - core if other else core))
    return jnp.where(theirs < mine, 0, 1)


def forward_kernel(places, own, last, span, width, order, table, *refs):
    count = len(places)
    queries, blocks, refs = refs[:2], refs[2 : 2 + count], refs[2 + count :]
    scale = LOG2E / math.sqrt(width)
    if own:
        before, outs = None, refs
    else:
        before, outs = refs[0], refs[1:]
    accum = outs[-1]
    ones = jnp.ones((span, width), BF)

    def weighted(rows, keys, values, allowed=None):
        scores = nt(rows, keys)
        probs = jnp.exp2(scores * scale)
        if allowed is not None:
            probs = jnp.where(allowed, probs, 0.0)
        return nn(probs.astype(BF), values)

    def extended(block, start):
        return jnp.concatenate([block[pl.ds(start, span), width:], ones], axis=1)

    keys = jnp.concatenate([block[:span, :width] for block in blocks], axis=0)
    values = jnp.concatenate([extended(block, 0) for block in blocks], axis=0)
    rows = jnp.concatenate([stacked(query, span, span, width) for query in queries], axis=0)
    high = weighted(rows, keys, values)
    for pair in range(2):
        part = high[pair * 2 * span : (pair + 1) * 2 * span]
        if own:
            allowed = causal(span, False)
            for side in range(2):
                block, start = blocks[pair], side * span
                met = weighted(
                    stacked(queries[pair], start, span, width),
                    block[start : start + span, :width],
                    extended(block, start),
                    allowed,
                )
                accum[0, pair, side] = met + part if side else met
        else:
            accum[0, pair, 0] = before[0, pair, 0]
            accum[0, pair, 1] = before[0, pair, 1] + part
    for i, (offset, other) in enumerate(places):
        for pair in range(2):
            if own and i == pair:
                continue
            side = side_met(order, table, pair, offset, other)
            start = pl.multiple_of(side * span, span)
            accum[0, pair, side] += weighted(
                stacked(queries[pair], start, span, width),
                blocks[i][pl.ds(start, span), :width],
                extended(blocks[i], start),
            )
    if last:
        wides, lows, logs = outs[0:2], outs[2:4], outs[4]
        for pair in range(2):
            for side in range(2):
                rows = slice(side * span, (side + 1) * span)
                whole = accum[0, pair, side]
                mass = whole[:, width:]
                out = whole[:, :width] / mass
                for head in range(2):
                    part = out[head * span : (head + 1) * span]
                    columns = slice(head * width, (head + 1) * width)
                    wides[pair][rows, columns] = part
                    lows[pair][rows, columns] = part.astype(BF)
                logs[0, pair, side] = jnp.log2(mass).T[:8]


def attention_forward(scalars, queries, blocks, places, before, own, last, after=()):
    rows, columns = queries[0].shape
    span, width = rows // 2, HEAD
    groups = columns // (2 * width)
    tile = pl.BlockSpec((rows, 2 * width), lambda g: (0, g))
    accum_block = (1, 2, 2, 2 * span, 2 * width)
    accum_spec = pl.BlockSpec(accum_block, lambda g: (g, 0, 0, 0, 0))
    args = [*scalars, *queries, *blocks]
    specs = [pl.BlockSpec(memory_space=pltpu.SMEM)] * 2 + [tile] * (2 + len(blocks))
    if not own:
        args.append(before)
        specs.append(accum_spec)
    taken = len(args)
    more_args, more_specs = waits(after)
    scratch = []
    if last:
        wide, low = jax.ShapeDtypeStruct((rows, columns), F32), jax.ShapeDtypeStruct((rows, columns), BF)
        outs = [wide, wide, low, low, jax.ShapeDtypeStruct((groups, 2, 2, 8, 2 * span), F32)]
        out_specs = [tile] * 4 + [pl.BlockSpec((1, 2, 2, 8, 2 * span), lambda g: (g, 0, 0, 0, 0))]
        scratch = [pltpu.VMEM(accum_block, F32)]
    else:
        outs = [jax.ShapeDtypeStruct((groups, *accum_block[1:]), F32)]
        out_specs = [accum_spec]

    def kernel(*refs):
        refs = refs[:taken] + refs[taken + len(more_args) :]
        forward_kernel(places, own, last, span, width, *refs)

    return pl.pallas_call(
        kernel,
        out_shape=outs,
        grid=(groups,),
        in_specs=specs + more_specs,
        out_specs=out_specs,
        scratch_shapes=scratch,
        compiler_params=pltpu.CompilerParams(vmem_limit_bytes=VMEM_LIMIT),
        cost_estimate=LIGHT,
    )(*args, *more_args)


def delta_kernel(grads, outs, delta):
    for pair in range(2):
        grad, out = grads[pair], outs[pair]
        width, span = grad.shape[1] // 2, grad.shape[0] // 2
        for side in range(2):
            rows = slice(side * span, (side + 1) * span)
            product = grad[rows, :].astype(F32) * out[rows, :]
            stack = jnp.concatenate([product[:, :width], product[:, width:]], axis=0)
            total = jnp.sum(stack.T, axis=0, keepdims=True)
            delta[0, pair, side] = jnp.broadcast_to(total, (8, 2 * span))


def attention_delta(grads, outs, after=()):
    rows, columns = grads[0].shape
    width, span = HEAD, rows // 2
    groups = columns // (2 * width)
    tile = pl.BlockSpec((rows, 2 * width), lambda g: (0, g))
    more_args, more_specs = waits(after)

    def kernel(*refs):
        delta_kernel(refs[:2], refs[2:4], refs[-1])

    return pl.pallas_call(
        kernel,
        out_shape=jax.ShapeDtypeStruct((groups, 2, 2, 8, 2 * span), F32),
        grid=(groups,),
        in_specs=[tile] * 4 + more_specs,
        out_specs=pl.BlockSpec((1, 2, 2, 8, 2 * span), lambda g: (g, 0, 0, 0, 0)),
        compiler_params=pltpu.CompilerParams(vmem_limit_bytes=VMEM_LIMIT),
        cost_estimate=LIGHT,
    )(*grads, *outs, *more_args)


def backward_kernel(places, own, first, last, split, span, width, order, table, *refs):
    count = len(places)
    queries, grads, (logs, delta), refs = refs[:2], refs[2:4], refs[4:6], refs[6:]
    blocks, refs = refs[:count], refs[count:]
    if not first:
        before, refs = refs[0], refs[1:]
    outs = refs[: count if split else count // 2]
    refs = refs[len(outs) :]
    if last:
        query_outs, accum = refs[:2], refs[2]
    else:
        accum = refs[0]
    scale = LOG2E / math.sqrt(width)
    factor = 1.0 / math.sqrt(width)

    def products(rows, row_grads, log, mean, keys, values, allowed=None):
        probs = jnp.exp2(nt(keys, rows) * scale - log)
        if allowed is not None:
            probs = jnp.where(allowed, probs, 0.0)
        prob_grad = nt(values, row_grads)
        score_grad = (probs * (prob_grad - mean)).astype(BF)
        return nn(score_grad, rows), nn(probs.astype(BF), row_grads), tn(keys, score_grad)

    def of_pair(pair, side, start, keys, values, allowed=None):
        return products(
            stacked(queries[pair], start, span, width),
            stacked(grads[pair], start, span, width),
            logs[0, pair, side, :1],
            delta[0, pair, side, :1],
            keys,
            values,
            allowed,
        )

    low_keys, low_values, high_query = products(
        jnp.concatenate([stacked(query, span, span, width) for query in queries], axis=0),
        jnp.concatenate([stacked(grad, span, span, width) for grad in grads], axis=0),
        jnp.concatenate([logs[0, pair, 1, :1] for pair in range(2)], axis=1),
        jnp.concatenate([delta[0, pair, 1, :1] for pair in range(2)], axis=1),
        jnp.concatenate([block[:span, :width] for block in blocks], axis=0),
        jnp.concatenate([block[:span, width:] for block in blocks], axis=0),
    )
    for pair in range(2):
        part = high_query[:, pair * 2 * span : (pair + 1) * 2 * span]
        if first:
            accum[0, pair, 0] = jnp.zeros_like(part)
            accum[0, pair, 1] = part
        else:
            accum[0, pair, 0] = before[0, pair, 0]
            accum[0, pair, 1] = before[0, pair, 1] + part
    for i, (offset, other) in enumerate(places):
        here = slice(i * span, (i + 1) * span)
        block = blocks[i]
        key_sums, value_sums = [low_keys[here], 0.0], [low_values[here], 0.0]
        for pair in range(2):
            if own and i == pair:
                allowed = causal(span, True)
                for side in range(2):
                    rows = slice(side * span, (side + 1) * span)
                    key_part, value_part, query_part = of_pair(
                        pair, side, side * span, block[rows, :width], block[rows, width:], allowed
                    )
                    accum[0, pair, side] += query_part
                    key_sums[side] = key_sums[side] + key_part
                    value_sums[side] = value_sums[side] + value_part
                continue
            side = side_met(order, table, pair, offset, other)
            start = pl.multiple_of(side * span, span)
            rows = pl.ds(start, span)
            key_part, value_part, query_part = of_pair(
                pair, side, start, block[rows, :width], block[rows, width:]
            )
            accum[0, pair, side] += query_part
            low = side == 0
            key_sums[0] = key_sums[0] + jnp.where(low, key_part, 0.0)
            value_sums[0] = value_sums[0] + jnp.where(low, value_part, 0.0)
            key_sums[1] = key_sums[1] + jnp.where(low, 0.0, key_part)
            value_sums[1] = value_sums[1] + jnp.where(low, 0.0, value_part)
        out = outs[i] if split else outs[i // 2]
        base = 0 if split else i % 2 * 2 * span
        for side in range(2):
            rows = slice(base + side * span, base + (side + 1) * span)
            out[rows, :width] = (key_sums[side] * factor).astype(BF)
            out[rows, width:] = value_sums[side].astype(BF)
    if last:
        for pair in range(2):
            for side in range(2):
                part = accum[0, pair, side].T * factor
                rows = slice(side * span, (side + 1) * span)
                query_outs[pair][rows, :width] = part[:span]
                query_outs[pair][rows, width:] = part[span:]


def attention_backward(
    scalars, queries, grads, logs, delta, blocks, places, before, own, last, split, after=()
):
    rows, columns = queries[0].shape
    span, width = rows // 2, HEAD
    groups = columns // (2 * width)
    count = len(blocks)
    first = before is None
    tile = pl.BlockSpec((rows, 2 * width), lambda g: (0, g))
    stat = pl.BlockSpec((1, 2, 2, 8, 2 * span), lambda g: (g, 0, 0, 0, 0))
    accum_block = (1, 2, 2, width, 2 * span)
    accum_spec = pl.BlockSpec(accum_block, lambda g: (g, 0, 0, 0, 0))
    args = [*scalars, *queries, *grads, logs, delta, *blocks]
    specs = [pl.BlockSpec(memory_space=pltpu.SMEM)] * 2 + [tile] * 4 + [stat] * 2 + [tile] * count
    if not first:
        args.append(before)
        specs.append(accum_spec)
    taken = len(args)
    more_args, more_specs = waits(after)
    if split:
        outs = [jax.ShapeDtypeStruct((rows, columns), BF)] * count
        out_specs = [tile] * count
    else:
        outs = [jax.ShapeDtypeStruct((2 * rows, columns), BF)] * (count // 2)
        out_specs = [pl.BlockSpec((2 * rows, 2 * width), lambda g: (0, g))] * (count // 2)
    scratch = []
    if last:
        outs += [jax.ShapeDtypeStruct((rows, columns), F32)] * 2
        out_specs += [tile] * 2
        scratch = [pltpu.VMEM(accum_block, F32)]
    else:
        outs.append(jax.ShapeDtypeStruct((groups, *accum_block[1:]), F32))
        out_specs.append(accum_spec)

    def kernel(*refs):
        refs = refs[:taken] + refs[taken + len(more_args) :]
        backward_kernel(places, own, first, last, split, span, width, *refs)

    return pl.pallas_call(
        kernel,
        out_shape=outs,
        grid=(groups,),
        in_specs=specs + more_specs,
        out_specs=out_specs,
        scratch_shapes=scratch,
        compiler_params=pltpu.CompilerParams(vmem_limit_bytes=VMEM_LIMIT),
        cost_estimate=LIGHT,
    )(*args, *more_args)


def body(
    devices,
    residual,
    cotangent,
    span_order,
    positions,
    attn_gain,
    query_weight,
    key_weight,
    value_weight,
    query_gain,
    key_gain,
    out_weight,
    mlp_gain,
    gate_weight,
    up_weight,
    down_weight,
):
    ring = Ring(devices)
    rows, model = residual.shape
    head_dim = query_gain.shape[0]
    span = rows // 2
    index = lax.axis_index("cp")
    scalars = [span_order, ring.table]
    table = [ring.table]
    ordered = lax.dynamic_slice_in_dim(span_order, 2 * index, 2)
    in_order = ordered[0] < ordered[1]

    def canonical(x):
        return jnp.where(in_order, x, jnp.roll(x, span, axis=0))

    half = head_dim // 2
    freq = ROPE_BASE ** (-(jnp.arange(half, dtype=F32) * 2.0) / head_dim)
    angle = positions.astype(F32)[:, None] * freq[None, :]
    cosine, sine = jnp.cos(angle), jnp.sin(angle)
    cosine = jnp.concatenate([cosine, cosine], axis=1)
    sine = jnp.concatenate([-sine, sine], axis=1)

    query_gain_row = query_gain.reshape(1, -1)
    key_gain_row = key_gain.reshape(1, -1)
    key_columns = key_weight.shape[1]
    query_columns = query_weight.shape[1]
    each = query_columns // 2

    residual, normed_low, keys_raw, cosine, sine, keep, give = whole_call(
        key_value_kernel,
        scalars,
        [((rows, model), BF), ((rows, model), BF), ((rows, key_columns), F32)]
        + [((rows, head_dim), F32)] * 2
        + [((rows, key_columns), BF)] * 2,
        residual, attn_gain.reshape(1, -1), key_weight, value_weight, key_gain_row, cosine, sine,
    )

    parts = [keep, ring.sibling(give)]
    ways = [(ring.send_up(part), ring.send_down(part)) for part in parts]
    queries_raw, query_keep, query_give = whole_call(
        query_kernel,
        table,
        [((rows, query_columns), F32)] + [((rows, each), BF)] * 2,
        normed_low, query_weight, query_gain_row, cosine, sine,
    )
    queries = [query_keep, ring.sibling(query_give)]

    def places_of(offsets):
        return [(offset, other) for offset in offsets for other in (False, True)]

    cotangent = canonical(cotangent)
    hidden_grad = nt(cotangent, down_weight)
    out_keep = lax.dynamic_slice_in_dim(out_weight, ring.core * each, each)
    out_give = lax.dynamic_slice_in_dim(out_weight, (1 - ring.core) * each, each)
    steps = ring.half
    calls = {0: ([0], parts)}
    state = None
    for step in range(1, steps):
        come = []
        for which in range(2):
            up, down = ways[which]
            if step > 1:
                up, down, state = tie(up, down, state)
            come.append((up, down))
            if step < steps - 1:
                ways[which] = ring.send_up(up), ring.send_down(down)
            else:
                ways[which] = ring.send_down(down) if which else ring.send_up(up)
        if step == 1:
            (state,) = attention_forward(
                scalars, queries, parts, places_of([0]), None, True, False, after=come[0]
            )
            state, hidden_grad, out_keep, out_give = tie(state, hidden_grad, out_keep, out_give)
        blocks = [come[0][0], come[1][0], come[0][1], come[1][1]]
        calls[step] = ([-step, step], blocks)
        (state,) = attention_forward(
            scalars, queries, blocks, places_of([-step, step]), state, False, False
        )
    *ways, state = tie(*ways, state)
    calls[steps] = ([steps], ways)
    *attended, low_keep, low_give, logs = attention_forward(
        scalars, queries, ways, places_of([steps]), state, False, True
    )
    low_other = ring.sibling(low_give)
    mixed_part = (nn(low_keep, out_keep) + nn(low_other, out_give)).astype(BF)

    residual_wide = residual.astype(F32)
    mixed = residual_wide + both(mixed_part, partner(mixed_part))
    normed_two, scale_two = norm_rows(mixed)
    normed_two_low = (normed_two * mlp_gain).astype(BF)
    gate = nn(normed_two_low, gate_weight)
    upward = nn(normed_two_low, up_weight)
    sigmoid_gate = jax.nn.sigmoid(gate)
    activated = gate * sigmoid_gate
    hidden_low = (activated * upward).astype(BF)
    gate_grad_low = (
        hidden_grad * upward * sigmoid_gate * (1.0 + gate * (1.0 - sigmoid_gate))
    ).astype(BF)
    up_grad_low = (hidden_grad * activated).astype(BF)
    normed_two_part = (nt(gate_grad_low, gate_weight) + nt(up_grad_low, up_weight)).astype(BF)
    normed_two_part, normed_two_low, hidden_low = tie(normed_two_part, normed_two_low, hidden_low)
    normed_two_other = partner(normed_two_part)

    units = gate_weight.shape[1]
    thirds = 2 * units // model
    gate_rows, down_rows = model // devices, units // thirds // devices
    wide = Gradients(
        ring,
        gate_rows + down_rows,
        2 * units,
        [
            ((1, gate_rows, 2 * units), [(0, 0)]),
            ((thirds, down_rows, model), [(gate_rows, i * model) for i in range(thirds)]),
        ],
    )
    both_grad_low = jnp.concatenate([gate_grad_low, up_grad_low], axis=1)
    wide.put(0, tn(normed_two_low, both_grad_low).astype(BF)[None])
    wide.put(1, tn(hidden_low, cotangent).astype(BF).reshape(thirds, -1, model))
    wide_steps = wide.scatter()
    wide_way, wide_token = next(wide_steps)
    normed_two_other, wide_token = tie(normed_two_other, wide_token)

    normed_two_grad = both(normed_two_part, normed_two_other)
    mlp_gain_term = jnp.sum(normed_two_grad * normed_two, axis=0)
    mixed_grad = cotangent.astype(F32) + norm_back(
        normed_two_grad * mlp_gain, normed_two, scale_two
    )
    mixed_grad_low = mixed_grad.astype(BF)
    grads = [
        nt(mixed_grad_low, out_keep).astype(BF),
        ring.sibling(nt(mixed_grad_low, out_give).astype(BF)),
    ]
    delta = attention_delta(grads, attended, after=[wide_token])

    def backward(step, state, after):
        offsets, blocks = calls[step]
        last = step == 0
        return attention_backward(
            scalars, queries, grads, logs, delta, blocks, places_of(offsets), state,
            last, last, last or step == steps, after,
        )

    up, down, state = backward(steps, None, [])
    token = up
    up, down = ring.send_up(up), ring.send_down(down)
    for step in range(steps - 1, 0, -1):
        back, front, state = backward(step, state, [token])
        wide_way, wide_token = wide_steps.send((wide_way, [state]))
        up, down, token = pair_add([front, back], [up, down], step == steps - 1, [wide_token])
        up, down = ring.send_up(up), ring.send_down(down)
    key_value_keep, key_value_give, grad_keep, grad_give = backward(0, state, [token])
    hidden_low, token = tie(hidden_low, token)
    layer_part = nn(hidden_low, down_weight).astype(BF)
    layer_other = partner(layer_part)
    query_grad_low, query_gain_term = whole_call(
        query_back_kernel,
        table,
        [((rows, query_columns), BF), ((8, head_dim), F32)],
        grad_keep, ring.sibling(grad_give), queries_raw, query_gain_row, cosine, sine,
    )
    wide_shard, wide_token = wide_steps.send((wide_way, [query_gain_term, token]))
    wide_outs = [(0, 0, units), (0, units, units), (1, 0, model)]
    wide_steps = wide.gather(wide_shard)
    wide_way, wide_ready = next(wide_steps)

    rows_each = model // devices
    narrow = Gradients(
        ring,
        rows_each,
        3 * model,
        [((1, rows_each, model), [(0, i * model)]) for i in range(3)],
    )
    narrow_outs = [(0, 0, model), (1, 0, model), (2, 0, key_columns), (2, key_columns, key_columns)]
    attended_low = jnp.where(
        ring.core == 0,
        jnp.concatenate([low_keep, low_other], axis=1),
        jnp.concatenate([low_other, low_keep], axis=1),
    )
    narrow.put(0, tn(attended_low, mixed_grad_low).astype(BF)[None])
    narrow.put(1, tn(normed_low, query_grad_low).astype(BF)[None])
    up, down, wide_token, layer_other, narrow.other[0], narrow.other[1] = tie(
        up, down, wide_token, layer_other, narrow.other[0], narrow.other[1]
    )
    up, down = up.astype(F32), down.astype(F32)
    key_value_give = (key_value_give.astype(F32) + up[rows:] + down[rows:]).astype(BF)
    key_value_keep = key_value_keep.astype(F32) + up[:rows] + down[:rows]
    key_value_other = ring.sibling(key_value_give)
    layer_out = canonical(mixed + both(layer_part, layer_other)).astype(BF)

    def own_ready(ready):
        return [(offset, part, False) for offset, part in ready]

    def other_ready(ready):
        return [(offset, ring.sibling(part), True) for offset, part in ready]

    wide_come = list(wide_ready)
    wide_results = wide.unpack(own_ready(wide_ready), wide_outs, None, [wide_token])
    key_value_grad, key_gain_term = whole_call(
        key_value_back_kernel,
        table,
        [((rows, 2 * key_columns), BF), ((8, head_dim), F32)],
        key_value_keep, key_value_other, keys_raw, key_gain_row, cosine, sine,
    )
    *wide_way, key_value_grad, wide_results[0] = tie(*wide_way, key_value_grad, wide_results[0])
    wide_way, wide_ready = wide_steps.send(wide_way)
    wide_come += wide_ready
    narrow.put(2, tn(normed_low, key_value_grad).astype(BF)[None])
    narrow_steps = narrow.scatter()
    narrow_way, token = next(narrow_steps)

    key_value_grad, token = tie(key_value_grad, token)
    normed_part = (
        nt(query_grad_low, query_weight)
        + nt(key_value_grad[:, :key_columns], key_weight)
        + nt(key_value_grad[:, key_columns:], value_weight)
    ).astype(BF)
    normed_other = partner(normed_part)
    gains = jnp.stack([jnp.sum(query_gain_term, axis=0), jnp.sum(key_gain_term, axis=0)])
    wide_results = wide.unpack(own_ready(wide_ready), wide_outs, wide_results, [token])

    narrow_way, token = narrow_steps.send((narrow_way, [wide_results[0]]))
    *wide_way, normed_other, token = tie(*wide_way, normed_other, token)
    wide_way, wide_ready = wide_steps.send(wide_way)
    wide_come += wide_ready
    gains = gains + partner(gains)
    normed_one, scale_one = norm_rows(residual_wide)
    normed_grad = both(normed_part, normed_other)
    attn_gain_term = jnp.sum(normed_grad * normed_one, axis=0)
    residual_grad = canonical(
        mixed_grad + norm_back(normed_grad * attn_gain, normed_one, scale_one)
    )
    wide_results = wide.unpack(own_ready(wide_ready), wide_outs, wide_results, [token])

    narrow_way, token = narrow_steps.send((narrow_way, [wide_results[0]]))
    small = SmallSum(
        devices,
        jnp.concatenate([attn_gain_term, mlp_gain_term, gains[0], gains[1]]).reshape(-1, 128),
    )
    for step in range(steps - 3):
        narrow_way, token = narrow_steps.send((narrow_way, [token]))
        *wide_way, token = tie(*wide_way, token)
        wide_way, wide_ready = wide_steps.send(wide_way)
        wide_come += wide_ready
        *came, token = tie(*small.under_way, token)
        small.came(came)
        wide_results = wide.unpack(own_ready(wide_ready), wide_outs, wide_results, [token])
    narrow_shard, token = narrow_steps.send((narrow_way, [wide_results[0]]))

    narrow_steps = narrow.gather(narrow_shard)
    narrow_way, narrow_ready = next(narrow_steps)
    wide_way, came, token = tie(wide_way, small.under_way, token)
    small.came(came)
    _, wide_ready = wide_steps.send(wide_way)
    wide_come += wide_ready
    wide_results = wide.unpack(own_ready(wide_ready), wide_outs, wide_results, [token])
    share = -(-len(wide_come) // steps)
    narrow_results = None
    for step in range(1, steps + 1):
        here = wide_come[(step - 1) * share : step * share]
        if here:
            wide_results = wide.unpack(other_ready(here), wide_outs, wide_results)
        ready = own_ready(narrow_ready) + other_ready(narrow_ready)
        narrow_results = narrow.unpack(ready, narrow_outs, narrow_results, [wide_results[0]])
        if step < steps:
            narrow_way, came, narrow_results[0] = tie(
                narrow_way, small.under_way, narrow_results[0]
            )
            small.came(came)
            narrow_way, narrow_ready = narrow_steps.send(narrow_way)
    while small.under_way:
        small.came(small.under_way)
    _, narrow_ready = narrow_steps.send(narrow_way)
    ready = own_ready(narrow_ready) + other_ready(narrow_ready)
    out_weight_sum, query_sum, key_sum, value_sum = narrow.unpack(
        ready, narrow_outs, narrow_results
    )
    gate_sum, up_sum, down_sum = wide_results
    small = small.total.reshape(-1)

    attn_gain_grad, mlp_gain_grad = small[:model], small[model : 2 * model]
    query_gain_grad = small[2 * model : 2 * model + head_dim]
    key_gain_grad = small[2 * model + head_dim :]
    return (
        layer_out,
        residual_grad,
        attn_gain_grad,
        query_sum[0],
        key_sum[0],
        value_sum[0],
        query_gain_grad,
        key_gain_grad,
        out_weight_sum[0],
        mlp_gain_grad,
        gate_sum[0],
        up_sum[0],
        down_sum.reshape(units, model),
    )


def solution(mesh):
    return jax.shard_map(
        functools.partial(body, mesh.shape["cp"]),
        mesh=mesh,
        in_specs=(
            P("cp", None),
            P("cp", None),
            P(),
            P("cp"),
            P(),
            P(None, "tp"),
            P(None, "tp"),
            P(None, "tp"),
            P(),
            P(),
            P("tp", None),
            P(),
            P(None, "tp"),
            P(None, "tp"),
            P("tp", None),
        ),
        out_specs=(
            P("cp", None),
            P("cp", None),
            P(),
            P(None, "tp"),
            P(None, "tp"),
            P(None, "tp"),
            P(),
            P(),
            P("tp", None),
            P(),
            P(None, "tp"),
            P(None, "tp"),
            P("tp", None),
        ),
        check_vma=False,
    )
```

```python
import functools
import math

import jax
import jax.numpy as jnp
from jax import lax
from jax.experimental import pallas as pl
from jax.experimental.pallas import tpu as pltpu
from jax.sharding import PartitionSpec as P

EPS = 1e-06
ROPE_BASE = 1000000.0
HEAD = 128
LOG2E = 1.4426950408889634
VMEM_LIMIT = 32 * 1024 * 1024


def cost(microseconds):
    return pl.CostEstimate(
        flops=1024 + int(microseconds * 1e9), bytes_accessed=1024, transcendentals=0
    )


LIGHT = cost(0)
FORWARD = cost(0)
HEAVY = 50
SOME = 4
BF = jnp.bfloat16
F32 = jnp.float32
TOKEN = jax.ShapeDtypeStruct((8, 128), jnp.float32)


def nn(a, b):
    return lax.dot_general(a, b, (((1,), (0,)), ((), ())), preferred_element_type=F32)


def nt(a, b):
    return lax.dot_general(a, b, (((1,), (1,)), ((), ())), preferred_element_type=F32)


def tn(a, b):
    return lax.dot_general(a, b, (((0,), (0,)), ((), ())), preferred_element_type=F32)


def norm_rows(values):
    scale_rows = lax.rsqrt(jnp.mean(values * values, axis=-1, keepdims=True) + EPS)
    return (values * scale_rows, scale_rows)


def norm_back(grad_normed, normed, scale_rows):
    return scale_rows * (
        grad_normed - normed * jnp.mean(grad_normed * normed, axis=-1, keepdims=True)
    )


def tie(*values):
    return lax.optimization_barrier(values)


def waits(after):
    return list(after), [pl.BlockSpec(memory_space=pl.ANY)] * len(after)


def in_hbm(x):
    return pltpu.with_memory_space_constraint(x, pltpu.HBM)


def ring_order(chips):
    if chips % 8:
        return list(range(chips))
    rows, cols = 4, chips // 4
    if cols % 2 or cols < 4:
        path = list(range(cols))
    else:
        path = list(range(cols // 2)) + list(range(cols - 1, cols // 2 - 1, -1))
    walk = []
    for row in range(rows):
        across = range(1, cols) if row % 2 == 0 else range(cols - 1, 0, -1)
        walk += [(row, col) for col in across]
    walk = [(0, 0)] + walk + [(row, 0) for row in range(rows - 1, 0, -1)]
    return [row * cols + path[col] for row, col in walk]


class Ring:
    def __init__(self, devices):
        self.devices = devices
        self.chips = devices // 2
        order = ring_order(self.chips)
        self.order = order
        size = self.chips
        self.up = [
            (2 * order[i] + core, 2 * order[(i + 1) % size] + core)
            for i in range(size)
            for core in range(2)
        ]
        self.down = [(b, a) for a, b in self.up]
        self.swap = [(i, i ^ 1) for i in range(devices)]
        place = [0] * size
        for i, chip in enumerate(order):
            place[chip] = i
        index = lax.axis_index("cp")
        self.core = index % 2
        self.here = jnp.asarray(place, jnp.int32)[index // 2]
        self.half = size // 2
        table = [
            [order[(place[chip] + i) % size] for i in range(size)] + [core]
            for chip in range(size)
            for core in range(2)
        ]
        self.table = lax.dynamic_index_in_dim(
            jnp.asarray(table, jnp.int32), index, 0, keepdims=False
        )

    def send_up(self, x):
        return lax.ppermute(x, "cp", self.up)

    def send_down(self, x):
        return lax.ppermute(x, "cp", self.down)

    def sibling(self, x):
        return lax.ppermute(x, "cp", self.swap)


def products(table, lefts, rights, chips, packed, row, column, before, after=(), price=0, thirds=1, halved=True):
    tokens = lefts[0].shape[0]
    high = lefts[0].shape[1] // thirds // (2 if halved else 1)
    rows = high // chips
    wide = rights[0].shape[1]
    tile = min(wide, 512)
    last = table.shape[0] - 1
    more_args, more_specs = waits(after)
    if before is not None:
        more_args, more_specs = [before] + more_args, [pl.BlockSpec(memory_space=pl.ANY)] + more_specs
    side = len(lefts)

    def kernel(table_ref, *refs):
        out, token, turned = refs[side + len(rights) + len(more_args) :]

        @pl.when(pl.program_id(1) == 0)
        def _():
            for i in range(side):
                turned[:, i * tokens : (i + 1) * tokens] = refs[i][...].T
            token[...] = jnp.zeros_like(token)

        total, start = 0.0, 0
        for right in refs[side : side + len(rights)]:
            stop = start + right.shape[0]
            total = total + nn(turned[:, start:stop], right[...])
            start = stop
        out[...] = total.reshape(chips, rows, tile).astype(BF)

    def left_place(j, i, t):
        return (0, 2 * j + t[last] if halved else j)

    across = packed[1] // tile

    def out_place(j, i, t):
        at = column // tile + i
        return (0, row // rows + j + at // across, at % across)

    shape = jax.ShapeDtypeStruct((chips, *packed), BF)
    return pl.pallas_call(
        kernel,
        out_shape=[shape, TOKEN],
        grid_spec=pltpu.PrefetchScalarGridSpec(
            num_scalar_prefetch=1,
            grid=(thirds, wide // tile),
            in_specs=[pl.BlockSpec((tokens, high), left_place)] * side
            + [pl.BlockSpec((right.shape[0], tile), lambda j, i, t: (0, i)) for right in rights]
            + more_specs,
            out_specs=[
                pl.BlockSpec((chips, rows, tile), out_place),
                pl.BlockSpec((8, 128), lambda j, i, t: (0, 0)),
            ],
            scratch_shapes=[pltpu.VMEM((high, side * tokens), BF)],
        ),
        input_output_aliases={} if before is None else {1 + side + len(rights): 0},
        compiler_params=pltpu.CompilerParams(vmem_limit_bytes=VMEM_LIMIT),
        cost_estimate=cost(price),
    )(table, *lefts, *rights, *more_args)


class Gradients:
    def __init__(self, ring, rows, columns, outs):
        self.ring, self.rows, self.columns, self.outs = ring, rows, columns, outs
        self.cut = -(-rows // 32) * 16
        self.packed = None

    def shards(self, offsets, received, halves, after=()):
        ring, columns, rows, cut = self.ring, self.columns, self.rows, self.cut
        spans = [(0, cut), (cut, rows)]
        sides = len(offsets)
        args = [self.packed] * sides
        specs = [
            pl.BlockSpec((1, rows, columns), lambda i, t, at=offset: (t[at % ring.chips], 0, 0))
            for offset in offsets
        ]
        args += received
        specs += [pl.BlockSpec(x.shape, lambda i, t: (0, 0)) for x in received]
        more_args, more_specs = waits(after)
        taken = len(args) + len(more_args)

        def kernel(table_ref, *refs):
            outs = refs[taken:]
            outs[-1][...] = jnp.zeros_like(outs[-1])
            gained = refs[sides : len(args)]
            for side in range(sides):
                mine = refs[side]
                if halves == "send":
                    for out, (start, stop) in zip(outs, spans):
                        out[...] = mine[0, start:stop]
                elif halves == "add":
                    for got, (start, stop) in zip([gained[side]], [spans[side]]):
                        outs[side][start:stop] = (
                            mine[0, start:stop].astype(F32) + got[...].astype(F32)
                        ).astype(BF)
                    start, stop = spans[1 - side]
                    outs[side][start:stop] = mine[0, start:stop]
                else:
                    total = mine[0].astype(F32)
                    for got in gained if halves == "sum" else [gained[side]]:
                        total = total + got[...].astype(F32)
                    outs[side][...] = total.astype(BF)

        highs = {"send": [cut, rows - cut], "sum": [rows]}.get(halves, [rows, rows])
        return pl.pallas_call(
            kernel,
            out_shape=[jax.ShapeDtypeStruct((high, columns), BF) for high in highs] + [TOKEN],
            grid_spec=pltpu.PrefetchScalarGridSpec(
                num_scalar_prefetch=1,
                grid=(1,),
                in_specs=specs + more_specs,
                out_specs=[pl.BlockSpec((high, columns), lambda i, t: (0, 0)) for high in highs]
                + [pl.BlockSpec((8, 128), lambda i, t: (0, 0))],
            ),
            compiler_params=pltpu.CompilerParams(vmem_limit_bytes=VMEM_LIMIT),
            cost_estimate=LIGHT,
        )(ring.table, *args, *more_args)

    def scatter(self, after=()):
        ring = self.ring
        up, down, token = self.shards([ring.half], [], "send", after)
        for step in range(ring.half - 1, -1, -1):
            (up, down), after = yield (ring.send_up(up), ring.send_down(down)), token
            if step:
                kind = "add" if step == ring.half - 1 else ""
                up, down, token = self.shards([step, -step], [up, down], kind, after)
        yield self.shards([0], [up, down], "sum", after)

    def gather(self, own):
        ring, cut = self.ring, self.cut
        up = down = own
        ready = [(0, own)]
        for step in range(1, ring.half):
            up, down = yield (ring.send_up(up), ring.send_down(down)), ready
            ready = [(-step, up), (step, down)]
        high, low = yield (ring.send_up(up[:cut]), ring.send_down(down[cut:])), ready
        yield None, [(ring.half, jnp.concatenate([high, low], axis=0))]

    def unpack_stack(self, stack, offsets, before, after=(), price=0):
        return self.unpack(
            [(offset, stack, True) for offset in offsets], before, after, price, True
        )

    def unpack(self, ready, before, after=(), price=0, stacked=False):
        ring, outs = self.ring, self.outs
        count = len(ready)
        args = [ready[0][1]] if stacked else [part for _, part, _ in ready]
        places_of = [(offset, other) for offset, _, other in ready]

        def write(part, results):
            for out, (_, _, _, moves) in zip(results, outs):
                for where, rows, columns in moves:
                    out[where] = part[rows, columns].astype(F32)

        def kernel(table_ref, *refs):
            step = pl.program_id(0)
            results = refs[-len(outs) - 1 : -1]
            refs[-1][...] = jnp.zeros_like(refs[-1])
            if stacked:
                write(refs[0].at[0], results)
                return
            for i in range(count):
                pl.when(step == i)(functools.partial(write, refs[i], results))

        def place(of_chip, i, table):
            chip, core = None, None
            for j, (offset, other) in enumerate(places_of):
                here = table[offset % ring.chips]
                mine = table[ring.chips]
                mine = 1 - mine if other else mine
                chip = here if chip is None else jnp.where(i == j, here, chip)
                core = mine if core is None else jnp.where(i == j, mine, core)
            return of_chip(chip, core)

        shapes, out_specs = [], []
        for shape, block, of_chip, _ in outs:
            shapes.append(pltpu.HBM(shape, F32))
            out_specs.append(pl.BlockSpec(block, functools.partial(place, of_chip)))
        shapes.append(TOKEN)
        out_specs.append(pl.BlockSpec((8, 128), lambda i, t: (0, 0)))
        if stacked:
            specs = [pl.BlockSpec((1, self.rows, self.columns), lambda i, t: (i, 0, 0))]
        else:
            specs = [pl.BlockSpec((self.rows, self.columns), lambda i, t: (0, 0))] * count
        aliases = {}
        if before is not None:
            aliases = {1 + len(args) + i: i for i in range(len(outs))}
            specs += [pl.BlockSpec(memory_space=pl.ANY)] * len(outs)
            args += [in_hbm(x) for x in before[: len(outs)]]
        more_args, more_specs = waits(after)
        args += more_args
        specs += more_specs
        return list(
            pl.pallas_call(
                kernel,
                out_shape=shapes,
                grid_spec=pltpu.PrefetchScalarGridSpec(
                    num_scalar_prefetch=1, grid=(count,), in_specs=specs, out_specs=out_specs
                ),
                input_output_aliases=aliases,
                compiler_params=pltpu.CompilerParams(vmem_limit_bytes=VMEM_LIMIT),
                cost_estimate=cost(price),
            )(ring.table, *args)
        )


def stack(parts, after=()):
    rows, columns = parts[0].shape
    count = len(parts)
    more_args, more_specs = waits(after)

    def kernel(*refs):
        token, semaphores = refs[-2], refs[-1]
        token[...] = jnp.zeros_like(token)
        out = refs[-3]
        copies = [
            pltpu.make_async_copy(refs[i], out.at[i], semaphores.at[i]) for i in range(count)
        ]
        for copy in copies:
            copy.start()
        for copy in copies:
            copy.wait()

    return pl.pallas_call(
        kernel,
        out_shape=[jax.ShapeDtypeStruct((count, rows, columns), parts[0].dtype), TOKEN],
        in_specs=[pl.BlockSpec(memory_space=pl.ANY)] * count + more_specs,
        out_specs=[pl.BlockSpec(memory_space=pl.ANY), pl.BlockSpec(memory_space=pltpu.VMEM)],
        scratch_shapes=[pltpu.SemaphoreType.DMA((count,))],
        compiler_params=pltpu.CompilerParams(vmem_limit_bytes=VMEM_LIMIT),
        cost_estimate=LIGHT,
    )(*parts, *more_args)


def pair_add(own, received, half, after=()):
    more_args, more_specs = waits(after)

    def kernel(*refs):
        refs, outs = refs[:4], refs[4 + len(more_args) :]
        outs[-1][...] = jnp.zeros_like(outs[-1])
        for side in range(2):
            mine, got, out = refs[side], refs[2 + side], outs[side]
            if half:
                rows = got.shape[0]
                here = slice(side * rows, (side + 1) * rows)
                rest = slice((1 - side) * rows, (2 - side) * rows)
                out[here] = (mine[here].astype(F32) + got[...].astype(F32)).astype(BF)
                out[rest] = mine[rest]
            else:
                out[...] = (mine[...].astype(F32) + got[...].astype(F32)).astype(BF)

    shape = jax.ShapeDtypeStruct(own[0].shape, BF)
    return pl.pallas_call(
        kernel,
        out_shape=[shape, shape, TOKEN],
        in_specs=[pl.BlockSpec(memory_space=pltpu.VMEM)] * 4 + more_specs,
        compiler_params=pltpu.CompilerParams(vmem_limit_bytes=VMEM_LIMIT),
        cost_estimate=LIGHT,
    )(*own, *received, *more_args)


class SmallSum:
    def __init__(self, devices, x):
        self.devices, self.bit, self.total = devices, 1, x
        self.under_way = []
        self.send()

    def send(self):
        pairs = [(i, i ^ self.bit) for i in range(self.devices)]
        self.under_way = [lax.ppermute(self.total, "cp", pairs)] if self.bit < self.devices else []
        self.bit *= 2

    def came(self, arrived):
        if arrived:
            self.total = self.total + arrived[0]
            self.send()


def partner(x):
    return lax.ppermute(x, "tp", [(0, 1), (1, 0)])


def both(mine, other):
    return mine.astype(F32) + other.astype(F32)


def turn(values, cosine, sine):
    return values * cosine + pltpu.roll(values, values.shape[-1] // 2, 1) * sine


def turn_back(values, cosine, sine):
    return values * cosine - pltpu.roll(values, values.shape[-1] // 2, 1) * sine


def lower_first(order, table, other):
    core = table[table.shape[0] - 1]
    device = 2 * table[0] + (1 - core if other else core)
    return order[2 * device] < order[2 * device + 1]


def key_value_kernel(order, table, residuals, gain, key_weight, value_weight, key_gain, angles, outs):
    residual_out, normed_outs, raw_outs, cosine_outs, sine_outs, packed_outs = outs
    width = key_gain.shape[1]
    span = residuals[0].shape[0] // 2
    for pair in range(2):
        start = jnp.where(lower_first(order, table, pair == 1), 0, span)

        def canonical(ref):
            return jnp.concatenate(
                [
                    ref[pl.ds(pl.multiple_of(start, span), span)],
                    ref[pl.ds(pl.multiple_of(span - start, span), span)],
                ],
                axis=0,
            )

        rows = canonical(residuals[pair])
        if pair == 0:
            residual_out[...] = rows
        unit, _ = norm_rows(rows.astype(F32))
        normed = (unit * gain[...]).astype(BF)
        normed_outs[pair][...] = normed
        cosine, sine = canonical(angles[2 * pair]), canonical(angles[2 * pair + 1])
        cosine_outs[pair][...], sine_outs[pair][...] = cosine, sine
        raw = nn(normed, key_weight[...])
        raw_outs[pair][...] = raw
        values = nn(normed, value_weight[...]).astype(BF)
        for group in range(raw.shape[1] // width):
            here = slice(group * width, (group + 1) * width)
            key_unit, _ = norm_rows(raw[:, here])
            packed = packed_outs[pair]
            packed[:, 2 * group * width : (2 * group + 1) * width] = turn(
                key_unit * key_gain[...], cosine, sine
            ).astype(BF)
            packed[:, (2 * group + 1) * width : (2 * group + 2) * width] = values[:, here]


def query_kernel(normeds, weight, gain, cosines, sines, raw_outs, low_outs):
    width = gain.shape[1]
    for pair in range(2):
        raw = nn(normeds[pair][...], weight[...])
        raw_outs[pair][...] = raw
        for head in range(raw.shape[1] // width):
            here = slice(head * width, (head + 1) * width)
            unit, _ = norm_rows(raw[:, here])
            low_outs[pair][:, here] = turn(
                unit * gain[...], cosines[pair][...], sines[pair][...]
            ).astype(BF)


def heads_back(grad_of, raws, gain, cosines, sines, out, total):
    width = gain.shape[1]
    rows = raws[0].shape[0]
    for pair in range(2):
        here_rows = slice(pair * rows, (pair + 1) * rows)
        for head in range(raws[pair].shape[1] // width):
            here = slice(head * width, (head + 1) * width)
            unit, scale_rows = norm_rows(raws[pair][:, here])
            turned = turn_back(grad_of(pair, head), cosines[pair][...], sines[pair][...])
            total = total + jnp.sum((turned * unit).reshape(-1, 8, width), axis=0)
            out[here_rows, here] = norm_back(turned * gain[...], unit, scale_rows).astype(BF)
    return total


def query_back_kernel(grads, raws, gain, cosines, sines, low_out, gain_out):
    width = gain.shape[1]
    gain_out[...] = heads_back(
        lambda pair, head: grads[pair][:, head * width : (head + 1) * width],
        raws, gain, cosines, sines, low_out, jnp.zeros((8, width), F32),
    )


def key_value_back_kernel(owns, upward, downward, raws, gain, cosines, sines, low_out, gain_out):
    width = gain.shape[1]
    rows, columns = raws[0].shape
    groups = columns // width

    def summed(pair, place):
        here = slice(place * width, (place + 1) * width)
        at = slice(pair * rows, (pair + 1) * rows)
        return (
            owns[pair][:, here].astype(F32)
            + upward[at, here].astype(F32)
            + downward[at, here].astype(F32)
        )

    gain_out[...] = heads_back(
        lambda pair, head: summed(pair, 2 * head),
        raws, gain, cosines, sines, low_out, jnp.zeros((8, width), F32),
    )
    for pair in range(2):
        for group in range(groups):
            low_out[
                pair * rows : (pair + 1) * rows,
                columns + group * width : columns + (group + 1) * width,
            ] = summed(pair, 2 * group + 1).astype(BF)


def whole_call(kernel, scalars, outs, args, after=()):
    more_args, more_specs = waits(after)
    count = len(scalars)
    arrays, specs = [], []
    for arg in args:
        array, block, place = arg if isinstance(arg, tuple) else (arg, arg.shape, None)
        arrays.append(array)
        if place is None:
            specs.append(pl.BlockSpec(block, lambda i, *t: (0, 0)))
        else:
            specs.append(
                pl.BlockSpec(
                    block, lambda i, *t, place=place: place(t[-1][t[-1].shape[0] - 1])
                )
            )
    taken = count + len(args)

    def run(*refs):
        kernel(*refs[:taken], *refs[taken + len(more_args) :])

    return list(
        pl.pallas_call(
            run,
            out_shape=[
                pltpu.HBM(shape, dtype) if far else jax.ShapeDtypeStruct(shape, dtype)
                for shape, dtype, *far in outs
            ],
            grid_spec=pltpu.PrefetchScalarGridSpec(
                num_scalar_prefetch=count,
                grid=(1,),
                in_specs=specs + more_specs,
                out_specs=[pl.BlockSpec(shape, lambda i, *t: (0, 0)) for shape, *_ in outs],
            ),
            compiler_params=pltpu.CompilerParams(vmem_limit_bytes=VMEM_LIMIT),
            cost_estimate=LIGHT,
        )(*scalars, *arrays, *more_args)
    )


def matmul(left, right, after=()):
    rows, inner = left.shape
    columns = right.shape[1]
    tile = min(columns, 512)
    more_args, more_specs = waits(after)

    def kernel(left_ref, right_ref, *refs):
        refs[-1][...] = nn(left_ref[...], right_ref[...]).astype(BF)

    return pl.pallas_call(
        kernel,
        out_shape=jax.ShapeDtypeStruct((rows, columns), BF),
        grid=(columns // tile,),
        in_specs=[
            pl.BlockSpec((rows, inner), lambda i: (0, 0)),
            pl.BlockSpec((inner, tile), lambda i: (0, i)),
        ]
        + more_specs,
        out_specs=pl.BlockSpec((rows, tile), lambda i: (0, i)),
        compiler_params=pltpu.CompilerParams(vmem_limit_bytes=VMEM_LIMIT),
        cost_estimate=LIGHT,
    )(left, in_hbm(right), *more_args)


def out_projection(table, keep, other, weight):
    rows, inner = keep.shape
    columns = weight.shape[1]
    tile = columns
    last = table.shape[0] - 1

    def kernel(table_ref, keep_ref, other_ref, mine, theirs, out):
        out[...] = (nn(keep_ref[...], mine[...]) + nn(other_ref[...], theirs[...])).astype(BF)

    return pl.pallas_call(
        kernel,
        out_shape=jax.ShapeDtypeStruct((rows, columns), BF),
        grid_spec=pltpu.PrefetchScalarGridSpec(
            num_scalar_prefetch=1,
            grid=(columns // tile,),
            in_specs=[
                pl.BlockSpec((rows, inner), lambda i, t: (0, 0)),
                pl.BlockSpec((rows, inner), lambda i, t: (0, 0)),
                pl.BlockSpec((inner, tile), lambda i, t: (t[last], i)),
                pl.BlockSpec((inner, tile), lambda i, t: (1 - t[last], i)),
            ],
            out_specs=pl.BlockSpec((rows, tile), lambda i, t: (0, i)),
        ),
        compiler_params=pltpu.CompilerParams(vmem_limit_bytes=VMEM_LIMIT),
        cost_estimate=LIGHT,
    )(table, keep, other, in_hbm(weight), in_hbm(weight))


def heads_products(table, rows, weight, after=()):
    high, columns = rows[0].shape
    inner = weight.shape[0] // 2
    tile = min(inner, 256)
    count = inner // tile
    last = table.shape[0] - 1
    more_args, more_specs = waits(after)

    def kernel(table_ref, first, second, mine, *refs):
        refs[-2][...] = nt(first[...], mine[...]).astype(BF)
        refs[-1][...] = nt(second[...], mine[...]).astype(BF)

    shape = jax.ShapeDtypeStruct((high, inner), BF)
    spec = pl.BlockSpec((high, tile), lambda i, t: (0, i))
    whole = pl.BlockSpec((high, columns), lambda i, t: (0, 0))
    return pl.pallas_call(
        kernel,
        out_shape=[shape, shape],
        grid_spec=pltpu.PrefetchScalarGridSpec(
            num_scalar_prefetch=1,
            grid=(count,),
            in_specs=[
                whole,
                whole,
                pl.BlockSpec((tile, columns), lambda i, t: (t[last] * count + i, 0)),
            ]
            + more_specs,
            out_specs=[spec, spec],
        ),
        compiler_params=pltpu.CompilerParams(vmem_limit_bytes=VMEM_LIMIT),
        cost_estimate=LIGHT,
    )(table, *rows, in_hbm(weight), *more_args)


def normed_products(table, query_grad, key_value_grad, query_weight, key_weight, value_weight, after=()):
    rows, wide = query_grad.shape
    narrow = key_value_grad.shape[1] // 2
    columns = query_weight.shape[0]
    tile = min(columns, 256)
    last = table.shape[0] - 1
    more_args, more_specs = waits(after)

    def kernel(table_ref, queries, others, query, key, value, *refs):
        total = (
            nt(queries[...], query[...])
            + nt(others[:, :narrow], key[...])
            + nt(others[:, narrow:], value[...])
        ).astype(BF)
        refs[-2][...] = total[: rows // 2]
        refs[-1][...] = total[rows // 2 :]

    shape = jax.ShapeDtypeStruct((rows // 2, columns), BF)
    spec = pl.BlockSpec((rows // 2, tile), lambda i, t: (0, i))
    return pl.pallas_call(
        kernel,
        out_shape=[shape, shape],
        grid_spec=pltpu.PrefetchScalarGridSpec(
            num_scalar_prefetch=1,
            grid=(columns // tile,),
            in_specs=[
                pl.BlockSpec((rows, wide), lambda i, t: (0, 0)),
                pl.BlockSpec((rows, 2 * narrow), lambda i, t: (0, 0)),
                pl.BlockSpec((tile, wide), lambda i, t: (i, t[last])),
                pl.BlockSpec((tile, narrow), lambda i, t: (i, t[last])),
                pl.BlockSpec((tile, narrow), lambda i, t: (i, t[last])),
            ]
            + more_specs,
            out_specs=[spec, spec],
        ),
        compiler_params=pltpu.CompilerParams(vmem_limit_bytes=VMEM_LIMIT),
        cost_estimate=cost(HEAVY),
    )(
        table, query_grad, key_value_grad, in_hbm(query_weight), in_hbm(key_weight),
        in_hbm(value_weight), *more_args,
    )


def stacked(ref, start, span, width):
    rows = pl.ds(start, span)
    return jnp.concatenate([ref[rows, :width], ref[rows, width:]], axis=0)


def causal(span, transposed):
    shape = (span, 2 * span) if transposed else (2 * span, span)
    key = lax.broadcasted_iota(jnp.int32, shape, 0 if transposed else 1)
    row = lax.broadcasted_iota(jnp.int32, shape, 1 if transposed else 0)
    return key <= row % span


def side_met(order, table, pair, offset, other):
    last = table.shape[0] - 1
    core = table[last]

    def lower(device):
        return jnp.minimum(order[2 * device], order[2 * device + 1])

    mine = lower(2 * table[0] + (1 - core if pair else core))
    theirs = lower(2 * table[offset % last] + (1 - core if other else core))
    return jnp.where(theirs < mine, 0, 1)


def forward_kernel(places, own, last, span, width, order, table, *refs):
    count = len(places)
    queries, blocks, refs = refs[:2], refs[2 : 2 + count], refs[2 + count :]
    scale = LOG2E / math.sqrt(width)
    if own:
        before, outs = None, refs
    else:
        before, outs = refs[0], refs[1:]
    accum = outs[-1]
    ones = jnp.ones((span, width), BF)

    def weighted(rows, keys, values, allowed=None):
        scores = nt(rows, keys)
        probs = jnp.exp2(scores * scale)
        if allowed is not None:
            probs = jnp.where(allowed, probs, 0.0)
        return nn(probs.astype(BF), values)

    def extended(block, start):
        return jnp.concatenate([block[pl.ds(start, span), width:], ones], axis=1)

    keys = jnp.concatenate([block[:span, :width] for block in blocks], axis=0)
    values = jnp.concatenate([extended(block, 0) for block in blocks], axis=0)
    rows = jnp.concatenate([stacked(query, span, span, width) for query in queries], axis=0)
    high = weighted(rows, keys, values)
    for pair in range(2):
        part = high[pair * 2 * span : (pair + 1) * 2 * span]
        if own:
            allowed = causal(span, False)
            for side in range(2):
                block, start = blocks[pair], side * span
                met = weighted(
                    stacked(queries[pair], start, span, width),
                    block[start : start + span, :width],
                    extended(block, start),
                    allowed,
                )
                accum[0, pair, side] = met + part if side else met
        else:
            accum[0, pair, 0] = before[0, pair, 0]
            accum[0, pair, 1] = before[0, pair, 1] + part
    for i, (offset, other) in enumerate(places):
        for pair in range(2):
            if own and i == pair:
                continue
            side = side_met(order, table, pair, offset, other)
            start = pl.multiple_of(side * span, span)
            accum[0, pair, side] += weighted(
                stacked(queries[pair], start, span, width),
                blocks[i][pl.ds(start, span), :width],
                extended(blocks[i], start),
            )
    if last:
        wides, lows, logs = outs[0:2], outs[2:4], outs[4]
        for pair in range(2):
            for side in range(2):
                rows = slice(side * span, (side + 1) * span)
                whole = accum[0, pair, side]
                mass = whole[:, width:]
                out = whole[:, :width] / mass
                for head in range(2):
                    part = out[head * span : (head + 1) * span]
                    columns = slice(head * width, (head + 1) * width)
                    wides[pair][rows, columns] = part
                    lows[pair][rows, columns] = part.astype(BF)
                logs[0, pair, side] = jnp.log2(mass).T[:8]


def attention_forward(scalars, queries, blocks, places, before, own, last, after=()):
    rows, columns = queries[0].shape
    span, width = rows // 2, HEAD
    groups = columns // (2 * width)
    tile = pl.BlockSpec((rows, 2 * width), lambda g: (0, g))
    accum_block = (1, 2, 2, 2 * span, 2 * width)
    accum_spec = pl.BlockSpec(accum_block, lambda g: (g, 0, 0, 0, 0))
    args = [*scalars, *queries, *(in_hbm(block) for block in blocks)]
    specs = [pl.BlockSpec(memory_space=pltpu.SMEM)] * 2 + [tile] * (2 + len(blocks))
    if not own:
        args.append(before)
        specs.append(accum_spec)
    taken = len(args)
    more_args, more_specs = waits(after)
    scratch = []
    if last:
        wide, low = pltpu.HBM((rows, columns), F32), jax.ShapeDtypeStruct((rows, columns), BF)
        outs = [wide, wide, low, low, jax.ShapeDtypeStruct((groups, 2, 2, 8, 2 * span), F32)]
        out_specs = [tile] * 4 + [pl.BlockSpec((1, 2, 2, 8, 2 * span), lambda g: (g, 0, 0, 0, 0))]
        scratch = [pltpu.VMEM(accum_block, F32)]
    else:
        outs = [jax.ShapeDtypeStruct((groups, *accum_block[1:]), F32)]
        out_specs = [accum_spec]

    def kernel(*refs):
        refs = refs[:taken] + refs[taken + len(more_args) :]
        forward_kernel(places, own, last, span, width, *refs)

    return pl.pallas_call(
        kernel,
        out_shape=outs,
        grid=(groups,),
        in_specs=specs + more_specs,
        out_specs=out_specs,
        scratch_shapes=scratch,
        input_output_aliases={} if own or last else {taken - 1: 0},
        compiler_params=pltpu.CompilerParams(vmem_limit_bytes=VMEM_LIMIT),
        cost_estimate=FORWARD,
    )(*args, *more_args)


def delta_kernel(grads, outs, delta):
    for pair in range(2):
        grad, out = grads[pair], outs[pair]
        width, span = grad.shape[1] // 2, grad.shape[0] // 2
        for side in range(2):
            rows = slice(side * span, (side + 1) * span)
            product = grad[rows, :].astype(F32) * out[rows, :]
            stack = jnp.concatenate([product[:, :width], product[:, width:]], axis=0)
            total = jnp.sum(stack.T, axis=0, keepdims=True)
            delta[0, pair, side] = jnp.broadcast_to(total, (8, 2 * span))


def attention_delta(grads, outs, after=()):
    rows, columns = grads[0].shape
    width, span = HEAD, rows // 2
    groups = columns // (2 * width)
    tile = pl.BlockSpec((rows, 2 * width), lambda g: (0, g))
    more_args, more_specs = waits(after)

    def kernel(*refs):
        delta_kernel(refs[:2], refs[2:4], refs[-1])

    return pl.pallas_call(
        kernel,
        out_shape=jax.ShapeDtypeStruct((groups, 2, 2, 8, 2 * span), F32),
        grid=(groups,),
        in_specs=[tile] * 4 + more_specs,
        out_specs=pl.BlockSpec((1, 2, 2, 8, 2 * span), lambda g: (g, 0, 0, 0, 0)),
        compiler_params=pltpu.CompilerParams(vmem_limit_bytes=VMEM_LIMIT),
        cost_estimate=LIGHT,
    )(*grads, *outs, *more_args)


def backward_kernel(places, own, first, last, split, span, width, order, table, *refs):
    count = len(places)
    queries, grads, (logs, delta), refs = refs[:2], refs[2:4], refs[4:6], refs[6:]
    blocks, refs = refs[:count], refs[count:]
    if not first:
        before, refs = refs[0], refs[1:]
    outs = refs[: count if split else count // 2]
    refs = refs[len(outs) :]
    refs[0][...] = jnp.zeros_like(refs[0])
    refs = refs[1:]
    if last:
        query_outs, accum = refs[:2], refs[2]
    else:
        accum = refs[0]
    scale = LOG2E / math.sqrt(width)
    factor = 1.0 / math.sqrt(width)

    def products(rows, row_grads, log, mean, keys, values, allowed=None):
        probs = jnp.exp2(nt(keys, rows) * scale - log)
        if allowed is not None:
            probs = jnp.where(allowed, probs, 0.0)
        prob_grad = nt(values, row_grads)
        score_grad = (probs * (prob_grad - mean)).astype(BF)
        return nn(score_grad, rows), nn(probs.astype(BF), row_grads), tn(keys, score_grad)

    def of_pair(pair, side, start, keys, values, allowed=None):
        return products(
            stacked(queries[pair], start, span, width),
            stacked(grads[pair], start, span, width),
            logs[0, pair, side, :1],
            delta[0, pair, side, :1],
            keys,
            values,
            allowed,
        )

    low_keys, low_values, high_query = products(
        jnp.concatenate([stacked(query, span, span, width) for query in queries], axis=0),
        jnp.concatenate([stacked(grad, span, span, width) for grad in grads], axis=0),
        jnp.concatenate([logs[0, pair, 1, :1] for pair in range(2)], axis=1),
        jnp.concatenate([delta[0, pair, 1, :1] for pair in range(2)], axis=1),
        jnp.concatenate([block[:span, :width] for block in blocks], axis=0),
        jnp.concatenate([block[:span, width:] for block in blocks], axis=0),
    )
    for pair in range(2):
        part = high_query[:, pair * 2 * span : (pair + 1) * 2 * span]
        if first:
            accum[0, pair, 0] = jnp.zeros_like(part)
            accum[0, pair, 1] = part
        else:
            accum[0, pair, 0] = before[0, pair, 0]
            accum[0, pair, 1] = before[0, pair, 1] + part
    for i, (offset, other) in enumerate(places):
        here = slice(i * span, (i + 1) * span)
        block = blocks[i]
        key_sums, value_sums = [low_keys[here], 0.0], [low_values[here], 0.0]
        for pair in range(2):
            if own and i == pair:
                allowed = causal(span, True)
                for side in range(2):
                    rows = slice(side * span, (side + 1) * span)
                    key_part, value_part, query_part = of_pair(
                        pair, side, side * span, block[rows, :width], block[rows, width:], allowed
                    )
                    accum[0, pair, side] += query_part
                    key_sums[side] = key_sums[side] + key_part
                    value_sums[side] = value_sums[side] + value_part
                continue
            side = side_met(order, table, pair, offset, other)
            start = pl.multiple_of(side * span, span)
            rows = pl.ds(start, span)
            key_part, value_part, query_part = of_pair(
                pair, side, start, block[rows, :width], block[rows, width:]
            )
            accum[0, pair, side] += query_part
            low = side == 0
            key_sums[0] = key_sums[0] + jnp.where(low, key_part, 0.0)
            value_sums[0] = value_sums[0] + jnp.where(low, value_part, 0.0)
            key_sums[1] = key_sums[1] + jnp.where(low, 0.0, key_part)
            value_sums[1] = value_sums[1] + jnp.where(low, 0.0, value_part)
        out = outs[i] if split else outs[i // 2]
        base = 0 if split else i % 2 * 2 * span
        for side in range(2):
            rows = slice(base + side * span, base + (side + 1) * span)
            out[rows, :width] = (key_sums[side] * factor).astype(BF)
            out[rows, width:] = value_sums[side].astype(BF)
    if last:
        for pair in range(2):
            for side in range(2):
                part = accum[0, pair, side].T * factor
                rows = slice(side * span, (side + 1) * span)
                query_outs[pair][rows, :width] = part[:span]
                query_outs[pair][rows, width:] = part[span:]


def attention_backward(
    scalars, queries, grads, logs, delta, blocks, places, before, own, last, split, after=()
):
    rows, columns = queries[0].shape
    span, width = rows // 2, HEAD
    groups = columns // (2 * width)
    count = len(blocks)
    first = before is None
    tile = pl.BlockSpec((rows, 2 * width), lambda g: (0, g))
    stat = pl.BlockSpec((1, 2, 2, 8, 2 * span), lambda g: (g, 0, 0, 0, 0))
    accum_block = (1, 2, 2, width, 2 * span)
    accum_spec = pl.BlockSpec(accum_block, lambda g: (g, 0, 0, 0, 0))
    args = [*scalars, *queries, *grads, logs, delta, *(in_hbm(block) for block in blocks)]
    specs = [pl.BlockSpec(memory_space=pltpu.SMEM)] * 2 + [tile] * 4 + [stat] * 2 + [tile] * count
    if not first:
        args.append(before)
        specs.append(accum_spec)
    taken = len(args)
    more_args, more_specs = waits(after)
    if split:
        outs = [jax.ShapeDtypeStruct((rows, columns), BF)] * count
        out_specs = [tile] * count
    else:
        outs = [jax.ShapeDtypeStruct((2 * rows, columns), BF)] * (count // 2)
        out_specs = [pl.BlockSpec((2 * rows, 2 * width), lambda g: (0, g))] * (count // 2)
    outs.append(TOKEN)
    out_specs.append(pl.BlockSpec((8, 128), lambda g: (0, 0)))
    scratch = []
    if last:
        outs += [jax.ShapeDtypeStruct((rows, columns), F32)] * 2
        out_specs += [tile] * 2
        scratch = [pltpu.VMEM(accum_block, F32)]
    else:
        outs.append(jax.ShapeDtypeStruct((groups, *accum_block[1:]), F32))
        out_specs.append(accum_spec)

    def kernel(*refs):
        refs = refs[:taken] + refs[taken + len(more_args) :]
        backward_kernel(places, own, first, last, split, span, width, *refs)

    return pl.pallas_call(
        kernel,
        out_shape=outs,
        grid=(groups,),
        in_specs=specs + more_specs,
        out_specs=out_specs,
        scratch_shapes=scratch,
        input_output_aliases={} if first or last else {taken - 1: len(outs) - 1},
        compiler_params=pltpu.CompilerParams(vmem_limit_bytes=VMEM_LIMIT),
        cost_estimate=cost(HEAVY),
    )(*args, *more_args)


def body(
    devices,
    residual,
    cotangent,
    span_order,
    positions,
    attn_gain,
    query_weight,
    key_weight,
    value_weight,
    query_gain,
    key_gain,
    out_weight,
    mlp_gain,
    gate_weight,
    up_weight,
    down_weight,
):
    ring = Ring(devices)
    rows, model = residual.shape
    head_dim = query_gain.shape[0]
    span = rows // 2
    index = lax.axis_index("cp")
    scalars = [span_order, ring.table]
    table = [ring.table]
    ordered = lax.dynamic_slice_in_dim(span_order, 2 * index, 2)
    in_order = ordered[0] < ordered[1]

    def canonical(x):
        return jnp.where(in_order, x, jnp.roll(x, span, axis=0))

    residual_other, positions_other = ring.sibling(residual), ring.sibling(positions)
    cotangent = canonical(cotangent)

    half = head_dim // 2
    freq = ROPE_BASE ** (-(jnp.arange(half, dtype=F32) * 2.0) / head_dim)
    angles = []
    for where in (positions, positions_other):
        angle = where.astype(F32)[:, None] * freq[None, :]
        cosine, sine = jnp.cos(angle), jnp.sin(angle)
        angles.append(jnp.concatenate([cosine, cosine], axis=1))
        angles.append(jnp.concatenate([-sine, sine], axis=1))

    query_gain_row = query_gain.reshape(1, -1)
    key_gain_row = key_gain.reshape(1, -1)
    key_columns = key_weight.shape[1]
    query_columns = query_weight.shape[1]
    few, each = key_columns // 2, query_columns // 2

    def project_keys(order, table_ref, first, second, gain, key, value, row, c0, s0, c1, s1, *outs):
        key_value_kernel(
            order, table_ref, (first, second), gain, key, value, row, (c0, s0, c1, s1),
            (outs[0], outs[1:3], outs[3:5], outs[5:7], outs[7:9], outs[9:11]),
        )

    residual, *results = whole_call(
        project_keys,
        scalars,
        [((rows, model), BF, 1)]
        + [((rows, model), BF)] * 2
        + [((rows, few), F32, 1)] * 2
        + [((rows, head_dim), F32)] * 4
        + [((rows, key_columns), BF)] * 2,
        [
            in_hbm(residual), residual_other, in_hbm(attn_gain.reshape(1, -1)),
            (in_hbm(key_weight), (model, few), lambda core: (0, core)),
            (in_hbm(value_weight), (model, few), lambda core: (0, core)),
            in_hbm(key_gain_row), *angles,
        ],
    )
    normeds, keys_raw, cosines, sines, parts = (results[i : i + 2] for i in range(0, 10, 2))

    ways = [(ring.send_up(part), ring.send_down(part)) for part in parts]

    def project_queries(table_ref, n0, n1, weight, gain, c0, c1, s0, s1, *outs):
        query_kernel((n0, n1), weight, gain, (c0, c1), (s0, s1), outs[:2], outs[2:])

    *queries_raw, first, second = whole_call(
        project_queries,
        table,
        [((rows, each), F32, 1)] * 2 + [((rows, each), BF)] * 2,
        [
            *normeds, (in_hbm(query_weight), (model, each), lambda core: (0, core)),
            in_hbm(query_gain_row), *cosines, *sines,
        ],
    )
    queries = [first, second]

    def places_of(offsets):
        return [(offset, other) for offset in offsets for other in (False, True)]

    steps = ring.half
    calls = {0: ([0], parts)}
    state = None
    for step in range(1, steps):
        come = []
        for which in range(2):
            up, down = ways[which]
            if step == 1 and which == 0:
                up, down, queries[0] = tie(up, down, queries[0])
            else:
                up, down, state = tie(up, down, state)
            come.append((up, down))
            if step < steps - 1:
                ways[which] = ring.send_up(up), ring.send_down(down)
            else:
                ways[which] = ring.send_down(down) if which else ring.send_up(up)
            if step == 1 and which == 0:
                (state,) = attention_forward(
                    scalars, queries, parts, places_of([0]), None, True, False, after=come[0]
                )
        blocks = [come[0][0], come[1][0], come[0][1], come[1][1]]
        calls[step] = ([-step, step], blocks)
        (state,) = attention_forward(
            scalars, queries, blocks, places_of([-step, step]), state, False, False
        )
    *ways, state = tie(*ways, state)
    calls[steps] = ([steps], ways)
    *attended, low_keep, low_give, logs = attention_forward(
        scalars, queries, ways, places_of([steps]), state, False, True
    )
    low_other = ring.sibling(low_give)
    mixed_part = out_projection(ring.table, low_keep, low_other, out_weight)
    mixed_part, cotangent = tie(mixed_part, cotangent)
    mixed_other = partner(mixed_part)
    cotangents = [cotangent, ring.sibling(cotangent)]
    hidden_grad = nt(cotangent, down_weight)
    mixed_other, hidden_grad, cotangents = tie(mixed_other, hidden_grad, cotangents)

    residual_wide = residual.astype(F32)
    mixed = residual_wide + both(mixed_part, mixed_other)
    normed_two, scale_two = norm_rows(mixed)
    normed_two_low = (normed_two * mlp_gain).astype(BF)
    gate = nn(normed_two_low, gate_weight)
    upward = nn(normed_two_low, up_weight)
    sigmoid_gate = jax.nn.sigmoid(gate)
    activated = gate * sigmoid_gate
    hidden_low = (activated * upward).astype(BF)
    gate_grad_low = (
        hidden_grad * upward * sigmoid_gate * (1.0 + gate * (1.0 - sigmoid_gate))
    ).astype(BF)
    up_grad_low = (hidden_grad * activated).astype(BF)
    normed_two_part = (nt(gate_grad_low, gate_weight) + nt(up_grad_low, up_weight)).astype(BF)
    normed_two_other = partner(normed_two_part)

    units = gate_weight.shape[1]
    thirds = 2 * units // model
    chips = ring.chips
    gate_rows = model // 2 // chips
    down_rows = units // thirds // 2 // chips
    out_row = thirds * gate_rows
    down_row = out_row + gate_rows
    packed_shape = (down_row + thirds * down_rows, model)

    def shard_of(chip, core):
        return core * chips + chip

    def columns_of(start):
        moves, done = [], 0
        while done < units:
            tile, column = divmod(start + done, model)
            wide = min(model - column, units - done)
            moves.append(
                (
                    (slice(None), slice(done, done + wide)),
                    slice(tile * gate_rows, (tile + 1) * gate_rows),
                    slice(column, column + wide),
                )
            )
            done += wide
        return moves

    everything = slice(None)
    wide = Gradients(
        ring,
        *packed_shape,
        [
            ((model, units), (gate_rows, units), lambda c, k: (shard_of(c, k), 0), columns_of(0)),
            ((model, units), (gate_rows, units), lambda c, k: (shard_of(c, k), 0), columns_of(units)),
            (
                (thirds, units // thirds, model),
                (thirds, down_rows, model),
                lambda c, k: (0, shard_of(c, k), 0),
                [
                    (i, slice(down_row + i * down_rows, down_row + (i + 1) * down_rows), everything)
                    for i in range(thirds)
                ],
            ),
            (
                (2 * each, model),
                (gate_rows, model),
                lambda c, k: (shard_of(c, k), 0),
                [((everything, everything), slice(out_row, out_row + gate_rows), everything)],
            ),
        ],
    )
    both_grad_low = jnp.concatenate([gate_grad_low, up_grad_low], axis=1)
    packed, token = products(
        ring.table, [normed_two_low, ring.sibling(normed_two_low)],
        [both_grad_low, ring.sibling(both_grad_low)], chips, packed_shape, 0, 0, None,
        [normed_two_part],
    )
    packed, token = products(
        ring.table, [hidden_low, ring.sibling(hidden_low)], cotangents, chips, packed_shape,
        down_row, 0, packed, [token], thirds=thirds,
    )
    normed_two_other, token = tie(normed_two_other, token)

    normed_two_grad = both(normed_two_part, normed_two_other)
    mlp_gain_term = jnp.sum(normed_two_grad * normed_two, axis=0)
    mixed_grad = cotangent.astype(F32) + norm_back(
        normed_two_grad * mlp_gain, normed_two, scale_two
    )
    mixed_grad_low = mixed_grad.astype(BF)
    mixed_grads = [mixed_grad_low, ring.sibling(mixed_grad_low)]
    wide.packed, token = products(
        ring.table, [low_keep, low_give], mixed_grads, chips, packed_shape, out_row, 0, packed,
        [token], halved=False,
    )
    wide_steps = wide.scatter()
    wide_way, wide_token = next(wide_steps)
    grads = heads_products(ring.table, mixed_grads, out_weight, [wide_token])
    delta = attention_delta(grads, attended)

    def backward(step, state, after):
        offsets, blocks = calls[step]
        last = step == 0
        return attention_backward(
            scalars, queries, grads, logs, delta, blocks, places_of(offsets), state,
            last, last, last or step == steps, after,
        )

    narrow_rows = model // chips
    narrow_shape = (narrow_rows, each + 2 * few)

    def narrow_out(start, wide):
        return (
            (model, 2 * wide),
            (narrow_rows, wide),
            lambda c, k: (c, k),
            [((everything, everything), everything, slice(start, start + wide))],
        )

    narrow = Gradients(
        ring,
        *narrow_shape,
        [narrow_out(0, each), narrow_out(each, few), narrow_out(each + few, few)],
    )
    up, down, token, state = backward(steps, None, [])
    up, down = ring.send_up(up), ring.send_down(down)
    for step in range(steps - 1, 0, -1):
        wide_way, wide_token = wide_steps.send((wide_way, [token]))
        if step == steps - 1:
            layer_part = matmul(hidden_low, down_weight, [wide_token])
            layer_other = partner(layer_part)
        if step == steps - 2:
            layer_other, wide_token = tie(layer_other, wide_token)
        back, front, token, state = backward(step, state, [wide_token])
        up, down, token = pair_add([front, back], [up, down], step == steps - 1, [token])
        up, down = ring.send_up(up), ring.send_down(down)
    wide_shard, wide_token = wide_steps.send((wide_way, [token]))
    wide_steps = wide.gather(wide_shard)
    wide_way, wide_ready = next(wide_steps)
    *key_value_own, token, first, second = backward(0, state, [wide_token])

    def back_queries(table_ref, g0, g1, r0, r1, gain, c0, c1, s0, s1, *outs):
        query_back_kernel((g0, g1), (r0, r1), gain, (c0, c1), (s0, s1), *outs)

    query_grad_low, query_gain_term = whole_call(
        back_queries,
        table,
        [((2 * rows, each), BF), ((8, head_dim), F32)],
        [first, second, *queries_raw, query_gain_row, *cosines, *sines],
    )
    packed, token = products(
        ring.table, normeds, [query_grad_low], chips, narrow_shape, 0, 0, None, halved=False
    )

    def own_ready(ready):
        return [(offset, part, False) for offset, part in ready]

    def other_ready(ready):
        return [(offset, ring.sibling(part), True) for offset, part in ready]

    wide_come = list(wide_ready)
    up, down, token = tie(up, down, token)

    def back_keys(table_ref, o0, o1, up_ref, down_ref, r0, r1, gain, c0, c1, s0, s1, *outs):
        key_value_back_kernel(
            (o0, o1), up_ref, down_ref, (r0, r1), gain, (c0, c1), (s0, s1), *outs
        )

    key_value_grad, key_gain_term = whole_call(
        back_keys,
        table,
        [((2 * rows, 2 * few), BF), ((8, head_dim), F32)],
        [*key_value_own, up, down, *keys_raw, key_gain_row, *cosines, *sines],
        after=[token],
    )
    narrow.packed, token = products(
        ring.table, normeds, [key_value_grad], chips, narrow_shape, 0, each, packed, halved=False
    )
    narrow_steps = narrow.scatter()
    narrow_way, token = next(narrow_steps)

    wide_way, token = tie(wide_way, token)
    wide_way, next_ready = wide_steps.send(wide_way)
    wide_ready = wide_ready + next_ready
    wide_come += next_ready
    narrow_way, token = narrow_steps.send((narrow_way, [token]))

    normed_own, normed_give = normed_products(
        ring.table, query_grad_low, key_value_grad, query_weight, key_weight, value_weight, [token]
    )
    normed_part = both(normed_own, ring.sibling(normed_give)).astype(BF)
    normed_other = partner(normed_part)
    gains = jnp.stack([jnp.sum(query_gain_term, axis=0), jnp.sum(key_gain_term, axis=0)])
    wide_results = wide.unpack(own_ready(wide_ready), None, [normed_give])

    narrow_way, token = narrow_steps.send((narrow_way, [wide_results[-1]]))
    wide_way, normed_other, token = tie(wide_way, normed_other, token)
    wide_way, wide_ready = wide_steps.send(wide_way)
    wide_come += wide_ready
    gains = gains + partner(gains)
    normed_one, scale_one = norm_rows(residual_wide)
    normed_grad = both(normed_part, normed_other)
    attn_gain_term = jnp.sum(normed_grad * normed_one, axis=0)
    residual_grad = canonical(
        mixed_grad + norm_back(normed_grad * attn_gain, normed_one, scale_one)
    )
    layer_out = canonical(mixed + both(layer_part, layer_other)).astype(BF)
    wide_results = wide.unpack(own_ready(wide_ready), wide_results, [token], HEAVY)

    small = SmallSum(
        devices,
        jnp.concatenate([attn_gain_term, mlp_gain_term, gains[0], gains[1]]).reshape(-1, 128),
    )
    for step in range(steps - 3):
        narrow_way, token = narrow_steps.send((narrow_way, [wide_results[-1]]))
        wide_way, came, token = tie(wide_way, small.under_way, token)
        wide_way, wide_ready = wide_steps.send(wide_way)
        wide_come += wide_ready
        small.came(came)
        wide_results = wide.unpack(own_ready(wide_ready), wide_results, [token], HEAVY)
    narrow_shard, token = narrow_steps.send((narrow_way, [wide_results[-1]]))

    narrow_steps = narrow.gather(narrow_shard)
    narrow_way, narrow_ready = next(narrow_steps)
    wide_way, came, token = tie(wide_way, small.under_way, token)
    small.came(came)
    _, wide_ready = wide_steps.send(wide_way)
    wide_come += wide_ready
    wide_results = wide.unpack(own_ready(wide_ready), wide_results, [token])
    lot, token = stack([part for _, part in wide_come], [wide_results[-1]])
    lot_offsets = [offset for offset, _ in wide_come]
    lot_other = ring.sibling(lot)
    narrow_results = None
    for step in range(1, steps + 1):
        ready = own_ready(narrow_ready) + other_ready(narrow_ready)
        narrow_results = narrow.unpack(ready, narrow_results, [token], HEAVY)
        narrow_way, came, residual_grad, layer_out, token = tie(
            narrow_way, small.under_way, residual_grad, layer_out, narrow_results[-1]
        )
        small.came(came)
        if step < steps:
            narrow_way, narrow_ready = narrow_steps.send(narrow_way)
        if step == steps - 2:
            wide_results = wide.unpack_stack(lot_other, lot_offsets, wide_results, [token])
            token = wide_results[-1]
    while small.under_way:
        small.came(small.under_way)
    _, narrow_ready = narrow_steps.send(narrow_way)
    ready = own_ready(narrow_ready) + other_ready(narrow_ready)
    query_sum, key_sum, value_sum, _ = narrow.unpack(
        ready, narrow_results, [token]
    )
    gate_sum, up_sum, down_sum, out_weight_sum, _ = wide_results
    small = small.total.reshape(-1)

    attn_gain_grad, mlp_gain_grad = small[:model], small[model : 2 * model]
    query_gain_grad = small[2 * model : 2 * model + head_dim]
    key_gain_grad = small[2 * model + head_dim :]
    return (
        layer_out,
        residual_grad,
        attn_gain_grad,
        query_sum,
        key_sum,
        value_sum,
        query_gain_grad,
        key_gain_grad,
        out_weight_sum,
        mlp_gain_grad,
        gate_sum,
        up_sum,
        down_sum.reshape(units, model),
    )


def solution(mesh):
    return jax.shard_map(
        functools.partial(body, mesh.shape["cp"]),
        mesh=mesh,
        in_specs=(
            P("cp", None),
            P("cp", None),
            P(),
            P("cp"),
            P(),
            P(None, "tp"),
            P(None, "tp"),
            P(None, "tp"),
            P(),
            P(),
            P("tp", None),
            P(),
            P(None, "tp"),
            P(None, "tp"),
            P("tp", None),
        ),
        out_specs=(
            P("cp", None),
            P("cp", None),
            P(),
            P(None, "tp"),
            P(None, "tp"),
            P(None, "tp"),
            P(),
            P(),
            P("tp", None),
            P(),
            P(None, "tp"),
            P(None, "tp"),
            P("tp", None),
        ),
        check_vma=False,
    )
```

```python
import functools
import math

import jax
import jax.numpy as jnp
from jax import lax
from jax.experimental import pallas as pl
from jax.experimental.pallas import tpu as pltpu
from jax.sharding import PartitionSpec as P

EPS = 1e-06
ROPE_BASE = 1000000.0
HEAD = 128
LOG2E = 1.4426950408889634
VMEM_LIMIT = 16 * 1024 * 1024


def cost(microseconds):
    return pl.CostEstimate(
        flops=1024 + int(microseconds * 1e9), bytes_accessed=1024, transcendentals=0
    )


LIGHT = cost(0)
FORWARD = cost(1)
HEAVY = 50
SOME = 5
BF = jnp.bfloat16
F32 = jnp.float32
TOKEN = jax.ShapeDtypeStruct((8, 128), jnp.float32)


def nn(a, b):
    return lax.dot_general(a, b, (((1,), (0,)), ((), ())), preferred_element_type=F32)


def nt(a, b):
    return lax.dot_general(a, b, (((1,), (1,)), ((), ())), preferred_element_type=F32)


def tn(a, b):
    return lax.dot_general(a, b, (((0,), (0,)), ((), ())), preferred_element_type=F32)


def norm_rows(values):
    scale_rows = lax.rsqrt(jnp.mean(values * values, axis=-1, keepdims=True) + EPS)
    return (values * scale_rows, scale_rows)


def norm_back(grad_normed, normed, scale_rows):
    return scale_rows * (
        grad_normed - normed * jnp.mean(grad_normed * normed, axis=-1, keepdims=True)
    )


def tie(*values):
    return lax.optimization_barrier(values)


def waits(after):
    return list(after), [pl.BlockSpec(memory_space=pl.ANY)] * len(after)


def in_hbm(x):
    return pltpu.with_memory_space_constraint(x, pltpu.HBM)


def ring_order(chips):
    if chips % 8:
        return list(range(chips))
    rows, cols = 4, chips // 4
    if cols % 2 or cols < 4:
        path = list(range(cols))
    else:
        path = list(range(cols // 2)) + list(range(cols - 1, cols // 2 - 1, -1))
    walk = []
    for row in range(rows):
        across = range(1, cols) if row % 2 == 0 else range(cols - 1, 0, -1)
        walk += [(row, col) for col in across]
    walk = [(0, 0)] + walk + [(row, 0) for row in range(rows - 1, 0, -1)]
    return [row * cols + path[col] for row, col in walk]


class Ring:
    def __init__(self, devices):
        self.devices = devices
        self.chips = devices // 2
        order = ring_order(self.chips)
        self.order = order
        size = self.chips
        self.up = [
            (2 * order[i] + core, 2 * order[(i + 1) % size] + core)
            for i in range(size)
            for core in range(2)
        ]
        self.down = [(b, a) for a, b in self.up]
        self.swap = [(i, i ^ 1) for i in range(devices)]
        place = [0] * size
        for i, chip in enumerate(order):
            place[chip] = i
        index = lax.axis_index("cp")
        self.core = index % 2
        self.here = jnp.asarray(place, jnp.int32)[index // 2]
        self.half = size // 2
        table = [
            [order[(place[chip] + i) % size] for i in range(size)] + [core]
            for chip in range(size)
            for core in range(2)
        ]
        self.table = lax.dynamic_index_in_dim(
            jnp.asarray(table, jnp.int32), index, 0, keepdims=False
        )

    def send_up(self, x):
        return lax.ppermute(x, "cp", self.up)

    def send_down(self, x):
        return lax.ppermute(x, "cp", self.down)

    def sibling(self, x):
        return lax.ppermute(x, "cp", self.swap)


def products(
    table, lefts, rights, chips, packed, row, column, before, after=(), thirds=1, halved=True
):
    tokens = lefts[0].shape[0]
    high = lefts[0].shape[1] // thirds // (2 if halved else 1)
    rows = high // chips
    wide = rights[0].shape[1]
    tile = min(wide, 512)
    last = table.shape[0] - 1
    more_args, more_specs = waits(after)
    if before is not None:
        more_args, more_specs = [before] + more_args, [pl.BlockSpec(memory_space=pl.ANY)] + more_specs
    side = len(lefts)

    def kernel(table_ref, *refs):
        out, token, turned = refs[side + len(rights) + len(more_args) :]

        @pl.when(pl.program_id(1) == 0)
        def _():
            for i in range(side):
                turned[:, i * tokens : (i + 1) * tokens] = refs[i][...].T
            token[...] = jnp.zeros_like(token)

        total, start = 0.0, 0
        for right in refs[side : side + len(rights)]:
            stop = start + right.shape[0]
            total = total + nn(turned[:, start:stop], right[...])
            start = stop
        out[...] = total.reshape(chips, rows, tile).astype(BF)

    def left_place(j, i, t):
        return (0, 2 * j + t[last] if halved else j)

    across = packed[1] // tile

    def out_place(j, i, t):
        at = column // tile + i
        return (0, row // rows + j + at // across, at % across)

    shape = (chips, *packed)
    return pl.pallas_call(
        kernel,
        out_shape=[jax.ShapeDtypeStruct(shape, BF), TOKEN],
        grid_spec=pltpu.PrefetchScalarGridSpec(
            num_scalar_prefetch=1,
            grid=(thirds, wide // tile),
            in_specs=[pl.BlockSpec((tokens, high), left_place)] * side
            + [pl.BlockSpec((right.shape[0], tile), lambda j, i, t: (0, i)) for right in rights]
            + more_specs,
            out_specs=[
                pl.BlockSpec((chips, rows, tile), out_place),
                pl.BlockSpec((8, 128), lambda j, i, t: (0, 0)),
            ],
            scratch_shapes=[pltpu.VMEM((high, side * tokens), BF)],
        ),
        input_output_aliases={} if before is None else {1 + side + len(rights): 0},
        compiler_params=pltpu.CompilerParams(vmem_limit_bytes=VMEM_LIMIT),
        cost_estimate=LIGHT,
    )(table, *lefts, *rights, *more_args)


class Gradients:
    def __init__(self, ring, rows, columns, outs, added=0):
        self.ring, self.rows, self.columns, self.outs = ring, rows, columns, outs
        self.added = added
        self.cut = -(-rows // 32) * 16
        self.packs = []

    def shards(self, offsets, received, halves, after=()):
        ring, columns, rows, cut = self.ring, self.columns, self.rows, self.cut
        spans = [(0, cut), (cut, rows)]
        sides, count = len(offsets), len(self.packs)
        args, specs = [], []
        for offset in offsets:
            for _, pack in self.packs:
                args.append(pack)
                specs.append(
                    pl.BlockSpec(
                        (1, *pack.shape[1:]), lambda i, t, at=offset: (t[at % ring.chips], 0, 0)
                    )
                )
        args += received
        specs += [pl.BlockSpec(x.shape, lambda i, t: (0, 0)) for x in received]
        more_args, more_specs = waits(after)
        taken = len(args) + len(more_args)

        def kernel(table_ref, *refs):
            outs = refs[taken:]
            outs[-1][...] = jnp.zeros_like(outs[-1])
            gained = refs[sides * count : len(args)]
            for side in range(sides):
                for number, (row, pack) in enumerate(self.packs):
                    mine = refs[side * count + number]
                    stop = row + pack.shape[1]
                    if halves == "send":
                        for out, (start, end) in zip(outs, spans):
                            first, last = max(row, start), min(stop, end)
                            if first < last:
                                out[first - start : last - start] = mine[0, first - row : last - row]
                        continue
                    start, end = spans[side] if halves == "add" else (0, rows)
                    for first, last, more in (
                        (row, min(stop, start), False),
                        (max(row, start), min(stop, end), True),
                        (max(row, end), stop, False),
                    ):
                        if first < last:
                            part = mine[0, first - row : last - row]
                            if more:
                                part = part.astype(F32)
                                for got in gained if halves == "sum" else [gained[side]]:
                                    part = part + got[first - start : last - start].astype(F32)
                            outs[side][first:last] = part.astype(BF)

        highs = {"send": [cut, rows - cut], "sum": [rows]}.get(halves, [rows, rows])
        return pl.pallas_call(
            kernel,
            out_shape=[jax.ShapeDtypeStruct((high, columns), BF) for high in highs] + [TOKEN],
            grid_spec=pltpu.PrefetchScalarGridSpec(
                num_scalar_prefetch=1,
                grid=(1,),
                in_specs=specs + more_specs,
                out_specs=[pl.BlockSpec((high, columns), lambda i, t: (0, 0)) for high in highs]
                + [pl.BlockSpec((8, 128), lambda i, t: (0, 0))],
            ),
            compiler_params=pltpu.CompilerParams(vmem_limit_bytes=VMEM_LIMIT),
            cost_estimate=LIGHT,
        )(ring.table, *args, *more_args)

    def scatter(self, after=()):
        ring = self.ring
        up, down, token = self.shards([ring.half], [], "send", after)
        for step in range(ring.half - 1, -1, -1):
            (up, down), after = yield (ring.send_up(up), ring.send_down(down)), token
            if step:
                kind = "add" if step == ring.half - 1 else ""
                up, down, token = self.shards([step, -step], [up, down], kind, after)
        yield self.shards([0], [up, down], "sum", after)

    def gather(self, own, split=False):
        ring, cut = self.ring, self.cut
        up = down = own
        ready = [(0, own)]
        for step in range(1, ring.half):
            up, down = yield (ring.send_up(up), ring.send_down(down)), ready
            ready = [(-step, up), (step, down)]
        high, low = yield (ring.send_up(up[:cut]), ring.send_down(down[cut:])), ready
        if split:
            yield None, [(ring.half, high), (ring.half, low)]
        else:
            yield None, [(ring.half, jnp.concatenate([high, low], axis=0))]

    def unpack_stack(self, stack, offsets, before, after=(), price=0):
        return self.unpack(
            [(offset, stack, True) for offset in offsets], before, after, price, True
        )

    def unpack(self, ready, before, after=(), price=0, stacked=False):
        ring, outs, added = self.ring, self.outs, max(self.added, 8)
        count = len(ready)
        parts = [part if isinstance(part, tuple) else (part, None) for _, part, _ in ready]
        args = []
        for array, _ in parts:
            if not any(array is x for x in args):
                args.append(array)
        which = [next(j for j, x in enumerate(args) if x is array) for array, _ in parts]
        highs = [array.shape[-2] for array, _ in parts]
        places_of = [(offset, other) for offset, _, other in ready]

        def write(part, start, results):
            stop = start + part.shape[0]
            for out, (_, _, _, moves) in zip(results, outs):
                for lead, across, (first, last), columns in moves:
                    low, high = max(first, start), min(last, stop)
                    if low < high:
                        rows = slice(low - first, high - first)
                        where = (rows, across) if lead is None else (lead, rows, across)
                        out[where] = part[low - start : high - start, columns].astype(F32)

        def start_of(i):
            same = [j for j in range(i) if places_of[j] == places_of[i]]
            return sum(highs[j] for j in same)

        starts = [0] * count if stacked else [start_of(i) for i in range(count)]

        def kernel(table_ref, *refs):
            step = pl.program_id(0)

            def part_of(i):
                ref, at = refs[which[i]], parts[i][1]
                return ref if at is None else ref.at[at]

            results = refs[-len(outs) - 2 : -2]
            refs[-1][...] = jnp.zeros_like(refs[-1])
            total = refs[-2]

            @pl.when(step == 0)
            def _():
                total[...] = jnp.zeros_like(total) if before is None else refs[sum_place][...]

            if self.added and stacked:
                total[...] += refs[0][0, self.rows - added :].astype(F32)
            elif self.added:
                for i in range(count):
                    if starts[i] + highs[i] == self.rows:

                        @pl.when(step == i)
                        def _(i=i):
                            total[...] += part_of(i)[highs[i] - added :].astype(F32)

            if stacked:
                write(refs[0].at[0], 0, results)
                return
            for i in range(count):
                pl.when(step == i)(functools.partial(write, part_of(i), starts[i], results))

        def place(of_chip, i, table):
            chip, core = None, None
            for j, (offset, other) in enumerate(places_of):
                here = table[offset % ring.chips]
                mine = table[ring.chips]
                mine = 1 - mine if other else mine
                chip = here if chip is None else jnp.where(i == j, here, chip)
                core = mine if core is None else jnp.where(i == j, mine, core)
            return of_chip(chip, core)

        shapes, out_specs = [], []
        for shape, block, of_chip, _ in outs:
            shapes.append(pltpu.HBM(shape, F32))
            out_specs.append(pl.BlockSpec(block, functools.partial(place, of_chip)))
        shapes += [jax.ShapeDtypeStruct((added, self.columns), F32), TOKEN]
        out_specs.append(pl.BlockSpec((added, self.columns), lambda i, t: (0, 0)))
        out_specs.append(pl.BlockSpec((8, 128), lambda i, t: (0, 0)))
        if stacked:
            specs = [pl.BlockSpec((1, self.rows, self.columns), lambda i, t: (i, 0, 0))]
        else:
            specs = [pl.BlockSpec(x.shape, lambda i, t, n=x.ndim: (0,) * n) for x in args]
        aliases = {}
        if before is not None:
            aliases = {1 + len(args) + i: i for i in range(len(outs))}
            specs += [pl.BlockSpec(memory_space=pl.ANY)] * len(outs)
            args += [in_hbm(x) for x in before[: len(outs)]]
            sum_place = len(args)
            args.append(before[len(outs)])
            specs.append(pl.BlockSpec((added, self.columns), lambda i, t: (0, 0)))
        more_args, more_specs = waits(after)
        args += more_args
        specs += more_specs
        return list(
            pl.pallas_call(
                kernel,
                out_shape=shapes,
                grid_spec=pltpu.PrefetchScalarGridSpec(
                    num_scalar_prefetch=1, grid=(count,), in_specs=specs, out_specs=out_specs
                ),
                input_output_aliases=aliases,
                compiler_params=pltpu.CompilerParams(vmem_limit_bytes=VMEM_LIMIT),
                cost_estimate=cost(price),
            )(ring.table, *args)
        )


def stack(parts, after=(), price=0):
    rows, columns = parts[0].shape
    count = len(parts)
    more_args, more_specs = waits(after)

    def kernel(*refs):
        out, token = refs[-2:]
        token[...] = jnp.zeros_like(token)
        for i in range(count):

            @pl.when(pl.program_id(0) == i)
            def _(i=i):
                out[0] = refs[i][...]

    return pl.pallas_call(
        kernel,
        out_shape=[jax.ShapeDtypeStruct((count, rows, columns), parts[0].dtype), TOKEN],
        grid=(count,),
        in_specs=[pl.BlockSpec((rows, columns), lambda i: (0, 0))] * count + more_specs,
        out_specs=[
            pl.BlockSpec((1, rows, columns), lambda i: (i, 0, 0)),
            pl.BlockSpec((8, 128), lambda i: (0, 0)),
        ],
        compiler_params=pltpu.CompilerParams(vmem_limit_bytes=VMEM_LIMIT),
        cost_estimate=cost(price),
    )(*parts, *more_args)


def pair_add(own, received, half, after=()):
    more_args, more_specs = waits(after)

    def kernel(*refs):
        refs, outs = refs[:4], refs[4 + len(more_args) :]
        outs[-1][...] = jnp.zeros_like(outs[-1])
        for side in range(2):
            mine, got, out = refs[side], refs[2 + side], outs[side]
            if half:
                rows = got.shape[0]
                here = slice(side * rows, (side + 1) * rows)
                rest = slice((1 - side) * rows, (2 - side) * rows)
                out[here] = (mine[here].astype(F32) + got[...].astype(F32)).astype(BF)
                out[rest] = mine[rest]
            else:
                out[...] = (mine[...].astype(F32) + got[...].astype(F32)).astype(BF)

    shape = jax.ShapeDtypeStruct(own[0].shape, BF)
    return pl.pallas_call(
        kernel,
        out_shape=[shape, shape, TOKEN],
        in_specs=[pl.BlockSpec(memory_space=pltpu.VMEM)] * 4 + more_specs,
        compiler_params=pltpu.CompilerParams(vmem_limit_bytes=VMEM_LIMIT),
        cost_estimate=LIGHT,
    )(*own, *received, *more_args)


def partner(x):
    return lax.ppermute(x, "tp", [(0, 1), (1, 0)])


def both(mine, other):
    return mine.astype(F32) + other.astype(F32)


def turn(values, cosine, sine):
    return values * cosine + pltpu.roll(values, values.shape[-1] // 2, 1) * sine


def turn_back(values, cosine, sine):
    return values * cosine - pltpu.roll(values, values.shape[-1] // 2, 1) * sine


def lower_first(order, table, other):
    core = table[table.shape[0] - 1]
    device = 2 * table[0] + (1 - core if other else core)
    return order[2 * device] < order[2 * device + 1]


def key_value_kernel(
    order, table, residuals, cotangent, gain, key_weight, value_weight, key_gain, angles, outs
):
    residual_out, cotangent_out, normed_outs, raw_outs, cosine_outs, sine_outs, packed_outs = outs
    width = key_gain.shape[1]
    span = residuals[0].shape[0] // 2
    for pair in range(2):
        start = jnp.where(lower_first(order, table, pair == 1), 0, span)

        def canonical(ref):
            return jnp.concatenate(
                [
                    ref[pl.ds(pl.multiple_of(start, span), span)],
                    ref[pl.ds(pl.multiple_of(span - start, span), span)],
                ],
                axis=0,
            )

        rows = canonical(residuals[pair])
        if pair == 0:
            residual_out[...] = rows
            cotangent_out[...] = canonical(cotangent)
        unit, _ = norm_rows(rows.astype(F32))
        normed = (unit * gain[...]).astype(BF)
        normed_outs[pair][...] = normed
        cosine, sine = canonical(angles[2 * pair]), canonical(angles[2 * pair + 1])
        cosine_outs[pair][...], sine_outs[pair][...] = cosine, sine
        raw = nn(normed, key_weight[...])
        raw_outs[pair][...] = raw
        values = nn(normed, value_weight[...]).astype(BF)
        for group in range(raw.shape[1] // width):
            here = slice(group * width, (group + 1) * width)
            key_unit, _ = norm_rows(raw[:, here])
            packed = packed_outs[pair]
            packed[:, 2 * group * width : (2 * group + 1) * width] = turn(
                key_unit * key_gain[...], cosine, sine
            ).astype(BF)
            packed[:, (2 * group + 1) * width : (2 * group + 2) * width] = values[:, here]


def query_kernel(normeds, weight, gain, cosines, sines, raw_outs, low_outs):
    width = gain.shape[1]
    for pair in range(2):
        raw = nn(normeds[pair][...], weight[...])
        raw_outs[pair][...] = raw
        for head in range(raw.shape[1] // width):
            here = slice(head * width, (head + 1) * width)
            unit, _ = norm_rows(raw[:, here])
            low_outs[pair][:, here] = turn(
                unit * gain[...], cosines[pair][...], sines[pair][...]
            ).astype(BF)


def heads_back(grad_of, raws, gain, cosines, sines, out, total):
    width = gain.shape[1]
    rows = raws[0].shape[0]
    for pair in range(2):
        here_rows = slice(pair * rows, (pair + 1) * rows)
        for head in range(raws[pair].shape[1] // width):
            here = slice(head * width, (head + 1) * width)
            unit, scale_rows = norm_rows(raws[pair][:, here])
            turned = turn_back(grad_of(pair, head), cosines[pair][...], sines[pair][...])
            total = total + jnp.sum((turned * unit).reshape(-1, 8, width), axis=0)
            out[here_rows, here] = norm_back(turned * gain[...], unit, scale_rows).astype(BF)
    return total


def query_back_kernel(grads, raws, gain, cosines, sines, low_out, gain_out):
    width = gain.shape[1]
    gain_out[...] = heads_back(
        lambda pair, head: grads[pair][:, head * width : (head + 1) * width],
        raws, gain, cosines, sines, low_out, jnp.zeros((8, width), F32),
    )


def key_value_back_kernel(owns, upward, downward, raws, gain, cosines, sines, low_out, gain_out):
    width = gain.shape[1]
    rows, columns = raws[0].shape
    groups = columns // width

    def summed(pair, place):
        here = slice(place * width, (place + 1) * width)
        at = slice(pair * rows, (pair + 1) * rows)
        return (
            owns[pair][:, here].astype(F32)
            + upward[at, here].astype(F32)
            + downward[at, here].astype(F32)
        )

    gain_out[...] = heads_back(
        lambda pair, head: summed(pair, 2 * head),
        raws, gain, cosines, sines, low_out, jnp.zeros((8, width), F32),
    )
    for pair in range(2):
        for group in range(groups):
            low_out[
                pair * rows : (pair + 1) * rows,
                columns + group * width : columns + (group + 1) * width,
            ] = summed(pair, 2 * group + 1).astype(BF)


def whole_call(kernel, scalars, outs, args, after=()):
    more_args, more_specs = waits(after)
    count = len(scalars)
    arrays, specs = [], []
    for arg in args:
        array, block, place = arg if isinstance(arg, tuple) else (arg, arg.shape, None)
        arrays.append(array)
        if place is None:
            specs.append(pl.BlockSpec(block, lambda i, *t: (0, 0)))
        else:
            specs.append(
                pl.BlockSpec(
                    block, lambda i, *t, place=place: place(t[-1][t[-1].shape[0] - 1])
                )
            )
    taken = count + len(args)

    def run(*refs):
        kernel(*refs[:taken], *refs[taken + len(more_args) :])

    return list(
        pl.pallas_call(
            run,
            out_shape=[
                pltpu.HBM(shape, dtype) if far else jax.ShapeDtypeStruct(shape, dtype)
                for shape, dtype, *far in outs
            ],
            grid_spec=pltpu.PrefetchScalarGridSpec(
                num_scalar_prefetch=count,
                grid=(1,),
                in_specs=specs + more_specs,
                out_specs=[pl.BlockSpec(shape, lambda i, *t: (0, 0)) for shape, *_ in outs],
            ),
            compiler_params=pltpu.CompilerParams(vmem_limit_bytes=VMEM_LIMIT),
            cost_estimate=LIGHT,
        )(*scalars, *arrays, *more_args)
    )


def matmul(left, right, after=()):
    rows, inner = left.shape
    columns = right.shape[1]
    tile = min(columns, 512)
    more_args, more_specs = waits(after)

    def kernel(left_ref, right_ref, *refs):
        refs[-1][...] = nn(left_ref[...], right_ref[...]).astype(BF)

    return pl.pallas_call(
        kernel,
        out_shape=jax.ShapeDtypeStruct((rows, columns), BF),
        grid=(columns // tile,),
        in_specs=[
            pl.BlockSpec((rows, inner), lambda i: (0, 0)),
            pl.BlockSpec((inner, tile), lambda i: (0, i)),
        ]
        + more_specs,
        out_specs=pl.BlockSpec((rows, tile), lambda i: (0, i)),
        compiler_params=pltpu.CompilerParams(vmem_limit_bytes=VMEM_LIMIT),
        cost_estimate=LIGHT,
    )(left, in_hbm(right), *more_args)


def out_projection(table, rows, weight, other, before=None):
    high, inner = rows.shape
    columns = weight.shape[1]
    tile = min(inner, 256)
    count = inner // tile
    last = table.shape[0] - 1
    dtype = F32 if before is None else BF

    def kernel(table_ref, rows_ref, weight_ref, *refs):
        out, total = refs[-2:]
        step = pl.program_id(0)
        part = nn(rows_ref[...], weight_ref[...])

        @pl.when(step == 0)
        def _():
            total[...] = part if before is None else part + refs[0][...]

        @pl.when(step > 0)
        def _():
            total[...] += part

        @pl.when(step == count - 1)
        def _():
            out[...] = total[...].astype(dtype)

    whole = pl.BlockSpec((high, columns), lambda i, t: (0, 0))
    extra = [] if before is None else [before]
    return pl.pallas_call(
        kernel,
        out_shape=jax.ShapeDtypeStruct((high, columns), dtype),
        grid_spec=pltpu.PrefetchScalarGridSpec(
            num_scalar_prefetch=1,
            grid=(count,),
            in_specs=[
                pl.BlockSpec((high, tile), lambda i, t: (0, i)),
                pl.BlockSpec(
                    (tile, columns),
                    lambda i, t: ((1 - t[last] if other else t[last]) * count + i, 0),
                ),
            ]
            + [whole] * len(extra),
            out_specs=whole,
            scratch_shapes=[pltpu.VMEM((high, columns), F32)],
        ),
        compiler_params=pltpu.CompilerParams(vmem_limit_bytes=VMEM_LIMIT),
        cost_estimate=LIGHT,
    )(table, rows, weight, *extra)


def heads_products(table, rows, weight, after=()):
    high, columns = rows[0].shape
    inner = weight.shape[0] // 2
    tile = min(inner, 256)
    count = inner // tile
    last = table.shape[0] - 1
    more_args, more_specs = waits(after)

    def kernel(table_ref, first, second, mine, *refs):
        refs[-2][...] = nt(first[...], mine[...]).astype(BF)
        refs[-1][...] = nt(second[...], mine[...]).astype(BF)

    shape = jax.ShapeDtypeStruct((high, inner), BF)
    spec = pl.BlockSpec((high, tile), lambda i, t: (0, i))
    whole = pl.BlockSpec((high, columns), lambda i, t: (0, 0))
    return pl.pallas_call(
        kernel,
        out_shape=[shape, shape],
        grid_spec=pltpu.PrefetchScalarGridSpec(
            num_scalar_prefetch=1,
            grid=(count,),
            in_specs=[
                whole,
                whole,
                pl.BlockSpec((tile, columns), lambda i, t: (t[last] * count + i, 0)),
            ]
            + more_specs,
            out_specs=[spec, spec],
        ),
        compiler_params=pltpu.CompilerParams(vmem_limit_bytes=VMEM_LIMIT),
        cost_estimate=LIGHT,
    )(table, *rows, in_hbm(weight), *more_args)


def normed_products(table, query_grad, key_value_grad, query_weight, key_weight, value_weight, after=()):
    rows, wide = query_grad.shape
    narrow = key_value_grad.shape[1] // 2
    columns = query_weight.shape[0]
    tile = min(columns, 256)
    last = table.shape[0] - 1
    more_args, more_specs = waits(after)

    def kernel(table_ref, queries, others, query, key, value, *refs):
        total = (
            nt(queries[...], query[...])
            + nt(others[:, :narrow], key[...])
            + nt(others[:, narrow:], value[...])
        ).astype(BF)
        refs[-2][...] = total[: rows // 2]
        refs[-1][...] = total[rows // 2 :]

    shape = jax.ShapeDtypeStruct((rows // 2, columns), BF)
    spec = pl.BlockSpec((rows // 2, tile), lambda i, t: (0, i))
    return pl.pallas_call(
        kernel,
        out_shape=[shape, shape],
        grid_spec=pltpu.PrefetchScalarGridSpec(
            num_scalar_prefetch=1,
            grid=(columns // tile,),
            in_specs=[
                pl.BlockSpec((rows, wide), lambda i, t: (0, 0)),
                pl.BlockSpec((rows, 2 * narrow), lambda i, t: (0, 0)),
                pl.BlockSpec((tile, wide), lambda i, t: (i, t[last])),
                pl.BlockSpec((tile, narrow), lambda i, t: (i, t[last])),
                pl.BlockSpec((tile, narrow), lambda i, t: (i, t[last])),
            ]
            + more_specs,
            out_specs=[spec, spec],
        ),
        compiler_params=pltpu.CompilerParams(vmem_limit_bytes=VMEM_LIMIT),
        cost_estimate=cost(HEAVY),
    )(
        table, query_grad, key_value_grad, in_hbm(query_weight), in_hbm(key_weight),
        in_hbm(value_weight), *more_args,
    )


def stacked(ref, start, span, width):
    rows = pl.ds(start, span)
    return jnp.concatenate([ref[rows, :width], ref[rows, width:]], axis=0)


def causal(span, transposed):
    shape = (span, 2 * span) if transposed else (2 * span, span)
    key = lax.broadcasted_iota(jnp.int32, shape, 0 if transposed else 1)
    row = lax.broadcasted_iota(jnp.int32, shape, 1 if transposed else 0)
    return key <= row % span


def side_met(order, table, pair, offset, other):
    last = table.shape[0] - 1
    core = table[last]

    def lower(device):
        return jnp.minimum(order[2 * device], order[2 * device + 1])

    mine = lower(2 * table[0] + (1 - core if pair else core))
    theirs = lower(2 * table[offset % last] + (1 - core if other else core))
    return jnp.where(theirs < mine, 0, 1)


def forward_kernel(places, own, last, span, width, order, table, *refs):
    count = len(places)
    queries, blocks, refs = refs[:2], refs[2 : 2 + count], refs[2 + count :]
    scale = LOG2E / math.sqrt(width)
    if own:
        before, outs = None, refs
    else:
        before, outs = refs[0], refs[1:]
    accum = outs[-1]
    ones = jnp.ones((span, width), BF)

    def weighted(rows, keys, values, allowed=None):
        scores = nt(rows, keys)
        probs = jnp.exp2(scores * scale)
        if allowed is not None:
            probs = jnp.where(allowed, probs, 0.0)
        return nn(probs.astype(BF), values)

    def extended(block, start):
        return jnp.concatenate([block[pl.ds(start, span), width:], ones], axis=1)

    keys = jnp.concatenate([block[:span, :width] for block in blocks], axis=0)
    values = jnp.concatenate([extended(block, 0) for block in blocks], axis=0)
    rows = jnp.concatenate([stacked(query, span, span, width) for query in queries], axis=0)
    high = weighted(rows, keys, values)
    for pair in range(2):
        part = high[pair * 2 * span : (pair + 1) * 2 * span]
        if own:
            allowed = causal(span, False)
            for side in range(2):
                block, start = blocks[pair], side * span
                met = weighted(
                    stacked(queries[pair], start, span, width),
                    block[start : start + span, :width],
                    extended(block, start),
                    allowed,
                )
                accum[0, pair, side] = met + part if side else met
        else:
            accum[0, pair, 0] = before[0, pair, 0]
            accum[0, pair, 1] = before[0, pair, 1] + part
    for i, (offset, other) in enumerate(places):
        for pair in range(2):
            if own and i == pair:
                continue
            side = side_met(order, table, pair, offset, other)
            start = pl.multiple_of(side * span, span)
            accum[0, pair, side] += weighted(
                stacked(queries[pair], start, span, width),
                blocks[i][pl.ds(start, span), :width],
                extended(blocks[i], start),
            )
    if last:
        wides, lows, logs = outs[0:2], outs[2:4], outs[4]
        for pair in range(2):
            for side in range(2):
                rows = slice(side * span, (side + 1) * span)
                whole = accum[0, pair, side]
                mass = whole[:, width:]
                out = whole[:, :width] / mass
                for head in range(2):
                    part = out[head * span : (head + 1) * span]
                    columns = slice(head * width, (head + 1) * width)
                    wides[pair][rows, columns] = part
                    lows[pair][rows, columns] = part.astype(BF)
                logs[0, pair, side] = jnp.log2(mass).T[:8]


def attention_forward(scalars, queries, blocks, places, before, own, last, after=()):
    rows, columns = queries[0].shape
    span, width = rows // 2, HEAD
    groups = columns // (2 * width)
    tile = pl.BlockSpec((rows, 2 * width), lambda g: (0, g))
    accum_block = (1, 2, 2, 2 * span, 2 * width)
    accum_spec = pl.BlockSpec(accum_block, lambda g: (g, 0, 0, 0, 0))
    args = [*scalars, *queries, *(in_hbm(block) for block in blocks)]
    specs = [pl.BlockSpec(memory_space=pltpu.SMEM)] * 2 + [tile] * (2 + len(blocks))
    if not own:
        args.append(before)
        specs.append(accum_spec)
    taken = len(args)
    more_args, more_specs = waits(after)
    scratch = []
    if last:
        wide, low = pltpu.HBM((rows, columns), F32), jax.ShapeDtypeStruct((rows, columns), BF)
        outs = [wide, wide, low, low, jax.ShapeDtypeStruct((groups, 2, 2, 8, 2 * span), F32), TOKEN]
        out_specs = [tile] * 4 + [
            pl.BlockSpec((1, 2, 2, 8, 2 * span), lambda g: (g, 0, 0, 0, 0)),
            pl.BlockSpec((8, 128), lambda g: (0, 0)),
        ]
        scratch = [pltpu.VMEM(accum_block, F32)]
    else:
        outs = [jax.ShapeDtypeStruct((groups, *accum_block[1:]), F32), TOKEN]
        out_specs = [accum_spec, pl.BlockSpec((8, 128), lambda g: (0, 0))]

    def kernel(*refs):
        refs = refs[:taken] + refs[taken + len(more_args) :]
        place = -2 if last else -1
        refs[place][...] = jnp.zeros_like(refs[place])
        refs = refs[:place] + (refs[-1:] if last else ())
        forward_kernel(places, own, last, span, width, *refs)

    return pl.pallas_call(
        kernel,
        out_shape=outs,
        grid=(groups,),
        in_specs=specs + more_specs,
        out_specs=out_specs,
        scratch_shapes=scratch,
        input_output_aliases={} if own or last else {taken - 1: 0},
        compiler_params=pltpu.CompilerParams(vmem_limit_bytes=VMEM_LIMIT),
        cost_estimate=FORWARD,
    )(*args, *more_args)


def delta_kernel(grads, outs, delta):
    for pair in range(2):
        grad, out = grads[pair], outs[pair]
        width, span = grad.shape[1] // 2, grad.shape[0] // 2
        for side in range(2):
            rows = slice(side * span, (side + 1) * span)
            product = grad[rows, :].astype(F32) * out[rows, :]
            stack = jnp.concatenate([product[:, :width], product[:, width:]], axis=0)
            total = jnp.sum(stack.T, axis=0, keepdims=True)
            delta[0, pair, side] = jnp.broadcast_to(total, (8, 2 * span))


def attention_delta(grads, outs, after=()):
    rows, columns = grads[0].shape
    width, span = HEAD, rows // 2
    groups = columns // (2 * width)
    tile = pl.BlockSpec((rows, 2 * width), lambda g: (0, g))
    more_args, more_specs = waits(after)

    def kernel(*refs):
        delta_kernel(refs[:2], refs[2:4], refs[-1])

    return pl.pallas_call(
        kernel,
        out_shape=jax.ShapeDtypeStruct((groups, 2, 2, 8, 2 * span), F32),
        grid=(groups,),
        in_specs=[tile] * 4 + more_specs,
        out_specs=pl.BlockSpec((1, 2, 2, 8, 2 * span), lambda g: (g, 0, 0, 0, 0)),
        compiler_params=pltpu.CompilerParams(vmem_limit_bytes=VMEM_LIMIT),
        cost_estimate=LIGHT,
    )(*grads, *outs, *more_args)


def backward_kernel(places, own, first, last, split, span, width, order, table, *refs):
    count = len(places)
    queries, grads, (logs, delta), refs = refs[:2], refs[2:4], refs[4:6], refs[6:]
    blocks, refs = refs[:count], refs[count:]
    if not first:
        before, refs = refs[0], refs[1:]
    outs = refs[: count if split else count // 2]
    refs = refs[len(outs) :]
    refs[0][...] = jnp.zeros_like(refs[0])
    refs = refs[1:]
    if last:
        query_outs, accum = refs[:2], refs[2]
    else:
        accum = refs[0]
    scale = LOG2E / math.sqrt(width)
    factor = 1.0 / math.sqrt(width)

    def products(rows, row_grads, log, mean, keys, values, allowed=None):
        probs = jnp.exp2(nt(keys, rows) * scale - log)
        if allowed is not None:
            probs = jnp.where(allowed, probs, 0.0)
        prob_grad = nt(values, row_grads)
        score_grad = (probs * (prob_grad - mean)).astype(BF)
        return nn(score_grad, rows), nn(probs.astype(BF), row_grads), tn(keys, score_grad)

    def of_pair(pair, side, start, keys, values, allowed=None):
        return products(
            stacked(queries[pair], start, span, width),
            stacked(grads[pair], start, span, width),
            logs[0, pair, side, :1],
            delta[0, pair, side, :1],
            keys,
            values,
            allowed,
        )

    low_keys, low_values, high_query = products(
        jnp.concatenate([stacked(query, span, span, width) for query in queries], axis=0),
        jnp.concatenate([stacked(grad, span, span, width) for grad in grads], axis=0),
        jnp.concatenate([logs[0, pair, 1, :1] for pair in range(2)], axis=1),
        jnp.concatenate([delta[0, pair, 1, :1] for pair in range(2)], axis=1),
        jnp.concatenate([block[:span, :width] for block in blocks], axis=0),
        jnp.concatenate([block[:span, width:] for block in blocks], axis=0),
    )
    for pair in range(2):
        part = high_query[:, pair * 2 * span : (pair + 1) * 2 * span]
        if first:
            accum[0, pair, 0] = jnp.zeros_like(part)
            accum[0, pair, 1] = part
        else:
            accum[0, pair, 0] = before[0, pair, 0]
            accum[0, pair, 1] = before[0, pair, 1] + part
    for i, (offset, other) in enumerate(places):
        here = slice(i * span, (i + 1) * span)
        block = blocks[i]
        key_sums, value_sums = [low_keys[here], 0.0], [low_values[here], 0.0]
        for pair in range(2):
            if own and i == pair:
                allowed = causal(span, True)
                for side in range(2):
                    rows = slice(side * span, (side + 1) * span)
                    key_part, value_part, query_part = of_pair(
                        pair, side, side * span, block[rows, :width], block[rows, width:], allowed
                    )
                    accum[0, pair, side] += query_part
                    key_sums[side] = key_sums[side] + key_part
                    value_sums[side] = value_sums[side] + value_part
                continue
            side = side_met(order, table, pair, offset, other)
            start = pl.multiple_of(side * span, span)
            rows = pl.ds(start, span)
            key_part, value_part, query_part = of_pair(
                pair, side, start, block[rows, :width], block[rows, width:]
            )
            accum[0, pair, side] += query_part
            low = side == 0
            key_sums[0] = key_sums[0] + jnp.where(low, key_part, 0.0)
            value_sums[0] = value_sums[0] + jnp.where(low, value_part, 0.0)
            key_sums[1] = key_sums[1] + jnp.where(low, 0.0, key_part)
            value_sums[1] = value_sums[1] + jnp.where(low, 0.0, value_part)
        out = outs[i] if split else outs[i // 2]
        base = 0 if split else i % 2 * 2 * span
        for side in range(2):
            rows = slice(base + side * span, base + (side + 1) * span)
            out[rows, :width] = (key_sums[side] * factor).astype(BF)
            out[rows, width:] = value_sums[side].astype(BF)
    if last:
        for pair in range(2):
            for side in range(2):
                part = accum[0, pair, side].T * factor
                rows = slice(side * span, (side + 1) * span)
                query_outs[pair][rows, :width] = part[:span]
                query_outs[pair][rows, width:] = part[span:]


def attention_backward(
    scalars, queries, grads, logs, delta, blocks, places, before, own, last, split, after=()
):
    rows, columns = queries[0].shape
    span, width = rows // 2, HEAD
    groups = columns // (2 * width)
    count = len(blocks)
    first = before is None
    tile = pl.BlockSpec((rows, 2 * width), lambda g: (0, g))
    stat = pl.BlockSpec((1, 2, 2, 8, 2 * span), lambda g: (g, 0, 0, 0, 0))
    accum_block = (1, 2, 2, width, 2 * span)
    accum_spec = pl.BlockSpec(accum_block, lambda g: (g, 0, 0, 0, 0))
    args = [*scalars, *queries, *grads, logs, delta, *(in_hbm(block) for block in blocks)]
    specs = [pl.BlockSpec(memory_space=pltpu.SMEM)] * 2 + [tile] * 4 + [stat] * 2 + [tile] * count
    if not first:
        args.append(before)
        specs.append(accum_spec)
    taken = len(args)
    more_args, more_specs = waits(after)
    if split:
        outs = [jax.ShapeDtypeStruct((rows, columns), BF)] * count
        out_specs = [tile] * count
    else:
        outs = [jax.ShapeDtypeStruct((2 * rows, columns), BF)] * (count // 2)
        out_specs = [pl.BlockSpec((2 * rows, 2 * width), lambda g: (0, g))] * (count // 2)
    outs.append(TOKEN)
    out_specs.append(pl.BlockSpec((8, 128), lambda g: (0, 0)))
    scratch = []
    if last:
        outs += [jax.ShapeDtypeStruct((rows, columns), F32)] * 2
        out_specs += [tile] * 2
        scratch = [pltpu.VMEM(accum_block, F32)]
    else:
        outs.append(jax.ShapeDtypeStruct((groups, *accum_block[1:]), F32))
        out_specs.append(accum_spec)

    def kernel(*refs):
        refs = refs[:taken] + refs[taken + len(more_args) :]
        backward_kernel(places, own, first, last, split, span, width, *refs)

    return pl.pallas_call(
        kernel,
        out_shape=outs,
        grid=(groups,),
        in_specs=specs + more_specs,
        out_specs=out_specs,
        scratch_shapes=scratch,
        input_output_aliases={} if first or last else {taken - 1: len(outs) - 1},
        compiler_params=pltpu.CompilerParams(vmem_limit_bytes=VMEM_LIMIT),
        cost_estimate=cost(HEAVY),
    )(*args, *more_args)


def body(
    devices,
    residual,
    cotangent,
    span_order,
    positions,
    attn_gain,
    query_weight,
    key_weight,
    value_weight,
    query_gain,
    key_gain,
    out_weight,
    mlp_gain,
    gate_weight,
    up_weight,
    down_weight,
):
    ring = Ring(devices)
    rows, model = residual.shape
    head_dim = query_gain.shape[0]
    span = rows // 2
    index = lax.axis_index("cp")
    scalars = [span_order, ring.table]
    table = [ring.table]
    ordered = lax.dynamic_slice_in_dim(span_order, 2 * index, 2)
    in_order = ordered[0] < ordered[1]

    def canonical(x):
        return jnp.where(in_order, x, jnp.roll(x, span, axis=0))

    residual_other, positions_other = ring.sibling(residual), ring.sibling(positions)

    half = head_dim // 2
    freq = ROPE_BASE ** (-(jnp.arange(half, dtype=F32) * 2.0) / head_dim)
    angles = []
    for where in (positions, positions_other):
        angle = where.astype(F32)[:, None] * freq[None, :]
        cosine, sine = jnp.cos(angle), jnp.sin(angle)
        angles.append(jnp.concatenate([cosine, cosine], axis=1))
        angles.append(jnp.concatenate([-sine, sine], axis=1))

    query_gain_row = query_gain.reshape(1, -1)
    key_gain_row = key_gain.reshape(1, -1)
    key_columns = key_weight.shape[1]
    query_columns = query_weight.shape[1]
    few, each = key_columns // 2, query_columns // 2

    def project_keys(order, table_ref, first, second, grad, gain, key, value, row, c0, s0, c1, s1, *outs):
        key_value_kernel(
            order, table_ref, (first, second), grad, gain, key, value, row, (c0, s0, c1, s1),
            (outs[0], outs[1], outs[2:4], outs[4:6], outs[6:8], outs[8:10], outs[10:12]),
        )

    residual, cotangent, *results = whole_call(
        project_keys,
        scalars,
        [((rows, model), BF, 1)] * 2
        + [((rows, model), BF)] * 2
        + [((rows, few), F32, 1)] * 2
        + [((rows, head_dim), F32)] * 4
        + [((rows, key_columns), BF)] * 2,
        [
            in_hbm(residual), residual_other, in_hbm(cotangent), in_hbm(attn_gain.reshape(1, -1)),
            (in_hbm(key_weight), (model, few), lambda core: (0, core)),
            (in_hbm(value_weight), (model, few), lambda core: (0, core)),
            in_hbm(key_gain_row), *angles,
        ],
    )
    normeds, keys_raw, cosines, sines, parts = (results[i : i + 2] for i in range(0, 10, 2))

    ways = [(ring.send_up(part), ring.send_down(part)) for part in parts]

    def project_queries(table_ref, n0, n1, weight, gain, c0, c1, s0, s1, *outs):
        query_kernel((n0, n1), weight, gain, (c0, c1), (s0, s1), outs[:2], outs[2:])

    *queries_raw, first, second = whole_call(
        project_queries,
        table,
        [((rows, each), F32, 1)] * 2 + [((rows, each), BF)] * 2,
        [
            *normeds, (in_hbm(query_weight), (model, each), lambda core: (0, core)),
            in_hbm(query_gain_row), *cosines, *sines,
        ],
    )
    queries = [first, second]

    def places_of(offsets):
        return [(offset, other) for offset in offsets for other in (False, True)]

    steps = ring.half
    calls = {0: ([0], parts)}
    state = None
    token = None
    for step in range(1, steps):
        come = []
        for which in range(2):
            up, down = ways[which]
            if step == 1 and which == 0:
                up, down, queries[0] = tie(up, down, queries[0])
            else:
                up, down, token = tie(up, down, token)
            come.append((up, down))
            if step < steps - 1:
                ways[which] = ring.send_up(up), ring.send_down(down)
            else:
                ways[which] = ring.send_down(down) if which else ring.send_up(up)
            if step == 1 and which == 0:
                state, token = attention_forward(
                    scalars, queries, parts, places_of([0]), None, True, False, come[0]
                )
        blocks = [come[0][0], come[1][0], come[0][1], come[1][1]]
        calls[step] = ([-step, step], blocks)
        state, token = attention_forward(
            scalars, queries, blocks, places_of([-step, step]), state, False, False, [token]
        )
    *ways, token = tie(*ways, token)
    calls[steps] = ([steps], ways)
    *attended, low_keep, low_give, logs, _ = attention_forward(
        scalars, queries, ways, places_of([steps]), state, False, True, [token]
    )
    low_other = ring.sibling(low_give)
    mixed_part = out_projection(ring.table, low_keep, out_weight, False)
    mixed_part = out_projection(ring.table, low_other, out_weight, True, mixed_part)
    mixed_part, cotangent = tie(mixed_part, cotangent)
    mixed_other = partner(mixed_part)
    cotangents = [cotangent, ring.sibling(cotangent)]
    hidden_grad = nt(cotangent, down_weight)
    mixed_other, hidden_grad, cotangents = tie(mixed_other, hidden_grad, cotangents)

    residual_wide = residual.astype(F32)
    mixed = residual_wide + both(mixed_part, mixed_other)
    normed_two, scale_two = norm_rows(mixed)
    normed_two_low = (normed_two * mlp_gain).astype(BF)
    gate = nn(normed_two_low, gate_weight)
    upward = nn(normed_two_low, up_weight)
    sigmoid_gate = jax.nn.sigmoid(gate)
    activated = gate * sigmoid_gate
    hidden_low = (activated * upward).astype(BF)
    gate_grad_low = (
        hidden_grad * upward * sigmoid_gate * (1.0 + gate * (1.0 - sigmoid_gate))
    ).astype(BF)
    up_grad_low = (hidden_grad * activated).astype(BF)
    normed_two_part = (nt(gate_grad_low, gate_weight) + nt(up_grad_low, up_weight)).astype(BF)
    normed_two_other = partner(normed_two_part)

    units = gate_weight.shape[1]
    thirds = 2 * units // model
    chips = ring.chips
    gate_rows = model // 2 // chips
    down_rows = units // thirds // 2 // chips
    out_row = thirds * gate_rows
    down_row = out_row + gate_rows
    packed_shape = (down_row + thirds * down_rows, model)

    def shard_of(chip, core):
        return core * chips + chip

    def columns_of(start):
        moves, done = [], 0
        while done < units:
            tile, column = divmod(start + done, model)
            wide = min(model - column, units - done)
            moves.append(
                (
                    None,
                    slice(done, done + wide),
                    (tile * gate_rows, (tile + 1) * gate_rows),
                    slice(column, column + wide),
                )
            )
            done += wide
        return moves

    everything = slice(None)
    wide = Gradients(
        ring,
        *packed_shape,
        [
            ((model, units), (gate_rows, units), lambda c, k: (shard_of(c, k), 0), columns_of(0)),
            ((model, units), (gate_rows, units), lambda c, k: (shard_of(c, k), 0), columns_of(units)),
            (
                (thirds, units // thirds, model),
                (thirds, down_rows, model),
                lambda c, k: (0, shard_of(c, k), 0),
                [
                    (i, everything, (down_row + i * down_rows, down_row + (i + 1) * down_rows), everything)
                    for i in range(thirds)
                ],
            ),
            (
                (2 * each, model),
                (gate_rows, model),
                lambda c, k: (shard_of(c, k), 0),
                [(None, everything, (out_row, out_row + gate_rows), everything)],
            ),
        ],
    )
    both_grad_low = jnp.concatenate([gate_grad_low, up_grad_low], axis=1)
    packed, token = products(
        ring.table, [normed_two_low, ring.sibling(normed_two_low)],
        [both_grad_low, ring.sibling(both_grad_low)], chips, (out_row, model), 0, 0, None,
        [normed_two_part],
    )
    wide.packs.append((0, packed))
    packed, token = products(
        ring.table, [hidden_low, ring.sibling(hidden_low)], cotangents, chips,
        (thirds * down_rows, model), 0, 0, None, [token], thirds=thirds,
    )
    wide.packs.append((down_row, packed))
    normed_two_other, token = tie(normed_two_other, token)

    normed_two_grad = both(normed_two_part, normed_two_other)
    mlp_gain_term = jnp.sum(normed_two_grad * normed_two, axis=0)
    mixed_grad = cotangent.astype(F32) + norm_back(
        normed_two_grad * mlp_gain, normed_two, scale_two
    )
    mixed_grad_low = mixed_grad.astype(BF)
    mixed_grads = [mixed_grad_low, ring.sibling(mixed_grad_low)]
    packed, token = products(
        ring.table, [low_keep, low_give], mixed_grads, chips, (gate_rows, model), 0, 0, None,
        [token], halved=False,
    )
    wide.packs.append((out_row, packed))
    wide_steps = wide.scatter()
    wide_way, wide_token = next(wide_steps)
    grads = heads_products(ring.table, mixed_grads, out_weight, [wide_token])
    delta = attention_delta(grads, attended)

    def backward(step, state, after):
        offsets, blocks = calls[step]
        last = step == 0
        return attention_backward(
            scalars, queries, grads, logs, delta, blocks, places_of(offsets), state,
            last, last, last or step == steps, after,
        )

    narrow_rows = model // chips
    narrow_shape = (narrow_rows, each + 2 * few)

    def narrow_out(start, wide):
        return (
            (model, 2 * wide),
            (narrow_rows, wide),
            lambda c, k: (c, k),
            [(None, everything, (0, narrow_rows), slice(start, start + wide))],
        )

    narrow = Gradients(
        ring,
        *narrow_shape,
        [narrow_out(0, each), narrow_out(each, few), narrow_out(each + few, few)],
    )
    up, down, token, state = backward(steps, None, [])
    up, down = ring.send_up(up), ring.send_down(down)
    for step in range(steps - 1, 0, -1):
        wide_way, wide_token = wide_steps.send((wide_way, [token]))
        if step == steps - 1:
            layer_part = matmul(hidden_low, down_weight, [wide_token])
            layer_other = partner(layer_part)
        if step == steps - 2:
            layer_other, wide_token = tie(layer_other, wide_token)
        back, front, token, state = backward(step, state, [wide_token])
        up, down, token = pair_add([front, back], [up, down], step == steps - 1, [token])
        up, down = ring.send_up(up), ring.send_down(down)
    wide_shard, wide_token = wide_steps.send((wide_way, [token]))
    wide_steps = wide.gather(wide_shard)
    wide_way, wide_ready = next(wide_steps)
    *key_value_own, token, first, second = backward(0, state, [wide_token])

    def back_queries(table_ref, g0, g1, r0, r1, gain, c0, c1, s0, s1, *outs):
        query_back_kernel((g0, g1), (r0, r1), gain, (c0, c1), (s0, s1), *outs)

    query_grad_low, query_gain_term = whole_call(
        back_queries,
        table,
        [((2 * rows, each), BF), ((8, head_dim), F32)],
        [first, second, *map(in_hbm, [*queries_raw, query_gain_row, *cosines, *sines])],
    )
    packed, token = products(
        ring.table, normeds, [query_grad_low], chips, narrow_shape, 0, 0, None, halved=False,
    )

    def own_ready(ready):
        return [(offset, part, False) for offset, part in ready]

    def other_ready(ready):
        return [(offset, ring.sibling(part), True) for offset, part in ready]

    first_other = ring.sibling(wide_shard)
    up, down, first_other, token = tie(up, down, first_other, token)

    def back_keys(table_ref, o0, o1, up_ref, down_ref, r0, r1, gain, c0, c1, s0, s1, *outs):
        key_value_back_kernel(
            (o0, o1), up_ref, down_ref, (r0, r1), gain, (c0, c1), (s0, s1), *outs
        )

    key_value_grad, key_gain_term = whole_call(
        back_keys,
        table,
        [((2 * rows, 2 * few), BF), ((8, head_dim), F32)],
        [
            *key_value_own, up, down, *map(in_hbm, [*keys_raw, key_gain_row, *cosines, *sines]),
        ],
        after=[token],
    )
    packed, token = products(
        ring.table, normeds, [key_value_grad], chips, narrow_shape, 0, each, packed, halved=False,
    )
    narrow.packs = [(0, packed)]
    narrow_steps = narrow.scatter()
    narrow_way, token = next(narrow_steps)

    gains = jnp.stack([jnp.sum(query_gain_term, axis=0), jnp.sum(key_gain_term, axis=0)])
    gains_other = partner(gains)
    wide_way, token = tie(wide_way, token)
    wide_way, pair = wide_steps.send(wide_way)
    narrow_way, gains_other, token = tie(narrow_way, gains_other, token)
    narrow_way, token = narrow_steps.send((narrow_way, [token]))

    def stacked_pair(ready, token, price=0):
        lot, token = stack([part for _, part in ready], [token], price)
        return (lot, [offset for offset, _ in ready]), token

    def fly(lots, token):
        flown = []
        for lot, offsets in lots:
            lot, token = tie(lot, token)
            other = ring.sibling(lot)
            flown.append((other, offsets))
        return flown, token

    def land(flown, results, token, price=0):
        for other, offsets in flown:
            other, token = tie(other, token)
            results = wide.unpack_stack(other, offsets, results, [token], price)
            token = results[-1]
        return results, token

    (lot, offsets), token = stacked_pair(pair, token)
    normed_own, normed_give = normed_products(
        ring.table, query_grad_low, key_value_grad, query_weight, key_weight, value_weight, [token]
    )
    narrow_way, normed_give = tie(narrow_way, normed_give)
    narrow_way, token = narrow_steps.send((narrow_way, []))
    flown, token = fly([(lot, offsets)], token)
    ready = own_ready(wide_ready + pair) + [(0, first_other, True)]
    wide_results = wide.unpack(ready, None, [token], SOME)
    narrow_way, wide_way, normed_give, token = tie(
        narrow_way, wide_way, normed_give, wide_results[-1]
    )
    normed_part = both(normed_own, ring.sibling(normed_give)).astype(BF)
    lots = []
    for step in range(steps - 3):
        narrow_way, token = narrow_steps.send((narrow_way, [token]))
        wide_way, pair = wide_steps.send(wide_way)
        if step == 0:
            normed_other = partner(normed_part)
        wide_results, token = land(flown, wide_results, token)
        lot, token = stacked_pair(pair, token)
        lots.append(lot)
        flown = []
        if step:
            flown, token = fly(lots, token)
            lots = []
        wide_results = wide.unpack(own_ready(pair), wide_results, [token], SOME)
        token = wide_results[-1]
        if step < steps - 4:
            wide_way, token = tie(wide_way, token)
    narrow_way, normed_other, token = tie(narrow_way, normed_other, token)
    narrow_shard, token = narrow_steps.send((narrow_way, [token]))

    normed_one, scale_one = norm_rows(residual_wide)
    normed_grad = both(normed_part, normed_other)
    attn_gain_term = jnp.sum(normed_grad * normed_one, axis=0)
    small = jnp.concatenate([attn_gain_term, mlp_gain_term, *(gains + gains_other)])
    small_rows = 16
    small = jnp.pad(small, (0, small_rows * model - small.shape[0])).reshape(small_rows, model)
    gathered = Gradients(ring, narrow_rows + small_rows, model, narrow.outs, small_rows)
    narrow_steps = gathered.gather(jnp.concatenate([narrow_shard, small.astype(BF)], axis=0), True)
    narrow_way, narrow_ready = next(narrow_steps)
    narrow_come = list(narrow_ready)
    more, token = fly(lots, token)
    wide_results, token = land(flown + more, wide_results, token, HEAVY)
    narrow_results = None
    for step in range(1, steps):
        narrow_way, token = tie(narrow_way, token)
        before = narrow_ready
        narrow_way, narrow_ready = narrow_steps.send(narrow_way)
        if step == 1:
            wide_way, token = tie(wide_way, token)
            wide_way, pair = wide_steps.send(wide_way)
            residual_grad = canonical(
                mixed_grad + norm_back(normed_grad * attn_gain, normed_one, scale_one)
            )
            layer_out = canonical(mixed + both(layer_part, layer_other)).astype(BF)
            residual_grad, layer_out, token = tie(residual_grad, layer_out, token)
            lot, token = stacked_pair(pair, token, HEAVY)
            wide_results = wide.unpack(own_ready(pair), wide_results, [token], 1)
            token = wide_results[-1]
        elif step == 2:
            flown, token = fly([lot], token)
            wide_way, token = tie(wide_way, token)
            _, far_ready = wide_steps.send(wide_way)
            far_other = other_ready(far_ready)
            first_own = own_ready(narrow_come)
            narrow_results = gathered.unpack(first_own, narrow_results, [token], HEAVY)
            token = narrow_results[-1]
        else:
            if step == 3:
                wide_results, token = land(flown, wide_results, token)
                wide_results = wide.unpack(
                    own_ready(far_ready) + far_other, wide_results, [token]
                )
                token = wide_results[-1]
            if step == steps - 1:
                narrow_lot, token = stack([part for _, part in narrow_come], [token])
                narrow_other = ring.sibling(narrow_lot)
            narrow_results = gathered.unpack(own_ready(before), narrow_results, [token], HEAVY)
            token = narrow_results[-1]
        narrow_come += narrow_ready
    narrow_way, token = tie(narrow_way, token)
    last_ready = narrow_ready
    _, narrow_ready = narrow_steps.send(narrow_way)
    last_ready = last_ready + narrow_ready
    last_other = other_ready(last_ready)
    offsets = [offset for offset, _ in narrow_come[: -len(last_ready) + len(narrow_ready)]]
    narrow_results = gathered.unpack(own_ready(last_ready), narrow_results, [token])
    ready = [(offset, (narrow_other, i), True) for i, offset in enumerate(offsets)] + last_other
    query_sum, key_sum, value_sum, small, _ = gathered.unpack(ready, narrow_results)
    gate_sum, up_sum, down_sum, out_weight_sum, _, _ = wide_results
    small = small.reshape(-1)

    attn_gain_grad, mlp_gain_grad = small[:model], small[model : 2 * model]
    query_gain_grad = small[2 * model : 2 * model + head_dim]
    key_gain_grad = small[2 * model + head_dim : 2 * model + 2 * head_dim]
    return (
        layer_out,
        residual_grad,
        attn_gain_grad,
        query_sum,
        key_sum,
        value_sum,
        query_gain_grad,
        key_gain_grad,
        out_weight_sum,
        mlp_gain_grad,
        gate_sum,
        up_sum,
        down_sum.reshape(units, model),
    )


def solution(mesh):
    return jax.shard_map(
        functools.partial(body, mesh.shape["cp"]),
        mesh=mesh,
        in_specs=(
            P("cp", None),
            P("cp", None),
            P(),
            P("cp"),
            P(),
            P(None, "tp"),
            P(None, "tp"),
            P(None, "tp"),
            P(),
            P(),
            P("tp", None),
            P(),
            P(None, "tp"),
            P(None, "tp"),
            P("tp", None),
        ),
        out_specs=(
            P("cp", None),
            P("cp", None),
            P(),
            P(None, "tp"),
            P(None, "tp"),
            P(None, "tp"),
            P(),
            P(),
            P("tp", None),
            P(),
            P(None, "tp"),
            P(None, "tp"),
            P("tp", None),
        ),
        check_vma=False,
    )
```

```python
import functools
import math

import jax
import jax.numpy as jnp
from jax import lax
from jax.experimental import pallas as pl
from jax.experimental.pallas import tpu as pltpu
from jax.sharding import PartitionSpec as P

EPS = 1e-06
ROPE_BASE = 1000000.0
HEAD = 128
LOG2E = 1.4426950408889634
VMEM_LIMIT = 16 * 1024 * 1024


def cost(microseconds):
    return pl.CostEstimate(
        flops=1024 + int(microseconds * 1e9), bytes_accessed=1024, transcendentals=0
    )


LIGHT = cost(0)
FORWARD = cost(1)
HEAVY = 50
SOME = 5
LITTLE = 4
BF = jnp.bfloat16
F32 = jnp.float32
TOKEN = jax.ShapeDtypeStruct((8, 128), jnp.float32)


def nn(a, b):
    return lax.dot_general(a, b, (((1,), (0,)), ((), ())), preferred_element_type=F32)


def nt(a, b):
    return lax.dot_general(a, b, (((1,), (1,)), ((), ())), preferred_element_type=F32)


def tn(a, b):
    return lax.dot_general(a, b, (((0,), (0,)), ((), ())), preferred_element_type=F32)


def norm_rows(values):
    scale_rows = lax.rsqrt(jnp.mean(values * values, axis=-1, keepdims=True) + EPS)
    return (values * scale_rows, scale_rows)


def norm_back(grad_normed, normed, scale_rows):
    return scale_rows * (
        grad_normed - normed * jnp.mean(grad_normed * normed, axis=-1, keepdims=True)
    )


def tie(*values):
    return lax.optimization_barrier(values)


def waits(after):
    return list(after), [pl.BlockSpec(memory_space=pl.ANY)] * len(after)


def in_hbm(x):
    return pltpu.with_memory_space_constraint(x, pltpu.HBM)


def ring_order(chips):
    if chips % 8:
        return list(range(chips))
    rows, cols = 4, chips // 4
    if cols % 2 or cols < 4:
        path = list(range(cols))
    else:
        path = list(range(cols // 2)) + list(range(cols - 1, cols // 2 - 1, -1))
    walk = []
    for row in range(rows):
        across = range(1, cols) if row % 2 == 0 else range(cols - 1, 0, -1)
        walk += [(row, col) for col in across]
    walk = [(0, 0)] + walk + [(row, 0) for row in range(rows - 1, 0, -1)]
    return [row * cols + path[col] for row, col in walk]


class Ring:
    def __init__(self, devices):
        self.devices = devices
        self.chips = devices // 2
        order = ring_order(self.chips)
        self.order = order
        size = self.chips
        self.up = [
            (2 * order[i] + core, 2 * order[(i + 1) % size] + core)
            for i in range(size)
            for core in range(2)
        ]
        self.down = [(b, a) for a, b in self.up]
        self.swap = [(i, i ^ 1) for i in range(devices)]
        place = [0] * size
        for i, chip in enumerate(order):
            place[chip] = i
        index = lax.axis_index("cp")
        self.core = index % 2
        self.here = jnp.asarray(place, jnp.int32)[index // 2]
        self.half = size // 2
        table = [
            [order[(place[chip] + i) % size] for i in range(size)] + [core]
            for chip in range(size)
            for core in range(2)
        ]
        self.table = lax.dynamic_index_in_dim(
            jnp.asarray(table, jnp.int32), index, 0, keepdims=False
        )

    def send_up(self, x):
        return lax.ppermute(x, "cp", self.up)

    def send_down(self, x):
        return lax.ppermute(x, "cp", self.down)

    def sibling(self, x):
        return lax.ppermute(x, "cp", self.swap)


def products(
    table, lefts, rights, chips, packed, row, column, before, after=(), thirds=1, halved=True
):
    tokens = lefts[0].shape[0]
    high = lefts[0].shape[1] // thirds // (2 if halved else 1)
    rows = high // chips
    wide = rights[0].shape[1]
    tile = min(wide, 512 if wide <= 1024 and thirds == 1 else 1024)
    last = table.shape[0] - 1
    more_args, more_specs = waits(after)
    if before is not None:
        more_args, more_specs = [before] + more_args, [pl.BlockSpec(memory_space=pl.ANY)] + more_specs
    side = len(lefts)

    def kernel(table_ref, *refs):
        out, token, turned = refs[side + len(rights) + len(more_args) :]

        @pl.when(pl.program_id(1) == 0)
        def _():
            for i in range(side):
                turned[:, i * tokens : (i + 1) * tokens] = refs[i][...].T
            token[...] = jnp.zeros_like(token)

        total, start = 0.0, 0
        for right in refs[side : side + len(rights)]:
            stop = start + right.shape[0]
            total = total + nn(turned[:, start:stop], right[...])
            start = stop
        out[...] = total.reshape(chips, rows, tile).astype(BF)

    def left_place(j, i, t):
        return (0, 2 * j + t[last] if halved else j)

    across = packed[1] // tile

    def out_place(j, i, t):
        at = column // tile + i
        return (0, row // rows + j + at // across, at % across)

    shape = (chips, *packed)
    return pl.pallas_call(
        kernel,
        out_shape=[jax.ShapeDtypeStruct(shape, BF), TOKEN],
        grid_spec=pltpu.PrefetchScalarGridSpec(
            num_scalar_prefetch=1,
            grid=(thirds, wide // tile),
            in_specs=[pl.BlockSpec((tokens, high), left_place)] * side
            + [pl.BlockSpec((right.shape[0], tile), lambda j, i, t: (0, i)) for right in rights]
            + more_specs,
            out_specs=[
                pl.BlockSpec((chips, rows, tile), out_place),
                pl.BlockSpec((8, 128), lambda j, i, t: (0, 0)),
            ],
            scratch_shapes=[pltpu.VMEM((high, side * tokens), BF)],
        ),
        input_output_aliases={} if before is None else {1 + side + len(rights): 0},
        compiler_params=pltpu.CompilerParams(vmem_limit_bytes=VMEM_LIMIT),
        cost_estimate=LIGHT,
    )(table, *lefts, *rights, *more_args)


class Gradients:
    def __init__(self, ring, rows, columns, outs, added=0):
        self.ring, self.rows, self.columns, self.outs = ring, rows, columns, outs
        self.added = added
        self.cut = -(-rows // 32) * 16
        self.packs = []

    def shards(self, offsets, received, halves, after=()):
        ring, columns, rows, cut = self.ring, self.columns, self.rows, self.cut
        spans = [(0, cut), (cut, rows)]
        sides, count = len(offsets), len(self.packs)
        args, specs = [], []
        for offset in offsets:
            for _, pack in self.packs:
                args.append(pack)
                specs.append(
                    pl.BlockSpec(
                        (1, *pack.shape[1:]), lambda i, t, at=offset: (t[at % ring.chips], 0, 0)
                    )
                )
        args += received
        specs += [pl.BlockSpec(x.shape, lambda i, t: (0, 0)) for x in received]
        more_args, more_specs = waits(after)
        taken = len(args) + len(more_args)

        def kernel(table_ref, *refs):
            outs = refs[taken:]
            outs[-1][...] = jnp.zeros_like(outs[-1])
            gained = refs[sides * count : len(args)]
            for side in range(sides):
                for number, (row, pack) in enumerate(self.packs):
                    mine = refs[side * count + number]
                    stop = row + pack.shape[1]
                    if halves == "send":
                        for out, (start, end) in zip(outs, spans):
                            first, last = max(row, start), min(stop, end)
                            if first < last:
                                out[first - start : last - start] = mine[0, first - row : last - row]
                        continue
                    start, end = spans[side] if halves == "add" else (0, rows)
                    for first, last, more in (
                        (row, min(stop, start), False),
                        (max(row, start), min(stop, end), True),
                        (max(row, end), stop, False),
                    ):
                        if first < last:
                            part = mine[0, first - row : last - row]
                            if more:
                                part = part.astype(F32)
                                for got in gained if halves == "sum" else [gained[side]]:
                                    part = part + got[first - start : last - start].astype(F32)
                            outs[side][first:last] = part.astype(BF)

        highs = {"send": [cut, rows - cut], "sum": [rows]}.get(halves, [rows, rows])
        return pl.pallas_call(
            kernel,
            out_shape=[jax.ShapeDtypeStruct((high, columns), BF) for high in highs] + [TOKEN],
            grid_spec=pltpu.PrefetchScalarGridSpec(
                num_scalar_prefetch=1,
                grid=(1,),
                in_specs=specs + more_specs,
                out_specs=[pl.BlockSpec((high, columns), lambda i, t: (0, 0)) for high in highs]
                + [pl.BlockSpec((8, 128), lambda i, t: (0, 0))],
            ),
            compiler_params=pltpu.CompilerParams(vmem_limit_bytes=VMEM_LIMIT),
            cost_estimate=LIGHT,
        )(ring.table, *args, *more_args)

    def scatter(self, after=()):
        ring = self.ring
        up, down, token = self.shards([ring.half], [], "send", after)
        for step in range(ring.half - 1, -1, -1):
            (up, down), after = yield (ring.send_up(up), ring.send_down(down)), token
            if step:
                kind = "add" if step == ring.half - 1 else ""
                up, down, token = self.shards([step, -step], [up, down], kind, after)
        yield self.shards([0], [up, down], "sum", after)

    def gather(self, own, split=False):
        ring, cut = self.ring, self.cut
        up = down = own
        ready = [(0, own)]
        for step in range(1, ring.half):
            up, down = yield (ring.send_up(up), ring.send_down(down)), ready
            ready = [(-step, up), (step, down)]
        high, low = yield (ring.send_up(up[:cut]), ring.send_down(down[cut:])), ready
        if split:
            yield None, [(ring.half, high), (ring.half, low)]
        else:
            yield None, [(ring.half, jnp.concatenate([high, low], axis=0))]

    def unpack_stack(self, stack, offsets, before, after=(), price=0):
        return self.unpack(
            [(offset, stack, True) for offset in offsets], before, after, price, True
        )

    def unpack(self, ready, before, after=(), price=0, stacked=False):
        ring, outs, added = self.ring, self.outs, max(self.added, 8)
        count = len(ready)
        parts = [part if isinstance(part, tuple) else (part, None) for _, part, _ in ready]
        args = []
        for array, _ in parts:
            if not any(array is x for x in args):
                args.append(array)
        which = [next(j for j, x in enumerate(args) if x is array) for array, _ in parts]
        highs = [array.shape[-2] for array, _ in parts]
        places_of = [(offset, other) for offset, _, other in ready]

        def write(part, start, results):
            stop = start + part.shape[0]
            for out, (_, _, _, moves) in zip(results, outs):
                for lead, across, (first, last), columns in moves:
                    low, high = max(first, start), min(last, stop)
                    if low < high:
                        rows = slice(low - first, high - first)
                        where = (rows, across) if lead is None else (lead, rows, across)
                        out[where] = part[low - start : high - start, columns].astype(F32)

        def start_of(i):
            same = [j for j in range(i) if places_of[j] == places_of[i]]
            return sum(highs[j] for j in same)

        starts = [0] * count if stacked else [start_of(i) for i in range(count)]

        def kernel(table_ref, *refs):
            step = pl.program_id(0)

            def part_of(i):
                ref, at = refs[which[i]], parts[i][1]
                return ref if at is None else ref.at[at]

            results = refs[-len(outs) - 2 : -2]
            refs[-1][...] = jnp.zeros_like(refs[-1])
            total = refs[-2]

            @pl.when(step == 0)
            def _():
                total[...] = jnp.zeros_like(total) if before is None else refs[sum_place][...]

            if self.added and stacked:
                total[...] += refs[0][0, self.rows - added :].astype(F32)
            elif self.added:
                for i in range(count):
                    if starts[i] + highs[i] == self.rows:

                        @pl.when(step == i)
                        def _(i=i):
                            total[...] += part_of(i)[highs[i] - added :].astype(F32)

            if stacked:
                write(refs[0].at[0], 0, results)
                return
            for i in range(count):
                pl.when(step == i)(functools.partial(write, part_of(i), starts[i], results))

        def place(of_chip, i, table):
            chip, core = None, None
            for j, (offset, other) in enumerate(places_of):
                here = table[offset % ring.chips]
                mine = table[ring.chips]
                mine = 1 - mine if other else mine
                chip = here if chip is None else jnp.where(i == j, here, chip)
                core = mine if core is None else jnp.where(i == j, mine, core)
            return of_chip(chip, core)

        shapes, out_specs = [], []
        for shape, block, of_chip, _ in outs:
            shapes.append(pltpu.HBM(shape, F32))
            out_specs.append(pl.BlockSpec(block, functools.partial(place, of_chip)))
        shapes += [jax.ShapeDtypeStruct((added, self.columns), F32), TOKEN]
        out_specs.append(pl.BlockSpec((added, self.columns), lambda i, t: (0, 0)))
        out_specs.append(pl.BlockSpec((8, 128), lambda i, t: (0, 0)))
        if stacked:
            specs = [pl.BlockSpec((1, self.rows, self.columns), lambda i, t: (i, 0, 0))]
        else:
            specs = [pl.BlockSpec(x.shape, lambda i, t, n=x.ndim: (0,) * n) for x in args]
        aliases = {}
        if before is not None:
            aliases = {1 + len(args) + i: i for i in range(len(outs))}
            specs += [pl.BlockSpec(memory_space=pl.ANY)] * len(outs)
            args += [in_hbm(x) for x in before[: len(outs)]]
            sum_place = len(args)
            args.append(before[len(outs)])
            specs.append(pl.BlockSpec((added, self.columns), lambda i, t: (0, 0)))
        more_args, more_specs = waits(after)
        args += more_args
        specs += more_specs
        return list(
            pl.pallas_call(
                kernel,
                out_shape=shapes,
                grid_spec=pltpu.PrefetchScalarGridSpec(
                    num_scalar_prefetch=1, grid=(count,), in_specs=specs, out_specs=out_specs
                ),
                input_output_aliases=aliases,
                compiler_params=pltpu.CompilerParams(vmem_limit_bytes=VMEM_LIMIT),
                cost_estimate=cost(price),
            )(ring.table, *args)
        )


def stack(parts, after=(), price=0):
    rows, columns = parts[0].shape
    count = len(parts)
    more_args, more_specs = waits(after)

    def kernel(*refs):
        out, token = refs[-2:]
        token[...] = jnp.zeros_like(token)
        for i in range(count):

            @pl.when(pl.program_id(0) == i)
            def _(i=i):
                out[0] = refs[i][...]

    return pl.pallas_call(
        kernel,
        out_shape=[jax.ShapeDtypeStruct((count, rows, columns), parts[0].dtype), TOKEN],
        grid=(count,),
        in_specs=[pl.BlockSpec((rows, columns), lambda i: (0, 0))] * count + more_specs,
        out_specs=[
            pl.BlockSpec((1, rows, columns), lambda i: (i, 0, 0)),
            pl.BlockSpec((8, 128), lambda i: (0, 0)),
        ],
        compiler_params=pltpu.CompilerParams(vmem_limit_bytes=VMEM_LIMIT),
        cost_estimate=cost(price),
    )(*parts, *more_args)


def pair_add(own, received, half, after=()):
    more_args, more_specs = waits(after)

    def kernel(*refs):
        refs, outs = refs[:4], refs[4 + len(more_args) :]
        outs[-1][...] = jnp.zeros_like(outs[-1])
        for side in range(2):
            mine, got, out = refs[side], refs[2 + side], outs[side]
            if half:
                rows = got.shape[0]
                here = slice(side * rows, (side + 1) * rows)
                rest = slice((1 - side) * rows, (2 - side) * rows)
                out[here] = (mine[here].astype(F32) + got[...].astype(F32)).astype(BF)
                out[rest] = mine[rest]
            else:
                out[...] = (mine[...].astype(F32) + got[...].astype(F32)).astype(BF)

    shape = jax.ShapeDtypeStruct(own[0].shape, BF)
    return pl.pallas_call(
        kernel,
        out_shape=[shape, shape, TOKEN],
        in_specs=[pl.BlockSpec(memory_space=pltpu.VMEM)] * 4 + more_specs,
        compiler_params=pltpu.CompilerParams(vmem_limit_bytes=VMEM_LIMIT),
        cost_estimate=LIGHT,
    )(*own, *received, *more_args)


def partner(x):
    return lax.ppermute(x, "tp", [(0, 1), (1, 0)])


def both(mine, other):
    return mine.astype(F32) + other.astype(F32)


def turn(values, cosine, sine):
    return values * cosine + pltpu.roll(values, values.shape[-1] // 2, 1) * sine


def turn_back(values, cosine, sine):
    return values * cosine - pltpu.roll(values, values.shape[-1] // 2, 1) * sine


def lower_first(order, table, other):
    core = table[table.shape[0] - 1]
    device = 2 * table[0] + (1 - core if other else core)
    return order[2 * device] < order[2 * device + 1]


def key_value_kernel(
    order, table, residuals, cotangent, gain, key_weight, value_weight, key_gain, angles, outs
):
    residual_out, cotangent_out, normed_outs, raw_outs, cosine_outs, sine_outs, packed_outs = outs
    width = key_gain.shape[1]
    span = residuals[0].shape[0] // 2
    for pair in range(2):
        start = jnp.where(lower_first(order, table, pair == 1), 0, span)

        def canonical(ref):
            return jnp.concatenate(
                [
                    ref[pl.ds(pl.multiple_of(start, span), span)],
                    ref[pl.ds(pl.multiple_of(span - start, span), span)],
                ],
                axis=0,
            )

        rows = canonical(residuals[pair])
        if pair == 0:
            residual_out[...] = rows
            cotangent_out[...] = canonical(cotangent)
        unit, _ = norm_rows(rows.astype(F32))
        normed = (unit * gain[...]).astype(BF)
        normed_outs[pair][...] = normed
        cosine, sine = canonical(angles[2 * pair]), canonical(angles[2 * pair + 1])
        cosine_outs[pair][...], sine_outs[pair][...] = cosine, sine
        raw = nn(normed, key_weight[...])
        raw_outs[pair][...] = raw
        values = nn(normed, value_weight[...]).astype(BF)
        for group in range(raw.shape[1] // width):
            here = slice(group * width, (group + 1) * width)
            key_unit, _ = norm_rows(raw[:, here])
            packed = packed_outs[pair]
            packed[:, 2 * group * width : (2 * group + 1) * width] = turn(
                key_unit * key_gain[...], cosine, sine
            ).astype(BF)
            packed[:, (2 * group + 1) * width : (2 * group + 2) * width] = values[:, here]


def query_kernel(normeds, weight, gain, cosines, sines, raw_outs, low_outs):
    width = gain.shape[1]
    for pair in range(2):
        raw = nn(normeds[pair][...], weight[...])
        raw_outs[pair][...] = raw
        for head in range(raw.shape[1] // width):
            here = slice(head * width, (head + 1) * width)
            unit, _ = norm_rows(raw[:, here])
            low_outs[pair][:, here] = turn(
                unit * gain[...], cosines[pair][...], sines[pair][...]
            ).astype(BF)


def heads_back(grad_of, raws, gain, cosines, sines, out, total):
    width = gain.shape[1]
    rows = raws[0].shape[0]
    for pair in range(2):
        here_rows = slice(pair * rows, (pair + 1) * rows)
        for head in range(raws[pair].shape[1] // width):
            here = slice(head * width, (head + 1) * width)
            unit, scale_rows = norm_rows(raws[pair][:, here])
            turned = turn_back(grad_of(pair, head), cosines[pair][...], sines[pair][...])
            total = total + jnp.sum((turned * unit).reshape(-1, 8, width), axis=0)
            out[here_rows, here] = norm_back(turned * gain[...], unit, scale_rows).astype(BF)
    return total


def query_back_kernel(grads, raws, gain, cosines, sines, low_out, gain_out):
    width = gain.shape[1]
    gain_out[...] = heads_back(
        lambda pair, head: grads[pair][:, head * width : (head + 1) * width],
        raws, gain, cosines, sines, low_out, jnp.zeros((8, width), F32),
    )


def key_value_back_kernel(owns, upward, downward, raws, gain, cosines, sines, low_out, gain_out):
    width = gain.shape[1]
    rows, columns = raws[0].shape
    groups = columns // width

    def summed(pair, place):
        here = slice(place * width, (place + 1) * width)
        at = slice(pair * rows, (pair + 1) * rows)
        return (
            owns[pair][:, here].astype(F32)
            + upward[at, here].astype(F32)
            + downward[at, here].astype(F32)
        )

    gain_out[...] = heads_back(
        lambda pair, head: summed(pair, 2 * head),
        raws, gain, cosines, sines, low_out, jnp.zeros((8, width), F32),
    )
    for pair in range(2):
        for group in range(groups):
            low_out[
                pair * rows : (pair + 1) * rows,
                columns + group * width : columns + (group + 1) * width,
            ] = summed(pair, 2 * group + 1).astype(BF)


def whole_call(kernel, scalars, outs, args, after=()):
    more_args, more_specs = waits(after)
    count = len(scalars)
    arrays, specs = [], []
    for arg in args:
        array, block, place = arg if isinstance(arg, tuple) else (arg, arg.shape, None)
        arrays.append(array)
        if place is None:
            specs.append(pl.BlockSpec(block, lambda i, *t: (0, 0)))
        else:
            specs.append(
                pl.BlockSpec(
                    block, lambda i, *t, place=place: place(t[-1][t[-1].shape[0] - 1])
                )
            )
    taken = count + len(args)

    def run(*refs):
        kernel(*refs[:taken], *refs[taken + len(more_args) :])

    return list(
        pl.pallas_call(
            run,
            out_shape=[
                pltpu.HBM(shape, dtype) if far else jax.ShapeDtypeStruct(shape, dtype)
                for shape, dtype, *far in outs
            ],
            grid_spec=pltpu.PrefetchScalarGridSpec(
                num_scalar_prefetch=count,
                grid=(1,),
                in_specs=specs + more_specs,
                out_specs=[pl.BlockSpec(shape, lambda i, *t: (0, 0)) for shape, *_ in outs],
            ),
            compiler_params=pltpu.CompilerParams(vmem_limit_bytes=VMEM_LIMIT),
            cost_estimate=LIGHT,
        )(*scalars, *arrays, *more_args)
    )


def matmul(left, right, after=(), price=0):
    rows, inner = left.shape
    columns = right.shape[1]
    tile = min(columns, 512)
    more_args, more_specs = waits(after)

    def kernel(left_ref, right_ref, *refs):
        refs[-1][...] = nn(left_ref[...], right_ref[...]).astype(BF)

    return pl.pallas_call(
        kernel,
        out_shape=jax.ShapeDtypeStruct((rows, columns), BF),
        grid=(columns // tile,),
        in_specs=[
            pl.BlockSpec((rows, inner), lambda i: (0, 0)),
            pl.BlockSpec((inner, tile), lambda i: (0, i)),
        ]
        + more_specs,
        out_specs=pl.BlockSpec((rows, tile), lambda i: (0, i)),
        compiler_params=pltpu.CompilerParams(vmem_limit_bytes=VMEM_LIMIT),
        cost_estimate=cost(price),
    )(left, in_hbm(right), *more_args)


def add_and_norm(part, other, residual, half, gain, price=0):
    rows, columns = part.shape

    def kernel(part_ref, other_ref, residual_ref, gain_ref, total, low):
        both_parts = part_ref[...].astype(F32) + other_ref[...].astype(F32)
        mixed = residual_ref[...].astype(F32) + both_parts
        total[...] = mixed
        normed, _ = norm_rows(mixed)
        low[...] = (normed * gain_ref[...]).astype(BF)

    whole = pl.BlockSpec((rows, columns), lambda i: (0, 0))
    return pl.pallas_call(
        kernel,
        out_shape=[
            jax.ShapeDtypeStruct((rows, columns), F32),
            jax.ShapeDtypeStruct((rows, columns), BF),
        ],
        grid=(1,),
        in_specs=[
            whole,
            whole,
            pl.BlockSpec((rows, columns), lambda i: (half, 0)),
            pl.BlockSpec((1, columns), lambda i: (0, 0)),
        ],
        out_specs=[whole, whole],
        compiler_params=pltpu.CompilerParams(vmem_limit_bytes=VMEM_LIMIT),
        cost_estimate=cost(price),
    )(part, other, residual, gain)


def finish(order, residual, mixed, mixed_grad, normed_parts, layer_parts, gain, after):
    rows, columns = residual.shape
    span = rows // 2
    more_args, more_specs = waits(after)

    def kernel(order_ref, row, mix, mix_grad, normed0, normed1, layer0, layer1, gain_ref, *refs):
        out, grad, token = refs[-3:]
        out[...] = (mix[...] + both(layer0[...], layer1[...])).astype(BF)
        normed, scale = norm_rows(row[...].astype(F32))
        normed_grad = both(normed0[...], normed1[...]) * gain_ref[...]
        grad[...] = mix_grad[...] + norm_back(normed_grad, normed, scale)
        token[...] = jnp.zeros_like(token)

    part = pl.BlockSpec((span, columns), lambda i, o: (i, 0))
    placed = pl.BlockSpec((span, columns), lambda i, o: (jnp.where(o[0] < o[1], i, 1 - i), 0))
    return pl.pallas_call(
        kernel,
        out_shape=[
            jax.ShapeDtypeStruct((rows, columns), BF),
            jax.ShapeDtypeStruct((rows, columns), F32),
            TOKEN,
        ],
        grid_spec=pltpu.PrefetchScalarGridSpec(
            num_scalar_prefetch=1,
            grid=(2,),
            in_specs=[part] * 7 + [pl.BlockSpec((1, columns), lambda i, o: (0, 0))] + more_specs,
            out_specs=[placed, placed, pl.BlockSpec(TOKEN.shape, lambda i, o: (0, 0))],
        ),
        compiler_params=pltpu.CompilerParams(vmem_limit_bytes=VMEM_LIMIT),
        cost_estimate=LIGHT,
    )(order, residual, mixed, mixed_grad, *normed_parts, *layer_parts, gain, *more_args)


def out_projection(table, rows, weight, other, before=None):
    high, inner = rows.shape
    columns = weight.shape[1]
    tile = min(inner, 256)
    count = inner // tile
    last = table.shape[0] - 1
    dtype = F32 if before is None else BF

    def kernel(table_ref, rows_ref, weight_ref, *refs):
        out, total = refs[-2:]
        step = pl.program_id(0)
        part = nn(rows_ref[...], weight_ref[...])

        @pl.when(step == 0)
        def _():
            total[...] = part if before is None else part + refs[0][...]

        @pl.when(step > 0)
        def _():
            total[...] += part

        @pl.when(step == count - 1)
        def _():
            out[...] = total[...].astype(dtype)

    whole = pl.BlockSpec((high, columns), lambda i, t: (0, 0))
    extra = [] if before is None else [before]
    return pl.pallas_call(
        kernel,
        out_shape=jax.ShapeDtypeStruct((high, columns), dtype),
        grid_spec=pltpu.PrefetchScalarGridSpec(
            num_scalar_prefetch=1,
            grid=(count,),
            in_specs=[
                pl.BlockSpec((high, tile), lambda i, t: (0, i)),
                pl.BlockSpec(
                    (tile, columns),
                    lambda i, t: ((1 - t[last] if other else t[last]) * count + i, 0),
                ),
            ]
            + [whole] * len(extra),
            out_specs=whole,
            scratch_shapes=[pltpu.VMEM((high, columns), F32)],
        ),
        compiler_params=pltpu.CompilerParams(vmem_limit_bytes=VMEM_LIMIT),
        cost_estimate=LIGHT,
    )(table, rows, weight, *extra)


def heads_products(table, rows, weight, after=()):
    high, columns = rows[0].shape
    inner = weight.shape[0] // 2
    tile = min(inner, 256)
    count = inner // tile
    last = table.shape[0] - 1
    more_args, more_specs = waits(after)

    def kernel(table_ref, first, second, mine, *refs):
        refs[-2][...] = nt(first[...], mine[...]).astype(BF)
        refs[-1][...] = nt(second[...], mine[...]).astype(BF)

    shape = jax.ShapeDtypeStruct((high, inner), BF)
    spec = pl.BlockSpec((high, tile), lambda i, t: (0, i))
    whole = pl.BlockSpec((high, columns), lambda i, t: (0, 0))
    return pl.pallas_call(
        kernel,
        out_shape=[shape, shape],
        grid_spec=pltpu.PrefetchScalarGridSpec(
            num_scalar_prefetch=1,
            grid=(count,),
            in_specs=[
                whole,
                whole,
                pl.BlockSpec((tile, columns), lambda i, t: (t[last] * count + i, 0)),
            ]
            + more_specs,
            out_specs=[spec, spec],
        ),
        compiler_params=pltpu.CompilerParams(vmem_limit_bytes=VMEM_LIMIT),
        cost_estimate=LIGHT,
    )(table, *rows, in_hbm(weight), *more_args)


def normed_products(
    table, normeds, query_grad, key_value_grad, query_weight, key_weight, value_weight, after=()
):
    rows, wide = query_grad.shape
    narrow = key_value_grad.shape[1] // 2
    columns = query_weight.shape[0]
    tile = min(columns, 256)
    last = table.shape[0] - 1
    more_args, more_specs = waits(after)

    def kernel(table_ref, first, second, queries, others, query, key, value, *refs):
        total = (
            nt(queries[...], query[...])
            + nt(others[:, :narrow], key[...])
            + nt(others[:, narrow:], value[...])
        ).astype(BF)
        upper, lower = total[: rows // 2], total[rows // 2 :]
        refs[-3][...] = upper
        refs[-2][...] = lower
        term = upper.astype(F32) * first[...].astype(F32) + lower.astype(F32) * second[...].astype(F32)
        refs[-1][...] = jnp.sum(term.reshape(-1, 8, tile), axis=0)

    shape = jax.ShapeDtypeStruct((rows // 2, columns), BF)
    spec = pl.BlockSpec((rows // 2, tile), lambda i, t: (0, i))
    return pl.pallas_call(
        kernel,
        out_shape=[shape, shape, jax.ShapeDtypeStruct((8, columns), F32)],
        grid_spec=pltpu.PrefetchScalarGridSpec(
            num_scalar_prefetch=1,
            grid=(columns // tile,),
            in_specs=[
                spec,
                spec,
                pl.BlockSpec((rows, wide), lambda i, t: (0, 0)),
                pl.BlockSpec((rows, 2 * narrow), lambda i, t: (0, 0)),
                pl.BlockSpec((tile, wide), lambda i, t: (i, t[last])),
                pl.BlockSpec((tile, narrow), lambda i, t: (i, t[last])),
                pl.BlockSpec((tile, narrow), lambda i, t: (i, t[last])),
            ]
            + more_specs,
            out_specs=[spec, spec, pl.BlockSpec((8, tile), lambda i, t: (0, i))],
        ),
        compiler_params=pltpu.CompilerParams(vmem_limit_bytes=VMEM_LIMIT),
        cost_estimate=cost(HEAVY),
    )(
        table, *normeds, query_grad, key_value_grad, in_hbm(query_weight), in_hbm(key_weight),
        in_hbm(value_weight), *more_args,
    )


def stacked(ref, start, span, width):
    rows = pl.ds(start, span)
    return jnp.concatenate([ref[rows, :width], ref[rows, width:]], axis=0)


def causal(span, transposed):
    shape = (span, 2 * span) if transposed else (2 * span, span)
    key = lax.broadcasted_iota(jnp.int32, shape, 0 if transposed else 1)
    row = lax.broadcasted_iota(jnp.int32, shape, 1 if transposed else 0)
    return key <= row % span


def side_met(order, table, pair, offset, other):
    last = table.shape[0] - 1
    core = table[last]

    def lower(device):
        return jnp.minimum(order[2 * device], order[2 * device + 1])

    mine = lower(2 * table[0] + (1 - core if pair else core))
    theirs = lower(2 * table[offset % last] + (1 - core if other else core))
    return jnp.where(theirs < mine, 0, 1)


def forward_kernel(places, own, last, span, width, order, table, *refs):
    count = len(places)
    queries, blocks, refs = refs[:2], refs[2 : 2 + count], refs[2 + count :]
    scale = LOG2E / math.sqrt(width)
    if own:
        before, outs = None, refs
    else:
        before, outs = refs[0], refs[1:]
    accum = outs[-1]
    ones = jnp.ones((span, width), BF)

    def weighted(rows, keys, values, allowed=None):
        scores = nt(rows, keys)
        probs = jnp.exp2(scores * scale)
        if allowed is not None:
            probs = jnp.where(allowed, probs, 0.0)
        return nn(probs.astype(BF), values)

    def extended(block, start):
        return jnp.concatenate([block[pl.ds(start, span), width:], ones], axis=1)

    keys = jnp.concatenate([block[:span, :width] for block in blocks], axis=0)
    values = jnp.concatenate([extended(block, 0) for block in blocks], axis=0)
    rows = jnp.concatenate([stacked(query, span, span, width) for query in queries], axis=0)
    high = weighted(rows, keys, values)
    for pair in range(2):
        part = high[pair * 2 * span : (pair + 1) * 2 * span]
        if own:
            allowed = causal(span, False)
            for side in range(2):
                block, start = blocks[pair], side * span
                met = weighted(
                    stacked(queries[pair], start, span, width),
                    block[start : start + span, :width],
                    extended(block, start),
                    allowed,
                )
                accum[0, pair, side] = met + part if side else met
        else:
            accum[0, pair, 0] = before[0, pair, 0]
            accum[0, pair, 1] = before[0, pair, 1] + part
    for i, (offset, other) in enumerate(places):
        for pair in range(2):
            if own and i == pair:
                continue
            side = side_met(order, table, pair, offset, other)
            start = pl.multiple_of(side * span, span)
            accum[0, pair, side] += weighted(
                stacked(queries[pair], start, span, width),
                blocks[i][pl.ds(start, span), :width],
                extended(blocks[i], start),
            )
    if last:
        wides, lows, logs = outs[0:2], outs[2:4], outs[4]
        for pair in range(2):
            for side in range(2):
                rows = slice(side * span, (side + 1) * span)
                whole = accum[0, pair, side]
                mass = whole[:, width:]
                out = whole[:, :width] / mass
                for head in range(2):
                    part = out[head * span : (head + 1) * span]
                    columns = slice(head * width, (head + 1) * width)
                    wides[pair][rows, columns] = part
                    lows[pair][rows, columns] = part.astype(BF)
                logs[0, pair, side] = jnp.log2(mass).T[:8]


def attention_forward(scalars, queries, blocks, places, before, own, last, after=()):
    rows, columns = queries[0].shape
    span, width = rows // 2, HEAD
    groups = columns // (2 * width)
    tile = pl.BlockSpec((rows, 2 * width), lambda g: (0, g))
    accum_block = (1, 2, 2, 2 * span, 2 * width)
    accum_spec = pl.BlockSpec(accum_block, lambda g: (g, 0, 0, 0, 0))
    args = [*scalars, *queries, *(in_hbm(block) for block in blocks)]
    specs = [pl.BlockSpec(memory_space=pltpu.SMEM)] * 2 + [tile] * (2 + len(blocks))
    if not own:
        args.append(before)
        specs.append(accum_spec)
    taken = len(args)
    more_args, more_specs = waits(after)
    scratch = []
    if last:
        wide, low = pltpu.HBM((rows, columns), F32), jax.ShapeDtypeStruct((rows, columns), BF)
        outs = [wide, wide, low, low, jax.ShapeDtypeStruct((groups, 2, 2, 8, 2 * span), F32), TOKEN]
        out_specs = [tile] * 4 + [
            pl.BlockSpec((1, 2, 2, 8, 2 * span), lambda g: (g, 0, 0, 0, 0)),
            pl.BlockSpec((8, 128), lambda g: (0, 0)),
        ]
        scratch = [pltpu.VMEM(accum_block, F32)]
    else:
        outs = [jax.ShapeDtypeStruct((groups, *accum_block[1:]), F32), TOKEN]
        out_specs = [accum_spec, pl.BlockSpec((8, 128), lambda g: (0, 0))]

    def kernel(*refs):
        refs = refs[:taken] + refs[taken + len(more_args) :]
        place = -2 if last else -1
        refs[place][...] = jnp.zeros_like(refs[place])
        refs = refs[:place] + (refs[-1:] if last else ())
        forward_kernel(places, own, last, span, width, *refs)

    return pl.pallas_call(
        kernel,
        out_shape=outs,
        grid=(groups,),
        in_specs=specs + more_specs,
        out_specs=out_specs,
        scratch_shapes=scratch,
        input_output_aliases={} if own or last else {taken - 1: 0},
        compiler_params=pltpu.CompilerParams(vmem_limit_bytes=VMEM_LIMIT),
        cost_estimate=FORWARD,
    )(*args, *more_args)


def delta_kernel(grads, outs, delta):
    for pair in range(2):
        grad, out = grads[pair], outs[pair]
        width, span = grad.shape[1] // 2, grad.shape[0] // 2
        for side in range(2):
            rows = slice(side * span, (side + 1) * span)
            product = grad[rows, :].astype(F32) * out[rows, :]
            stack = jnp.concatenate([product[:, :width], product[:, width:]], axis=0)
            total = jnp.sum(stack.T, axis=0, keepdims=True)
            delta[0, pair, side] = jnp.broadcast_to(total, (8, 2 * span))


def attention_delta(grads, outs, after=()):
    rows, columns = grads[0].shape
    width, span = HEAD, rows // 2
    groups = columns // (2 * width)
    tile = pl.BlockSpec((rows, 2 * width), lambda g: (0, g))
    more_args, more_specs = waits(after)

    def kernel(*refs):
        delta_kernel(refs[:2], refs[2:4], refs[-1])

    return pl.pallas_call(
        kernel,
        out_shape=jax.ShapeDtypeStruct((groups, 2, 2, 8, 2 * span), F32),
        grid=(groups,),
        in_specs=[tile] * 4 + more_specs,
        out_specs=pl.BlockSpec((1, 2, 2, 8, 2 * span), lambda g: (g, 0, 0, 0, 0)),
        compiler_params=pltpu.CompilerParams(vmem_limit_bytes=VMEM_LIMIT),
        cost_estimate=LIGHT,
    )(*grads, *outs, *more_args)


def backward_kernel(places, own, first, last, split, span, width, order, table, *refs):
    count = len(places)
    queries, grads, (logs, delta), refs = refs[:2], refs[2:4], refs[4:6], refs[6:]
    blocks, refs = refs[:count], refs[count:]
    if not first:
        before, refs = refs[0], refs[1:]
    outs = refs[: count if split else count // 2]
    refs = refs[len(outs) :]
    refs[0][...] = jnp.zeros_like(refs[0])
    refs = refs[1:]
    if last:
        query_outs, accum = refs[:2], refs[2]
    else:
        accum = refs[0]
    scale = LOG2E / math.sqrt(width)
    factor = 1.0 / math.sqrt(width)

    def products(rows, row_grads, log, mean, keys, values, allowed=None):
        probs = jnp.exp2(nt(keys, rows) * scale - log)
        if allowed is not None:
            probs = jnp.where(allowed, probs, 0.0)
        prob_grad = nt(values, row_grads)
        score_grad = (probs * (prob_grad - mean)).astype(BF)
        return nn(score_grad, rows), nn(probs.astype(BF), row_grads), tn(keys, score_grad)

    def of_pair(pair, side, start, keys, values, allowed=None):
        return products(
            stacked(queries[pair], start, span, width),
            stacked(grads[pair], start, span, width),
            logs[0, pair, side, :1],
            delta[0, pair, side, :1],
            keys,
            values,
            allowed,
        )

    low_keys, low_values, high_query = products(
        jnp.concatenate([stacked(query, span, span, width) for query in queries], axis=0),
        jnp.concatenate([stacked(grad, span, span, width) for grad in grads], axis=0),
        jnp.concatenate([logs[0, pair, 1, :1] for pair in range(2)], axis=1),
        jnp.concatenate([delta[0, pair, 1, :1] for pair in range(2)], axis=1),
        jnp.concatenate([block[:span, :width] for block in blocks], axis=0),
        jnp.concatenate([block[:span, width:] for block in blocks], axis=0),
    )
    for pair in range(2):
        part = high_query[:, pair * 2 * span : (pair + 1) * 2 * span]
        if first:
            accum[0, pair, 0] = jnp.zeros_like(part)
            accum[0, pair, 1] = part
        else:
            accum[0, pair, 0] = before[0, pair, 0]
            accum[0, pair, 1] = before[0, pair, 1] + part
    for i, (offset, other) in enumerate(places):
        here = slice(i * span, (i + 1) * span)
        block = blocks[i]
        key_sums, value_sums = [low_keys[here], 0.0], [low_values[here], 0.0]
        for pair in range(2):
            if own and i == pair:
                allowed = causal(span, True)
                for side in range(2):
                    rows = slice(side * span, (side + 1) * span)
                    key_part, value_part, query_part = of_pair(
                        pair, side, side * span, block[rows, :width], block[rows, width:], allowed
                    )
                    accum[0, pair, side] += query_part
                    key_sums[side] = key_sums[side] + key_part
                    value_sums[side] = value_sums[side] + value_part
                continue
            side = side_met(order, table, pair, offset, other)
            start = pl.multiple_of(side * span, span)
            rows = pl.ds(start, span)
            key_part, value_part, query_part = of_pair(
                pair, side, start, block[rows, :width], block[rows, width:]
            )
            accum[0, pair, side] += query_part
            low = side == 0
            key_sums[0] = key_sums[0] + jnp.where(low, key_part, 0.0)
            value_sums[0] = value_sums[0] + jnp.where(low, value_part, 0.0)
            key_sums[1] = key_sums[1] + jnp.where(low, 0.0, key_part)
            value_sums[1] = value_sums[1] + jnp.where(low, 0.0, value_part)
        out = outs[i] if split else outs[i // 2]
        base = 0 if split else i % 2 * 2 * span
        for side in range(2):
            rows = slice(base + side * span, base + (side + 1) * span)
            out[rows, :width] = (key_sums[side] * factor).astype(BF)
            out[rows, width:] = value_sums[side].astype(BF)
    if last:
        for pair in range(2):
            for side in range(2):
                part = accum[0, pair, side].T * factor
                rows = slice(side * span, (side + 1) * span)
                query_outs[pair][rows, :width] = part[:span]
                query_outs[pair][rows, width:] = part[span:]


def attention_backward(
    scalars, queries, grads, logs, delta, blocks, places, before, own, last, split, after=()
):
    rows, columns = queries[0].shape
    span, width = rows // 2, HEAD
    groups = columns // (2 * width)
    count = len(blocks)
    first = before is None
    tile = pl.BlockSpec((rows, 2 * width), lambda g: (0, g))
    stat = pl.BlockSpec((1, 2, 2, 8, 2 * span), lambda g: (g, 0, 0, 0, 0))
    accum_block = (1, 2, 2, width, 2 * span)
    accum_spec = pl.BlockSpec(accum_block, lambda g: (g, 0, 0, 0, 0))
    args = [*scalars, *queries, *grads, logs, delta, *(in_hbm(block) for block in blocks)]
    specs = [pl.BlockSpec(memory_space=pltpu.SMEM)] * 2 + [tile] * 4 + [stat] * 2 + [tile] * count
    if not first:
        args.append(before)
        specs.append(accum_spec)
    taken = len(args)
    more_args, more_specs = waits(after)
    if split:
        outs = [jax.ShapeDtypeStruct((rows, columns), BF)] * count
        out_specs = [tile] * count
    else:
        outs = [jax.ShapeDtypeStruct((2 * rows, columns), BF)] * (count // 2)
        out_specs = [pl.BlockSpec((2 * rows, 2 * width), lambda g: (0, g))] * (count // 2)
    outs.append(TOKEN)
    out_specs.append(pl.BlockSpec((8, 128), lambda g: (0, 0)))
    scratch = []
    if last:
        outs += [jax.ShapeDtypeStruct((rows, columns), F32)] * 2
        out_specs += [tile] * 2
        scratch = [pltpu.VMEM(accum_block, F32)]
    else:
        outs.append(jax.ShapeDtypeStruct((groups, *accum_block[1:]), F32))
        out_specs.append(accum_spec)

    def kernel(*refs):
        refs = refs[:taken] + refs[taken + len(more_args) :]
        backward_kernel(places, own, first, last, split, span, width, *refs)

    return pl.pallas_call(
        kernel,
        out_shape=outs,
        grid=(groups,),
        in_specs=specs + more_specs,
        out_specs=out_specs,
        scratch_shapes=scratch,
        input_output_aliases={} if first or last else {taken - 1: len(outs) - 1},
        compiler_params=pltpu.CompilerParams(vmem_limit_bytes=VMEM_LIMIT),
        cost_estimate=cost(HEAVY),
    )(*args, *more_args)


def body(
    devices,
    residual,
    cotangent,
    span_order,
    positions,
    attn_gain,
    query_weight,
    key_weight,
    value_weight,
    query_gain,
    key_gain,
    out_weight,
    mlp_gain,
    gate_weight,
    up_weight,
    down_weight,
):
    ring = Ring(devices)
    rows, model = residual.shape
    head_dim = query_gain.shape[0]
    span = rows // 2
    index = lax.axis_index("cp")
    scalars = [span_order, ring.table]
    table = [ring.table]
    residual_other, positions_other = ring.sibling(residual), ring.sibling(positions)

    half = head_dim // 2
    freq = ROPE_BASE ** (-(jnp.arange(half, dtype=F32) * 2.0) / head_dim)
    angles = []
    for where in (positions, positions_other):
        angle = where.astype(F32)[:, None] * freq[None, :]
        cosine, sine = jnp.cos(angle), jnp.sin(angle)
        angles.append(jnp.concatenate([cosine, cosine], axis=1))
        angles.append(jnp.concatenate([-sine, sine], axis=1))

    query_gain_row = query_gain.reshape(1, -1)
    key_gain_row = key_gain.reshape(1, -1)
    key_columns = key_weight.shape[1]
    query_columns = query_weight.shape[1]
    few, each = key_columns // 2, query_columns // 2

    def project_keys(order, table_ref, first, second, grad, gain, key, value, row, c0, s0, c1, s1, *outs):
        key_value_kernel(
            order, table_ref, (first, second), grad, gain, key, value, row, (c0, s0, c1, s1),
            (outs[0], outs[1], outs[2:4], outs[4:6], outs[6:8], outs[8:10], outs[10:12]),
        )

    residual, cotangent, *results = whole_call(
        project_keys,
        scalars,
        [((rows, model), BF, 1)] * 2
        + [((rows, model), BF)] * 2
        + [((rows, few), F32, 1)] * 2
        + [((rows, head_dim), F32)] * 4
        + [((rows, key_columns), BF)] * 2,
        [
            in_hbm(residual), residual_other, in_hbm(cotangent), in_hbm(attn_gain.reshape(1, -1)),
            (in_hbm(key_weight), (model, few), lambda core: (0, core)),
            (in_hbm(value_weight), (model, few), lambda core: (0, core)),
            in_hbm(key_gain_row), *angles,
        ],
    )
    normeds, keys_raw, cosines, sines, parts = (results[i : i + 2] for i in range(0, 10, 2))

    ways = [(ring.send_up(part), ring.send_down(part)) for part in parts]

    def project_queries(table_ref, n0, n1, weight, gain, c0, c1, s0, s1, *outs):
        query_kernel((n0, n1), weight, gain, (c0, c1), (s0, s1), outs[:2], outs[2:])

    *queries_raw, first, second = whole_call(
        project_queries,
        table,
        [((rows, each), F32, 1)] * 2 + [((rows, each), BF)] * 2,
        [
            *normeds, (in_hbm(query_weight), (model, each), lambda core: (0, core)),
            in_hbm(query_gain_row), *cosines, *sines,
        ],
    )
    queries = [first, second]

    def places_of(offsets):
        return [(offset, other) for offset in offsets for other in (False, True)]

    steps = ring.half
    calls = {0: ([0], parts)}
    state = None
    token = None
    for step in range(1, steps):
        come = []
        for which in range(2):
            up, down = ways[which]
            if step == 1 and which == 0:
                up, down, queries[0] = tie(up, down, queries[0])
            else:
                up, down, token = tie(up, down, token)
            come.append((up, down))
            if step < steps - 1:
                ways[which] = ring.send_up(up), ring.send_down(down)
            else:
                ways[which] = ring.send_down(down) if which else ring.send_up(up)
            if step == 1 and which == 0:
                state, token = attention_forward(
                    scalars, queries, parts, places_of([0]), None, True, False, come[0]
                )
        blocks = [come[0][0], come[1][0], come[0][1], come[1][1]]
        calls[step] = ([-step, step], blocks)
        state, token = attention_forward(
            scalars, queries, blocks, places_of([-step, step]), state, False, False, [token]
        )
    *ways, token = tie(*ways, token)
    calls[steps] = ([steps], ways)
    *attended, low_keep, low_give, logs, _ = attention_forward(
        scalars, queries, ways, places_of([steps]), state, False, True, [token]
    )
    low_other = ring.sibling(low_give)
    mixed_part = out_projection(ring.table, low_keep, out_weight, False)
    mixed_part = out_projection(ring.table, low_other, out_weight, True, mixed_part)
    mixed_part, cotangent = tie(mixed_part, cotangent)
    mixed_parts = [mixed_part[:span], mixed_part[span:]]
    mixed_others = [partner(part) for part in mixed_parts]
    cotangents = [cotangent, ring.sibling(cotangent)]
    hidden_grad = nt(cotangent, down_weight)
    mixed_others[0], hidden_grad, cotangents = tie(mixed_others[0], hidden_grad, cotangents)

    residual_wide = residual.astype(F32)

    def feed_forward(half, part, other, price):
        rows = slice(half * span, (half + 1) * span)
        mixed, low = add_and_norm(part, other, residual, half, mlp_gain.reshape(1, -1), price)
        gate = nn(low, gate_weight)
        upward = nn(low, up_weight)
        sigmoid_gate = jax.nn.sigmoid(gate)
        activated = gate * sigmoid_gate
        hidden = (activated * upward).astype(BF)
        gate_grad = (
            hidden_grad[rows] * upward * sigmoid_gate * (1.0 + gate * (1.0 - sigmoid_gate))
        ).astype(BF)
        up_grad = (hidden_grad[rows] * activated).astype(BF)
        back = (nt(gate_grad, gate_weight) + nt(up_grad, up_weight)).astype(BF)
        return (mixed, low, hidden, gate_grad, up_grad), back

    upper, upper_back = feed_forward(0, mixed_parts[0], mixed_others[0], 0)
    upper_back, mixed_others[1] = tie(upper_back, mixed_others[1])
    upper_other = partner(upper_back)
    lower, lower_back = feed_forward(1, mixed_parts[1], mixed_others[1], HEAVY)
    lower_other = partner(lower_back)
    mixed, normed_two_low, hidden_low, gate_grad_low, up_grad_low = (
        jnp.concatenate(pair, axis=0) for pair in zip(upper, lower)
    )
    normed_two, scale_two = norm_rows(mixed)

    units = gate_weight.shape[1]
    thirds = 2 * units // model
    chips = ring.chips
    gate_rows = model // 2 // chips
    down_rows = units // thirds // 2 // chips
    down_row = thirds * gate_rows
    out_row = down_row + thirds * down_rows
    packed_shape = (out_row + gate_rows, model)

    def shard_of(chip, core):
        return core * chips + chip

    def columns_of(start):
        moves, done = [], 0
        while done < units:
            tile, column = divmod(start + done, model)
            wide = min(model - column, units - done)
            moves.append(
                (
                    None,
                    slice(done, done + wide),
                    (tile * gate_rows, (tile + 1) * gate_rows),
                    slice(column, column + wide),
                )
            )
            done += wide
        return moves

    everything = slice(None)
    wide = Gradients(
        ring,
        *packed_shape,
        [
            ((model, units), (gate_rows, units), lambda c, k: (shard_of(c, k), 0), columns_of(0)),
            ((model, units), (gate_rows, units), lambda c, k: (shard_of(c, k), 0), columns_of(units)),
            (
                (thirds, units // thirds, model),
                (thirds, down_rows, model),
                lambda c, k: (0, shard_of(c, k), 0),
                [
                    (i, everything, (down_row + i * down_rows, down_row + (i + 1) * down_rows), everything)
                    for i in range(thirds)
                ],
            ),
            (
                (2 * each, model),
                (gate_rows, model),
                lambda c, k: (shard_of(c, k), 0),
                [(None, everything, (out_row, out_row + gate_rows), everything)],
            ),
        ],
    )
    both_grad_low = jnp.concatenate([gate_grad_low, up_grad_low], axis=1)
    packed, token = products(
        ring.table, [normed_two_low, ring.sibling(normed_two_low)],
        [both_grad_low, ring.sibling(both_grad_low)], chips, (down_row, model), 0, 0, None,
        [upper_back, lower_back],
    )
    wide.packs.append((0, in_hbm(packed)))
    packed, token = products(
        ring.table, [hidden_low, ring.sibling(hidden_low)], cotangents, chips,
        (thirds * down_rows, model), 0, 0, None, [token], thirds=thirds,
    )
    wide.packs.append((down_row, in_hbm(packed)))
    upper_other, lower_other, token = tie(upper_other, lower_other, token)

    normed_two_grad = jnp.concatenate(
        [both(upper_back, upper_other), both(lower_back, lower_other)], axis=0
    )
    mlp_gain_term = jnp.sum(normed_two_grad * normed_two, axis=0)
    mixed_grad = cotangent.astype(F32) + norm_back(
        normed_two_grad * mlp_gain, normed_two, scale_two
    )
    mixed_grad_low = mixed_grad.astype(BF)
    mixed_grads = [mixed_grad_low, ring.sibling(mixed_grad_low)]
    packed, token = products(
        ring.table, [low_keep, low_give], mixed_grads, chips, (gate_rows, model), 0, 0, None,
        [token], halved=False,
    )
    wide.packs.append((out_row, packed))
    wide_steps = wide.scatter([token])
    wide_way, token = next(wide_steps)
    grads = heads_products(ring.table, mixed_grads, out_weight, [token])
    delta = attention_delta(grads, attended)

    def backward(step, state, after):
        offsets, blocks = calls[step]
        last = step == 0
        return attention_backward(
            scalars, queries, grads, logs, delta, blocks, places_of(offsets), state,
            last, last, last or step == steps, after,
        )

    narrow_rows = query_rows = model // chips
    narrow_shape = (query_rows, each + 2 * few)

    def narrow_out(start, wide):
        return (
            (model, 2 * wide),
            (query_rows, wide),
            lambda c, k: (c, k),
            [(None, everything, (0, query_rows), slice(start, start + wide))],
        )

    narrow = Gradients(
        ring,
        narrow_rows,
        model,
        [
            narrow_out(0, each),
            narrow_out(each, few),
            narrow_out(each + few, few),
        ],
    )
    up, down, token, state = backward(steps, None, [])
    up, down = ring.send_up(up), ring.send_down(down)
    for step in range(steps - 1, 0, -1):
        if step == 1:
            layer_part = matmul(hidden_low, down_weight, [token])
            wide_way, layer_part, token = tie(wide_way, layer_part, token)
            layer_other = partner(layer_part)
        wide_way, wide_token = wide_steps.send((wide_way, [token]))
        back, front, token, state = backward(step, state, [wide_token])
        if step == 1:
            layer_other, token = tie(layer_other, token)
        up, down, token = pair_add([front, back], [up, down], step == steps - 1, [token])
        up, down = ring.send_up(up), ring.send_down(down)
    wide_shard, wide_token = wide_steps.send((wide_way, [token]))
    wide_steps = wide.gather(wide_shard)
    wide_way, wide_ready = next(wide_steps)
    *key_value_own, token, first, second = backward(0, state, [wide_token])

    def back_queries(table_ref, g0, g1, r0, r1, gain, c0, c1, s0, s1, *outs):
        query_back_kernel((g0, g1), (r0, r1), gain, (c0, c1), (s0, s1), *outs)

    query_grad_low, query_gain_term = whole_call(
        back_queries,
        table,
        [((2 * rows, each), BF), ((8, head_dim), F32)],
        [first, second, *map(in_hbm, [*queries_raw, query_gain_row, *cosines, *sines])],
    )
    packed, token = products(
        ring.table, normeds, [query_grad_low], chips, narrow_shape, 0, 0, None, halved=False,
    )

    def own_ready(ready):
        return [(offset, part, False) for offset, part in ready]

    def other_ready(ready):
        return [(offset, ring.sibling(part), True) for offset, part in ready]

    first_other = ring.sibling(wide_shard)
    up, down, first_other, token = tie(up, down, first_other, token)

    def back_keys(table_ref, o0, o1, up_ref, down_ref, r0, r1, gain, c0, c1, s0, s1, *outs):
        key_value_back_kernel(
            (o0, o1), up_ref, down_ref, (r0, r1), gain, (c0, c1), (s0, s1), *outs
        )

    key_value_grad, key_gain_term = whole_call(
        back_keys,
        table,
        [((2 * rows, 2 * few), BF), ((8, head_dim), F32)],
        [
            *key_value_own, up, down, *map(in_hbm, [*keys_raw, key_gain_row, *cosines, *sines]),
        ],
        after=[token],
    )
    packed, token = products(
        ring.table, normeds, [key_value_grad], chips, narrow_shape, 0, each, packed, halved=False,
    )
    narrow.packs = [(0, packed)]
    narrow_steps = narrow.scatter()
    narrow_way, token = next(narrow_steps)
    wide_way, token = tie(wide_way, token)
    wide_way, pair = wide_steps.send(wide_way)
    narrow_way, token = tie(narrow_way, token)
    narrow_way, token = narrow_steps.send((narrow_way, [token]))
    normed_own, normed_give, attn_gain_term = normed_products(
        ring.table, normeds, query_grad_low, key_value_grad, query_weight, key_weight, value_weight,
        [token],
    )

    def stacked_pair(ready, token, price=0):
        lot, token = stack([part for _, part in ready], [token], price)
        return (lot, [offset for offset, _ in ready]), token

    def fly(lots, token):
        flown = []
        for lot, offsets in lots:
            lot, token = tie(lot, token)
            other = ring.sibling(lot)
            flown.append((other, offsets))
        return flown, token

    def land(flown, results, token, price=0):
        for other, offsets in flown:
            other, token = tie(other, token)
            results = wide.unpack_stack(other, offsets, results, [token], price)
            token = results[-1]
        return results, token

    small = jnp.concatenate(
        [
            jnp.sum(attn_gain_term, axis=0) / attn_gain,
            0.5 * mlp_gain_term,
            jnp.sum(query_gain_term, axis=0),
            jnp.sum(key_gain_term, axis=0),
        ]
    )
    small_rows = 16
    small = jnp.pad(small, (0, small_rows * model - small.shape[0])).reshape(small_rows, model)
    small = small.astype(BF)
    small_other = partner(small)
    first_lot, token = stacked_pair(pair, attn_gain_term)
    narrow_way, normed_give, small_other, token = tie(narrow_way, normed_give, small_other, token)
    narrow_way, token = narrow_steps.send((narrow_way, [token]))
    ready = own_ready(wide_ready + pair) + [(0, first_other, True)]
    wide_way, pair = wide_steps.send(wide_way)
    normed_sibling = ring.sibling(normed_give)
    wide_results = wide.unpack(own_ready(pair), None, [token], HEAVY)
    normed_sibling, token = tie(normed_sibling, wide_results[-1])
    normed_part = both(normed_own, normed_sibling).astype(BF)
    lot, token = stacked_pair(pair, token)
    ready_lots = [lot, first_lot]
    narrow_way, normed_part, token = tie(narrow_way, normed_part, token)
    for step in range(steps - 3):
        narrow_way, token = narrow_steps.send((narrow_way, [token]))
        if step == 0:
            normed_other = partner(normed_part)
            wide_results = wide.unpack(ready, wide_results, [token], SOME + 1)
            token = wide_results[-1]
        if step < steps - 4:
            wide_way, pair = wide_steps.send(wide_way)
            wide_results = wide.unpack(own_ready(pair), wide_results, [token])
            lot, token = stacked_pair(pair, wide_results[-1])
            ready_lots.append(lot)
            wide_way, token = tie(wide_way, token)
    narrow_way, wide_way, normed_other, token = tie(narrow_way, wide_way, normed_other, token)
    wide_way, pair = wide_steps.send(wide_way)
    narrow_shard, token = narrow_steps.send((narrow_way, [token]))

    small = both(small, small_other)
    gathered = Gradients(ring, narrow_rows + small_rows, model, narrow.outs, small_rows)
    narrow_steps = gathered.gather(jnp.concatenate([narrow_shard, small.astype(BF)], axis=0), True)
    narrow_way, narrow_ready = next(narrow_steps)

    narrow_results = None
    for step in range(1, steps + 1):
        share = -(-len(ready_lots) // max(1, steps - step)) if step > 1 else 1
        lots, ready_lots = ready_lots[:share], ready_lots[share:]
        own = own_ready(narrow_ready)
        if step == 1:
            flown, token = fly(lots, token)
            wide_results = wide.unpack(own_ready(pair), wide_results, [token], HEAVY)
            lot, token = stacked_pair(pair, wide_results[-1])
            (last,), (flown, token) = flown, fly([lot], token)
            wide_results, token = land([last], wide_results, token, HEAVY)
            narrow_ready = [(offset, tie(part, token)[0]) for offset, part in narrow_ready]
            wide_results, token = land(flown, wide_results, token, HEAVY)
        else:
            flown, token = fly(lots, token)
            price = HEAVY
            if step == 2:
                wide_way, token = tie(wide_way, token)
                _, pair = wide_steps.send(wide_way)
                wide_results = wide.unpack(own_ready(pair), wide_results, [token], price)
                lot, token = stacked_pair(pair, wide_results[-1])
                ready_lots.append(lot)
                price = 0
            elif not lots:
                narrow_results = gathered.unpack(own, narrow_results, [token], price)
                token = narrow_results[-1]
                own = []
            wide_results, token = land(flown, wide_results, token, price)
            if step == steps - 1:
                layer_out, residual_grad, token = finish(
                    lax.dynamic_slice_in_dim(span_order, 2 * index, 2), residual, mixed, mixed_grad,
                    [normed_part, normed_other], [layer_part, layer_other], attn_gain.reshape(1, -1),
                    [token],
                )
        narrow_results = gathered.unpack(own + other_ready(narrow_ready), narrow_results, [token])
        narrow_way, token = tie(narrow_way, narrow_results[-1])
        if step < steps:
            narrow_way, narrow_ready = narrow_steps.send(narrow_way)
    _, narrow_ready = narrow_steps.send(narrow_way)
    narrow_results = gathered.unpack(own_ready(narrow_ready), narrow_results, [token])
    query_sum, key_sum, value_sum, small, _ = gathered.unpack(
        other_ready(narrow_ready), narrow_results
    )
    gate_sum, up_sum, down_sum, out_weight_sum, _, _ = wide_results
    small = small.reshape(-1)

    attn_gain_grad, mlp_gain_grad = small[:model], small[model : 2 * model]
    query_gain_grad = small[2 * model : 2 * model + head_dim]
    key_gain_grad = small[2 * model + head_dim : 2 * model + 2 * head_dim]
    return (
        layer_out,
        residual_grad,
        attn_gain_grad,
        query_sum,
        key_sum,
        value_sum,
        query_gain_grad,
        key_gain_grad,
        out_weight_sum,
        mlp_gain_grad,
        gate_sum,
        up_sum,
        down_sum.reshape(units, model),
    )


def solution(mesh):
    return jax.shard_map(
        functools.partial(body, mesh.shape["cp"]),
        mesh=mesh,
        in_specs=(
            P("cp", None),
            P("cp", None),
            P(),
            P("cp"),
            P(),
            P(None, "tp"),
            P(None, "tp"),
            P(None, "tp"),
            P(),
            P(),
            P("tp", None),
            P(),
            P(None, "tp"),
            P(None, "tp"),
            P("tp", None),
        ),
        out_specs=(
            P("cp", None),
            P("cp", None),
            P(),
            P(None, "tp"),
            P(None, "tp"),
            P(None, "tp"),
            P(),
            P(),
            P("tp", None),
            P(),
            P(None, "tp"),
            P(None, "tp"),
            P("tp", None),
        ),
        check_vma=False,
    )
```

```python
import functools
import math

import jax
import jax.numpy as jnp
from jax import lax
from jax.experimental import pallas as pl
from jax.experimental.pallas import tpu as pltpu
from jax.sharding import PartitionSpec as P

EPS = 1e-06
ROPE_BASE = 1000000.0
HEAD = 128
LOG2E = 1.4426950408889634
VMEM_LIMIT = 16 * 1024 * 1024


def cost(microseconds):
    return pl.CostEstimate(
        flops=1024 + int(microseconds * 1e9), bytes_accessed=1024, transcendentals=0
    )


LIGHT = cost(0)
FORWARD = cost(1)
HEAVY = 50
SOME = 5
LITTLE = 4
BF = jnp.bfloat16
F32 = jnp.float32
TOKEN = jax.ShapeDtypeStruct((8, 128), jnp.float32)


def nn(a, b):
    return lax.dot_general(a, b, (((1,), (0,)), ((), ())), preferred_element_type=F32)


def nt(a, b):
    return lax.dot_general(a, b, (((1,), (1,)), ((), ())), preferred_element_type=F32)


def tn(a, b):
    return lax.dot_general(a, b, (((0,), (0,)), ((), ())), preferred_element_type=F32)


def norm_rows(values):
    scale_rows = lax.rsqrt(jnp.mean(values * values, axis=-1, keepdims=True) + EPS)
    return (values * scale_rows, scale_rows)


def norm_back(grad_normed, normed, scale_rows):
    return scale_rows * (
        grad_normed - normed * jnp.mean(grad_normed * normed, axis=-1, keepdims=True)
    )


def tie(*values):
    return lax.optimization_barrier(values)


def waits(after):
    return list(after), [pl.BlockSpec(memory_space=pl.ANY)] * len(after)


def in_hbm(x):
    return pltpu.with_memory_space_constraint(x, pltpu.HBM)


def ring_order(chips):
    if chips % 8:
        return list(range(chips))
    rows, cols = 4, chips // 4
    if cols % 2 or cols < 4:
        path = list(range(cols))
    else:
        path = list(range(cols // 2)) + list(range(cols - 1, cols // 2 - 1, -1))
    walk = []
    for row in range(rows):
        across = range(1, cols) if row % 2 == 0 else range(cols - 1, 0, -1)
        walk += [(row, col) for col in across]
    walk = [(0, 0)] + walk + [(row, 0) for row in range(rows - 1, 0, -1)]
    return [row * cols + path[col] for row, col in walk]


class Ring:
    def __init__(self, devices):
        self.devices = devices
        self.chips = devices // 2
        order = ring_order(self.chips)
        self.order = order
        size = self.chips
        self.up = [
            (2 * order[i] + core, 2 * order[(i + 1) % size] + core)
            for i in range(size)
            for core in range(2)
        ]
        self.down = [(b, a) for a, b in self.up]
        self.swap = [(i, i ^ 1) for i in range(devices)]
        place = [0] * size
        for i, chip in enumerate(order):
            place[chip] = i
        index = lax.axis_index("cp")
        self.core = index % 2
        self.here = jnp.asarray(place, jnp.int32)[index // 2]
        self.half = size // 2
        table = [
            [order[(place[chip] + i) % size] for i in range(size)] + [core]
            for chip in range(size)
            for core in range(2)
        ]
        self.table = lax.dynamic_index_in_dim(
            jnp.asarray(table, jnp.int32), index, 0, keepdims=False
        )

    def send_up(self, x):
        return lax.ppermute(x, "cp", self.up)

    def send_down(self, x):
        return lax.ppermute(x, "cp", self.down)

    def sibling(self, x):
        return lax.ppermute(x, "cp", self.swap)


def products(
    table, lefts, rights, chips, packed, row, column, before, after=(), thirds=1, halved=True
):
    tokens = lefts[0].shape[0]
    high = lefts[0].shape[1] // thirds // (2 if halved else 1)
    rows = high // chips
    wide = rights[0].shape[1]
    tile = min(wide, 512 if wide <= 1024 and thirds == 1 else 1024)
    last = table.shape[0] - 1
    more_args, more_specs = waits(after)
    if before is not None:
        more_args, more_specs = [before] + more_args, [pl.BlockSpec(memory_space=pl.ANY)] + more_specs
    side = len(lefts)

    def kernel(table_ref, *refs):
        out, token, turned = refs[side + len(rights) + len(more_args) :]

        @pl.when(pl.program_id(1) == 0)
        def _():
            for i in range(side):
                turned[:, i * tokens : (i + 1) * tokens] = refs[i][...].T
            token[...] = jnp.zeros_like(token)

        total, start = 0.0, 0
        for right in refs[side : side + len(rights)]:
            stop = start + right.shape[0]
            total = total + nn(turned[:, start:stop], right[...])
            start = stop
        out[...] = total.reshape(chips, rows, tile).astype(BF)

    def left_place(j, i, t):
        return (0, 2 * j + t[last] if halved else j)

    across = packed[1] // tile

    def out_place(j, i, t):
        at = column // tile + i
        return (0, row // rows + j + at // across, at % across)

    shape = (chips, *packed)
    return pl.pallas_call(
        kernel,
        out_shape=[jax.ShapeDtypeStruct(shape, BF), TOKEN],
        grid_spec=pltpu.PrefetchScalarGridSpec(
            num_scalar_prefetch=1,
            grid=(thirds, wide // tile),
            in_specs=[pl.BlockSpec((tokens, high), left_place)] * side
            + [pl.BlockSpec((right.shape[0], tile), lambda j, i, t: (0, i)) for right in rights]
            + more_specs,
            out_specs=[
                pl.BlockSpec((chips, rows, tile), out_place),
                pl.BlockSpec((8, 128), lambda j, i, t: (0, 0)),
            ],
            scratch_shapes=[pltpu.VMEM((high, side * tokens), BF)],
        ),
        input_output_aliases={} if before is None else {1 + side + len(rights): 0},
        compiler_params=pltpu.CompilerParams(vmem_limit_bytes=VMEM_LIMIT),
        cost_estimate=LIGHT,
    )(table, *lefts, *rights, *more_args)


class Gradients:
    def __init__(self, ring, rows, columns, outs, added=0):
        self.ring, self.rows, self.columns, self.outs = ring, rows, columns, outs
        self.added = added
        self.cut = -(-rows // 32) * 16
        self.packs = []

    def shards(self, offsets, received, halves, after=()):
        ring, columns, rows, cut = self.ring, self.columns, self.rows, self.cut
        spans = [(0, cut), (cut, rows)]
        sides, count = len(offsets), len(self.packs)
        args, specs = [], []
        for offset in offsets:
            for _, pack in self.packs:
                args.append(pack)
                specs.append(
                    pl.BlockSpec(
                        (1, *pack.shape[1:]), lambda i, t, at=offset: (t[at % ring.chips], 0, 0)
                    )
                )
        args += received
        specs += [pl.BlockSpec(x.shape, lambda i, t: (0, 0)) for x in received]
        more_args, more_specs = waits(after)
        taken = len(args) + len(more_args)

        def kernel(table_ref, *refs):
            outs = refs[taken:]
            outs[-1][...] = jnp.zeros_like(outs[-1])
            gained = refs[sides * count : len(args)]
            for side in range(sides):
                for number, (row, pack) in enumerate(self.packs):
                    mine = refs[side * count + number]
                    stop = row + pack.shape[1]
                    if halves == "send":
                        for out, (start, end) in zip(outs, spans):
                            first, last = max(row, start), min(stop, end)
                            if first < last:
                                out[first - start : last - start] = mine[0, first - row : last - row]
                        continue
                    start, end = spans[side] if halves == "add" else (0, rows)
                    for first, last, more in (
                        (row, min(stop, start), False),
                        (max(row, start), min(stop, end), True),
                        (max(row, end), stop, False),
                    ):
                        if first < last:
                            part = mine[0, first - row : last - row]
                            if more:
                                part = part.astype(F32)
                                for got in gained if halves == "sum" else [gained[side]]:
                                    part = part + got[first - start : last - start].astype(F32)
                            outs[side][first:last] = part.astype(BF)

        highs = {"send": [cut, rows - cut], "sum": [rows]}.get(halves, [rows, rows])
        return pl.pallas_call(
            kernel,
            out_shape=[jax.ShapeDtypeStruct((high, columns), BF) for high in highs] + [TOKEN],
            grid_spec=pltpu.PrefetchScalarGridSpec(
                num_scalar_prefetch=1,
                grid=(1,),
                in_specs=specs + more_specs,
                out_specs=[pl.BlockSpec((high, columns), lambda i, t: (0, 0)) for high in highs]
                + [pl.BlockSpec((8, 128), lambda i, t: (0, 0))],
            ),
            compiler_params=pltpu.CompilerParams(vmem_limit_bytes=VMEM_LIMIT),
            cost_estimate=LIGHT,
        )(ring.table, *args, *more_args)

    def scatter(self, after=()):
        ring = self.ring
        up, down, token = self.shards([ring.half], [], "send", after)
        for step in range(ring.half - 1, -1, -1):
            (up, down), after = yield (ring.send_up(up), ring.send_down(down)), token
            if step:
                kind = "add" if step == ring.half - 1 else ""
                up, down, token = self.shards([step, -step], [up, down], kind, after)
        yield self.shards([0], [up, down], "sum", after)

    def gather(self, own, split=False):
        ring, cut = self.ring, self.cut
        up = down = own
        ready = [(0, own)]
        for step in range(1, ring.half):
            up, down = yield (ring.send_up(up), ring.send_down(down)), ready
            ready = [(-step, up), (step, down)]
        high, low = yield (ring.send_up(up[:cut]), ring.send_down(down[cut:])), ready
        if split:
            yield None, [(ring.half, high), (ring.half, low)]
        else:
            yield None, [(ring.half, jnp.concatenate([high, low], axis=0))]

    def unpack_stack(self, stack, offsets, before, after=(), price=0):
        return self.unpack(
            [(offset, stack, True) for offset in offsets], before, after, price, True
        )

    def unpack(self, ready, before, after=(), price=0, stacked=False):
        ring, outs, added = self.ring, self.outs, max(self.added, 8)
        count = len(ready)
        parts = [part if isinstance(part, tuple) else (part, None) for _, part, _ in ready]
        args = []
        for array, _ in parts:
            if not any(array is x for x in args):
                args.append(array)
        which = [next(j for j, x in enumerate(args) if x is array) for array, _ in parts]
        highs = [array.shape[-2] for array, _ in parts]
        places_of = [(offset, other) for offset, _, other in ready]

        def write(part, start, results):
            stop = start + part.shape[0]
            for out, (_, _, _, moves) in zip(results, outs):
                for lead, across, (first, last), columns in moves:
                    low, high = max(first, start), min(last, stop)
                    if low < high:
                        rows = slice(low - first, high - first)
                        where = (rows, across) if lead is None else (lead, rows, across)
                        out[where] = part[low - start : high - start, columns].astype(F32)

        def start_of(i):
            same = [j for j in range(i) if places_of[j] == places_of[i]]
            return sum(highs[j] for j in same)

        starts = [0] * count if stacked else [start_of(i) for i in range(count)]

        def kernel(table_ref, *refs):
            step = pl.program_id(0)

            def part_of(i):
                ref, at = refs[which[i]], parts[i][1]
                return ref if at is None else ref.at[at]

            results = refs[-len(outs) - 2 : -2]
            refs[-1][...] = jnp.zeros_like(refs[-1])
            total = refs[-2]

            @pl.when(step == 0)
            def _():
                total[...] = jnp.zeros_like(total) if before is None else refs[sum_place][...]

            if self.added and stacked:
                total[...] += refs[0][0, self.rows - added :].astype(F32)
            elif self.added:
                for i in range(count):
                    if starts[i] + highs[i] == self.rows:

                        @pl.when(step == i)
                        def _(i=i):
                            total[...] += part_of(i)[highs[i] - added :].astype(F32)

            if stacked:
                write(refs[0].at[0], 0, results)
                return
            for i in range(count):
                pl.when(step == i)(functools.partial(write, part_of(i), starts[i], results))

        def place(of_chip, i, table):
            chip, core = None, None
            for j, (offset, other) in enumerate(places_of):
                here = table[offset % ring.chips]
                mine = table[ring.chips]
                mine = 1 - mine if other else mine
                chip = here if chip is None else jnp.where(i == j, here, chip)
                core = mine if core is None else jnp.where(i == j, mine, core)
            return of_chip(chip, core)

        shapes, out_specs = [], []
        for shape, block, of_chip, _ in outs:
            shapes.append(pltpu.HBM(shape, F32))
            out_specs.append(pl.BlockSpec(block, functools.partial(place, of_chip)))
        shapes += [jax.ShapeDtypeStruct((added, self.columns), F32), TOKEN]
        out_specs.append(pl.BlockSpec((added, self.columns), lambda i, t: (0, 0)))
        out_specs.append(pl.BlockSpec((8, 128), lambda i, t: (0, 0)))
        if stacked:
            specs = [pl.BlockSpec((1, self.rows, self.columns), lambda i, t: (i, 0, 0))]
        else:
            specs = [pl.BlockSpec(x.shape, lambda i, t, n=x.ndim: (0,) * n) for x in args]
        aliases = {}
        if before is not None:
            aliases = {1 + len(args) + i: i for i in range(len(outs))}
            specs += [pl.BlockSpec(memory_space=pl.ANY)] * len(outs)
            args += [in_hbm(x) for x in before[: len(outs)]]
            sum_place = len(args)
            args.append(before[len(outs)])
            specs.append(pl.BlockSpec((added, self.columns), lambda i, t: (0, 0)))
        more_args, more_specs = waits(after)
        args += more_args
        specs += more_specs
        return list(
            pl.pallas_call(
                kernel,
                out_shape=shapes,
                grid_spec=pltpu.PrefetchScalarGridSpec(
                    num_scalar_prefetch=1, grid=(count,), in_specs=specs, out_specs=out_specs
                ),
                input_output_aliases=aliases,
                compiler_params=pltpu.CompilerParams(vmem_limit_bytes=VMEM_LIMIT),
                cost_estimate=cost(price),
            )(ring.table, *args)
        )


def stack(parts, after=(), price=0):
    rows, columns = parts[0].shape
    count = len(parts)
    more_args, more_specs = waits(after)

    def kernel(*refs):
        out, token = refs[-2:]
        token[...] = jnp.zeros_like(token)
        for i in range(count):

            @pl.when(pl.program_id(0) == i)
            def _(i=i):
                out[0] = refs[i][...]

    return pl.pallas_call(
        kernel,
        out_shape=[jax.ShapeDtypeStruct((count, rows, columns), parts[0].dtype), TOKEN],
        grid=(count,),
        in_specs=[pl.BlockSpec((rows, columns), lambda i: (0, 0))] * count + more_specs,
        out_specs=[
            pl.BlockSpec((1, rows, columns), lambda i: (i, 0, 0)),
            pl.BlockSpec((8, 128), lambda i: (0, 0)),
        ],
        compiler_params=pltpu.CompilerParams(vmem_limit_bytes=VMEM_LIMIT),
        cost_estimate=cost(price),
    )(*parts, *more_args)


def pair_add(own, received, half, after=()):
    more_args, more_specs = waits(after)

    def kernel(*refs):
        refs, outs = refs[:4], refs[4 + len(more_args) :]
        outs[-1][...] = jnp.zeros_like(outs[-1])
        for side in range(2):
            mine, got, out = refs[side], refs[2 + side], outs[side]
            if half:
                rows = got.shape[0]
                here = slice(side * rows, (side + 1) * rows)
                rest = slice((1 - side) * rows, (2 - side) * rows)
                out[here] = (mine[here].astype(F32) + got[...].astype(F32)).astype(BF)
                out[rest] = mine[rest]
            else:
                out[...] = (mine[...].astype(F32) + got[...].astype(F32)).astype(BF)

    shape = jax.ShapeDtypeStruct(own[0].shape, BF)
    return pl.pallas_call(
        kernel,
        out_shape=[shape, shape, TOKEN],
        in_specs=[pl.BlockSpec(memory_space=pltpu.VMEM)] * 4 + more_specs,
        compiler_params=pltpu.CompilerParams(vmem_limit_bytes=VMEM_LIMIT),
        cost_estimate=LIGHT,
    )(*own, *received, *more_args)


def partner(x):
    return lax.ppermute(x, "tp", [(0, 1), (1, 0)])


def both(mine, other):
    return mine.astype(F32) + other.astype(F32)


def turn(values, cosine, sine):
    return values * cosine + pltpu.roll(values, values.shape[-1] // 2, 1) * sine


def turn_back(values, cosine, sine):
    return values * cosine - pltpu.roll(values, values.shape[-1] // 2, 1) * sine


def lower_first(order, table, other):
    core = table[table.shape[0] - 1]
    device = 2 * table[0] + (1 - core if other else core)
    return order[2 * device] < order[2 * device + 1]


def key_value_kernel(
    order, table, residuals, cotangent, gain, key_weight, value_weight, key_gain, angles, outs
):
    residual_out, cotangent_out, normed_outs, raw_outs, cosine_outs, sine_outs, packed_outs = outs
    width = key_gain.shape[1]
    span = residuals[0].shape[0] // 2
    for pair in range(2):
        start = jnp.where(lower_first(order, table, pair == 1), 0, span)

        def canonical(ref):
            return jnp.concatenate(
                [
                    ref[pl.ds(pl.multiple_of(start, span), span)],
                    ref[pl.ds(pl.multiple_of(span - start, span), span)],
                ],
                axis=0,
            )

        rows = canonical(residuals[pair])
        if pair == 0:
            residual_out[...] = rows
            cotangent_out[...] = canonical(cotangent)
        unit, _ = norm_rows(rows.astype(F32))
        normed = (unit * gain[...]).astype(BF)
        normed_outs[pair][...] = normed
        cosine, sine = canonical(angles[2 * pair]), canonical(angles[2 * pair + 1])
        cosine_outs[pair][...], sine_outs[pair][...] = cosine, sine
        raw = nn(normed, key_weight[...])
        raw_outs[pair][...] = raw
        values = nn(normed, value_weight[...]).astype(BF)
        for group in range(raw.shape[1] // width):
            here = slice(group * width, (group + 1) * width)
            key_unit, _ = norm_rows(raw[:, here])
            packed = packed_outs[pair]
            packed[:, 2 * group * width : (2 * group + 1) * width] = turn(
                key_unit * key_gain[...], cosine, sine
            ).astype(BF)
            packed[:, (2 * group + 1) * width : (2 * group + 2) * width] = values[:, here]


def query_kernel(normeds, weight, gain, cosines, sines, raw_outs, low_outs):
    width = gain.shape[1]
    for pair in range(2):
        raw = nn(normeds[pair][...], weight[...])
        raw_outs[pair][...] = raw
        for head in range(raw.shape[1] // width):
            here = slice(head * width, (head + 1) * width)
            unit, _ = norm_rows(raw[:, here])
            low_outs[pair][:, here] = turn(
                unit * gain[...], cosines[pair][...], sines[pair][...]
            ).astype(BF)


def heads_back(grad_of, raws, gain, cosines, sines, out, total):
    width = gain.shape[1]
    rows = raws[0].shape[0]
    for pair in range(2):
        here_rows = slice(pair * rows, (pair + 1) * rows)
        for head in range(raws[pair].shape[1] // width):
            here = slice(head * width, (head + 1) * width)
            unit, scale_rows = norm_rows(raws[pair][:, here])
            turned = turn_back(grad_of(pair, head), cosines[pair][...], sines[pair][...])
            total = total + jnp.sum((turned * unit).reshape(-1, 8, width), axis=0)
            out[here_rows, here] = norm_back(turned * gain[...], unit, scale_rows).astype(BF)
    return total


def query_back_kernel(grads, raws, gain, cosines, sines, low_out, gain_out):
    width = gain.shape[1]
    gain_out[...] = heads_back(
        lambda pair, head: grads[pair][:, head * width : (head + 1) * width],
        raws, gain, cosines, sines, low_out, jnp.zeros((8, width), F32),
    )


def key_value_back_kernel(owns, upward, downward, raws, gain, cosines, sines, low_out, gain_out):
    width = gain.shape[1]
    rows, columns = raws[0].shape
    groups = columns // width

    def summed(pair, place):
        here = slice(place * width, (place + 1) * width)
        at = slice(pair * rows, (pair + 1) * rows)
        return (
            owns[pair][:, here].astype(F32)
            + upward[at, here].astype(F32)
            + downward[at, here].astype(F32)
        )

    gain_out[...] = heads_back(
        lambda pair, head: summed(pair, 2 * head),
        raws, gain, cosines, sines, low_out, jnp.zeros((8, width), F32),
    )
    for pair in range(2):
        for group in range(groups):
            low_out[
                pair * rows : (pair + 1) * rows,
                columns + group * width : columns + (group + 1) * width,
            ] = summed(pair, 2 * group + 1).astype(BF)


def whole_call(kernel, scalars, outs, args, after=()):
    more_args, more_specs = waits(after)
    count = len(scalars)
    arrays, specs = [], []
    for arg in args:
        array, block, place = arg if isinstance(arg, tuple) else (arg, arg.shape, None)
        arrays.append(array)
        if place is None:
            specs.append(pl.BlockSpec(block, lambda i, *t: (0, 0)))
        else:
            specs.append(
                pl.BlockSpec(
                    block, lambda i, *t, place=place: place(t[-1][t[-1].shape[0] - 1])
                )
            )
    taken = count + len(args)

    def run(*refs):
        kernel(*refs[:taken], *refs[taken + len(more_args) :])

    return list(
        pl.pallas_call(
            run,
            out_shape=[
                pltpu.HBM(shape, dtype) if far else jax.ShapeDtypeStruct(shape, dtype)
                for shape, dtype, *far in outs
            ],
            grid_spec=pltpu.PrefetchScalarGridSpec(
                num_scalar_prefetch=count,
                grid=(1,),
                in_specs=specs + more_specs,
                out_specs=[pl.BlockSpec(shape, lambda i, *t: (0, 0)) for shape, *_ in outs],
            ),
            compiler_params=pltpu.CompilerParams(vmem_limit_bytes=VMEM_LIMIT),
            cost_estimate=LIGHT,
        )(*scalars, *arrays, *more_args)
    )


def matmul(left, right, after=(), price=0):
    rows, inner = left.shape
    columns = right.shape[1]
    tile = min(columns, 512)
    more_args, more_specs = waits(after)

    def kernel(left_ref, right_ref, *refs):
        refs[-1][...] = nn(left_ref[...], right_ref[...]).astype(BF)

    return pl.pallas_call(
        kernel,
        out_shape=jax.ShapeDtypeStruct((rows, columns), BF),
        grid=(columns // tile,),
        in_specs=[
            pl.BlockSpec((rows, inner), lambda i: (0, 0)),
            pl.BlockSpec((inner, tile), lambda i: (0, i)),
        ]
        + more_specs,
        out_specs=pl.BlockSpec((rows, tile), lambda i: (0, i)),
        compiler_params=pltpu.CompilerParams(vmem_limit_bytes=VMEM_LIMIT),
        cost_estimate=cost(price),
    )(left, in_hbm(right), *more_args)


def add_and_norm(part, other, residual, half, gain, price=0):
    rows, columns = part.shape

    def kernel(part_ref, other_ref, residual_ref, gain_ref, total, low):
        both_parts = part_ref[...].astype(F32) + other_ref[...].astype(F32)
        mixed = residual_ref[...].astype(F32) + both_parts
        total[...] = mixed
        normed, _ = norm_rows(mixed)
        low[...] = (normed * gain_ref[...]).astype(BF)

    whole = pl.BlockSpec((rows, columns), lambda i: (0, 0))
    return pl.pallas_call(
        kernel,
        out_shape=[
            jax.ShapeDtypeStruct((rows, columns), F32),
            jax.ShapeDtypeStruct((rows, columns), BF),
        ],
        grid=(1,),
        in_specs=[
            whole,
            whole,
            pl.BlockSpec((rows, columns), lambda i: (half, 0)),
            pl.BlockSpec((1, columns), lambda i: (0, 0)),
        ],
        out_specs=[whole, whole],
        compiler_params=pltpu.CompilerParams(vmem_limit_bytes=VMEM_LIMIT),
        cost_estimate=cost(price),
    )(part, other, residual, gain)


def finish(order, residual, mixed, mixed_grad, normed_parts, layer_parts, gain, after):
    rows, columns = residual.shape
    span = rows // 2
    more_args, more_specs = waits(after)

    def kernel(order_ref, row, mix, mix_grad, normed0, normed1, layer0, layer1, gain_ref, *refs):
        out, grad, token = refs[-3:]
        out[...] = (mix[...] + both(layer0[...], layer1[...])).astype(BF)
        normed, scale = norm_rows(row[...].astype(F32))
        normed_grad = both(normed0[...], normed1[...]) * gain_ref[...]
        grad[...] = mix_grad[...] + norm_back(normed_grad, normed, scale)
        token[...] = jnp.zeros_like(token)

    part = pl.BlockSpec((span, columns), lambda i, o: (i, 0))
    placed = pl.BlockSpec((span, columns), lambda i, o: (jnp.where(o[0] < o[1], i, 1 - i), 0))
    return pl.pallas_call(
        kernel,
        out_shape=[
            jax.ShapeDtypeStruct((rows, columns), BF),
            jax.ShapeDtypeStruct((rows, columns), F32),
            TOKEN,
        ],
        grid_spec=pltpu.PrefetchScalarGridSpec(
            num_scalar_prefetch=1,
            grid=(2,),
            in_specs=[part] * 7 + [pl.BlockSpec((1, columns), lambda i, o: (0, 0))] + more_specs,
            out_specs=[placed, placed, pl.BlockSpec(TOKEN.shape, lambda i, o: (0, 0))],
        ),
        compiler_params=pltpu.CompilerParams(vmem_limit_bytes=VMEM_LIMIT),
        cost_estimate=LIGHT,
    )(order, residual, mixed, mixed_grad, *normed_parts, *layer_parts, gain, *more_args)


def out_projection(table, rows, weight, other, before=None):
    high, inner = rows.shape
    columns = weight.shape[1]
    tile = min(inner, 256)
    count = inner // tile
    last = table.shape[0] - 1
    dtype = F32 if before is None else BF

    def kernel(table_ref, rows_ref, weight_ref, *refs):
        out, total = refs[-2:]
        step = pl.program_id(0)
        part = nn(rows_ref[...], weight_ref[...])

        @pl.when(step == 0)
        def _():
            total[...] = part if before is None else part + refs[0][...]

        @pl.when(step > 0)
        def _():
            total[...] += part

        @pl.when(step == count - 1)
        def _():
            out[...] = total[...].astype(dtype)

    whole = pl.BlockSpec((high, columns), lambda i, t: (0, 0))
    extra = [] if before is None else [before]
    return pl.pallas_call(
        kernel,
        out_shape=jax.ShapeDtypeStruct((high, columns), dtype),
        grid_spec=pltpu.PrefetchScalarGridSpec(
            num_scalar_prefetch=1,
            grid=(count,),
            in_specs=[
                pl.BlockSpec((high, tile), lambda i, t: (0, i)),
                pl.BlockSpec(
                    (tile, columns),
                    lambda i, t: ((1 - t[last] if other else t[last]) * count + i, 0),
                ),
            ]
            + [whole] * len(extra),
            out_specs=whole,
            scratch_shapes=[pltpu.VMEM((high, columns), F32)],
        ),
        compiler_params=pltpu.CompilerParams(vmem_limit_bytes=VMEM_LIMIT),
        cost_estimate=LIGHT,
    )(table, rows, weight, *extra)


def heads_products(table, rows, weight, after=()):
    high, columns = rows[0].shape
    inner = weight.shape[0] // 2
    tile = min(inner, 256)
    count = inner // tile
    last = table.shape[0] - 1
    more_args, more_specs = waits(after)

    def kernel(table_ref, first, second, mine, *refs):
        refs[-2][...] = nt(first[...], mine[...]).astype(BF)
        refs[-1][...] = nt(second[...], mine[...]).astype(BF)

    shape = jax.ShapeDtypeStruct((high, inner), BF)
    spec = pl.BlockSpec((high, tile), lambda i, t: (0, i))
    whole = pl.BlockSpec((high, columns), lambda i, t: (0, 0))
    return pl.pallas_call(
        kernel,
        out_shape=[shape, shape],
        grid_spec=pltpu.PrefetchScalarGridSpec(
            num_scalar_prefetch=1,
            grid=(count,),
            in_specs=[
                whole,
                whole,
                pl.BlockSpec((tile, columns), lambda i, t: (t[last] * count + i, 0)),
            ]
            + more_specs,
            out_specs=[spec, spec],
        ),
        compiler_params=pltpu.CompilerParams(vmem_limit_bytes=VMEM_LIMIT),
        cost_estimate=LIGHT,
    )(table, *rows, in_hbm(weight), *more_args)


def normed_products(
    table, normeds, query_grad, key_value_grad, query_weight, key_weight, value_weight, after=()
):
    rows, wide = query_grad.shape
    narrow = key_value_grad.shape[1] // 2
    columns = query_weight.shape[0]
    tile = min(columns, 256)
    last = table.shape[0] - 1
    more_args, more_specs = waits(after)

    def kernel(table_ref, first, second, queries, others, query, key, value, *refs):
        total = (
            nt(queries[...], query[...])
            + nt(others[:, :narrow], key[...])
            + nt(others[:, narrow:], value[...])
        ).astype(BF)
        upper, lower = total[: rows // 2], total[rows // 2 :]
        refs[-3][...] = upper
        refs[-2][...] = lower
        term = upper.astype(F32) * first[...].astype(F32) + lower.astype(F32) * second[...].astype(F32)
        refs[-1][...] = jnp.sum(term.reshape(-1, 8, tile), axis=0)

    shape = jax.ShapeDtypeStruct((rows // 2, columns), BF)
    spec = pl.BlockSpec((rows // 2, tile), lambda i, t: (0, i))
    return pl.pallas_call(
        kernel,
        out_shape=[shape, shape, jax.ShapeDtypeStruct((8, columns), F32)],
        grid_spec=pltpu.PrefetchScalarGridSpec(
            num_scalar_prefetch=1,
            grid=(columns // tile,),
            in_specs=[
                spec,
                spec,
                pl.BlockSpec((rows, wide), lambda i, t: (0, 0)),
                pl.BlockSpec((rows, 2 * narrow), lambda i, t: (0, 0)),
                pl.BlockSpec((tile, wide), lambda i, t: (i, t[last])),
                pl.BlockSpec((tile, narrow), lambda i, t: (i, t[last])),
                pl.BlockSpec((tile, narrow), lambda i, t: (i, t[last])),
            ]
            + more_specs,
            out_specs=[spec, spec, pl.BlockSpec((8, tile), lambda i, t: (0, i))],
        ),
        compiler_params=pltpu.CompilerParams(vmem_limit_bytes=VMEM_LIMIT),
        cost_estimate=cost(HEAVY),
    )(
        table, *normeds, query_grad, key_value_grad, in_hbm(query_weight), in_hbm(key_weight),
        in_hbm(value_weight), *more_args,
    )


def stacked(ref, start, span, width):
    rows = pl.ds(start, span)
    return jnp.concatenate([ref[rows, :width], ref[rows, width:]], axis=0)


def causal(span, transposed):
    shape = (span, 2 * span) if transposed else (2 * span, span)
    key = lax.broadcasted_iota(jnp.int32, shape, 0 if transposed else 1)
    row = lax.broadcasted_iota(jnp.int32, shape, 1 if transposed else 0)
    return key <= row % span


def side_met(order, table, pair, offset, other):
    last = table.shape[0] - 1
    core = table[last]

    def lower(device):
        return jnp.minimum(order[2 * device], order[2 * device + 1])

    mine = lower(2 * table[0] + (1 - core if pair else core))
    theirs = lower(2 * table[offset % last] + (1 - core if other else core))
    return jnp.where(theirs < mine, 0, 1)


def forward_kernel(places, own, last, span, width, order, table, *refs):
    count = len(places)
    queries, blocks, refs = refs[:2], refs[2 : 2 + count], refs[2 + count :]
    scale = LOG2E / math.sqrt(width)
    if own:
        before, outs = None, refs
    else:
        before, outs = refs[0], refs[1:]
    accum = outs[-1]
    ones = jnp.ones((span, width), BF)

    def weighted(rows, keys, values, allowed=None):
        scores = nt(rows, keys)
        probs = jnp.exp2(scores * scale)
        if allowed is not None:
            probs = jnp.where(allowed, probs, 0.0)
        return nn(probs.astype(BF), values)

    def extended(block, start):
        return jnp.concatenate([block[pl.ds(start, span), width:], ones], axis=1)

    keys = jnp.concatenate([block[:span, :width] for block in blocks], axis=0)
    values = jnp.concatenate([extended(block, 0) for block in blocks], axis=0)
    rows = jnp.concatenate([stacked(query, span, span, width) for query in queries], axis=0)
    high = weighted(rows, keys, values)
    for pair in range(2):
        part = high[pair * 2 * span : (pair + 1) * 2 * span]
        if own:
            allowed = causal(span, False)
            for side in range(2):
                block, start = blocks[pair], side * span
                met = weighted(
                    stacked(queries[pair], start, span, width),
                    block[start : start + span, :width],
                    extended(block, start),
                    allowed,
                )
                accum[0, pair, side] = met + part if side else met
        else:
            accum[0, pair, 0] = before[0, pair, 0]
            accum[0, pair, 1] = before[0, pair, 1] + part
    for i, (offset, other) in enumerate(places):
        for pair in range(2):
            if own and i == pair:
                continue
            side = side_met(order, table, pair, offset, other)
            start = pl.multiple_of(side * span, span)
            accum[0, pair, side] += weighted(
                stacked(queries[pair], start, span, width),
                blocks[i][pl.ds(start, span), :width],
                extended(blocks[i], start),
            )
    if last:
        wides, lows, logs = outs[0:2], outs[2:4], outs[4]
        for pair in range(2):
            for side in range(2):
                rows = slice(side * span, (side + 1) * span)
                whole = accum[0, pair, side]
                mass = whole[:, width:]
                out = whole[:, :width] / mass
                for head in range(2):
                    part = out[head * span : (head + 1) * span]
                    columns = slice(head * width, (head + 1) * width)
                    wides[pair][rows, columns] = part
                    lows[pair][rows, columns] = part.astype(BF)
                logs[0, pair, side] = jnp.log2(mass).T[:8]


def attention_forward(scalars, queries, blocks, places, before, own, last, after=()):
    rows, columns = queries[0].shape
    span, width = rows // 2, HEAD
    groups = columns // (2 * width)
    tile = pl.BlockSpec((rows, 2 * width), lambda g: (0, g))
    accum_block = (1, 2, 2, 2 * span, 2 * width)
    accum_spec = pl.BlockSpec(accum_block, lambda g: (g, 0, 0, 0, 0))
    args = [*scalars, *queries, *(in_hbm(block) for block in blocks)]
    specs = [pl.BlockSpec(memory_space=pltpu.SMEM)] * 2 + [tile] * (2 + len(blocks))
    if not own:
        args.append(before)
        specs.append(accum_spec)
    taken = len(args)
    more_args, more_specs = waits(after)
    scratch = []
    if last:
        wide, low = pltpu.HBM((rows, columns), F32), jax.ShapeDtypeStruct((rows, columns), BF)
        outs = [wide, wide, low, low, jax.ShapeDtypeStruct((groups, 2, 2, 8, 2 * span), F32), TOKEN]
        out_specs = [tile] * 4 + [
            pl.BlockSpec((1, 2, 2, 8, 2 * span), lambda g: (g, 0, 0, 0, 0)),
            pl.BlockSpec((8, 128), lambda g: (0, 0)),
        ]
        scratch = [pltpu.VMEM(accum_block, F32)]
    else:
        outs = [jax.ShapeDtypeStruct((groups, *accum_block[1:]), F32), TOKEN]
        out_specs = [accum_spec, pl.BlockSpec((8, 128), lambda g: (0, 0))]

    def kernel(*refs):
        refs = refs[:taken] + refs[taken + len(more_args) :]
        place = -2 if last else -1
        refs[place][...] = jnp.zeros_like(refs[place])
        refs = refs[:place] + (refs[-1:] if last else ())
        forward_kernel(places, own, last, span, width, *refs)

    return pl.pallas_call(
        kernel,
        out_shape=outs,
        grid=(groups,),
        in_specs=specs + more_specs,
        out_specs=out_specs,
        scratch_shapes=scratch,
        input_output_aliases={} if own or last else {taken - 1: 0},
        compiler_params=pltpu.CompilerParams(vmem_limit_bytes=VMEM_LIMIT),
        cost_estimate=FORWARD,
    )(*args, *more_args)


def delta_kernel(grads, outs, delta):
    for pair in range(2):
        grad, out = grads[pair], outs[pair]
        width, span = grad.shape[1] // 2, grad.shape[0] // 2
        for side in range(2):
            rows = slice(side * span, (side + 1) * span)
            product = grad[rows, :].astype(F32) * out[rows, :]
            stack = jnp.concatenate([product[:, :width], product[:, width:]], axis=0)
            total = jnp.sum(stack.T, axis=0, keepdims=True)
            delta[0, pair, side] = jnp.broadcast_to(total, (8, 2 * span))


def attention_delta(grads, outs, after=()):
    rows, columns = grads[0].shape
    width, span = HEAD, rows // 2
    groups = columns // (2 * width)
    tile = pl.BlockSpec((rows, 2 * width), lambda g: (0, g))
    more_args, more_specs = waits(after)

    def kernel(*refs):
        delta_kernel(refs[:2], refs[2:4], refs[-1])

    return pl.pallas_call(
        kernel,
        out_shape=jax.ShapeDtypeStruct((groups, 2, 2, 8, 2 * span), F32),
        grid=(groups,),
        in_specs=[tile] * 4 + more_specs,
        out_specs=pl.BlockSpec((1, 2, 2, 8, 2 * span), lambda g: (g, 0, 0, 0, 0)),
        compiler_params=pltpu.CompilerParams(vmem_limit_bytes=VMEM_LIMIT),
        cost_estimate=LIGHT,
    )(*grads, *outs, *more_args)


def backward_kernel(places, own, first, last, split, span, width, order, table, *refs):
    count = len(places)
    queries, grads, (logs, delta), refs = refs[:2], refs[2:4], refs[4:6], refs[6:]
    blocks, refs = refs[:count], refs[count:]
    if not first:
        before, refs = refs[0], refs[1:]
    outs = refs[: count if split else count // 2]
    refs = refs[len(outs) :]
    refs[0][...] = jnp.zeros_like(refs[0])
    refs = refs[1:]
    if last:
        query_outs, accum = refs[:2], refs[2]
    else:
        accum = refs[0]
    scale = LOG2E / math.sqrt(width)
    factor = 1.0 / math.sqrt(width)

    def products(rows, row_grads, log, mean, keys, values, allowed=None):
        probs = jnp.exp2(nt(keys, rows) * scale - log)
        if allowed is not None:
            probs = jnp.where(allowed, probs, 0.0)
        prob_grad = nt(values, row_grads)
        score_grad = (probs * (prob_grad - mean)).astype(BF)
        return nn(score_grad, rows), nn(probs.astype(BF), row_grads), tn(keys, score_grad)

    def of_pair(pair, side, start, keys, values, allowed=None):
        return products(
            stacked(queries[pair], start, span, width),
            stacked(grads[pair], start, span, width),
            logs[0, pair, side, :1],
            delta[0, pair, side, :1],
            keys,
            values,
            allowed,
        )

    low_keys, low_values, high_query = products(
        jnp.concatenate([stacked(query, span, span, width) for query in queries], axis=0),
        jnp.concatenate([stacked(grad, span, span, width) for grad in grads], axis=0),
        jnp.concatenate([logs[0, pair, 1, :1] for pair in range(2)], axis=1),
        jnp.concatenate([delta[0, pair, 1, :1] for pair in range(2)], axis=1),
        jnp.concatenate([block[:span, :width] for block in blocks], axis=0),
        jnp.concatenate([block[:span, width:] for block in blocks], axis=0),
    )
    for pair in range(2):
        part = high_query[:, pair * 2 * span : (pair + 1) * 2 * span]
        if first:
            accum[0, pair, 0] = jnp.zeros_like(part)
            accum[0, pair, 1] = part
        else:
            accum[0, pair, 0] = before[0, pair, 0]
            accum[0, pair, 1] = before[0, pair, 1] + part
    for i, (offset, other) in enumerate(places):
        here = slice(i * span, (i + 1) * span)
        block = blocks[i]
        key_sums, value_sums = [low_keys[here], 0.0], [low_values[here], 0.0]
        for pair in range(2):
            if own and i == pair:
                allowed = causal(span, True)
                for side in range(2):
                    rows = slice(side * span, (side + 1) * span)
                    key_part, value_part, query_part = of_pair(
                        pair, side, side * span, block[rows, :width], block[rows, width:], allowed
                    )
                    accum[0, pair, side] += query_part
                    key_sums[side] = key_sums[side] + key_part
                    value_sums[side] = value_sums[side] + value_part
                continue
            side = side_met(order, table, pair, offset, other)
            start = pl.multiple_of(side * span, span)
            rows = pl.ds(start, span)
            key_part, value_part, query_part = of_pair(
                pair, side, start, block[rows, :width], block[rows, width:]
            )
            accum[0, pair, side] += query_part
            low = side == 0
            key_sums[0] = key_sums[0] + jnp.where(low, key_part, 0.0)
            value_sums[0] = value_sums[0] + jnp.where(low, value_part, 0.0)
            key_sums[1] = key_sums[1] + jnp.where(low, 0.0, key_part)
            value_sums[1] = value_sums[1] + jnp.where(low, 0.0, value_part)
        out = outs[i] if split else outs[i // 2]
        base = 0 if split else i % 2 * 2 * span
        for side in range(2):
            rows = slice(base + side * span, base + (side + 1) * span)
            out[rows, :width] = (key_sums[side] * factor).astype(BF)
            out[rows, width:] = value_sums[side].astype(BF)
    if last:
        for pair in range(2):
            for side in range(2):
                part = accum[0, pair, side].T * factor
                rows = slice(side * span, (side + 1) * span)
                query_outs[pair][rows, :width] = part[:span]
                query_outs[pair][rows, width:] = part[span:]


def attention_backward(
    scalars, queries, grads, logs, delta, blocks, places, before, own, last, split, after=()
):
    rows, columns = queries[0].shape
    span, width = rows // 2, HEAD
    groups = columns // (2 * width)
    count = len(blocks)
    first = before is None
    tile = pl.BlockSpec((rows, 2 * width), lambda g: (0, g))
    stat = pl.BlockSpec((1, 2, 2, 8, 2 * span), lambda g: (g, 0, 0, 0, 0))
    accum_block = (1, 2, 2, width, 2 * span)
    accum_spec = pl.BlockSpec(accum_block, lambda g: (g, 0, 0, 0, 0))
    args = [*scalars, *queries, *grads, logs, delta, *(in_hbm(block) for block in blocks)]
    specs = [pl.BlockSpec(memory_space=pltpu.SMEM)] * 2 + [tile] * 4 + [stat] * 2 + [tile] * count
    if not first:
        args.append(before)
        specs.append(accum_spec)
    taken = len(args)
    more_args, more_specs = waits(after)
    if split:
        outs = [jax.ShapeDtypeStruct((rows, columns), BF)] * count
        out_specs = [tile] * count
    else:
        outs = [jax.ShapeDtypeStruct((2 * rows, columns), BF)] * (count // 2)
        out_specs = [pl.BlockSpec((2 * rows, 2 * width), lambda g: (0, g))] * (count // 2)
    outs.append(TOKEN)
    out_specs.append(pl.BlockSpec((8, 128), lambda g: (0, 0)))
    scratch = []
    if last:
        outs += [jax.ShapeDtypeStruct((rows, columns), F32)] * 2
        out_specs += [tile] * 2
        scratch = [pltpu.VMEM(accum_block, F32)]
    else:
        outs.append(jax.ShapeDtypeStruct((groups, *accum_block[1:]), F32))
        out_specs.append(accum_spec)

    def kernel(*refs):
        refs = refs[:taken] + refs[taken + len(more_args) :]
        backward_kernel(places, own, first, last, split, span, width, *refs)

    return pl.pallas_call(
        kernel,
        out_shape=outs,
        grid=(groups,),
        in_specs=specs + more_specs,
        out_specs=out_specs,
        scratch_shapes=scratch,
        input_output_aliases={} if first or last else {taken - 1: len(outs) - 1},
        compiler_params=pltpu.CompilerParams(vmem_limit_bytes=VMEM_LIMIT),
        cost_estimate=cost(HEAVY),
    )(*args, *more_args)


def body(
    devices,
    residual,
    cotangent,
    span_order,
    positions,
    attn_gain,
    query_weight,
    key_weight,
    value_weight,
    query_gain,
    key_gain,
    out_weight,
    mlp_gain,
    gate_weight,
    up_weight,
    down_weight,
):
    ring = Ring(devices)
    rows, model = residual.shape
    head_dim = query_gain.shape[0]
    span = rows // 2
    index = lax.axis_index("cp")
    scalars = [span_order, ring.table]
    table = [ring.table]
    residual_other, positions_other = ring.sibling(residual), ring.sibling(positions)

    half = head_dim // 2
    freq = ROPE_BASE ** (-(jnp.arange(half, dtype=F32) * 2.0) / head_dim)
    angles = []
    for where in (positions, positions_other):
        angle = where.astype(F32)[:, None] * freq[None, :]
        cosine, sine = jnp.cos(angle), jnp.sin(angle)
        angles.append(jnp.concatenate([cosine, cosine], axis=1))
        angles.append(jnp.concatenate([-sine, sine], axis=1))

    query_gain_row = query_gain.reshape(1, -1)
    key_gain_row = key_gain.reshape(1, -1)
    key_columns = key_weight.shape[1]
    query_columns = query_weight.shape[1]
    few, each = key_columns // 2, query_columns // 2

    def project_keys(order, table_ref, first, second, grad, gain, key, value, row, c0, s0, c1, s1, *outs):
        key_value_kernel(
            order, table_ref, (first, second), grad, gain, key, value, row, (c0, s0, c1, s1),
            (outs[0], outs[1], outs[2:4], outs[4:6], outs[6:8], outs[8:10], outs[10:12]),
        )

    residual, cotangent, *results = whole_call(
        project_keys,
        scalars,
        [((rows, model), BF, 1)] * 2
        + [((rows, model), BF)] * 2
        + [((rows, few), F32, 1)] * 2
        + [((rows, head_dim), F32)] * 4
        + [((rows, key_columns), BF)] * 2,
        [
            in_hbm(residual), residual_other, in_hbm(cotangent), in_hbm(attn_gain.reshape(1, -1)),
            (in_hbm(key_weight), (model, few), lambda core: (0, core)),
            (in_hbm(value_weight), (model, few), lambda core: (0, core)),
            in_hbm(key_gain_row), *angles,
        ],
    )
    normeds, keys_raw, cosines, sines, parts = (results[i : i + 2] for i in range(0, 10, 2))

    ways = [(ring.send_up(part), ring.send_down(part)) for part in parts]

    def project_queries(table_ref, n0, n1, weight, gain, c0, c1, s0, s1, *outs):
        query_kernel((n0, n1), weight, gain, (c0, c1), (s0, s1), outs[:2], outs[2:])

    *queries_raw, first, second = whole_call(
        project_queries,
        table,
        [((rows, each), F32, 1)] * 2 + [((rows, each), BF)] * 2,
        [
            *normeds, (in_hbm(query_weight), (model, each), lambda core: (0, core)),
            in_hbm(query_gain_row), *cosines, *sines,
        ],
    )
    queries = [first, second]

    def places_of(offsets):
        return [(offset, other) for offset in offsets for other in (False, True)]

    steps = ring.half
    calls = {0: ([0], parts)}
    state = None
    token = None
    for step in range(1, steps):
        come = []
        for which in range(2):
            up, down = ways[which]
            if step == 1 and which == 0:
                up, down, queries[0] = tie(up, down, queries[0])
            else:
                up, down, token = tie(up, down, token)
            come.append((up, down))
            if step < steps - 1:
                ways[which] = ring.send_up(up), ring.send_down(down)
            else:
                ways[which] = ring.send_down(down) if which else ring.send_up(up)
            if step == 1 and which == 0:
                state, token = attention_forward(
                    scalars, queries, parts, places_of([0]), None, True, False, come[0]
                )
        blocks = [come[0][0], come[1][0], come[0][1], come[1][1]]
        calls[step] = ([-step, step], blocks)
        state, token = attention_forward(
            scalars, queries, blocks, places_of([-step, step]), state, False, False, [token]
        )
    *ways, token = tie(*ways, token)
    calls[steps] = ([steps], ways)
    *attended, low_keep, low_give, logs, _ = attention_forward(
        scalars, queries, ways, places_of([steps]), state, False, True, [token]
    )
    low_other = ring.sibling(low_give)
    mixed_part = out_projection(ring.table, low_keep, out_weight, False)
    mixed_part = out_projection(ring.table, low_other, out_weight, True, mixed_part)
    mixed_part, cotangent = tie(mixed_part, cotangent)
    mixed_parts = [mixed_part[:span], mixed_part[span:]]
    mixed_others = [partner(part) for part in mixed_parts]
    cotangents = [cotangent, ring.sibling(cotangent)]
    hidden_grad = nt(cotangent, down_weight)
    mixed_others[0], hidden_grad, cotangents = tie(mixed_others[0], hidden_grad, cotangents)

    residual_wide = residual.astype(F32)

    def feed_forward(half, part, other, price):
        rows = slice(half * span, (half + 1) * span)
        mixed, low = add_and_norm(part, other, residual, half, mlp_gain.reshape(1, -1), price)
        gate = nn(low, gate_weight)
        upward = nn(low, up_weight)
        sigmoid_gate = jax.nn.sigmoid(gate)
        activated = gate * sigmoid_gate
        hidden = (activated * upward).astype(BF)
        gate_grad = (
            hidden_grad[rows] * upward * sigmoid_gate * (1.0 + gate * (1.0 - sigmoid_gate))
        ).astype(BF)
        up_grad = (hidden_grad[rows] * activated).astype(BF)
        back = (nt(gate_grad, gate_weight) + nt(up_grad, up_weight)).astype(BF)
        return (mixed, low, hidden, gate_grad, up_grad), back

    upper, upper_back = feed_forward(0, mixed_parts[0], mixed_others[0], 0)
    upper_back, mixed_others[1] = tie(upper_back, mixed_others[1])
    upper_other = partner(upper_back)
    lower, lower_back = feed_forward(1, mixed_parts[1], mixed_others[1], HEAVY)
    lower_other = partner(lower_back)
    mixed, normed_two_low, hidden_low, gate_grad_low, up_grad_low = (
        jnp.concatenate(pair, axis=0) for pair in zip(upper, lower)
    )
    normed_two, scale_two = norm_rows(mixed)

    units = gate_weight.shape[1]
    thirds = 2 * units // model
    chips = ring.chips
    gate_rows = model // 2 // chips
    down_rows = units // thirds // 2 // chips
    down_row = thirds * gate_rows
    out_row = down_row + thirds * down_rows
    packed_shape = (out_row + gate_rows, model)

    def shard_of(chip, core):
        return core * chips + chip

    def columns_of(start):
        moves, done = [], 0
        while done < units:
            tile, column = divmod(start + done, model)
            wide = min(model - column, units - done)
            moves.append(
                (
                    None,
                    slice(done, done + wide),
                    (tile * gate_rows, (tile + 1) * gate_rows),
                    slice(column, column + wide),
                )
            )
            done += wide
        return moves

    everything = slice(None)
    wide = Gradients(
        ring,
        *packed_shape,
        [
            ((model, units), (gate_rows, units), lambda c, k: (shard_of(c, k), 0), columns_of(0)),
            ((model, units), (gate_rows, units), lambda c, k: (shard_of(c, k), 0), columns_of(units)),
            (
                (thirds, units // thirds, model),
                (thirds, down_rows, model),
                lambda c, k: (0, shard_of(c, k), 0),
                [
                    (i, everything, (down_row + i * down_rows, down_row + (i + 1) * down_rows), everything)
                    for i in range(thirds)
                ],
            ),
            (
                (2 * each, model),
                (gate_rows, model),
                lambda c, k: (shard_of(c, k), 0),
                [(None, everything, (out_row, out_row + gate_rows), everything)],
            ),
        ],
    )
    both_grad_low = jnp.concatenate([gate_grad_low, up_grad_low], axis=1)
    packed, token = products(
        ring.table, [normed_two_low, ring.sibling(normed_two_low)],
        [both_grad_low, ring.sibling(both_grad_low)], chips, (down_row, model), 0, 0, None,
        [upper_back, lower_back],
    )
    wide.packs.append((0, in_hbm(packed)))
    packed, token = products(
        ring.table, [hidden_low, ring.sibling(hidden_low)], cotangents, chips,
        (thirds * down_rows, model), 0, 0, None, [token], thirds=thirds,
    )
    wide.packs.append((down_row, in_hbm(packed)))
    upper_other, lower_other, token = tie(upper_other, lower_other, token)

    normed_two_grad = jnp.concatenate(
        [both(upper_back, upper_other), both(lower_back, lower_other)], axis=0
    )
    mlp_gain_term = jnp.sum(normed_two_grad * normed_two, axis=0)
    mixed_grad = cotangent.astype(F32) + norm_back(
        normed_two_grad * mlp_gain, normed_two, scale_two
    )
    mixed_grad_low = mixed_grad.astype(BF)
    mixed_grads = [mixed_grad_low, ring.sibling(mixed_grad_low)]
    packed, token = products(
        ring.table, [low_keep, low_give], mixed_grads, chips, (gate_rows, model), 0, 0, None,
        [token], halved=False,
    )
    wide.packs.append((out_row, packed))
    wide_steps = wide.scatter([token])
    wide_way, token = next(wide_steps)
    grads = heads_products(ring.table, mixed_grads, out_weight, [token])
    delta = attention_delta(grads, attended)

    def backward(step, state, after):
        offsets, blocks = calls[step]
        last = step == 0
        return attention_backward(
            scalars, queries, grads, logs, delta, blocks, places_of(offsets), state,
            last, last, last or step == steps, after,
        )

    narrow_rows = query_rows = model // chips
    narrow_shape = (query_rows, each + 2 * few)

    def narrow_out(start, wide):
        return (
            (model, 2 * wide),
            (query_rows, wide),
            lambda c, k: (c, k),
            [(None, everything, (0, query_rows), slice(start, start + wide))],
        )

    narrow = Gradients(
        ring,
        narrow_rows,
        model,
        [
            narrow_out(0, each),
            narrow_out(each, few),
            narrow_out(each + few, few),
        ],
    )
    up, down, token, state = backward(steps, None, [])
    up, down = ring.send_up(up), ring.send_down(down)
    for step in range(steps - 1, 0, -1):
        if step == 1:
            layer_part = matmul(hidden_low, down_weight, [token])
            wide_way, layer_part, token = tie(wide_way, layer_part, token)
            layer_other = partner(layer_part)
        wide_way, wide_token = wide_steps.send((wide_way, [token]))
        back, front, token, state = backward(step, state, [wide_token])
        if step == 1:
            layer_other, token = tie(layer_other, token)
        up, down, token = pair_add([front, back], [up, down], step == steps - 1, [token])
        up, down = ring.send_up(up), ring.send_down(down)
    wide_shard, wide_token = wide_steps.send((wide_way, [token]))
    wide_steps = wide.gather(wide_shard)
    wide_way, wide_ready = next(wide_steps)
    *key_value_own, token, first, second = backward(0, state, [wide_token])

    def back_queries(table_ref, g0, g1, r0, r1, gain, c0, c1, s0, s1, *outs):
        query_back_kernel((g0, g1), (r0, r1), gain, (c0, c1), (s0, s1), *outs)

    query_grad_low, query_gain_term = whole_call(
        back_queries,
        table,
        [((2 * rows, each), BF), ((8, head_dim), F32)],
        [first, second, *map(in_hbm, [*queries_raw, query_gain_row, *cosines, *sines])],
    )
    packed, token = products(
        ring.table, normeds, [query_grad_low], chips, narrow_shape, 0, 0, None, halved=False,
    )

    def own_ready(ready):
        return [(offset, part, False) for offset, part in ready]

    def other_ready(ready):
        return [(offset, ring.sibling(part), True) for offset, part in ready]

    first_other = ring.sibling(wide_shard)
    up, down, first_other, token = tie(up, down, first_other, token)

    def back_keys(table_ref, o0, o1, up_ref, down_ref, r0, r1, gain, c0, c1, s0, s1, *outs):
        key_value_back_kernel(
            (o0, o1), up_ref, down_ref, (r0, r1), gain, (c0, c1), (s0, s1), *outs
        )

    key_value_grad, key_gain_term = whole_call(
        back_keys,
        table,
        [((2 * rows, 2 * few), BF), ((8, head_dim), F32)],
        [
            *key_value_own, up, down, *map(in_hbm, [*keys_raw, key_gain_row, *cosines, *sines]),
        ],
        after=[token],
    )
    packed, token = products(
        ring.table, normeds, [key_value_grad], chips, narrow_shape, 0, each, packed, halved=False,
    )
    narrow.packs = [(0, packed)]
    narrow_steps = narrow.scatter()
    narrow_way, token = next(narrow_steps)
    wide_way, token = tie(wide_way, token)
    wide_way, pair = wide_steps.send(wide_way)
    narrow_way, token = tie(narrow_way, token)
    narrow_way, token = narrow_steps.send((narrow_way, [token]))

    def stacked_pair(ready, token, price=0):
        lot, token = stack([part for _, part in ready], [token], price)
        return (lot, [offset for offset, _ in ready]), token

    def fly(lots, token):
        flown = []
        for lot, offsets in lots:
            lot, token = tie(lot, token)
            other = ring.sibling(lot)
            flown.append((other, offsets))
        return flown, token

    def land(flown, results, token, price=0):
        for other, offsets in flown:
            other, token = tie(other, token)
            results = wide.unpack_stack(other, offsets, results, [token], price)
            token = results[-1]
        return results, token

    lot, token = stacked_pair(pair, token)
    flown, token = fly([lot], token)
    normed_own, normed_give, attn_gain_term = normed_products(
        ring.table, normeds, query_grad_low, key_value_grad, query_weight, key_weight, value_weight,
        [token],
    )
    wide_results, token = land(flown, None, attn_gain_term)
    small = jnp.concatenate(
        [
            jnp.sum(attn_gain_term, axis=0) / attn_gain,
            0.5 * mlp_gain_term,
            jnp.sum(query_gain_term, axis=0),
            jnp.sum(key_gain_term, axis=0),
        ]
    )
    small_rows = 16
    small = jnp.pad(small, (0, small_rows * model - small.shape[0])).reshape(small_rows, model)
    small = small.astype(BF)
    small_other = partner(small)
    narrow_way, normed_give, small_other, token = tie(narrow_way, normed_give, small_other, token)
    narrow_way, token = narrow_steps.send((narrow_way, [token]))
    ready = own_ready(wide_ready + pair) + [(0, first_other, True)]
    wide_way, pair = wide_steps.send(wide_way)
    normed_sibling = ring.sibling(normed_give)
    wide_results = wide.unpack(own_ready(pair), wide_results, [token], HEAVY)
    normed_sibling, token = tie(normed_sibling, wide_results[-1])
    normed_part = both(normed_own, normed_sibling).astype(BF)
    normed_part, token = tie(normed_part, token)
    lot, token = stacked_pair(pair, token, 2)
    ready_lots = [lot]
    normed_other = partner(normed_part)
    narrow_way, token = tie(narrow_way, token)
    for step in range(steps - 3):
        narrow_way, token = narrow_steps.send((narrow_way, [token]))
        if step == 0:
            wide_results = wide.unpack(ready, wide_results, [token], LITTLE)
            token = wide_results[-1]
        if step < steps - 4:
            wide_way, pair = wide_steps.send(wide_way)
            wide_results = wide.unpack(own_ready(pair), wide_results, [token])
            lot, token = stacked_pair(pair, wide_results[-1])
            ready_lots.append(lot)
            wide_way, token = tie(wide_way, token)
    narrow_way, wide_way, normed_other, token = tie(narrow_way, wide_way, normed_other, token)
    wide_way, pair = wide_steps.send(wide_way)
    narrow_shard, token = narrow_steps.send((narrow_way, [token]))

    small = both(small, small_other)
    gathered = Gradients(ring, narrow_rows + small_rows, model, narrow.outs, small_rows)
    narrow_steps = gathered.gather(jnp.concatenate([narrow_shard, small.astype(BF)], axis=0), True)
    narrow_way, narrow_ready = next(narrow_steps)

    narrow_results = None
    for step in range(1, steps + 1):
        share = -(-len(ready_lots) // max(1, steps - step)) if step > 1 else 1
        lots, ready_lots = ready_lots[:share], ready_lots[share:]
        own = own_ready(narrow_ready)
        if step == 1:
            flown, token = fly(lots, token)
            wide_results = wide.unpack(own_ready(pair), wide_results, [token], HEAVY)
            lot, token = stacked_pair(pair, wide_results[-1])
            ready_lots.append(lot)
            narrow_ready = [(offset, tie(part, token)[0]) for offset, part in narrow_ready]
            wide_results, token = land(flown, wide_results, token, HEAVY)
        else:
            flown, token = fly(lots, token)
            price = HEAVY
            if step == 2:
                wide_way, token = tie(wide_way, token)
                _, pair = wide_steps.send(wide_way)
                wide_results = wide.unpack(own_ready(pair), wide_results, [token], price)
                lot, token = stacked_pair(pair, wide_results[-1])
                ready_lots.append(lot)
                price = 0
            elif not lots:
                narrow_results = gathered.unpack(own, narrow_results, [token], price)
                token = narrow_results[-1]
                own = []
            wide_results, token = land(flown, wide_results, token, price)
            if step == steps - 1:
                layer_out, residual_grad, token = finish(
                    lax.dynamic_slice_in_dim(span_order, 2 * index, 2), residual, mixed, mixed_grad,
                    [normed_part, normed_other], [layer_part, layer_other], attn_gain.reshape(1, -1),
                    [token],
                )
        narrow_results = gathered.unpack(own + other_ready(narrow_ready), narrow_results, [token])
        narrow_way, token = tie(narrow_way, narrow_results[-1])
        if step < steps:
            narrow_way, narrow_ready = narrow_steps.send(narrow_way)
    _, narrow_ready = narrow_steps.send(narrow_way)
    narrow_results = gathered.unpack(own_ready(narrow_ready), narrow_results, [token])
    query_sum, key_sum, value_sum, small, _ = gathered.unpack(
        other_ready(narrow_ready), narrow_results
    )
    gate_sum, up_sum, down_sum, out_weight_sum, _, _ = wide_results
    small = small.reshape(-1)

    attn_gain_grad, mlp_gain_grad = small[:model], small[model : 2 * model]
    query_gain_grad = small[2 * model : 2 * model + head_dim]
    key_gain_grad = small[2 * model + head_dim : 2 * model + 2 * head_dim]
    return (
        layer_out,
        residual_grad,
        attn_gain_grad,
        query_sum,
        key_sum,
        value_sum,
        query_gain_grad,
        key_gain_grad,
        out_weight_sum,
        mlp_gain_grad,
        gate_sum,
        up_sum,
        down_sum.reshape(units, model),
    )


def solution(mesh):
    return jax.shard_map(
        functools.partial(body, mesh.shape["cp"]),
        mesh=mesh,
        in_specs=(
            P("cp", None),
            P("cp", None),
            P(),
            P("cp"),
            P(),
            P(None, "tp"),
            P(None, "tp"),
            P(None, "tp"),
            P(),
            P(),
            P("tp", None),
            P(),
            P(None, "tp"),
            P(None, "tp"),
            P("tp", None),
        ),
        out_specs=(
            P("cp", None),
            P("cp", None),
            P(),
            P(None, "tp"),
            P(None, "tp"),
            P(None, "tp"),
            P(),
            P(),
            P("tp", None),
            P(),
            P(None, "tp"),
            P(None, "tp"),
            P("tp", None),
        ),
        check_vma=False,
    )
```

```python
import functools
import math

import jax
import jax.numpy as jnp
from jax import lax
from jax.experimental import pallas as pl
from jax.experimental.pallas import tpu as pltpu
from jax.sharding import PartitionSpec as P

EPS = 1e-06
ROPE_BASE = 1000000.0
HEAD = 128
LOG2E = 1.4426950408889634
VMEM_LIMIT = 16 * 1024 * 1024


def cost(microseconds):
    return pl.CostEstimate(
        flops=1024 + int(microseconds * 1e9), bytes_accessed=1024, transcendentals=0
    )


LIGHT = cost(0)
FORWARD = cost(1)
HEAVY = 50
SOME = 5
LITTLE = 4
BF = jnp.bfloat16
F32 = jnp.float32
TOKEN = jax.ShapeDtypeStruct((8, 128), jnp.float32)


def nn(a, b):
    return lax.dot_general(a, b, (((1,), (0,)), ((), ())), preferred_element_type=F32)


def nt(a, b):
    return lax.dot_general(a, b, (((1,), (1,)), ((), ())), preferred_element_type=F32)


def tn(a, b):
    return lax.dot_general(a, b, (((0,), (0,)), ((), ())), preferred_element_type=F32)


def norm_rows(values):
    scale_rows = lax.rsqrt(jnp.mean(values * values, axis=-1, keepdims=True) + EPS)
    return (values * scale_rows, scale_rows)


def norm_back(grad_normed, normed, scale_rows):
    return scale_rows * (
        grad_normed - normed * jnp.mean(grad_normed * normed, axis=-1, keepdims=True)
    )


def tie(*values):
    return lax.optimization_barrier(values)


def waits(after):
    return list(after), [pl.BlockSpec(memory_space=pl.ANY)] * len(after)


def in_hbm(x):
    return pltpu.with_memory_space_constraint(x, pltpu.HBM)


def ring_order(chips):
    if chips % 8:
        return list(range(chips))
    rows, cols = 4, chips // 4
    if cols % 2 or cols < 4:
        path = list(range(cols))
    else:
        path = list(range(cols // 2)) + list(range(cols - 1, cols // 2 - 1, -1))
    walk = []
    for row in range(rows):
        across = range(1, cols) if row % 2 == 0 else range(cols - 1, 0, -1)
        walk += [(row, col) for col in across]
    walk = [(0, 0)] + walk + [(row, 0) for row in range(rows - 1, 0, -1)]
    return [row * cols + path[col] for row, col in walk]


class Ring:
    def __init__(self, devices):
        self.devices = devices
        self.chips = devices // 2
        order = ring_order(self.chips)
        self.order = order
        size = self.chips
        self.up = [
            (2 * order[i] + core, 2 * order[(i + 1) % size] + core)
            for i in range(size)
            for core in range(2)
        ]
        self.down = [(b, a) for a, b in self.up]
        self.swap = [(i, i ^ 1) for i in range(devices)]
        place = [0] * size
        for i, chip in enumerate(order):
            place[chip] = i
        index = lax.axis_index("cp")
        self.core = index % 2
        self.here = jnp.asarray(place, jnp.int32)[index // 2]
        self.half = size // 2
        table = [
            [order[(place[chip] + i) % size] for i in range(size)] + [core]
            for chip in range(size)
            for core in range(2)
        ]
        self.table = lax.dynamic_index_in_dim(
            jnp.asarray(table, jnp.int32), index, 0, keepdims=False
        )

    def send_up(self, x):
        return lax.ppermute(x, "cp", self.up)

    def send_down(self, x):
        return lax.ppermute(x, "cp", self.down)

    def sibling(self, x):
        return lax.ppermute(x, "cp", self.swap)


def products(
    table, lefts, rights, chips, packed, row, column, before, after=(), thirds=1, halved=True, price=0
):
    tokens = lefts[0].shape[0]
    high = lefts[0].shape[1] // thirds // (2 if halved else 1)
    rows = high // chips
    wide = rights[0].shape[1]
    tile = min(wide, 512 if wide <= 1024 and thirds == 1 else 1024)
    last = table.shape[0] - 1
    more_args, more_specs = waits(after)
    if before is not None:
        more_args, more_specs = [before] + more_args, [pl.BlockSpec(memory_space=pl.ANY)] + more_specs
    side = len(lefts)

    def kernel(table_ref, *refs):
        out, token, turned = refs[side + len(rights) + len(more_args) :]

        @pl.when(pl.program_id(1) == 0)
        def _():
            for i in range(side):
                turned[:, i * tokens : (i + 1) * tokens] = refs[i][...].T
            token[...] = jnp.zeros_like(token)

        total, start = 0.0, 0
        for right in refs[side : side + len(rights)]:
            stop = start + right.shape[0]
            total = total + nn(turned[:, start:stop], right[...])
            start = stop
        out[...] = total.reshape(chips, rows, tile).astype(BF)

    def left_place(j, i, t):
        return (0, 2 * j + t[last] if halved else j)

    across = packed[1] // tile

    def out_place(j, i, t):
        at = column // tile + i
        return (0, row // rows + j + at // across, at % across)

    shape = (chips, *packed)
    return pl.pallas_call(
        kernel,
        out_shape=[jax.ShapeDtypeStruct(shape, BF), TOKEN],
        grid_spec=pltpu.PrefetchScalarGridSpec(
            num_scalar_prefetch=1,
            grid=(thirds, wide // tile),
            in_specs=[pl.BlockSpec((tokens, high), left_place)] * side
            + [pl.BlockSpec((right.shape[0], tile), lambda j, i, t: (0, i)) for right in rights]
            + more_specs,
            out_specs=[
                pl.BlockSpec((chips, rows, tile), out_place),
                pl.BlockSpec((8, 128), lambda j, i, t: (0, 0)),
            ],
            scratch_shapes=[pltpu.VMEM((high, side * tokens), BF)],
        ),
        input_output_aliases={} if before is None else {1 + side + len(rights): 0},
        compiler_params=pltpu.CompilerParams(vmem_limit_bytes=VMEM_LIMIT),
        cost_estimate=cost(price),
    )(table, *lefts, *rights, *more_args)


class Gradients:
    def __init__(self, ring, rows, columns, outs, added=0):
        self.ring, self.rows, self.columns, self.outs = ring, rows, columns, outs
        self.added = added
        self.cut = -(-rows // 32) * 16
        self.packs = []

    def shards(self, offsets, received, halves, after=()):
        ring, columns, rows, cut = self.ring, self.columns, self.rows, self.cut
        spans = [(0, cut), (cut, rows)]
        sides, count = len(offsets), len(self.packs)
        args, specs = [], []
        for offset in offsets:
            for _, pack in self.packs:
                args.append(pack)
                specs.append(
                    pl.BlockSpec(
                        (1, *pack.shape[1:]), lambda i, t, at=offset: (t[at % ring.chips], 0, 0)
                    )
                )
        args += received
        specs += [pl.BlockSpec(x.shape, lambda i, t: (0, 0)) for x in received]
        more_args, more_specs = waits(after)
        taken = len(args) + len(more_args)

        def kernel(table_ref, *refs):
            outs = refs[taken:]
            outs[-1][...] = jnp.zeros_like(outs[-1])
            gained = refs[sides * count : len(args)]
            for side in range(sides):
                for number, (row, pack) in enumerate(self.packs):
                    mine = refs[side * count + number]
                    stop = row + pack.shape[1]
                    if halves == "send":
                        for out, (start, end) in zip(outs, spans):
                            first, last = max(row, start), min(stop, end)
                            if first < last:
                                out[first - start : last - start] = mine[0, first - row : last - row]
                        continue
                    start, end = spans[side] if halves == "add" else (0, rows)
                    for first, last, more in (
                        (row, min(stop, start), False),
                        (max(row, start), min(stop, end), True),
                        (max(row, end), stop, False),
                    ):
                        if first < last:
                            part = mine[0, first - row : last - row]
                            if more:
                                part = part.astype(F32)
                                for got in gained if halves == "sum" else [gained[side]]:
                                    part = part + got[first - start : last - start].astype(F32)
                            outs[side][first:last] = part.astype(BF)

        highs = {"send": [cut, rows - cut], "sum": [rows]}.get(halves, [rows, rows])
        return pl.pallas_call(
            kernel,
            out_shape=[jax.ShapeDtypeStruct((high, columns), BF) for high in highs] + [TOKEN],
            grid_spec=pltpu.PrefetchScalarGridSpec(
                num_scalar_prefetch=1,
                grid=(1,),
                in_specs=specs + more_specs,
                out_specs=[pl.BlockSpec((high, columns), lambda i, t: (0, 0)) for high in highs]
                + [pl.BlockSpec((8, 128), lambda i, t: (0, 0))],
            ),
            compiler_params=pltpu.CompilerParams(vmem_limit_bytes=VMEM_LIMIT),
            cost_estimate=LIGHT,
        )(ring.table, *args, *more_args)

    def scatter(self, after=()):
        ring = self.ring
        up, down, token = self.shards([ring.half], [], "send", after)
        for step in range(ring.half - 1, -1, -1):
            (up, down), after = yield (ring.send_up(up), ring.send_down(down)), token
            if step:
                kind = "add" if step == ring.half - 1 else ""
                up, down, token = self.shards([step, -step], [up, down], kind, after)
        yield self.shards([0], [up, down], "sum", after)

    def gather(self, own, split=False):
        ring, cut = self.ring, self.cut
        up = down = own
        ready = [(0, own)]
        for step in range(1, ring.half):
            up, down = yield (ring.send_up(up), ring.send_down(down)), ready
            ready = [(-step, up), (step, down)]
        high, low = yield (ring.send_up(up[:cut]), ring.send_down(down[cut:])), ready
        if split:
            yield None, [(ring.half, high), (ring.half, low)]
        else:
            yield None, [(ring.half, jnp.concatenate([high, low], axis=0))]

    def unpack_stack(self, stack, offsets, before, after=(), price=0):
        return self.unpack(
            [(offset, stack, True) for offset in offsets], before, after, price, True
        )

    def unpack(self, ready, before, after=(), price=0, stacked=False):
        ring, outs, added = self.ring, self.outs, max(self.added, 8)
        count = len(ready)
        parts = [part if isinstance(part, tuple) else (part, None) for _, part, _ in ready]
        args = []
        for array, _ in parts:
            if not any(array is x for x in args):
                args.append(array)
        which = [next(j for j, x in enumerate(args) if x is array) for array, _ in parts]
        highs = [array.shape[-2] for array, _ in parts]
        places_of = [(offset, other) for offset, _, other in ready]

        def write(part, start, results):
            stop = start + part.shape[0]
            for out, (_, _, _, moves) in zip(results, outs):
                for lead, across, (first, last), columns in moves:
                    low, high = max(first, start), min(last, stop)
                    if low < high:
                        rows = slice(low - first, high - first)
                        where = (rows, across) if lead is None else (lead, rows, across)
                        out[where] = part[low - start : high - start, columns].astype(F32)

        def start_of(i):
            same = [j for j in range(i) if places_of[j] == places_of[i]]
            return sum(highs[j] for j in same)

        starts = [0] * count if stacked else [start_of(i) for i in range(count)]

        def kernel(table_ref, *refs):
            step = pl.program_id(0)

            def part_of(i):
                ref, at = refs[which[i]], parts[i][1]
                return ref if at is None else ref.at[at]

            results = refs[-len(outs) - 2 : -2]
            refs[-1][...] = jnp.zeros_like(refs[-1])
            total = refs[-2]

            @pl.when(step == 0)
            def _():
                total[...] = jnp.zeros_like(total) if before is None else refs[sum_place][...]

            if self.added and stacked:
                total[...] += refs[0][0, self.rows - added :].astype(F32)
            elif self.added:
                for i in range(count):
                    if starts[i] + highs[i] == self.rows:

                        @pl.when(step == i)
                        def _(i=i):
                            total[...] += part_of(i)[highs[i] - added :].astype(F32)

            if stacked:
                write(refs[0].at[0], 0, results)
                return
            for i in range(count):
                pl.when(step == i)(functools.partial(write, part_of(i), starts[i], results))

        def place(of_chip, i, table):
            chip, core = None, None
            for j, (offset, other) in enumerate(places_of):
                here = table[offset % ring.chips]
                mine = table[ring.chips]
                mine = 1 - mine if other else mine
                chip = here if chip is None else jnp.where(i == j, here, chip)
                core = mine if core is None else jnp.where(i == j, mine, core)
            return of_chip(chip, core)

        shapes, out_specs = [], []
        for shape, block, of_chip, _ in outs:
            shapes.append(pltpu.HBM(shape, F32))
            out_specs.append(pl.BlockSpec(block, functools.partial(place, of_chip)))
        shapes += [jax.ShapeDtypeStruct((added, self.columns), F32), TOKEN]
        out_specs.append(pl.BlockSpec((added, self.columns), lambda i, t: (0, 0)))
        out_specs.append(pl.BlockSpec((8, 128), lambda i, t: (0, 0)))
        if stacked:
            specs = [pl.BlockSpec((1, self.rows, self.columns), lambda i, t: (i, 0, 0))]
        else:
            specs = [pl.BlockSpec(x.shape, lambda i, t, n=x.ndim: (0,) * n) for x in args]
        aliases = {}
        if before is not None:
            aliases = {1 + len(args) + i: i for i in range(len(outs))}
            specs += [pl.BlockSpec(memory_space=pl.ANY)] * len(outs)
            args += [in_hbm(x) for x in before[: len(outs)]]
            sum_place = len(args)
            args.append(before[len(outs)])
            specs.append(pl.BlockSpec((added, self.columns), lambda i, t: (0, 0)))
        more_args, more_specs = waits(after)
        args += more_args
        specs += more_specs
        return list(
            pl.pallas_call(
                kernel,
                out_shape=shapes,
                grid_spec=pltpu.PrefetchScalarGridSpec(
                    num_scalar_prefetch=1, grid=(count,), in_specs=specs, out_specs=out_specs
                ),
                input_output_aliases=aliases,
                compiler_params=pltpu.CompilerParams(vmem_limit_bytes=VMEM_LIMIT),
                cost_estimate=cost(price),
            )(ring.table, *args)
        )


def stack(parts, after=(), price=0):
    rows, columns = parts[0].shape
    count = len(parts)
    more_args, more_specs = waits(after)

    def kernel(*refs):
        out, token = refs[-2:]
        token[...] = jnp.zeros_like(token)
        for i in range(count):

            @pl.when(pl.program_id(0) == i)
            def _(i=i):
                out[0] = refs[i][...]

    return pl.pallas_call(
        kernel,
        out_shape=[jax.ShapeDtypeStruct((count, rows, columns), parts[0].dtype), TOKEN],
        grid=(count,),
        in_specs=[pl.BlockSpec((rows, columns), lambda i: (0, 0))] * count + more_specs,
        out_specs=[
            pl.BlockSpec((1, rows, columns), lambda i: (i, 0, 0)),
            pl.BlockSpec((8, 128), lambda i: (0, 0)),
        ],
        compiler_params=pltpu.CompilerParams(vmem_limit_bytes=VMEM_LIMIT),
        cost_estimate=cost(price),
    )(*parts, *more_args)


def pair_add(own, received, half, after=()):
    more_args, more_specs = waits(after)

    def kernel(*refs):
        refs, outs = refs[:4], refs[4 + len(more_args) :]
        outs[-1][...] = jnp.zeros_like(outs[-1])
        for side in range(2):
            mine, got, out = refs[side], refs[2 + side], outs[side]
            if half:
                rows = got.shape[0]
                here = slice(side * rows, (side + 1) * rows)
                rest = slice((1 - side) * rows, (2 - side) * rows)
                out[here] = (mine[here].astype(F32) + got[...].astype(F32)).astype(BF)
                out[rest] = mine[rest]
            else:
                out[...] = (mine[...].astype(F32) + got[...].astype(F32)).astype(BF)

    shape = jax.ShapeDtypeStruct(own[0].shape, BF)
    return pl.pallas_call(
        kernel,
        out_shape=[shape, shape, TOKEN],
        in_specs=[pl.BlockSpec(memory_space=pltpu.VMEM)] * 4 + more_specs,
        compiler_params=pltpu.CompilerParams(vmem_limit_bytes=VMEM_LIMIT),
        cost_estimate=LIGHT,
    )(*own, *received, *more_args)


def partner(x):
    return lax.ppermute(x, "tp", [(0, 1), (1, 0)])


def both(mine, other):
    return mine.astype(F32) + other.astype(F32)


def turn(values, cosine, sine):
    return values * cosine + pltpu.roll(values, values.shape[-1] // 2, 1) * sine


def turn_back(values, cosine, sine):
    return values * cosine - pltpu.roll(values, values.shape[-1] // 2, 1) * sine


def lower_first(order, table, other):
    core = table[table.shape[0] - 1]
    device = 2 * table[0] + (1 - core if other else core)
    return order[2 * device] < order[2 * device + 1]


def key_value_kernel(
    order, table, residuals, cotangent, gain, key_weight, value_weight, key_gain, angles, outs
):
    residual_out, cotangent_out, normed_outs, raw_outs, cosine_outs, sine_outs, packed_outs = outs
    width = key_gain.shape[1]
    span = residuals[0].shape[0] // 2
    for pair in range(2):
        start = jnp.where(lower_first(order, table, pair == 1), 0, span)

        def canonical(ref):
            return jnp.concatenate(
                [
                    ref[pl.ds(pl.multiple_of(start, span), span)],
                    ref[pl.ds(pl.multiple_of(span - start, span), span)],
                ],
                axis=0,
            )

        rows = canonical(residuals[pair])
        if pair == 0:
            residual_out[...] = rows
            cotangent_out[...] = canonical(cotangent)
        unit, _ = norm_rows(rows.astype(F32))
        normed = (unit * gain[...]).astype(BF)
        normed_outs[pair][...] = normed
        cosine, sine = canonical(angles[2 * pair]), canonical(angles[2 * pair + 1])
        cosine_outs[pair][...], sine_outs[pair][...] = cosine, sine
        raw = nn(normed, key_weight[...])
        raw_outs[pair][...] = raw
        values = nn(normed, value_weight[...]).astype(BF)
        for group in range(raw.shape[1] // width):
            here = slice(group * width, (group + 1) * width)
            key_unit, _ = norm_rows(raw[:, here])
            packed = packed_outs[pair]
            packed[:, 2 * group * width : (2 * group + 1) * width] = turn(
                key_unit * key_gain[...], cosine, sine
            ).astype(BF)
            packed[:, (2 * group + 1) * width : (2 * group + 2) * width] = values[:, here]


def query_kernel(normeds, weight, gain, cosines, sines, raw_outs, low_outs):
    width = gain.shape[1]
    for pair in range(2):
        raw = nn(normeds[pair][...], weight[...])
        raw_outs[pair][...] = raw
        for head in range(raw.shape[1] // width):
            here = slice(head * width, (head + 1) * width)
            unit, _ = norm_rows(raw[:, here])
            low_outs[pair][:, here] = turn(
                unit * gain[...], cosines[pair][...], sines[pair][...]
            ).astype(BF)


def heads_back(grad_of, raws, gain, cosines, sines, out, total):
    width = gain.shape[1]
    rows = raws[0].shape[0]
    for pair in range(2):
        here_rows = slice(pair * rows, (pair + 1) * rows)
        for head in range(raws[pair].shape[1] // width):
            here = slice(head * width, (head + 1) * width)
            unit, scale_rows = norm_rows(raws[pair][:, here])
            turned = turn_back(grad_of(pair, head), cosines[pair][...], sines[pair][...])
            total = total + jnp.sum((turned * unit).reshape(-1, 8, width), axis=0)
            out[here_rows, here] = norm_back(turned * gain[...], unit, scale_rows).astype(BF)
    return total


def query_back_kernel(grads, raws, gain, cosines, sines, low_out, gain_out):
    width = gain.shape[1]
    gain_out[...] = heads_back(
        lambda pair, head: grads[pair][:, head * width : (head + 1) * width],
        raws, gain, cosines, sines, low_out, jnp.zeros((8, width), F32),
    )


def key_value_back_kernel(owns, upward, downward, raws, gain, cosines, sines, low_out, gain_out):
    width = gain.shape[1]
    rows, columns = raws[0].shape
    groups = columns // width

    def summed(pair, place):
        here = slice(place * width, (place + 1) * width)
        at = slice(pair * rows, (pair + 1) * rows)
        return (
            owns[pair][:, here].astype(F32)
            + upward[at, here].astype(F32)
            + downward[at, here].astype(F32)
        )

    gain_out[...] = heads_back(
        lambda pair, head: summed(pair, 2 * head),
        raws, gain, cosines, sines, low_out, jnp.zeros((8, width), F32),
    )
    for pair in range(2):
        for group in range(groups):
            low_out[
                pair * rows : (pair + 1) * rows,
                columns + group * width : columns + (group + 1) * width,
            ] = summed(pair, 2 * group + 1).astype(BF)


def whole_call(kernel, scalars, outs, args, after=()):
    more_args, more_specs = waits(after)
    count = len(scalars)
    arrays, specs = [], []
    for arg in args:
        array, block, place = arg if isinstance(arg, tuple) else (arg, arg.shape, None)
        arrays.append(array)
        if place is None:
            specs.append(pl.BlockSpec(block, lambda i, *t: (0, 0)))
        else:
            specs.append(
                pl.BlockSpec(
                    block, lambda i, *t, place=place: place(t[-1][t[-1].shape[0] - 1])
                )
            )
    taken = count + len(args)

    def run(*refs):
        kernel(*refs[:taken], *refs[taken + len(more_args) :])

    return list(
        pl.pallas_call(
            run,
            out_shape=[
                pltpu.HBM(shape, dtype) if far else jax.ShapeDtypeStruct(shape, dtype)
                for shape, dtype, *far in outs
            ],
            grid_spec=pltpu.PrefetchScalarGridSpec(
                num_scalar_prefetch=count,
                grid=(1,),
                in_specs=specs + more_specs,
                out_specs=[pl.BlockSpec(shape, lambda i, *t: (0, 0)) for shape, *_ in outs],
            ),
            compiler_params=pltpu.CompilerParams(vmem_limit_bytes=VMEM_LIMIT),
            cost_estimate=LIGHT,
        )(*scalars, *arrays, *more_args)
    )


def matmul(left, right, after=(), price=0):
    rows, inner = left.shape
    columns = right.shape[1]
    tile = min(columns, 512)
    more_args, more_specs = waits(after)

    def kernel(left_ref, right_ref, *refs):
        refs[-1][...] = nn(left_ref[...], right_ref[...]).astype(BF)

    return pl.pallas_call(
        kernel,
        out_shape=jax.ShapeDtypeStruct((rows, columns), BF),
        grid=(columns // tile,),
        in_specs=[
            pl.BlockSpec((rows, inner), lambda i: (0, 0)),
            pl.BlockSpec((inner, tile), lambda i: (0, i)),
        ]
        + more_specs,
        out_specs=pl.BlockSpec((rows, tile), lambda i: (0, i)),
        compiler_params=pltpu.CompilerParams(vmem_limit_bytes=VMEM_LIMIT),
        cost_estimate=cost(price),
    )(left, in_hbm(right), *more_args)


def add_and_norm(part, other, residual, half, gain, price=0):
    rows, columns = part.shape

    def kernel(part_ref, other_ref, residual_ref, gain_ref, total, low):
        both_parts = part_ref[...].astype(F32) + other_ref[...].astype(F32)
        mixed = residual_ref[...].astype(F32) + both_parts
        total[...] = mixed
        normed, _ = norm_rows(mixed)
        low[...] = (normed * gain_ref[...]).astype(BF)

    whole = pl.BlockSpec((rows, columns), lambda i: (0, 0))
    return pl.pallas_call(
        kernel,
        out_shape=[
            jax.ShapeDtypeStruct((rows, columns), F32),
            jax.ShapeDtypeStruct((rows, columns), BF),
        ],
        grid=(1,),
        in_specs=[
            whole,
            whole,
            pl.BlockSpec((rows, columns), lambda i: (half, 0)),
            pl.BlockSpec((1, columns), lambda i: (0, 0)),
        ],
        out_specs=[whole, whole],
        compiler_params=pltpu.CompilerParams(vmem_limit_bytes=VMEM_LIMIT),
        cost_estimate=cost(price),
    )(part, other, residual, gain)


def finish(order, residual, mixed, mixed_grad, normed_parts, layer_parts, gain, after, price):
    rows, columns = residual.shape
    span = rows // 2
    more_args, more_specs = waits(after)

    def kernel(order_ref, row, mix, mix_grad, normed0, normed1, layer0, layer1, gain_ref, *refs):
        out, grad, token = refs[-3:]
        out[...] = (mix[...] + both(layer0[...], layer1[...])).astype(BF)
        normed, scale = norm_rows(row[...].astype(F32))
        normed_grad = both(normed0[...], normed1[...]) * gain_ref[...]
        grad[...] = mix_grad[...] + norm_back(normed_grad, normed, scale)
        token[...] = jnp.zeros_like(token)

    part = pl.BlockSpec((span, columns), lambda i, o: (i, 0))
    placed = pl.BlockSpec((span, columns), lambda i, o: (jnp.where(o[0] < o[1], i, 1 - i), 0))
    return pl.pallas_call(
        kernel,
        out_shape=[
            jax.ShapeDtypeStruct((rows, columns), BF),
            jax.ShapeDtypeStruct((rows, columns), F32),
            TOKEN,
        ],
        grid_spec=pltpu.PrefetchScalarGridSpec(
            num_scalar_prefetch=1,
            grid=(2,),
            in_specs=[part] * 7 + [pl.BlockSpec((1, columns), lambda i, o: (0, 0))] + more_specs,
            out_specs=[placed, placed, pl.BlockSpec(TOKEN.shape, lambda i, o: (0, 0))],
        ),
        compiler_params=pltpu.CompilerParams(vmem_limit_bytes=VMEM_LIMIT),
        cost_estimate=cost(price),
    )(order, residual, mixed, mixed_grad, *normed_parts, *layer_parts, gain, *more_args)


def out_projection(table, rows, weight, other, before=None):
    high, inner = rows.shape
    columns = weight.shape[1]
    tile = min(inner, 256)
    count = inner // tile
    last = table.shape[0] - 1
    dtype = F32 if before is None else BF

    def kernel(table_ref, rows_ref, weight_ref, *refs):
        out, total = refs[-2:]
        step = pl.program_id(0)
        part = nn(rows_ref[...], weight_ref[...])

        @pl.when(step == 0)
        def _():
            total[...] = part if before is None else part + refs[0][...]

        @pl.when(step > 0)
        def _():
            total[...] += part

        @pl.when(step == count - 1)
        def _():
            out[...] = total[...].astype(dtype)

    whole = pl.BlockSpec((high, columns), lambda i, t: (0, 0))
    extra = [] if before is None else [before]
    return pl.pallas_call(
        kernel,
        out_shape=jax.ShapeDtypeStruct((high, columns), dtype),
        grid_spec=pltpu.PrefetchScalarGridSpec(
            num_scalar_prefetch=1,
            grid=(count,),
            in_specs=[
                pl.BlockSpec((high, tile), lambda i, t: (0, i)),
                pl.BlockSpec(
                    (tile, columns),
                    lambda i, t: ((1 - t[last] if other else t[last]) * count + i, 0),
                ),
            ]
            + [whole] * len(extra),
            out_specs=whole,
            scratch_shapes=[pltpu.VMEM((high, columns), F32)],
        ),
        compiler_params=pltpu.CompilerParams(vmem_limit_bytes=VMEM_LIMIT),
        cost_estimate=LIGHT,
    )(table, rows, weight, *extra)


def heads_products(table, rows, weight, after=()):
    high, columns = rows[0].shape
    inner = weight.shape[0] // 2
    tile = min(inner, 256)
    count = inner // tile
    last = table.shape[0] - 1
    more_args, more_specs = waits(after)

    def kernel(table_ref, first, second, mine, *refs):
        refs[-2][...] = nt(first[...], mine[...]).astype(BF)
        refs[-1][...] = nt(second[...], mine[...]).astype(BF)

    shape = jax.ShapeDtypeStruct((high, inner), BF)
    spec = pl.BlockSpec((high, tile), lambda i, t: (0, i))
    whole = pl.BlockSpec((high, columns), lambda i, t: (0, 0))
    return pl.pallas_call(
        kernel,
        out_shape=[shape, shape],
        grid_spec=pltpu.PrefetchScalarGridSpec(
            num_scalar_prefetch=1,
            grid=(count,),
            in_specs=[
                whole,
                whole,
                pl.BlockSpec((tile, columns), lambda i, t: (t[last] * count + i, 0)),
            ]
            + more_specs,
            out_specs=[spec, spec],
        ),
        compiler_params=pltpu.CompilerParams(vmem_limit_bytes=VMEM_LIMIT),
        cost_estimate=LIGHT,
    )(table, *rows, in_hbm(weight), *more_args)


def normed_products(
    table, normeds, query_grad, key_value_grad, query_weight, key_weight, value_weight, after=()
):
    rows, wide = query_grad.shape
    narrow = key_value_grad.shape[1] // 2
    columns = query_weight.shape[0]
    tile = min(columns, 256)
    last = table.shape[0] - 1
    more_args, more_specs = waits(after)

    def kernel(table_ref, first, second, queries, others, query, key, value, *refs):
        total = (
            nt(queries[...], query[...])
            + nt(others[:, :narrow], key[...])
            + nt(others[:, narrow:], value[...])
        ).astype(BF)
        upper, lower = total[: rows // 2], total[rows // 2 :]
        refs[-3][...] = upper
        refs[-2][...] = lower
        term = upper.astype(F32) * first[...].astype(F32) + lower.astype(F32) * second[...].astype(F32)
        refs[-1][...] = jnp.sum(term.reshape(-1, 8, tile), axis=0)

    shape = pltpu.HBM((rows // 2, columns), BF)
    spec = pl.BlockSpec((rows // 2, tile), lambda i, t: (0, i))
    return pl.pallas_call(
        kernel,
        out_shape=[shape, shape, jax.ShapeDtypeStruct((8, columns), F32)],
        grid_spec=pltpu.PrefetchScalarGridSpec(
            num_scalar_prefetch=1,
            grid=(columns // tile,),
            in_specs=[
                spec,
                spec,
                pl.BlockSpec((rows, wide), lambda i, t: (0, 0)),
                pl.BlockSpec((rows, 2 * narrow), lambda i, t: (0, 0)),
                pl.BlockSpec((tile, wide), lambda i, t: (i, t[last])),
                pl.BlockSpec((tile, narrow), lambda i, t: (i, t[last])),
                pl.BlockSpec((tile, narrow), lambda i, t: (i, t[last])),
            ]
            + more_specs,
            out_specs=[spec, spec, pl.BlockSpec((8, tile), lambda i, t: (0, i))],
        ),
        compiler_params=pltpu.CompilerParams(vmem_limit_bytes=VMEM_LIMIT),
        cost_estimate=cost(HEAVY),
    )(
        table, *normeds, query_grad, key_value_grad, in_hbm(query_weight), in_hbm(key_weight),
        in_hbm(value_weight), *more_args,
    )


def stacked(ref, start, span, width):
    rows = pl.ds(start, span)
    return jnp.concatenate([ref[rows, :width], ref[rows, width:]], axis=0)


def causal(span, transposed):
    shape = (span, 2 * span) if transposed else (2 * span, span)
    key = lax.broadcasted_iota(jnp.int32, shape, 0 if transposed else 1)
    row = lax.broadcasted_iota(jnp.int32, shape, 1 if transposed else 0)
    return key <= row % span


def side_met(order, table, pair, offset, other):
    last = table.shape[0] - 1
    core = table[last]

    def lower(device):
        return jnp.minimum(order[2 * device], order[2 * device + 1])

    mine = lower(2 * table[0] + (1 - core if pair else core))
    theirs = lower(2 * table[offset % last] + (1 - core if other else core))
    return jnp.where(theirs < mine, 0, 1)


def forward_kernel(places, own, last, span, width, order, table, *refs):
    count = len(places)
    queries, blocks, refs = refs[:2], refs[2 : 2 + count], refs[2 + count :]
    scale = LOG2E / math.sqrt(width)
    if own:
        before, outs = None, refs
    else:
        before, outs = refs[0], refs[1:]
    accum = outs[-1]
    ones = jnp.ones((span, width), BF)

    def weighted(rows, keys, values, allowed=None):
        scores = nt(rows, keys)
        probs = jnp.exp2(scores * scale)
        if allowed is not None:
            probs = jnp.where(allowed, probs, 0.0)
        return nn(probs.astype(BF), values)

    def extended(block, start):
        return jnp.concatenate([block[pl.ds(start, span), width:], ones], axis=1)

    keys = jnp.concatenate([block[:span, :width] for block in blocks], axis=0)
    values = jnp.concatenate([extended(block, 0) for block in blocks], axis=0)
    rows = jnp.concatenate([stacked(query, span, span, width) for query in queries], axis=0)
    high = weighted(rows, keys, values)
    for pair in range(2):
        part = high[pair * 2 * span : (pair + 1) * 2 * span]
        if own:
            allowed = causal(span, False)
            for side in range(2):
                block, start = blocks[pair], side * span
                met = weighted(
                    stacked(queries[pair], start, span, width),
                    block[start : start + span, :width],
                    extended(block, start),
                    allowed,
                )
                accum[0, pair, side] = met + part if side else met
        else:
            accum[0, pair, 0] = before[0, pair, 0]
            accum[0, pair, 1] = before[0, pair, 1] + part
    for i, (offset, other) in enumerate(places):
        for pair in range(2):
            if own and i == pair:
                continue
            side = side_met(order, table, pair, offset, other)
            start = pl.multiple_of(side * span, span)
            accum[0, pair, side] += weighted(
                stacked(queries[pair], start, span, width),
                blocks[i][pl.ds(start, span), :width],
                extended(blocks[i], start),
            )
    if last:
        wides, lows, logs = outs[0:2], outs[2:4], outs[4]
        for pair in range(2):
            for side in range(2):
                rows = slice(side * span, (side + 1) * span)
                whole = accum[0, pair, side]
                mass = whole[:, width:]
                out = whole[:, :width] / mass
                for head in range(2):
                    part = out[head * span : (head + 1) * span]
                    columns = slice(head * width, (head + 1) * width)
                    wides[pair][rows, columns] = part
                    lows[pair][rows, columns] = part.astype(BF)
                logs[0, pair, side] = jnp.log2(mass).T[:8]


def attention_forward(scalars, queries, blocks, places, before, own, last, after=()):
    rows, columns = queries[0].shape
    span, width = rows // 2, HEAD
    groups = columns // (2 * width)
    tile = pl.BlockSpec((rows, 2 * width), lambda g: (0, g))
    accum_block = (1, 2, 2, 2 * span, 2 * width)
    accum_spec = pl.BlockSpec(accum_block, lambda g: (g, 0, 0, 0, 0))
    args = [*scalars, *queries, *(in_hbm(block) for block in blocks)]
    specs = [pl.BlockSpec(memory_space=pltpu.SMEM)] * 2 + [tile] * (2 + len(blocks))
    if not own:
        args.append(before)
        specs.append(accum_spec)
    taken = len(args)
    more_args, more_specs = waits(after)
    scratch = []
    if last:
        wide, low = pltpu.HBM((rows, columns), F32), jax.ShapeDtypeStruct((rows, columns), BF)
        outs = [wide, wide, low, low, jax.ShapeDtypeStruct((groups, 2, 2, 8, 2 * span), F32), TOKEN]
        out_specs = [tile] * 4 + [
            pl.BlockSpec((1, 2, 2, 8, 2 * span), lambda g: (g, 0, 0, 0, 0)),
            pl.BlockSpec((8, 128), lambda g: (0, 0)),
        ]
        scratch = [pltpu.VMEM(accum_block, F32)]
    else:
        outs = [jax.ShapeDtypeStruct((groups, *accum_block[1:]), F32), TOKEN]
        out_specs = [accum_spec, pl.BlockSpec((8, 128), lambda g: (0, 0))]

    def kernel(*refs):
        refs = refs[:taken] + refs[taken + len(more_args) :]
        place = -2 if last else -1
        refs[place][...] = jnp.zeros_like(refs[place])
        refs = refs[:place] + (refs[-1:] if last else ())
        forward_kernel(places, own, last, span, width, *refs)

    return pl.pallas_call(
        kernel,
        out_shape=outs,
        grid=(groups,),
        in_specs=specs + more_specs,
        out_specs=out_specs,
        scratch_shapes=scratch,
        input_output_aliases={} if own or last else {taken - 1: 0},
        compiler_params=pltpu.CompilerParams(vmem_limit_bytes=VMEM_LIMIT),
        cost_estimate=FORWARD,
    )(*args, *more_args)


def delta_kernel(grads, outs, delta):
    for pair in range(2):
        grad, out = grads[pair], outs[pair]
        width, span = grad.shape[1] // 2, grad.shape[0] // 2
        for side in range(2):
            rows = slice(side * span, (side + 1) * span)
            product = grad[rows, :].astype(F32) * out[rows, :]
            stack = jnp.concatenate([product[:, :width], product[:, width:]], axis=0)
            total = jnp.sum(stack.T, axis=0, keepdims=True)
            delta[0, pair, side] = jnp.broadcast_to(total, (8, 2 * span))


def attention_delta(grads, outs, after=()):
    rows, columns = grads[0].shape
    width, span = HEAD, rows // 2
    groups = columns // (2 * width)
    tile = pl.BlockSpec((rows, 2 * width), lambda g: (0, g))
    more_args, more_specs = waits(after)

    def kernel(*refs):
        delta_kernel(refs[:2], refs[2:4], refs[-1])

    return pl.pallas_call(
        kernel,
        out_shape=jax.ShapeDtypeStruct((groups, 2, 2, 8, 2 * span), F32),
        grid=(groups,),
        in_specs=[tile] * 4 + more_specs,
        out_specs=pl.BlockSpec((1, 2, 2, 8, 2 * span), lambda g: (g, 0, 0, 0, 0)),
        compiler_params=pltpu.CompilerParams(vmem_limit_bytes=VMEM_LIMIT),
        cost_estimate=LIGHT,
    )(*grads, *outs, *more_args)


def backward_kernel(places, own, first, last, split, span, width, order, table, *refs):
    count = len(places)
    queries, grads, (logs, delta), refs = refs[:2], refs[2:4], refs[4:6], refs[6:]
    blocks, refs = refs[:count], refs[count:]
    if not first:
        before, refs = refs[0], refs[1:]
    outs = refs[: count if split else count // 2]
    refs = refs[len(outs) :]
    refs[0][...] = jnp.zeros_like(refs[0])
    refs = refs[1:]
    if last:
        query_outs, accum = refs[:2], refs[2]
    else:
        accum = refs[0]
    scale = LOG2E / math.sqrt(width)
    factor = 1.0 / math.sqrt(width)

    def products(rows, row_grads, log, mean, keys, values, allowed=None):
        probs = jnp.exp2(nt(keys, rows) * scale - log)
        if allowed is not None:
            probs = jnp.where(allowed, probs, 0.0)
        prob_grad = nt(values, row_grads)
        score_grad = (probs * (prob_grad - mean)).astype(BF)
        return nn(score_grad, rows), nn(probs.astype(BF), row_grads), tn(keys, score_grad)

    def of_pair(pair, side, start, keys, values, allowed=None):
        return products(
            stacked(queries[pair], start, span, width),
            stacked(grads[pair], start, span, width),
            logs[0, pair, side, :1],
            delta[0, pair, side, :1],
            keys,
            values,
            allowed,
        )

    low_keys, low_values, high_query = products(
        jnp.concatenate([stacked(query, span, span, width) for query in queries], axis=0),
        jnp.concatenate([stacked(grad, span, span, width) for grad in grads], axis=0),
        jnp.concatenate([logs[0, pair, 1, :1] for pair in range(2)], axis=1),
        jnp.concatenate([delta[0, pair, 1, :1] for pair in range(2)], axis=1),
        jnp.concatenate([block[:span, :width] for block in blocks], axis=0),
        jnp.concatenate([block[:span, width:] for block in blocks], axis=0),
    )
    for pair in range(2):
        part = high_query[:, pair * 2 * span : (pair + 1) * 2 * span]
        if first:
            accum[0, pair, 0] = jnp.zeros_like(part)
            accum[0, pair, 1] = part
        else:
            accum[0, pair, 0] = before[0, pair, 0]
            accum[0, pair, 1] = before[0, pair, 1] + part
    for i, (offset, other) in enumerate(places):
        here = slice(i * span, (i + 1) * span)
        block = blocks[i]
        key_sums, value_sums = [low_keys[here], 0.0], [low_values[here], 0.0]
        for pair in range(2):
            if own and i == pair:
                allowed = causal(span, True)
                for side in range(2):
                    rows = slice(side * span, (side + 1) * span)
                    key_part, value_part, query_part = of_pair(
                        pair, side, side * span, block[rows, :width], block[rows, width:], allowed
                    )
                    accum[0, pair, side] += query_part
                    key_sums[side] = key_sums[side] + key_part
                    value_sums[side] = value_sums[side] + value_part
                continue
            side = side_met(order, table, pair, offset, other)
            start = pl.multiple_of(side * span, span)
            rows = pl.ds(start, span)
            key_part, value_part, query_part = of_pair(
                pair, side, start, block[rows, :width], block[rows, width:]
            )
            accum[0, pair, side] += query_part
            low = side == 0
            key_sums[0] = key_sums[0] + jnp.where(low, key_part, 0.0)
            value_sums[0] = value_sums[0] + jnp.where(low, value_part, 0.0)
            key_sums[1] = key_sums[1] + jnp.where(low, 0.0, key_part)
            value_sums[1] = value_sums[1] + jnp.where(low, 0.0, value_part)
        out = outs[i] if split else outs[i // 2]
        base = 0 if split else i % 2 * 2 * span
        for side in range(2):
            rows = slice(base + side * span, base + (side + 1) * span)
            out[rows, :width] = (key_sums[side] * factor).astype(BF)
            out[rows, width:] = value_sums[side].astype(BF)
    if last:
        for pair in range(2):
            for side in range(2):
                part = accum[0, pair, side].T * factor
                rows = slice(side * span, (side + 1) * span)
                query_outs[pair][rows, :width] = part[:span]
                query_outs[pair][rows, width:] = part[span:]


def attention_backward(
    scalars, queries, grads, logs, delta, blocks, places, before, own, last, split, after=()
):
    rows, columns = queries[0].shape
    span, width = rows // 2, HEAD
    groups = columns // (2 * width)
    count = len(blocks)
    first = before is None
    tile = pl.BlockSpec((rows, 2 * width), lambda g: (0, g))
    stat = pl.BlockSpec((1, 2, 2, 8, 2 * span), lambda g: (g, 0, 0, 0, 0))
    accum_block = (1, 2, 2, width, 2 * span)
    accum_spec = pl.BlockSpec(accum_block, lambda g: (g, 0, 0, 0, 0))
    args = [*scalars, *queries, *grads, logs, delta, *(in_hbm(block) for block in blocks)]
    specs = [pl.BlockSpec(memory_space=pltpu.SMEM)] * 2 + [tile] * 4 + [stat] * 2 + [tile] * count
    if not first:
        args.append(before)
        specs.append(accum_spec)
    taken = len(args)
    more_args, more_specs = waits(after)
    if split:
        outs = [jax.ShapeDtypeStruct((rows, columns), BF)] * count
        out_specs = [tile] * count
    else:
        outs = [jax.ShapeDtypeStruct((2 * rows, columns), BF)] * (count // 2)
        out_specs = [pl.BlockSpec((2 * rows, 2 * width), lambda g: (0, g))] * (count // 2)
    outs.append(TOKEN)
    out_specs.append(pl.BlockSpec((8, 128), lambda g: (0, 0)))
    scratch = []
    if last:
        outs += [jax.ShapeDtypeStruct((rows, columns), F32)] * 2
        out_specs += [tile] * 2
        scratch = [pltpu.VMEM(accum_block, F32)]
    else:
        outs.append(jax.ShapeDtypeStruct((groups, *accum_block[1:]), F32))
        out_specs.append(accum_spec)

    def kernel(*refs):
        refs = refs[:taken] + refs[taken + len(more_args) :]
        backward_kernel(places, own, first, last, split, span, width, *refs)

    return pl.pallas_call(
        kernel,
        out_shape=outs,
        grid=(groups,),
        in_specs=specs + more_specs,
        out_specs=out_specs,
        scratch_shapes=scratch,
        input_output_aliases={} if first or last else {taken - 1: len(outs) - 1},
        compiler_params=pltpu.CompilerParams(vmem_limit_bytes=VMEM_LIMIT),
        cost_estimate=cost(HEAVY),
    )(*args, *more_args)


def body(
    devices,
    residual,
    cotangent,
    span_order,
    positions,
    attn_gain,
    query_weight,
    key_weight,
    value_weight,
    query_gain,
    key_gain,
    out_weight,
    mlp_gain,
    gate_weight,
    up_weight,
    down_weight,
):
    ring = Ring(devices)
    rows, model = residual.shape
    head_dim = query_gain.shape[0]
    span = rows // 2
    index = lax.axis_index("cp")
    scalars = [span_order, ring.table]
    table = [ring.table]
    residual_other, positions_other = ring.sibling(residual), ring.sibling(positions)

    half = head_dim // 2
    freq = ROPE_BASE ** (-(jnp.arange(half, dtype=F32) * 2.0) / head_dim)
    angles = []
    for where in (positions, positions_other):
        angle = where.astype(F32)[:, None] * freq[None, :]
        cosine, sine = jnp.cos(angle), jnp.sin(angle)
        angles.append(jnp.concatenate([cosine, cosine], axis=1))
        angles.append(jnp.concatenate([-sine, sine], axis=1))

    query_gain_row = query_gain.reshape(1, -1)
    key_gain_row = key_gain.reshape(1, -1)
    key_columns = key_weight.shape[1]
    query_columns = query_weight.shape[1]
    few, each = key_columns // 2, query_columns // 2

    def project_keys(order, table_ref, first, second, grad, gain, key, value, row, c0, s0, c1, s1, *outs):
        key_value_kernel(
            order, table_ref, (first, second), grad, gain, key, value, row, (c0, s0, c1, s1),
            (outs[0], outs[1], outs[2:4], outs[4:6], outs[6:8], outs[8:10], outs[10:12]),
        )

    residual, cotangent, *results = whole_call(
        project_keys,
        scalars,
        [((rows, model), BF, 1)] * 2
        + [((rows, model), BF)] * 2
        + [((rows, few), F32, 1)] * 2
        + [((rows, head_dim), F32)] * 4
        + [((rows, key_columns), BF)] * 2,
        [
            in_hbm(residual), residual_other, in_hbm(cotangent), in_hbm(attn_gain.reshape(1, -1)),
            (in_hbm(key_weight), (model, few), lambda core: (0, core)),
            (in_hbm(value_weight), (model, few), lambda core: (0, core)),
            in_hbm(key_gain_row), *angles,
        ],
    )
    normeds, keys_raw, cosines, sines, parts = (results[i : i + 2] for i in range(0, 10, 2))

    ways = [(ring.send_up(part), ring.send_down(part)) for part in parts]

    def project_queries(table_ref, n0, n1, weight, gain, c0, c1, s0, s1, *outs):
        query_kernel((n0, n1), weight, gain, (c0, c1), (s0, s1), outs[:2], outs[2:])

    *queries_raw, first, second = whole_call(
        project_queries,
        table,
        [((rows, each), F32, 1)] * 2 + [((rows, each), BF)] * 2,
        [
            *normeds, (in_hbm(query_weight), (model, each), lambda core: (0, core)),
            in_hbm(query_gain_row), *cosines, *sines,
        ],
    )
    queries = [first, second]

    def places_of(offsets):
        return [(offset, other) for offset in offsets for other in (False, True)]

    steps = ring.half
    calls = {0: ([0], parts)}
    state = None
    token = None
    for step in range(1, steps):
        come = []
        for which in range(2):
            up, down = ways[which]
            if step == 1 and which == 0:
                up, down, queries[0] = tie(up, down, queries[0])
            else:
                up, down, token = tie(up, down, token)
            come.append((up, down))
            if step < steps - 1:
                ways[which] = ring.send_up(up), ring.send_down(down)
            else:
                ways[which] = ring.send_down(down) if which else ring.send_up(up)
            if step == 1 and which == 0:
                state, token = attention_forward(
                    scalars, queries, parts, places_of([0]), None, True, False, come[0]
                )
        blocks = [come[0][0], come[1][0], come[0][1], come[1][1]]
        calls[step] = ([-step, step], blocks)
        state, token = attention_forward(
            scalars, queries, blocks, places_of([-step, step]), state, False, False, [token]
        )
    *ways, token = tie(*ways, token)
    calls[steps] = ([steps], ways)
    *attended, low_keep, low_give, logs, _ = attention_forward(
        scalars, queries, ways, places_of([steps]), state, False, True, [token]
    )
    low_other = ring.sibling(low_give)
    mixed_part = out_projection(ring.table, low_keep, out_weight, False)
    mixed_part = out_projection(ring.table, low_other, out_weight, True, mixed_part)
    mixed_part, cotangent = tie(mixed_part, cotangent)
    mixed_parts = [mixed_part[:span], mixed_part[span:]]
    mixed_others = [partner(part) for part in mixed_parts]
    cotangents = [cotangent, ring.sibling(cotangent)]
    hidden_grad = nt(cotangent, down_weight)
    mixed_others[0], hidden_grad, cotangents = tie(mixed_others[0], hidden_grad, cotangents)

    residual_wide = residual.astype(F32)

    def feed_forward(half, part, other, price):
        rows = slice(half * span, (half + 1) * span)
        mixed, low = add_and_norm(part, other, residual, half, mlp_gain.reshape(1, -1), price)
        gate = nn(low, gate_weight)
        upward = nn(low, up_weight)
        sigmoid_gate = jax.nn.sigmoid(gate)
        activated = gate * sigmoid_gate
        hidden = (activated * upward).astype(BF)
        gate_grad = (
            hidden_grad[rows] * upward * sigmoid_gate * (1.0 + gate * (1.0 - sigmoid_gate))
        ).astype(BF)
        up_grad = (hidden_grad[rows] * activated).astype(BF)
        back = (nt(gate_grad, gate_weight) + nt(up_grad, up_weight)).astype(BF)
        return (mixed, low, hidden, gate_grad, up_grad), back

    upper, upper_back = feed_forward(0, mixed_parts[0], mixed_others[0], 0)
    upper_back, mixed_others[1] = tie(upper_back, mixed_others[1])
    upper_other = partner(upper_back)
    lower, lower_back = feed_forward(1, mixed_parts[1], mixed_others[1], HEAVY)
    lower_other = partner(lower_back)
    mixed, normed_two_low, hidden_low, gate_grad_low, up_grad_low = (
        jnp.concatenate(pair, axis=0) for pair in zip(upper, lower)
    )
    normed_two, scale_two = norm_rows(mixed)

    units = gate_weight.shape[1]
    thirds = 2 * units // model
    chips = ring.chips
    gate_rows = model // 2 // chips
    down_rows = units // thirds // 2 // chips
    down_row = thirds * gate_rows
    out_row = down_row + thirds * down_rows
    packed_shape = (out_row + gate_rows, model)

    def shard_of(chip, core):
        return core * chips + chip

    def columns_of(start):
        moves, done = [], 0
        while done < units:
            tile, column = divmod(start + done, model)
            wide = min(model - column, units - done)
            moves.append(
                (
                    None,
                    slice(done, done + wide),
                    (tile * gate_rows, (tile + 1) * gate_rows),
                    slice(column, column + wide),
                )
            )
            done += wide
        return moves

    everything = slice(None)
    wide = Gradients(
        ring,
        *packed_shape,
        [
            ((model, units), (gate_rows, units), lambda c, k: (shard_of(c, k), 0), columns_of(0)),
            ((model, units), (gate_rows, units), lambda c, k: (shard_of(c, k), 0), columns_of(units)),
            (
                (thirds, units // thirds, model),
                (thirds, down_rows, model),
                lambda c, k: (0, shard_of(c, k), 0),
                [
                    (i, everything, (down_row + i * down_rows, down_row + (i + 1) * down_rows), everything)
                    for i in range(thirds)
                ],
            ),
            (
                (2 * each, model),
                (gate_rows, model),
                lambda c, k: (shard_of(c, k), 0),
                [(None, everything, (out_row, out_row + gate_rows), everything)],
            ),
        ],
    )
    both_grad_low = jnp.concatenate([gate_grad_low, up_grad_low], axis=1)
    both_grads = [both_grad_low, ring.sibling(both_grad_low)]
    both_grads, upper_other = tie(both_grads, upper_other)
    packed, token = products(
        ring.table, [normed_two_low, ring.sibling(normed_two_low)], both_grads, chips,
        (down_row, model), 0, 0, None, [upper_back, lower_back], price=LITTLE,
    )
    wide.packs.append((0, packed))
    packed, token = products(
        ring.table, [hidden_low, ring.sibling(hidden_low)], cotangents, chips,
        (thirds * down_rows, model), 0, 0, None, [token], thirds=thirds,
    )
    wide.packs.append((down_row, packed))
    upper_other, lower_other, token = tie(upper_other, lower_other, token)

    normed_two_grad = jnp.concatenate(
        [both(upper_back, upper_other), both(lower_back, lower_other)], axis=0
    )
    mlp_gain_term = jnp.sum(normed_two_grad * normed_two, axis=0)
    mixed_grad = cotangent.astype(F32) + norm_back(
        normed_two_grad * mlp_gain, normed_two, scale_two
    )
    mixed_grad_low = mixed_grad.astype(BF)
    mixed_grads = [mixed_grad_low, ring.sibling(mixed_grad_low)]
    packed, token = products(
        ring.table, [low_keep, low_give], mixed_grads, chips, (gate_rows, model), 0, 0, None,
        [token], halved=False,
    )
    wide.packs.append((out_row, packed))
    wide_steps = wide.scatter([token])
    wide_way, token = next(wide_steps)
    grads = heads_products(ring.table, mixed_grads, out_weight, [token])
    delta = attention_delta(grads, attended)

    def backward(step, state, after):
        offsets, blocks = calls[step]
        last = step == 0
        return attention_backward(
            scalars, queries, grads, logs, delta, blocks, places_of(offsets), state,
            last, last, last or step == steps, after,
        )

    narrow_rows = query_rows = model // chips
    narrow_shape = (query_rows, each + 2 * few)

    def narrow_out(start, wide):
        return (
            (model, 2 * wide),
            (query_rows, wide),
            lambda c, k: (c, k),
            [(None, everything, (0, query_rows), slice(start, start + wide))],
        )

    narrow = Gradients(
        ring,
        narrow_rows,
        model,
        [
            narrow_out(0, each),
            narrow_out(each, few),
            narrow_out(each + few, few),
        ],
    )
    up, down, token, state = backward(steps, None, [])
    up, down = ring.send_up(up), ring.send_down(down)
    for step in range(steps - 1, 0, -1):
        if step == 1:
            layer_part = matmul(hidden_low, down_weight, [token])
            wide_way, layer_part, token = tie(wide_way, layer_part, token)
            layer_other = partner(layer_part)
        wide_way, wide_token = wide_steps.send((wide_way, [token]))
        back, front, token, state = backward(step, state, [wide_token])
        if step == 1:
            layer_other, token = tie(layer_other, token)
        up, down, token = pair_add([front, back], [up, down], step == steps - 1, [token])
        up, down = ring.send_up(up), ring.send_down(down)
    wide_shard, wide_token = wide_steps.send((wide_way, [token]))
    wide_steps = wide.gather(wide_shard)
    wide_way, wide_ready = next(wide_steps)
    *key_value_own, token, first, second = backward(0, state, [wide_token])

    def back_queries(table_ref, g0, g1, r0, r1, gain, c0, c1, s0, s1, *outs):
        query_back_kernel((g0, g1), (r0, r1), gain, (c0, c1), (s0, s1), *outs)

    query_grad_low, query_gain_term = whole_call(
        back_queries,
        table,
        [((2 * rows, each), BF), ((8, head_dim), F32)],
        [first, second, *map(in_hbm, [*queries_raw, query_gain_row, *cosines, *sines])],
    )
    packed, token = products(
        ring.table, normeds, [query_grad_low], chips, narrow_shape, 0, 0, None, halved=False,
    )

    def own_ready(ready):
        return [(offset, part, False) for offset, part in ready]

    def other_ready(ready):
        return [(offset, ring.sibling(part), True) for offset, part in ready]

    first_other = ring.sibling(wide_shard)
    up, down, first_other, token = tie(up, down, first_other, token)

    def back_keys(table_ref, o0, o1, up_ref, down_ref, r0, r1, gain, c0, c1, s0, s1, *outs):
        key_value_back_kernel(
            (o0, o1), up_ref, down_ref, (r0, r1), gain, (c0, c1), (s0, s1), *outs
        )

    key_value_grad, key_gain_term = whole_call(
        back_keys,
        table,
        [((2 * rows, 2 * few), BF), ((8, head_dim), F32)],
        [
            *key_value_own, up, down, *map(in_hbm, [*keys_raw, key_gain_row, *cosines, *sines]),
        ],
        after=[token],
    )
    packed, token = products(
        ring.table, normeds, [key_value_grad], chips, narrow_shape, 0, each, packed, halved=False,
    )
    narrow.packs = [(0, packed)]
    narrow_steps = narrow.scatter()
    narrow_way, token = next(narrow_steps)
    wide_way, token = tie(wide_way, token)
    wide_way, pair = wide_steps.send(wide_way)
    narrow_way, token = tie(narrow_way, token)
    narrow_way, token = narrow_steps.send((narrow_way, [token]))

    def stacked_pair(ready, token, price=0):
        lot, token = stack([part for _, part in ready], [token], price)
        return (lot, [offset for offset, _ in ready]), token

    def fly(lots, token):
        flown = []
        for lot, offsets in lots:
            lot, token = tie(lot, token)
            other = ring.sibling(lot)
            flown.append((other, offsets))
        return flown, token

    def land(flown, results, token, price=0):
        for other, offsets in flown:
            other, token = tie(other, token)
            results = wide.unpack_stack(other, offsets, results, [token], price)
            token = results[-1]
        return results, token

    lot, token = stacked_pair(pair, token)
    flown, token = fly([lot], token)
    normed_own, normed_give, attn_gain_term = normed_products(
        ring.table, normeds, query_grad_low, key_value_grad, query_weight, key_weight, value_weight,
        [token],
    )
    wide_results, token = land(flown, None, attn_gain_term)
    small = jnp.concatenate(
        [
            jnp.sum(attn_gain_term, axis=0) / attn_gain,
            0.5 * mlp_gain_term,
            jnp.sum(query_gain_term, axis=0),
            jnp.sum(key_gain_term, axis=0),
        ]
    )
    small_rows = 16
    small = jnp.pad(small, (0, small_rows * model - small.shape[0])).reshape(small_rows, model)
    small = small.astype(BF)
    small_other = partner(small)
    narrow_way, normed_give, small_other, token = tie(narrow_way, normed_give, small_other, token)
    narrow_way, token = narrow_steps.send((narrow_way, [token]))
    ready = own_ready(wide_ready + pair) + [(0, first_other, True)]
    wide_way, pair = wide_steps.send(wide_way)
    normed_sibling = ring.sibling(normed_give)
    wide_results = wide.unpack(own_ready(pair), wide_results, [token], HEAVY)
    normed_sibling, token = tie(normed_sibling, wide_results[-1])
    normed_part = both(normed_own, normed_sibling).astype(BF)
    normed_part, token = tie(normed_part, token)
    lot, token = stacked_pair(pair, token, 2)
    ready_lots = [lot]
    normed_other = partner(normed_part)
    narrow_way, token = tie(narrow_way, token)
    for step in range(steps - 3):
        narrow_way, token = narrow_steps.send((narrow_way, [token]))
        if step == 0:
            wide_results = wide.unpack(ready, wide_results, [token], LITTLE)
            token = wide_results[-1]
        if step < steps - 4:
            wide_way, pair = wide_steps.send(wide_way)
            wide_results = wide.unpack(own_ready(pair), wide_results, [token])
            lot, token = stacked_pair(pair, wide_results[-1])
            ready_lots.append(lot)
            wide_way, token = tie(wide_way, token)
    narrow_way, wide_way, normed_other, token = tie(narrow_way, wide_way, normed_other, token)
    wide_way, pair = wide_steps.send(wide_way)
    narrow_shard, token = narrow_steps.send((narrow_way, [token]))

    small = both(small, small_other)
    gathered = Gradients(ring, narrow_rows + small_rows, model, narrow.outs, small_rows)
    narrow_steps = gathered.gather(jnp.concatenate([narrow_shard, small.astype(BF)], axis=0), True)
    narrow_way, narrow_ready = next(narrow_steps)

    narrow_results = None
    for step in range(1, steps + 1):
        share = -(-len(ready_lots) // max(1, steps - step)) if step > 1 else 1
        lots, ready_lots = ready_lots[:share], ready_lots[share:]
        own = own_ready(narrow_ready)
        if step == 1:
            flown, token = fly(lots, token)
            wide_results = wide.unpack(own_ready(pair), wide_results, [token], HEAVY)
            lot, token = stacked_pair(pair, wide_results[-1])
            ready_lots.append(lot)
            narrow_ready = [(offset, tie(part, token)[0]) for offset, part in narrow_ready]
            wide_results, token = land(flown, wide_results, token, HEAVY)
        else:
            flown, token = fly(lots, token)
            price = HEAVY
            if step == 2:
                layer_out, residual_grad, token = finish(
                    lax.dynamic_slice_in_dim(span_order, 2 * index, 2), residual, mixed, mixed_grad,
                    [normed_part, normed_other], [layer_part, layer_other], attn_gain.reshape(1, -1),
                    [token], HEAVY,
                )
                wide_way, token = tie(wide_way, token)
                _, pair = wide_steps.send(wide_way)
                wide_results = wide.unpack(own_ready(pair), wide_results, [token], price)
                lot, token = stacked_pair(pair, wide_results[-1])
                ready_lots.append(lot)
                price = 0
            elif not lots:
                narrow_results = gathered.unpack(own, narrow_results, [token], price)
                token = narrow_results[-1]
                own = []
            wide_results, token = land(flown, wide_results, token, price)
        narrow_results = gathered.unpack(own + other_ready(narrow_ready), narrow_results, [token])
        narrow_way, token = tie(narrow_way, narrow_results[-1])
        if step < steps:
            narrow_way, narrow_ready = narrow_steps.send(narrow_way)
    _, narrow_ready = narrow_steps.send(narrow_way)
    narrow_results = gathered.unpack(own_ready(narrow_ready), narrow_results, [token])
    query_sum, key_sum, value_sum, small, _ = gathered.unpack(
        other_ready(narrow_ready), narrow_results
    )
    gate_sum, up_sum, down_sum, out_weight_sum, _, _ = wide_results
    small = small.reshape(-1)

    attn_gain_grad, mlp_gain_grad = small[:model], small[model : 2 * model]
    query_gain_grad = small[2 * model : 2 * model + head_dim]
    key_gain_grad = small[2 * model + head_dim : 2 * model + 2 * head_dim]
    return (
        layer_out,
        residual_grad,
        attn_gain_grad,
        query_sum,
        key_sum,
        value_sum,
        query_gain_grad,
        key_gain_grad,
        out_weight_sum,
        mlp_gain_grad,
        gate_sum,
        up_sum,
        down_sum.reshape(units, model),
    )


def solution(mesh):
    return jax.shard_map(
        functools.partial(body, mesh.shape["cp"]),
        mesh=mesh,
        in_specs=(
            P("cp", None),
            P("cp", None),
            P(),
            P("cp"),
            P(),
            P(None, "tp"),
            P(None, "tp"),
            P(None, "tp"),
            P(),
            P(),
            P("tp", None),
            P(),
            P(None, "tp"),
            P(None, "tp"),
            P("tp", None),
        ),
        out_specs=(
            P("cp", None),
            P("cp", None),
            P(),
            P(None, "tp"),
            P(None, "tp"),
            P(None, "tp"),
            P(),
            P(),
            P("tp", None),
            P(),
            P(None, "tp"),
            P(None, "tp"),
            P("tp", None),
        ),
        check_vma=False,
    )
```

```python
import functools
import math

import jax
import jax.numpy as jnp
from jax import lax
from jax.experimental import pallas as pl
from jax.experimental.pallas import tpu as pltpu
from jax.sharding import PartitionSpec as P

EPS = 1e-06
ROPE_BASE = 1000000.0
HEAD = 128
LOG2E = 1.4426950408889634
VMEM_LIMIT = 16 * 1024 * 1024


def cost(microseconds):
    return pl.CostEstimate(
        flops=1024 + int(microseconds * 1e9), bytes_accessed=1024, transcendentals=0
    )


LIGHT = cost(0)
FORWARD = cost(1)
HEAVY = 50
SOME = 5
LITTLE = 4
BF = jnp.bfloat16
F32 = jnp.float32
TOKEN = jax.ShapeDtypeStruct((8, 128), jnp.float32)


def nn(a, b):
    return lax.dot_general(a, b, (((1,), (0,)), ((), ())), preferred_element_type=F32)


def nt(a, b):
    return lax.dot_general(a, b, (((1,), (1,)), ((), ())), preferred_element_type=F32)


def tn(a, b):
    return lax.dot_general(a, b, (((0,), (0,)), ((), ())), preferred_element_type=F32)


def norm_rows(values):
    scale_rows = lax.rsqrt(jnp.mean(values * values, axis=-1, keepdims=True) + EPS)
    return (values * scale_rows, scale_rows)


def norm_back(grad_normed, normed, scale_rows):
    return scale_rows * (
        grad_normed - normed * jnp.mean(grad_normed * normed, axis=-1, keepdims=True)
    )


def tie(*values):
    return lax.optimization_barrier(values)


def waits(after):
    return list(after), [pl.BlockSpec(memory_space=pl.ANY)] * len(after)


def in_hbm(x):
    return pltpu.with_memory_space_constraint(x, pltpu.HBM)


def ring_order(chips):
    if chips % 8:
        return list(range(chips))
    rows, cols = 4, chips // 4
    if cols % 2 or cols < 4:
        path = list(range(cols))
    else:
        path = list(range(cols // 2)) + list(range(cols - 1, cols // 2 - 1, -1))
    walk = []
    for row in range(rows):
        across = range(1, cols) if row % 2 == 0 else range(cols - 1, 0, -1)
        walk += [(row, col) for col in across]
    walk = [(0, 0)] + walk + [(row, 0) for row in range(rows - 1, 0, -1)]
    return [row * cols + path[col] for row, col in walk]


class Ring:
    def __init__(self, devices):
        self.devices = devices
        self.chips = devices // 2
        order = ring_order(self.chips)
        self.order = order
        size = self.chips
        self.up = [
            (2 * order[i] + core, 2 * order[(i + 1) % size] + core)
            for i in range(size)
            for core in range(2)
        ]
        self.down = [(b, a) for a, b in self.up]
        self.swap = [(i, i ^ 1) for i in range(devices)]
        place = [0] * size
        for i, chip in enumerate(order):
            place[chip] = i
        index = lax.axis_index("cp")
        self.core = index % 2
        self.here = jnp.asarray(place, jnp.int32)[index // 2]
        self.half = size // 2
        table = [
            [order[(place[chip] + i) % size] for i in range(size)] + [core]
            for chip in range(size)
            for core in range(2)
        ]
        self.table = lax.dynamic_index_in_dim(
            jnp.asarray(table, jnp.int32), index, 0, keepdims=False
        )

    def send_up(self, x):
        return lax.ppermute(x, "cp", self.up)

    def send_down(self, x):
        return lax.ppermute(x, "cp", self.down)

    def sibling(self, x):
        return lax.ppermute(x, "cp", self.swap)


def products(
    table, lefts, rights, chips, packed, row, column, before, after=(), thirds=1, halved=True, price=0
):
    tokens = lefts[0].shape[0]
    high = lefts[0].shape[1] // thirds // (2 if halved else 1)
    rows = high // chips
    wide = rights[0].shape[1]
    tile = min(wide, 512 if wide <= 1024 and thirds == 1 else 1024)
    last = table.shape[0] - 1
    more_args, more_specs = waits(after)
    if before is not None:
        more_args, more_specs = [before] + more_args, [pl.BlockSpec(memory_space=pl.ANY)] + more_specs
    side = len(lefts)

    def kernel(table_ref, *refs):
        out, token, turned = refs[side + len(rights) + len(more_args) :]

        @pl.when(pl.program_id(1) == 0)
        def _():
            for i in range(side):
                turned[:, i * tokens : (i + 1) * tokens] = refs[i][...].T
            token[...] = jnp.zeros_like(token)

        total, start = 0.0, 0
        for right in refs[side : side + len(rights)]:
            stop = start + right.shape[0]
            total = total + nn(turned[:, start:stop], right[...])
            start = stop
        out[...] = total.reshape(chips, rows, tile).astype(BF)

    def left_place(j, i, t):
        return (0, 2 * j + t[last] if halved else j)

    across = packed[1] // tile

    def out_place(j, i, t):
        at = column // tile + i
        return (0, row // rows + j + at // across, at % across)

    shape = (chips, *packed)
    return pl.pallas_call(
        kernel,
        out_shape=[jax.ShapeDtypeStruct(shape, BF), TOKEN],
        grid_spec=pltpu.PrefetchScalarGridSpec(
            num_scalar_prefetch=1,
            grid=(thirds, wide // tile),
            in_specs=[pl.BlockSpec((tokens, high), left_place)] * side
            + [pl.BlockSpec((right.shape[0], tile), lambda j, i, t: (0, i)) for right in rights]
            + more_specs,
            out_specs=[
                pl.BlockSpec((chips, rows, tile), out_place),
                pl.BlockSpec((8, 128), lambda j, i, t: (0, 0)),
            ],
            scratch_shapes=[pltpu.VMEM((high, side * tokens), BF)],
        ),
        input_output_aliases={} if before is None else {1 + side + len(rights): 0},
        compiler_params=pltpu.CompilerParams(vmem_limit_bytes=VMEM_LIMIT),
        cost_estimate=cost(price),
    )(table, *lefts, *rights, *more_args)


class Gradients:
    def __init__(self, ring, rows, columns, outs, added=0):
        self.ring, self.rows, self.columns, self.outs = ring, rows, columns, outs
        self.added = added
        self.cut = -(-rows // 32) * 16
        self.extra = []
        self.packs = []

    def shards(self, offsets, received, halves, after=()):
        ring, columns, rows, cut = self.ring, self.columns, self.rows, self.cut
        spans = [(0, cut), (cut, rows)]
        sides, count = len(offsets), len(self.packs)
        args, specs = [], []
        for offset in offsets:
            for _, pack in self.packs:
                args.append(pack)
                specs.append(
                    pl.BlockSpec(
                        (1, *pack.shape[1:]), lambda i, t, at=offset: (t[at % ring.chips], 0, 0)
                    )
                )
        extra = self.extra if halves == "sum" else []
        added = extra[0].shape[0] if extra else 0
        args += [*received, *extra]
        specs += [pl.BlockSpec(x.shape, lambda i, t: (0, 0)) for x in [*received, *extra]]
        more_args, more_specs = waits(after)
        taken = len(args) + len(more_args)

        def kernel(table_ref, *refs):
            outs = refs[taken:]
            outs[-1][...] = jnp.zeros_like(outs[-1])
            gained = refs[sides * count : sides * count + len(received)]
            if extra:
                one, other = refs[len(args) - 2 : len(args)]
                outs[0][rows:] = both(one[...], other[...]).astype(BF)
            for side in range(sides):
                for number, (row, pack) in enumerate(self.packs):
                    mine = refs[side * count + number]
                    stop = row + pack.shape[1]
                    if halves == "send":
                        for out, (start, end) in zip(outs, spans):
                            first, last = max(row, start), min(stop, end)
                            if first < last:
                                out[first - start : last - start] = mine[0, first - row : last - row]
                        continue
                    start, end = spans[side] if halves == "add" else (0, rows)
                    for first, last, more in (
                        (row, min(stop, start), False),
                        (max(row, start), min(stop, end), True),
                        (max(row, end), stop, False),
                    ):
                        if first < last:
                            part = mine[0, first - row : last - row]
                            if more:
                                part = part.astype(F32)
                                for got in gained if halves == "sum" else [gained[side]]:
                                    part = part + got[first - start : last - start].astype(F32)
                            outs[side][first:last] = part.astype(BF)

        highs = {"send": [cut, rows - cut], "sum": [rows + added]}.get(halves, [rows, rows])
        return pl.pallas_call(
            kernel,
            out_shape=[jax.ShapeDtypeStruct((high, columns), BF) for high in highs] + [TOKEN],
            grid_spec=pltpu.PrefetchScalarGridSpec(
                num_scalar_prefetch=1,
                grid=(1,),
                in_specs=specs + more_specs,
                out_specs=[pl.BlockSpec((high, columns), lambda i, t: (0, 0)) for high in highs]
                + [pl.BlockSpec((8, 128), lambda i, t: (0, 0))],
            ),
            compiler_params=pltpu.CompilerParams(vmem_limit_bytes=VMEM_LIMIT),
            cost_estimate=LIGHT,
        )(ring.table, *args, *more_args)

    def scatter(self, after=()):
        ring = self.ring
        up, down, token = self.shards([ring.half], [], "send", after)
        for step in range(ring.half - 1, -1, -1):
            (up, down), after = yield (ring.send_up(up), ring.send_down(down)), token
            if step:
                kind = "add" if step == ring.half - 1 else ""
                up, down, token = self.shards([step, -step], [up, down], kind, after)
        yield self.shards([0], [up, down], "sum", after)

    def gather(self, own, split=False):
        ring, cut = self.ring, self.cut
        up = down = own
        ready = [(0, own)]
        for step in range(1, ring.half):
            up, down = yield (ring.send_up(up), ring.send_down(down)), ready
            ready = [(-step, up), (step, down)]
        high, low = yield (ring.send_up(up[:cut]), ring.send_down(down[cut:])), ready
        if split:
            yield None, [(ring.half, high), (ring.half, low)]
        else:
            yield None, [(ring.half, jnp.concatenate([high, low], axis=0))]

    def unpack_stack(self, stack, offsets, before, after=(), price=0):
        return self.unpack(
            [(offset, stack, True) for offset in offsets], before, after, price, True
        )

    def unpack(self, ready, before, after=(), price=0, stacked=False):
        ring, outs, added = self.ring, self.outs, max(self.added, 8)
        count = len(ready)
        parts = [part if isinstance(part, tuple) else (part, None) for _, part, _ in ready]
        args = []
        for array, _ in parts:
            if not any(array is x for x in args):
                args.append(array)
        which = [next(j for j, x in enumerate(args) if x is array) for array, _ in parts]
        highs = [array.shape[-2] for array, _ in parts]
        places_of = [(offset, other) for offset, _, other in ready]

        def write(part, start, results):
            stop = start + part.shape[0]
            for out, (_, _, _, moves) in zip(results, outs):
                for lead, across, (first, last), columns in moves:
                    low, high = max(first, start), min(last, stop)
                    if low < high:
                        rows = slice(low - first, high - first)
                        where = (rows, across) if lead is None else (lead, rows, across)
                        out[where] = part[low - start : high - start, columns].astype(F32)

        def start_of(i):
            same = [j for j in range(i) if places_of[j] == places_of[i]]
            return sum(highs[j] for j in same)

        starts = [0] * count if stacked else [start_of(i) for i in range(count)]

        def kernel(table_ref, *refs):
            step = pl.program_id(0)

            def part_of(i):
                ref, at = refs[which[i]], parts[i][1]
                return ref if at is None else ref.at[at]

            results = refs[-len(outs) - 2 : -2]
            refs[-1][...] = jnp.zeros_like(refs[-1])
            total = refs[-2]

            @pl.when(step == 0)
            def _():
                total[...] = jnp.zeros_like(total) if before is None else refs[sum_place][...]

            if self.added and stacked:
                total[...] += refs[0][0, self.rows - added :].astype(F32)
            elif self.added:
                for i in range(count):
                    if starts[i] + highs[i] == self.rows:

                        @pl.when(step == i)
                        def _(i=i):
                            total[...] += part_of(i)[highs[i] - added :].astype(F32)

            if stacked:
                write(refs[0].at[0], 0, results)
                return
            for i in range(count):
                pl.when(step == i)(functools.partial(write, part_of(i), starts[i], results))

        def place(of_chip, i, table):
            chip, core = None, None
            for j, (offset, other) in enumerate(places_of):
                here = table[offset % ring.chips]
                mine = table[ring.chips]
                mine = 1 - mine if other else mine
                chip = here if chip is None else jnp.where(i == j, here, chip)
                core = mine if core is None else jnp.where(i == j, mine, core)
            return of_chip(chip, core)

        shapes, out_specs = [], []
        for shape, block, of_chip, _ in outs:
            shapes.append(pltpu.HBM(shape, F32))
            out_specs.append(pl.BlockSpec(block, functools.partial(place, of_chip)))
        shapes += [jax.ShapeDtypeStruct((added, self.columns), F32), TOKEN]
        out_specs.append(pl.BlockSpec((added, self.columns), lambda i, t: (0, 0)))
        out_specs.append(pl.BlockSpec((8, 128), lambda i, t: (0, 0)))
        if stacked:
            specs = [pl.BlockSpec((1, self.rows, self.columns), lambda i, t: (i, 0, 0))]
        else:
            specs = [pl.BlockSpec(x.shape, lambda i, t, n=x.ndim: (0,) * n) for x in args]
        aliases = {}
        if before is not None:
            aliases = {1 + len(args) + i: i for i in range(len(outs))}
            specs += [pl.BlockSpec(memory_space=pl.ANY)] * len(outs)
            args += [in_hbm(x) for x in before[: len(outs)]]
            sum_place = len(args)
            args.append(before[len(outs)])
            specs.append(pl.BlockSpec((added, self.columns), lambda i, t: (0, 0)))
        more_args, more_specs = waits(after)
        args += more_args
        specs += more_specs
        return list(
            pl.pallas_call(
                kernel,
                out_shape=shapes,
                grid_spec=pltpu.PrefetchScalarGridSpec(
                    num_scalar_prefetch=1, grid=(count,), in_specs=specs, out_specs=out_specs
                ),
                input_output_aliases=aliases,
                compiler_params=pltpu.CompilerParams(vmem_limit_bytes=VMEM_LIMIT),
                cost_estimate=cost(price),
            )(ring.table, *args)
        )


def stack(parts, after=(), price=0):
    rows, columns = parts[0].shape
    count = len(parts)
    more_args, more_specs = waits(after)

    def kernel(*refs):
        out, token = refs[-2:]
        token[...] = jnp.zeros_like(token)
        for i in range(count):

            @pl.when(pl.program_id(0) == i)
            def _(i=i):
                out[0] = refs[i][...]

    return pl.pallas_call(
        kernel,
        out_shape=[jax.ShapeDtypeStruct((count, rows, columns), parts[0].dtype), TOKEN],
        grid=(count,),
        in_specs=[pl.BlockSpec((rows, columns), lambda i: (0, 0))] * count + more_specs,
        out_specs=[
            pl.BlockSpec((1, rows, columns), lambda i: (i, 0, 0)),
            pl.BlockSpec((8, 128), lambda i: (0, 0)),
        ],
        compiler_params=pltpu.CompilerParams(vmem_limit_bytes=VMEM_LIMIT),
        cost_estimate=cost(price),
    )(*parts, *more_args)


def pair_add(own, received, half, after=()):
    more_args, more_specs = waits(after)

    def kernel(*refs):
        refs, outs = refs[:4], refs[4 + len(more_args) :]
        outs[-1][...] = jnp.zeros_like(outs[-1])
        for side in range(2):
            mine, got, out = refs[side], refs[2 + side], outs[side]
            if half:
                rows = got.shape[0]
                here = slice(side * rows, (side + 1) * rows)
                rest = slice((1 - side) * rows, (2 - side) * rows)
                out[here] = (mine[here].astype(F32) + got[...].astype(F32)).astype(BF)
                out[rest] = mine[rest]
            else:
                out[...] = (mine[...].astype(F32) + got[...].astype(F32)).astype(BF)

    shape = jax.ShapeDtypeStruct(own[0].shape, BF)
    return pl.pallas_call(
        kernel,
        out_shape=[shape, shape, TOKEN],
        in_specs=[pl.BlockSpec(memory_space=pltpu.VMEM)] * 4 + more_specs,
        compiler_params=pltpu.CompilerParams(vmem_limit_bytes=VMEM_LIMIT),
        cost_estimate=LIGHT,
    )(*own, *received, *more_args)


def partner(x):
    return lax.ppermute(x, "tp", [(0, 1), (1, 0)])


def both(mine, other):
    return mine.astype(F32) + other.astype(F32)


def turn(values, cosine, sine):
    return values * cosine + pltpu.roll(values, values.shape[-1] // 2, 1) * sine


def turn_back(values, cosine, sine):
    return values * cosine - pltpu.roll(values, values.shape[-1] // 2, 1) * sine


def lower_first(order, table, other):
    core = table[table.shape[0] - 1]
    device = 2 * table[0] + (1 - core if other else core)
    return order[2 * device] < order[2 * device + 1]


def key_value_kernel(
    order, table, residuals, cotangent, gain, key_weight, value_weight, key_gain, angles, outs
):
    residual_out, cotangent_out, normed_outs, raw_outs, cosine_outs, sine_outs, packed_outs = outs
    width = key_gain.shape[1]
    span = residuals[0].shape[0] // 2
    for pair in range(2):
        start = jnp.where(lower_first(order, table, pair == 1), 0, span)

        def canonical(ref):
            return jnp.concatenate(
                [
                    ref[pl.ds(pl.multiple_of(start, span), span)],
                    ref[pl.ds(pl.multiple_of(span - start, span), span)],
                ],
                axis=0,
            )

        rows = canonical(residuals[pair])
        if pair == 0:
            residual_out[...] = rows
            cotangent_out[...] = canonical(cotangent)
        unit, _ = norm_rows(rows.astype(F32))
        normed = (unit * gain[...]).astype(BF)
        normed_outs[pair][...] = normed
        cosine, sine = canonical(angles[2 * pair]), canonical(angles[2 * pair + 1])
        cosine_outs[pair][...], sine_outs[pair][...] = cosine, sine
        raw = nn(normed, key_weight[...])
        raw_outs[pair][...] = raw
        values = nn(normed, value_weight[...]).astype(BF)
        for group in range(raw.shape[1] // width):
            here = slice(group * width, (group + 1) * width)
            key_unit, _ = norm_rows(raw[:, here])
            packed = packed_outs[pair]
            packed[:, 2 * group * width : (2 * group + 1) * width] = turn(
                key_unit * key_gain[...], cosine, sine
            ).astype(BF)
            packed[:, (2 * group + 1) * width : (2 * group + 2) * width] = values[:, here]


def query_kernel(normeds, weight, gain, cosines, sines, raw_outs, low_outs):
    width = gain.shape[1]
    for pair in range(2):
        raw = nn(normeds[pair][...], weight[...])
        raw_outs[pair][...] = raw
        for head in range(raw.shape[1] // width):
            here = slice(head * width, (head + 1) * width)
            unit, _ = norm_rows(raw[:, here])
            low_outs[pair][:, here] = turn(
                unit * gain[...], cosines[pair][...], sines[pair][...]
            ).astype(BF)


def heads_back(grad_of, raws, gain, cosines, sines, out, total):
    width = gain.shape[1]
    rows = raws[0].shape[0]
    for pair in range(2):
        here_rows = slice(pair * rows, (pair + 1) * rows)
        for head in range(raws[pair].shape[1] // width):
            here = slice(head * width, (head + 1) * width)
            unit, scale_rows = norm_rows(raws[pair][:, here])
            turned = turn_back(grad_of(pair, head), cosines[pair][...], sines[pair][...])
            total = total + jnp.sum((turned * unit).reshape(-1, 8, width), axis=0)
            out[here_rows, here] = norm_back(turned * gain[...], unit, scale_rows).astype(BF)
    return total


def query_back_kernel(grads, raws, gain, cosines, sines, low_out, gain_out):
    width = gain.shape[1]
    gain_out[...] = heads_back(
        lambda pair, head: grads[pair][:, head * width : (head + 1) * width],
        raws, gain, cosines, sines, low_out, jnp.zeros((8, width), F32),
    )


def key_value_back_kernel(owns, upward, downward, raws, gain, cosines, sines, low_out, gain_out):
    width = gain.shape[1]
    rows, columns = raws[0].shape
    groups = columns // width

    def summed(pair, place):
        here = slice(place * width, (place + 1) * width)
        at = slice(pair * rows, (pair + 1) * rows)
        return (
            owns[pair][:, here].astype(F32)
            + upward[at, here].astype(F32)
            + downward[at, here].astype(F32)
        )

    gain_out[...] = heads_back(
        lambda pair, head: summed(pair, 2 * head),
        raws, gain, cosines, sines, low_out, jnp.zeros((8, width), F32),
    )
    for pair in range(2):
        for group in range(groups):
            low_out[
                pair * rows : (pair + 1) * rows,
                columns + group * width : columns + (group + 1) * width,
            ] = summed(pair, 2 * group + 1).astype(BF)


def whole_call(kernel, scalars, outs, args, after=()):
    more_args, more_specs = waits(after)
    count = len(scalars)
    arrays, specs = [], []
    for arg in args:
        array, block, place = arg if isinstance(arg, tuple) else (arg, arg.shape, None)
        arrays.append(array)
        if place is None:
            specs.append(pl.BlockSpec(block, lambda i, *t: (0, 0)))
        else:
            specs.append(
                pl.BlockSpec(
                    block, lambda i, *t, place=place: place(t[-1][t[-1].shape[0] - 1])
                )
            )
    taken = count + len(args)

    def run(*refs):
        kernel(*refs[:taken], *refs[taken + len(more_args) :])

    return list(
        pl.pallas_call(
            run,
            out_shape=[
                pltpu.HBM(shape, dtype) if far else jax.ShapeDtypeStruct(shape, dtype)
                for shape, dtype, *far in outs
            ],
            grid_spec=pltpu.PrefetchScalarGridSpec(
                num_scalar_prefetch=count,
                grid=(1,),
                in_specs=specs + more_specs,
                out_specs=[pl.BlockSpec(shape, lambda i, *t: (0, 0)) for shape, *_ in outs],
            ),
            compiler_params=pltpu.CompilerParams(vmem_limit_bytes=VMEM_LIMIT),
            cost_estimate=LIGHT,
        )(*scalars, *arrays, *more_args)
    )


def matmul(left, right, after=(), price=0):
    rows, inner = left.shape
    columns = right.shape[1]
    tile = min(columns, 512)
    more_args, more_specs = waits(after)

    def kernel(left_ref, right_ref, *refs):
        refs[-1][...] = nn(left_ref[...], right_ref[...]).astype(BF)

    return pl.pallas_call(
        kernel,
        out_shape=jax.ShapeDtypeStruct((rows, columns), BF),
        grid=(columns // tile,),
        in_specs=[
            pl.BlockSpec((rows, inner), lambda i: (0, 0)),
            pl.BlockSpec((inner, tile), lambda i: (0, i)),
        ]
        + more_specs,
        out_specs=pl.BlockSpec((rows, tile), lambda i: (0, i)),
        compiler_params=pltpu.CompilerParams(vmem_limit_bytes=VMEM_LIMIT),
        cost_estimate=cost(price),
    )(left, in_hbm(right), *more_args)


def add_and_norm(part, other, residual, half, gain, price=0):
    rows, columns = part.shape

    def kernel(part_ref, other_ref, residual_ref, gain_ref, total, low):
        both_parts = part_ref[...].astype(F32) + other_ref[...].astype(F32)
        mixed = residual_ref[...].astype(F32) + both_parts
        total[...] = mixed
        normed, _ = norm_rows(mixed)
        low[...] = (normed * gain_ref[...]).astype(BF)

    whole = pl.BlockSpec((rows, columns), lambda i: (0, 0))
    return pl.pallas_call(
        kernel,
        out_shape=[
            jax.ShapeDtypeStruct((rows, columns), F32),
            jax.ShapeDtypeStruct((rows, columns), BF),
        ],
        grid=(1,),
        in_specs=[
            whole,
            whole,
            pl.BlockSpec((rows, columns), lambda i: (half, 0)),
            pl.BlockSpec((1, columns), lambda i: (0, 0)),
        ],
        out_specs=[whole, whole],
        compiler_params=pltpu.CompilerParams(vmem_limit_bytes=VMEM_LIMIT),
        cost_estimate=cost(price),
    )(part, other, residual, gain)


def finish(order, residual, mixed, mixed_grad, normed_parts, layer_parts, gain, after, price):
    rows, columns = residual.shape
    span = rows // 2
    more_args, more_specs = waits(after)

    def kernel(order_ref, row, mix, mix_grad, normed0, normed1, layer0, layer1, gain_ref, *refs):
        out, grad, token = refs[-3:]
        out[...] = (mix[...] + both(layer0[...], layer1[...])).astype(BF)
        normed, scale = norm_rows(row[...].astype(F32))
        normed_grad = both(normed0[...], normed1[...]) * gain_ref[...]
        grad[...] = mix_grad[...] + norm_back(normed_grad, normed, scale)
        token[...] = jnp.zeros_like(token)

    part = pl.BlockSpec((span, columns), lambda i, o: (i, 0))
    placed = pl.BlockSpec((span, columns), lambda i, o: (jnp.where(o[0] < o[1], i, 1 - i), 0))
    return pl.pallas_call(
        kernel,
        out_shape=[
            jax.ShapeDtypeStruct((rows, columns), BF),
            jax.ShapeDtypeStruct((rows, columns), F32),
            TOKEN,
        ],
        grid_spec=pltpu.PrefetchScalarGridSpec(
            num_scalar_prefetch=1,
            grid=(2,),
            in_specs=[part] * 7 + [pl.BlockSpec((1, columns), lambda i, o: (0, 0))] + more_specs,
            out_specs=[placed, placed, pl.BlockSpec(TOKEN.shape, lambda i, o: (0, 0))],
        ),
        compiler_params=pltpu.CompilerParams(vmem_limit_bytes=VMEM_LIMIT),
        cost_estimate=cost(price),
    )(order, residual, mixed, mixed_grad, *normed_parts, *layer_parts, gain, *more_args)


def out_projection(table, rows, weight, other, before=None):
    high, inner = rows.shape
    columns = weight.shape[1]
    tile = min(inner, 256)
    count = inner // tile
    last = table.shape[0] - 1
    dtype = F32 if before is None else BF

    def kernel(table_ref, rows_ref, weight_ref, *refs):
        out, total = refs[-2:]
        step = pl.program_id(0)
        part = nn(rows_ref[...], weight_ref[...])

        @pl.when(step == 0)
        def _():
            total[...] = part if before is None else part + refs[0][...]

        @pl.when(step > 0)
        def _():
            total[...] += part

        @pl.when(step == count - 1)
        def _():
            out[...] = total[...].astype(dtype)

    whole = pl.BlockSpec((high, columns), lambda i, t: (0, 0))
    extra = [] if before is None else [before]
    return pl.pallas_call(
        kernel,
        out_shape=jax.ShapeDtypeStruct((high, columns), dtype),
        grid_spec=pltpu.PrefetchScalarGridSpec(
            num_scalar_prefetch=1,
            grid=(count,),
            in_specs=[
                pl.BlockSpec((high, tile), lambda i, t: (0, i)),
                pl.BlockSpec(
                    (tile, columns),
                    lambda i, t: ((1 - t[last] if other else t[last]) * count + i, 0),
                ),
            ]
            + [whole] * len(extra),
            out_specs=whole,
            scratch_shapes=[pltpu.VMEM((high, columns), F32)],
        ),
        compiler_params=pltpu.CompilerParams(vmem_limit_bytes=VMEM_LIMIT),
        cost_estimate=LIGHT,
    )(table, rows, weight, *extra)


def heads_products(table, rows, weight, after=()):
    high, columns = rows[0].shape
    inner = weight.shape[0] // 2
    tile = min(inner, 256)
    count = inner // tile
    last = table.shape[0] - 1
    more_args, more_specs = waits(after)

    def kernel(table_ref, first, second, mine, *refs):
        refs[-2][...] = nt(first[...], mine[...]).astype(BF)
        refs[-1][...] = nt(second[...], mine[...]).astype(BF)

    shape = jax.ShapeDtypeStruct((high, inner), BF)
    spec = pl.BlockSpec((high, tile), lambda i, t: (0, i))
    whole = pl.BlockSpec((high, columns), lambda i, t: (0, 0))
    return pl.pallas_call(
        kernel,
        out_shape=[shape, shape],
        grid_spec=pltpu.PrefetchScalarGridSpec(
            num_scalar_prefetch=1,
            grid=(count,),
            in_specs=[
                whole,
                whole,
                pl.BlockSpec((tile, columns), lambda i, t: (t[last] * count + i, 0)),
            ]
            + more_specs,
            out_specs=[spec, spec],
        ),
        compiler_params=pltpu.CompilerParams(vmem_limit_bytes=VMEM_LIMIT),
        cost_estimate=LIGHT,
    )(table, *rows, in_hbm(weight), *more_args)


def normed_products(
    table, normeds, query_grad, key_value_grad, query_weight, key_weight, value_weight, after=()
):
    rows, wide = query_grad.shape
    narrow = key_value_grad.shape[1] // 2
    columns = query_weight.shape[0]
    tile = min(columns, 256)
    last = table.shape[0] - 1
    more_args, more_specs = waits(after)

    def kernel(table_ref, first, second, queries, others, query, key, value, *refs):
        total = (
            nt(queries[...], query[...])
            + nt(others[:, :narrow], key[...])
            + nt(others[:, narrow:], value[...])
        ).astype(BF)
        upper, lower = total[: rows // 2], total[rows // 2 :]
        refs[-3][...] = upper
        refs[-2][...] = lower
        term = upper.astype(F32) * first[...].astype(F32) + lower.astype(F32) * second[...].astype(F32)
        refs[-1][...] = jnp.sum(term.reshape(-1, 8, tile), axis=0)

    shape = pltpu.HBM((rows // 2, columns), BF)
    spec = pl.BlockSpec((rows // 2, tile), lambda i, t: (0, i))
    return pl.pallas_call(
        kernel,
        out_shape=[shape, shape, jax.ShapeDtypeStruct((8, columns), F32)],
        grid_spec=pltpu.PrefetchScalarGridSpec(
            num_scalar_prefetch=1,
            grid=(columns // tile,),
            in_specs=[
                spec,
                spec,
                pl.BlockSpec((rows, wide), lambda i, t: (0, 0)),
                pl.BlockSpec((rows, 2 * narrow), lambda i, t: (0, 0)),
                pl.BlockSpec((tile, wide), lambda i, t: (i, t[last])),
                pl.BlockSpec((tile, narrow), lambda i, t: (i, t[last])),
                pl.BlockSpec((tile, narrow), lambda i, t: (i, t[last])),
            ]
            + more_specs,
            out_specs=[spec, spec, pl.BlockSpec((8, tile), lambda i, t: (0, i))],
        ),
        compiler_params=pltpu.CompilerParams(vmem_limit_bytes=VMEM_LIMIT),
        cost_estimate=cost(HEAVY),
    )(
        table, *normeds, query_grad, key_value_grad, in_hbm(query_weight), in_hbm(key_weight),
        in_hbm(value_weight), *more_args,
    )


def stacked(ref, start, span, width):
    rows = pl.ds(start, span)
    return jnp.concatenate([ref[rows, :width], ref[rows, width:]], axis=0)


def causal(span, transposed):
    shape = (span, 2 * span) if transposed else (2 * span, span)
    key = lax.broadcasted_iota(jnp.int32, shape, 0 if transposed else 1)
    row = lax.broadcasted_iota(jnp.int32, shape, 1 if transposed else 0)
    return key <= row % span


def side_met(order, table, pair, offset, other):
    last = table.shape[0] - 1
    core = table[last]

    def lower(device):
        return jnp.minimum(order[2 * device], order[2 * device + 1])

    mine = lower(2 * table[0] + (1 - core if pair else core))
    theirs = lower(2 * table[offset % last] + (1 - core if other else core))
    return jnp.where(theirs < mine, 0, 1)


def forward_kernel(places, own, last, span, width, order, table, *refs):
    count = len(places)
    queries, blocks, refs = refs[:2], refs[2 : 2 + count], refs[2 + count :]
    scale = LOG2E / math.sqrt(width)
    if own:
        before, outs = None, refs
    else:
        before, outs = refs[0], refs[1:]
    accum = outs[-1]
    ones = jnp.ones((span, width), BF)

    def weighted(rows, keys, values, allowed=None):
        scores = nt(rows, keys)
        probs = jnp.exp2(scores * scale)
        if allowed is not None:
            probs = jnp.where(allowed, probs, 0.0)
        return nn(probs.astype(BF), values)

    def extended(block, start):
        return jnp.concatenate([block[pl.ds(start, span), width:], ones], axis=1)

    keys = jnp.concatenate([block[:span, :width] for block in blocks], axis=0)
    values = jnp.concatenate([extended(block, 0) for block in blocks], axis=0)
    rows = jnp.concatenate([stacked(query, span, span, width) for query in queries], axis=0)
    high = weighted(rows, keys, values)
    for pair in range(2):
        part = high[pair * 2 * span : (pair + 1) * 2 * span]
        if own:
            allowed = causal(span, False)
            for side in range(2):
                block, start = blocks[pair], side * span
                met = weighted(
                    stacked(queries[pair], start, span, width),
                    block[start : start + span, :width],
                    extended(block, start),
                    allowed,
                )
                accum[0, pair, side] = met + part if side else met
        else:
            accum[0, pair, 0] = before[0, pair, 0]
            accum[0, pair, 1] = before[0, pair, 1] + part
    for i, (offset, other) in enumerate(places):
        for pair in range(2):
            if own and i == pair:
                continue
            side = side_met(order, table, pair, offset, other)
            start = pl.multiple_of(side * span, span)
            accum[0, pair, side] += weighted(
                stacked(queries[pair], start, span, width),
                blocks[i][pl.ds(start, span), :width],
                extended(blocks[i], start),
            )
    if last:
        wides, lows, logs = outs[0:2], outs[2:4], outs[4]
        for pair in range(2):
            for side in range(2):
                rows = slice(side * span, (side + 1) * span)
                whole = accum[0, pair, side]
                mass = whole[:, width:]
                out = whole[:, :width] / mass
                for head in range(2):
                    part = out[head * span : (head + 1) * span]
                    columns = slice(head * width, (head + 1) * width)
                    wides[pair][rows, columns] = part
                    lows[pair][rows, columns] = part.astype(BF)
                logs[0, pair, side] = jnp.log2(mass).T[:8]


def attention_forward(scalars, queries, blocks, places, before, own, last, after=()):
    rows, columns = queries[0].shape
    span, width = rows // 2, HEAD
    groups = columns // (2 * width)
    tile = pl.BlockSpec((rows, 2 * width), lambda g: (0, g))
    accum_block = (1, 2, 2, 2 * span, 2 * width)
    accum_spec = pl.BlockSpec(accum_block, lambda g: (g, 0, 0, 0, 0))
    args = [*scalars, *queries, *(in_hbm(block) for block in blocks)]
    specs = [pl.BlockSpec(memory_space=pltpu.SMEM)] * 2 + [tile] * (2 + len(blocks))
    if not own:
        args.append(before)
        specs.append(accum_spec)
    taken = len(args)
    more_args, more_specs = waits(after)
    scratch = []
    if last:
        wide, low = pltpu.HBM((rows, columns), F32), jax.ShapeDtypeStruct((rows, columns), BF)
        outs = [wide, wide, low, low, jax.ShapeDtypeStruct((groups, 2, 2, 8, 2 * span), F32), TOKEN]
        out_specs = [tile] * 4 + [
            pl.BlockSpec((1, 2, 2, 8, 2 * span), lambda g: (g, 0, 0, 0, 0)),
            pl.BlockSpec((8, 128), lambda g: (0, 0)),
        ]
        scratch = [pltpu.VMEM(accum_block, F32)]
    else:
        outs = [jax.ShapeDtypeStruct((groups, *accum_block[1:]), F32), TOKEN]
        out_specs = [accum_spec, pl.BlockSpec((8, 128), lambda g: (0, 0))]

    def kernel(*refs):
        refs = refs[:taken] + refs[taken + len(more_args) :]
        place = -2 if last else -1
        refs[place][...] = jnp.zeros_like(refs[place])
        refs = refs[:place] + (refs[-1:] if last else ())
        forward_kernel(places, own, last, span, width, *refs)

    return pl.pallas_call(
        kernel,
        out_shape=outs,
        grid=(groups,),
        in_specs=specs + more_specs,
        out_specs=out_specs,
        scratch_shapes=scratch,
        input_output_aliases={} if own or last else {taken - 1: 0},
        compiler_params=pltpu.CompilerParams(vmem_limit_bytes=VMEM_LIMIT),
        cost_estimate=FORWARD,
    )(*args, *more_args)


def delta_kernel(grads, outs, delta):
    for pair in range(2):
        grad, out = grads[pair], outs[pair]
        width, span = grad.shape[1] // 2, grad.shape[0] // 2
        for side in range(2):
            rows = slice(side * span, (side + 1) * span)
            product = grad[rows, :].astype(F32) * out[rows, :]
            stack = jnp.concatenate([product[:, :width], product[:, width:]], axis=0)
            total = jnp.sum(stack.T, axis=0, keepdims=True)
            delta[0, pair, side] = jnp.broadcast_to(total, (8, 2 * span))


def attention_delta(grads, outs, after=()):
    rows, columns = grads[0].shape
    width, span = HEAD, rows // 2
    groups = columns // (2 * width)
    tile = pl.BlockSpec((rows, 2 * width), lambda g: (0, g))
    more_args, more_specs = waits(after)

    def kernel(*refs):
        delta_kernel(refs[:2], refs[2:4], refs[-1])

    return pl.pallas_call(
        kernel,
        out_shape=jax.ShapeDtypeStruct((groups, 2, 2, 8, 2 * span), F32),
        grid=(groups,),
        in_specs=[tile] * 4 + more_specs,
        out_specs=pl.BlockSpec((1, 2, 2, 8, 2 * span), lambda g: (g, 0, 0, 0, 0)),
        compiler_params=pltpu.CompilerParams(vmem_limit_bytes=VMEM_LIMIT),
        cost_estimate=LIGHT,
    )(*grads, *outs, *more_args)


def backward_kernel(places, own, first, last, split, span, width, order, table, *refs):
    count = len(places)
    queries, grads, (logs, delta), refs = refs[:2], refs[2:4], refs[4:6], refs[6:]
    blocks, refs = refs[:count], refs[count:]
    if not first:
        before, refs = refs[0], refs[1:]
    outs = refs[: count if split else count // 2]
    refs = refs[len(outs) :]
    refs[0][...] = jnp.zeros_like(refs[0])
    refs = refs[1:]
    if last:
        query_outs, accum = refs[:2], refs[2]
    else:
        accum = refs[0]
    scale = LOG2E / math.sqrt(width)
    factor = 1.0 / math.sqrt(width)

    def products(rows, row_grads, log, mean, keys, values, allowed=None):
        probs = jnp.exp2(nt(keys, rows) * scale - log)
        if allowed is not None:
            probs = jnp.where(allowed, probs, 0.0)
        prob_grad = nt(values, row_grads)
        score_grad = (probs * (prob_grad - mean)).astype(BF)
        return nn(score_grad, rows), nn(probs.astype(BF), row_grads), tn(keys, score_grad)

    def of_pair(pair, side, start, keys, values, allowed=None):
        return products(
            stacked(queries[pair], start, span, width),
            stacked(grads[pair], start, span, width),
            logs[0, pair, side, :1],
            delta[0, pair, side, :1],
            keys,
            values,
            allowed,
        )

    low_keys, low_values, high_query = products(
        jnp.concatenate([stacked(query, span, span, width) for query in queries], axis=0),
        jnp.concatenate([stacked(grad, span, span, width) for grad in grads], axis=0),
        jnp.concatenate([logs[0, pair, 1, :1] for pair in range(2)], axis=1),
        jnp.concatenate([delta[0, pair, 1, :1] for pair in range(2)], axis=1),
        jnp.concatenate([block[:span, :width] for block in blocks], axis=0),
        jnp.concatenate([block[:span, width:] for block in blocks], axis=0),
    )
    for pair in range(2):
        part = high_query[:, pair * 2 * span : (pair + 1) * 2 * span]
        if first:
            accum[0, pair, 0] = jnp.zeros_like(part)
            accum[0, pair, 1] = part
        else:
            accum[0, pair, 0] = before[0, pair, 0]
            accum[0, pair, 1] = before[0, pair, 1] + part
    for i, (offset, other) in enumerate(places):
        here = slice(i * span, (i + 1) * span)
        block = blocks[i]
        key_sums, value_sums = [low_keys[here], 0.0], [low_values[here], 0.0]
        for pair in range(2):
            if own and i == pair:
                allowed = causal(span, True)
                for side in range(2):
                    rows = slice(side * span, (side + 1) * span)
                    key_part, value_part, query_part = of_pair(
                        pair, side, side * span, block[rows, :width], block[rows, width:], allowed
                    )
                    accum[0, pair, side] += query_part
                    key_sums[side] = key_sums[side] + key_part
                    value_sums[side] = value_sums[side] + value_part
                continue
            side = side_met(order, table, pair, offset, other)
            start = pl.multiple_of(side * span, span)
            rows = pl.ds(start, span)
            key_part, value_part, query_part = of_pair(
                pair, side, start, block[rows, :width], block[rows, width:]
            )
            accum[0, pair, side] += query_part
            low = side == 0
            key_sums[0] = key_sums[0] + jnp.where(low, key_part, 0.0)
            value_sums[0] = value_sums[0] + jnp.where(low, value_part, 0.0)
            key_sums[1] = key_sums[1] + jnp.where(low, 0.0, key_part)
            value_sums[1] = value_sums[1] + jnp.where(low, 0.0, value_part)
        out = outs[i] if split else outs[i // 2]
        base = 0 if split else i % 2 * 2 * span
        for side in range(2):
            rows = slice(base + side * span, base + (side + 1) * span)
            out[rows, :width] = (key_sums[side] * factor).astype(BF)
            out[rows, width:] = value_sums[side].astype(BF)
    if last:
        for pair in range(2):
            for side in range(2):
                part = accum[0, pair, side].T * factor
                rows = slice(side * span, (side + 1) * span)
                query_outs[pair][rows, :width] = part[:span]
                query_outs[pair][rows, width:] = part[span:]


def attention_backward(
    scalars, queries, grads, logs, delta, blocks, places, before, own, last, split, after=()
):
    rows, columns = queries[0].shape
    span, width = rows // 2, HEAD
    groups = columns // (2 * width)
    count = len(blocks)
    first = before is None
    tile = pl.BlockSpec((rows, 2 * width), lambda g: (0, g))
    stat = pl.BlockSpec((1, 2, 2, 8, 2 * span), lambda g: (g, 0, 0, 0, 0))
    accum_block = (1, 2, 2, width, 2 * span)
    accum_spec = pl.BlockSpec(accum_block, lambda g: (g, 0, 0, 0, 0))
    args = [*scalars, *queries, *grads, logs, delta, *(in_hbm(block) for block in blocks)]
    specs = [pl.BlockSpec(memory_space=pltpu.SMEM)] * 2 + [tile] * 4 + [stat] * 2 + [tile] * count
    if not first:
        args.append(before)
        specs.append(accum_spec)
    taken = len(args)
    more_args, more_specs = waits(after)
    if split:
        outs = [jax.ShapeDtypeStruct((rows, columns), BF)] * count
        out_specs = [tile] * count
    else:
        outs = [jax.ShapeDtypeStruct((2 * rows, columns), BF)] * (count // 2)
        out_specs = [pl.BlockSpec((2 * rows, 2 * width), lambda g: (0, g))] * (count // 2)
    outs.append(TOKEN)
    out_specs.append(pl.BlockSpec((8, 128), lambda g: (0, 0)))
    scratch = []
    if last:
        outs += [jax.ShapeDtypeStruct((rows, columns), F32)] * 2
        out_specs += [tile] * 2
        scratch = [pltpu.VMEM(accum_block, F32)]
    else:
        outs.append(jax.ShapeDtypeStruct((groups, *accum_block[1:]), F32))
        out_specs.append(accum_spec)

    def kernel(*refs):
        refs = refs[:taken] + refs[taken + len(more_args) :]
        backward_kernel(places, own, first, last, split, span, width, *refs)

    return pl.pallas_call(
        kernel,
        out_shape=outs,
        grid=(groups,),
        in_specs=specs + more_specs,
        out_specs=out_specs,
        scratch_shapes=scratch,
        input_output_aliases={} if first or last else {taken - 1: len(outs) - 1},
        compiler_params=pltpu.CompilerParams(vmem_limit_bytes=VMEM_LIMIT),
        cost_estimate=cost(HEAVY),
    )(*args, *more_args)


def body(
    devices,
    residual,
    cotangent,
    span_order,
    positions,
    attn_gain,
    query_weight,
    key_weight,
    value_weight,
    query_gain,
    key_gain,
    out_weight,
    mlp_gain,
    gate_weight,
    up_weight,
    down_weight,
):
    ring = Ring(devices)
    rows, model = residual.shape
    head_dim = query_gain.shape[0]
    span = rows // 2
    index = lax.axis_index("cp")
    scalars = [span_order, ring.table]
    table = [ring.table]
    residual_other, positions_other = ring.sibling(residual), ring.sibling(positions)

    half = head_dim // 2
    freq = ROPE_BASE ** (-(jnp.arange(half, dtype=F32) * 2.0) / head_dim)
    angles = []
    for where in (positions, positions_other):
        angle = where.astype(F32)[:, None] * freq[None, :]
        cosine, sine = jnp.cos(angle), jnp.sin(angle)
        angles.append(jnp.concatenate([cosine, cosine], axis=1))
        angles.append(jnp.concatenate([-sine, sine], axis=1))

    query_gain_row = query_gain.reshape(1, -1)
    key_gain_row = key_gain.reshape(1, -1)
    key_columns = key_weight.shape[1]
    query_columns = query_weight.shape[1]
    few, each = key_columns // 2, query_columns // 2

    def project_keys(order, table_ref, first, second, grad, gain, key, value, row, c0, s0, c1, s1, *outs):
        key_value_kernel(
            order, table_ref, (first, second), grad, gain, key, value, row, (c0, s0, c1, s1),
            (outs[0], outs[1], outs[2:4], outs[4:6], outs[6:8], outs[8:10], outs[10:12]),
        )

    residual, cotangent, *results = whole_call(
        project_keys,
        scalars,
        [((rows, model), BF, 1)] * 2
        + [((rows, model), BF)] * 2
        + [((rows, few), F32, 1)] * 2
        + [((rows, head_dim), F32)] * 4
        + [((rows, key_columns), BF)] * 2,
        [
            in_hbm(residual), residual_other, in_hbm(cotangent), in_hbm(attn_gain.reshape(1, -1)),
            (in_hbm(key_weight), (model, few), lambda core: (0, core)),
            (in_hbm(value_weight), (model, few), lambda core: (0, core)),
            in_hbm(key_gain_row), *angles,
        ],
    )
    normeds, keys_raw, cosines, sines, parts = (results[i : i + 2] for i in range(0, 10, 2))

    ways = [(ring.send_up(part), ring.send_down(part)) for part in parts]

    def project_queries(table_ref, n0, n1, weight, gain, c0, c1, s0, s1, *outs):
        query_kernel((n0, n1), weight, gain, (c0, c1), (s0, s1), outs[:2], outs[2:])

    *queries_raw, first, second = whole_call(
        project_queries,
        table,
        [((rows, each), F32, 1)] * 2 + [((rows, each), BF)] * 2,
        [
            *normeds, (in_hbm(query_weight), (model, each), lambda core: (0, core)),
            in_hbm(query_gain_row), *cosines, *sines,
        ],
    )
    queries = [first, second]

    def places_of(offsets):
        return [(offset, other) for offset in offsets for other in (False, True)]

    steps = ring.half
    calls = {0: ([0], parts)}
    state = None
    token = None
    for step in range(1, steps):
        come = []
        for which in range(2):
            up, down = ways[which]
            if step == 1 and which == 0:
                up, down, queries[0] = tie(up, down, queries[0])
            else:
                up, down, token = tie(up, down, token)
            come.append((up, down))
            if step < steps - 1:
                ways[which] = ring.send_up(up), ring.send_down(down)
            else:
                ways[which] = ring.send_down(down) if which else ring.send_up(up)
            if step == 1 and which == 0:
                state, token = attention_forward(
                    scalars, queries, parts, places_of([0]), None, True, False, come[0]
                )
        blocks = [come[0][0], come[1][0], come[0][1], come[1][1]]
        calls[step] = ([-step, step], blocks)
        state, token = attention_forward(
            scalars, queries, blocks, places_of([-step, step]), state, False, False, [token]
        )
    *ways, token = tie(*ways, token)
    calls[steps] = ([steps], ways)
    *attended, low_keep, low_give, logs, _ = attention_forward(
        scalars, queries, ways, places_of([steps]), state, False, True, [token]
    )
    low_other = ring.sibling(low_give)
    mixed_part = out_projection(ring.table, low_keep, out_weight, False)
    mixed_part = out_projection(ring.table, low_other, out_weight, True, mixed_part)
    mixed_part, cotangent = tie(mixed_part, cotangent)
    mixed_parts = [mixed_part[:span], mixed_part[span:]]
    mixed_others = [partner(part) for part in mixed_parts]
    cotangents = [cotangent, ring.sibling(cotangent)]
    hidden_grad = nt(cotangent, down_weight)
    mixed_others[0], hidden_grad, cotangents = tie(mixed_others[0], hidden_grad, cotangents)

    residual_wide = residual.astype(F32)

    def feed_forward(half, part, other, price):
        rows = slice(half * span, (half + 1) * span)
        mixed, low = add_and_norm(part, other, residual, half, mlp_gain.reshape(1, -1), price)
        gate = nn(low, gate_weight)
        upward = nn(low, up_weight)
        sigmoid_gate = jax.nn.sigmoid(gate)
        activated = gate * sigmoid_gate
        hidden = (activated * upward).astype(BF)
        gate_grad = (
            hidden_grad[rows] * upward * sigmoid_gate * (1.0 + gate * (1.0 - sigmoid_gate))
        ).astype(BF)
        up_grad = (hidden_grad[rows] * activated).astype(BF)
        back = (nt(gate_grad, gate_weight) + nt(up_grad, up_weight)).astype(BF)
        return (mixed, low, hidden, gate_grad, up_grad), back

    upper, upper_back = feed_forward(0, mixed_parts[0], mixed_others[0], 0)
    upper_back, mixed_others[1] = tie(upper_back, mixed_others[1])
    upper_other = partner(upper_back)
    lower, lower_back = feed_forward(1, mixed_parts[1], mixed_others[1], HEAVY)
    lower_other = partner(lower_back)
    mixed, normed_two_low, hidden_low, gate_grad_low, up_grad_low = (
        jnp.concatenate(pair, axis=0) for pair in zip(upper, lower)
    )
    normed_two, scale_two = norm_rows(mixed)

    units = gate_weight.shape[1]
    thirds = 2 * units // model
    chips = ring.chips
    gate_rows = model // 2 // chips
    down_rows = units // thirds // 2 // chips
    down_row = thirds * gate_rows
    out_row = down_row + thirds * down_rows
    packed_shape = (out_row + gate_rows, model)

    def shard_of(chip, core):
        return core * chips + chip

    def columns_of(start):
        moves, done = [], 0
        while done < units:
            tile, column = divmod(start + done, model)
            wide = min(model - column, units - done)
            moves.append(
                (
                    None,
                    slice(done, done + wide),
                    (tile * gate_rows, (tile + 1) * gate_rows),
                    slice(column, column + wide),
                )
            )
            done += wide
        return moves

    everything = slice(None)
    wide = Gradients(
        ring,
        *packed_shape,
        [
            ((model, units), (gate_rows, units), lambda c, k: (shard_of(c, k), 0), columns_of(0)),
            ((model, units), (gate_rows, units), lambda c, k: (shard_of(c, k), 0), columns_of(units)),
            (
                (thirds, units // thirds, model),
                (thirds, down_rows, model),
                lambda c, k: (0, shard_of(c, k), 0),
                [
                    (i, everything, (down_row + i * down_rows, down_row + (i + 1) * down_rows), everything)
                    for i in range(thirds)
                ],
            ),
            (
                (2 * each, model),
                (gate_rows, model),
                lambda c, k: (shard_of(c, k), 0),
                [(None, everything, (out_row, out_row + gate_rows), everything)],
            ),
        ],
    )
    both_grad_low = jnp.concatenate([gate_grad_low, up_grad_low], axis=1)
    both_grads = [both_grad_low, ring.sibling(both_grad_low)]
    both_grads, upper_other = tie(both_grads, upper_other)
    packed, token = products(
        ring.table, [normed_two_low, ring.sibling(normed_two_low)], both_grads, chips,
        (down_row, model), 0, 0, None, [upper_back, lower_back], price=LITTLE,
    )
    wide.packs.append((0, packed))
    packed, token = products(
        ring.table, [hidden_low, ring.sibling(hidden_low)], cotangents, chips,
        (thirds * down_rows, model), 0, 0, None, [token], thirds=thirds,
    )
    wide.packs.append((down_row, packed))
    upper_other, lower_other, token = tie(upper_other, lower_other, token)

    normed_two_grad = jnp.concatenate(
        [both(upper_back, upper_other), both(lower_back, lower_other)], axis=0
    )
    mlp_gain_term = jnp.sum(normed_two_grad * normed_two, axis=0)
    mixed_grad = cotangent.astype(F32) + norm_back(
        normed_two_grad * mlp_gain, normed_two, scale_two
    )
    mixed_grad_low = mixed_grad.astype(BF)
    mixed_grads = [mixed_grad_low, ring.sibling(mixed_grad_low)]
    packed, token = products(
        ring.table, [low_keep, low_give], mixed_grads, chips, (gate_rows, model), 0, 0, None,
        [token], halved=False,
    )
    wide.packs.append((out_row, packed))
    wide_steps = wide.scatter([token])
    wide_way, token = next(wide_steps)
    grads = heads_products(ring.table, mixed_grads, out_weight, [token])
    delta = attention_delta(grads, attended)

    def backward(step, state, after):
        offsets, blocks = calls[step]
        last = step == 0
        return attention_backward(
            scalars, queries, grads, logs, delta, blocks, places_of(offsets), state,
            last, last, last or step == steps, after,
        )

    narrow_rows = query_rows = model // chips
    narrow_shape = (query_rows, each + 2 * few)

    def narrow_out(start, wide):
        return (
            (model, 2 * wide),
            (query_rows, wide),
            lambda c, k: (c, k),
            [(None, everything, (0, query_rows), slice(start, start + wide))],
        )

    narrow = Gradients(
        ring,
        narrow_rows,
        model,
        [
            narrow_out(0, each),
            narrow_out(each, few),
            narrow_out(each + few, few),
        ],
    )
    up, down, token, state = backward(steps, None, [])
    up, down = ring.send_up(up), ring.send_down(down)
    for step in range(steps - 1, 0, -1):
        if step == 1:
            layer_part = matmul(hidden_low, down_weight, [token])
            wide_way, layer_part, token = tie(wide_way, layer_part, token)
            layer_other = partner(layer_part)
        wide_way, wide_token = wide_steps.send((wide_way, [token]))
        back, front, token, state = backward(step, state, [wide_token])
        if step == 1:
            layer_other, token = tie(layer_other, token)
        up, down, token = pair_add([front, back], [up, down], step == steps - 1, [token])
        up, down = ring.send_up(up), ring.send_down(down)
    wide_shard, wide_token = wide_steps.send((wide_way, [token]))
    wide_steps = wide.gather(wide_shard)
    wide_way, wide_ready = next(wide_steps)
    *key_value_own, token, first, second = backward(0, state, [wide_token])

    def back_queries(table_ref, g0, g1, r0, r1, gain, c0, c1, s0, s1, *outs):
        query_back_kernel((g0, g1), (r0, r1), gain, (c0, c1), (s0, s1), *outs)

    query_grad_low, query_gain_term = whole_call(
        back_queries,
        table,
        [((2 * rows, each), BF), ((8, head_dim), F32)],
        [first, second, *map(in_hbm, [*queries_raw, query_gain_row, *cosines, *sines])],
    )
    packed, token = products(
        ring.table, normeds, [query_grad_low], chips, narrow_shape, 0, 0, None, halved=False,
    )

    def own_ready(ready):
        return [(offset, part, False) for offset, part in ready]

    def other_ready(ready):
        return [(offset, ring.sibling(part), True) for offset, part in ready]

    first_other = ring.sibling(wide_shard)
    up, down, first_other, token = tie(up, down, first_other, token)

    def back_keys(table_ref, o0, o1, up_ref, down_ref, r0, r1, gain, c0, c1, s0, s1, *outs):
        key_value_back_kernel(
            (o0, o1), up_ref, down_ref, (r0, r1), gain, (c0, c1), (s0, s1), *outs
        )

    key_value_grad, key_gain_term = whole_call(
        back_keys,
        table,
        [((2 * rows, 2 * few), BF), ((8, head_dim), F32)],
        [
            *key_value_own, up, down, *map(in_hbm, [*keys_raw, key_gain_row, *cosines, *sines]),
        ],
        after=[token],
    )
    packed, token = products(
        ring.table, normeds, [key_value_grad], chips, narrow_shape, 0, each, packed, halved=False,
    )
    narrow.packs = [(0, packed)]
    narrow_steps = narrow.scatter()
    narrow_way, token = next(narrow_steps)
    wide_way, token = tie(wide_way, token)
    wide_way, pair = wide_steps.send(wide_way)
    narrow_way, token = tie(narrow_way, token)
    narrow_way, token = narrow_steps.send((narrow_way, [token]))

    def stacked_pair(ready, token, price=0):
        lot, token = stack([part for _, part in ready], [token], price)
        return (lot, [offset for offset, _ in ready]), token

    def fly(lots, token):
        flown = []
        for lot, offsets in lots:
            lot, token = tie(lot, token)
            other = ring.sibling(lot)
            flown.append((other, offsets))
        return flown, token

    def land(flown, results, token, price=0):
        for other, offsets in flown:
            other, token = tie(other, token)
            results = wide.unpack_stack(other, offsets, results, [token], price)
            token = results[-1]
        return results, token

    lot, token = stacked_pair(pair, token)
    flown, token = fly([lot], token)
    normed_own, normed_give, attn_gain_term = normed_products(
        ring.table, normeds, query_grad_low, key_value_grad, query_weight, key_weight, value_weight,
        [token],
    )
    wide_results, token = land(flown, None, attn_gain_term)
    small = jnp.concatenate(
        [
            jnp.sum(attn_gain_term, axis=0) / attn_gain,
            0.5 * mlp_gain_term,
            jnp.sum(query_gain_term, axis=0),
            jnp.sum(key_gain_term, axis=0),
        ]
    )
    small_rows = 16
    small = jnp.pad(small, (0, small_rows * model - small.shape[0])).reshape(small_rows, model)
    small = small.astype(BF)
    small_other = partner(small)
    narrow_way, normed_give, small_other, token = tie(narrow_way, normed_give, small_other, token)
    narrow_way, token = narrow_steps.send((narrow_way, [token]))
    ready = own_ready(wide_ready + pair) + [(0, first_other, True)]
    wide_way, pair = wide_steps.send(wide_way)
    normed_sibling = ring.sibling(normed_give)
    wide_results = wide.unpack(own_ready(pair), wide_results, [token], HEAVY)
    normed_sibling, token = tie(normed_sibling, wide_results[-1])
    normed_part = both(normed_own, normed_sibling).astype(BF)
    normed_part, token = tie(normed_part, token)
    lot, token = stacked_pair(pair, token, 2)
    ready_lots = [lot]
    normed_other = partner(normed_part)
    narrow_way, token = tie(narrow_way, token)
    for step in range(steps - 3):
        narrow_way, token = narrow_steps.send((narrow_way, [token]))
        if step == 0:
            wide_results = wide.unpack(ready, wide_results, [token], LITTLE)
            token = wide_results[-1]
        if step < steps - 4:
            wide_way, pair = wide_steps.send(wide_way)
            wide_results = wide.unpack(own_ready(pair), wide_results, [token])
            lot, token = stacked_pair(pair, wide_results[-1])
            ready_lots.append(lot)
            wide_way, token = tie(wide_way, token)
    narrow_way, wide_way, normed_other, token = tie(narrow_way, wide_way, normed_other, token)
    wide_way, pair = wide_steps.send(wide_way)
    narrow.extra = [small, small_other]
    narrow_shard, token = narrow_steps.send((narrow_way, [token]))

    gathered = Gradients(ring, narrow_rows + small_rows, model, narrow.outs, small_rows)
    narrow_steps = gathered.gather(narrow_shard, True)
    narrow_way, narrow_ready = next(narrow_steps)

    narrow_results = None
    for step in range(1, steps + 1):
        share = -(-len(ready_lots) // max(1, steps - step)) if step > 1 else 1
        lots, ready_lots = ready_lots[:share], ready_lots[share:]
        own = own_ready(narrow_ready)
        if step == 1:
            flown, token = fly(lots, token)
            wide_results = wide.unpack(own_ready(pair), wide_results, [token], HEAVY)
            lot, token = stacked_pair(pair, wide_results[-1])
            ready_lots.append(lot)
            narrow_ready = [(offset, tie(part, token)[0]) for offset, part in narrow_ready]
            wide_results, token = land(flown, wide_results, token, HEAVY)
        else:
            flown, token = fly(lots, token)
            price = HEAVY
            if step == 2:
                layer_out, residual_grad, token = finish(
                    lax.dynamic_slice_in_dim(span_order, 2 * index, 2), residual, mixed, mixed_grad,
                    [normed_part, normed_other], [layer_part, layer_other], attn_gain.reshape(1, -1),
                    [token], HEAVY,
                )
                wide_way, token = tie(wide_way, token)
                _, pair = wide_steps.send(wide_way)
                wide_results = wide.unpack(own_ready(pair), wide_results, [token], price)
                lot, token = stacked_pair(pair, wide_results[-1])
                ready_lots.append(lot)
                price = 0
            elif not lots:
                narrow_results = gathered.unpack(own, narrow_results, [token], price)
                token = narrow_results[-1]
                own = []
            wide_results, token = land(flown, wide_results, token, price)
        narrow_results = gathered.unpack(own + other_ready(narrow_ready), narrow_results, [token])
        narrow_way, token = tie(narrow_way, narrow_results[-1])
        if step < steps:
            narrow_way, narrow_ready = narrow_steps.send(narrow_way)
    _, narrow_ready = narrow_steps.send(narrow_way)
    narrow_results = gathered.unpack(own_ready(narrow_ready), narrow_results, [token])
    query_sum, key_sum, value_sum, small, _ = gathered.unpack(
        other_ready(narrow_ready), narrow_results
    )
    gate_sum, up_sum, down_sum, out_weight_sum, _, _ = wide_results
    small = small.reshape(-1)

    attn_gain_grad, mlp_gain_grad = small[:model], small[model : 2 * model]
    query_gain_grad = small[2 * model : 2 * model + head_dim]
    key_gain_grad = small[2 * model + head_dim : 2 * model + 2 * head_dim]
    return (
        layer_out,
        residual_grad,
        attn_gain_grad,
        query_sum,
        key_sum,
        value_sum,
        query_gain_grad,
        key_gain_grad,
        out_weight_sum,
        mlp_gain_grad,
        gate_sum,
        up_sum,
        down_sum.reshape(units, model),
    )


def solution(mesh):
    return jax.shard_map(
        functools.partial(body, mesh.shape["cp"]),
        mesh=mesh,
        in_specs=(
            P("cp", None),
            P("cp", None),
            P(),
            P("cp"),
            P(),
            P(None, "tp"),
            P(None, "tp"),
            P(None, "tp"),
            P(),
            P(),
            P("tp", None),
            P(),
            P(None, "tp"),
            P(None, "tp"),
            P("tp", None),
        ),
        out_specs=(
            P("cp", None),
            P("cp", None),
            P(),
            P(None, "tp"),
            P(None, "tp"),
            P(None, "tp"),
            P(),
            P(),
            P("tp", None),
            P(),
            P(None, "tp"),
            P(None, "tp"),
            P("tp", None),
        ),
        check_vma=False,
    )
```
